32 devices in a mesh: dp: 8 (over y, x, core), mp: 4 (over z).
Axes of the slice: x: 2, y: 2, z: 4, core: 2. Of those that a mesh axis runs over, the one named last changes fastest.
Arguments:
- tokens: bfloat16 [32, 2048, 1024], P(('dp', 'mp')), may hold values from -6 to 6
- cotangent: bfloat16 [32, 2048, 1024], P(('dp', 'mp')), may hold values from -6 to 6
- routed: int32 [32, 256], P(('dp', 'mp')), may hold values from 0 to 2047, as said below
- valid_mask: int32 [32, 2048], P(('dp', 'mp')), may hold values 0 or 1
- w_router: float32 [1024], replicated, may hold values from -0.1875 to 0.1875
- first_gain: float32 [1024], replicated, may hold values from 0.25 to 1.75
- query_weight: bfloat16 [1024, 1024], P(None, 'mp'), may hold values from -0.1875 to 0.1875
- key_weight: bfloat16 [1024, 1024], P(None, 'mp'), may hold values from -0.1875 to 0.1875
- value_weight: bfloat16 [1024, 1024], P(None, 'mp'), may hold values from -0.1875 to 0.1875
- output_weight: bfloat16 [1024, 1024], P('mp'), may hold values from -1.5 to 1.5
- second_gain: float32 [1024], replicated, may hold values from 0.25 to 1.75
- up_weight: bfloat16 [1024, 4096], P(None, 'mp'), may hold values from -0.1875 to 0.1875
- down_weight: bfloat16 [4096, 1024], P('mp'), may hold values from -0.09375 to 0.09375
Outputs:
- residual: bfloat16 [32, 2048, 1024], P(('dp', 'mp'))
- grad_tokens: bfloat16 [32, 2048, 1024], P(('dp', 'mp'))
- sublayer_rms: float32 [32], P(('dp', 'mp'))
- grad_router: float32 [1024], replicated
- grad_first: float32 [1024], replicated
- grad_query: float32 [1024, 1024], P('dp', 'mp')
- grad_key: float32 [1024, 1024], P('dp', 'mp')
- grad_value: float32 [1024, 1024], P('dp', 'mp')
- grad_output: float32 [1024, 1024], P('mp', 'dp')
- grad_second: float32 [1024], replicated
- grad_up: float32 [1024, 4096], P('dp', 'mp')
- grad_down: float32 [4096, 1024], P('mp', 'dp')
The draws below stay inside these ranges and needn't reach their ends.
Inputs may be any that keep to these rules, and one draw needn't show every extreme that they name: `routed`: each row holds 256 distinct positions of its sequence in increasing order.
All inputs are finite; a program needn't handle non-finite values. No bound on the sum of `valid_mask` on one device may be relied on, other than what follows from the above.
Results may differ from the reference program's by a relative error of at most 0.018.
Values may be sent and summed in bfloat16 or wider, within the bound.
A program may use at most 256 MiB of HBM per device.

```python
import jax
import jax.numpy as jnp
from jax import lax

D = 1024
HEADS = 16
HEAD_DIM = 64
FF = 4096
LENGTH = 2048
ROUTED = 256
SEQS = 32
N_MP = 4


def draw_routed(key, part):
    key = jax.random.fold_in(key, 7)
    first_key, second_key = jax.random.split(key)
    noise_rank = jax.vmap(lambda row_key: jax.random.permutation(row_key, LENGTH))(jax.random.split(first_key, SEQS))
    bunched = jax.random.randint(second_key, (SEQS, 1), 0, 2)
    position = jnp.arange(LENGTH)[None, :]
    ranking = noise_rank.astype(jnp.int32) + bunched * (position < 2 * ROUTED).astype(jnp.int32) * LENGTH
    chosen = lax.top_k(ranking, ROUTED)[1]
    return jnp.sort(chosen, axis=1).astype(jnp.int32)


def set_ends(values, key, smallest, largest):
    longest = values.shape.index(max(values.shape))
    spots = []
    for shift in (0, 1):
        where = [jax.random.randint(jax.random.fold_in(key, axis), (), 0, length) for axis, length in enumerate(values.shape)]
        where[longest] = (where[longest] + shift) % values.shape[longest]
        spots.append(tuple(where))
    return values.at[spots[0]].set(smallest).at[spots[1]].set(largest)


def raised(array, rng, source, target, blocks, factor):
    owner, partner = [(jnp.arange(array.shape[dim]) // (array.shape[dim] // blocks)).reshape([-1 if axis == dim else 1 for axis in range(array.ndim)]) for dim in (source, target)]
    chosen = jax.random.permutation(rng, blocks)[partner]
    strong = (owner == chosen) | (owner == (partner + blocks // 2) % blocks)
    return jnp.where(strong, factor * array, array)


def block_scale(own_key, extent, pieces, least, largest):
    def one(axis_at, shards_of):
        draws = jax.random.uniform(jax.random.fold_in(jax.random.fold_in(own_key, 6), axis_at), (shards_of,), jnp.float32, least / len(pieces), largest / len(pieces))
        return jnp.repeat(jnp.exp(draws), extent[axis_at] // shards_of).reshape((-1,) + (1,) * (len(extent) - axis_at - 1))

    loudness = one(*pieces[0])
    for cut in pieces[1:]:
        loudness = loudness * one(*cut)
    return loudness


def bell_draw(key, shape, spread, reach, pieces=(), kind=jnp.bfloat16):
    values = spread * jax.random.normal(key, shape, jnp.float32)
    if pieces:
        values = values * block_scale(key, shape, pieces, -0.22, 0.18)
    return jnp.clip(values, -reach, reach).astype(kind)


def noise_with(key, dims, deviation, limit, shards, heavy, kind=jnp.bfloat16):
    values = deviation * jax.random.normal(key, dims, jnp.float32)
    if shards:
        values = values * block_scale(key, dims, shards, -0.22, 0.18)
    return jnp.clip(raised(values, jax.random.fold_in(key, 3), *heavy), -limit, limit).astype(kind)


def setup_inputs(seed: int = 0) -> dict:
    keys = jax.random.split(jax.random.key(seed), 14)
    tokens = noise_with(keys[0], (SEQS, LENGTH, D), 1.0, 6.0, ((0, 32),), (0, 2, 32, 2.75))
    cotangent = noise_with(keys[1], (SEQS, LENGTH, D), 1.0, 6.0, ((0, 32),), (0, 2, 32, 2.75))
    routed = draw_routed(jax.random.fold_in(keys[13], 71), 0)
    valid_mask = set_ends((jax.random.randint(keys[3], (SEQS, LENGTH), 0, 8) < 7).astype(jnp.int32), jax.random.fold_in(keys[3], 1), 0, 1)
    w_router = bell_draw(keys[4], (D,), D ** -0.5, 0.1875, (), jnp.float32)
    first_gain = jnp.clip(1.0 + 0.15 * jax.random.normal(keys[5], (D,), jnp.float32), 0.25, 1.75)
    query_weight = bell_draw(keys[6], (D, HEADS * HEAD_DIM), D ** -0.5, 0.1875, ((1, 4),))
    key_weight = bell_draw(keys[7], (D, HEADS * HEAD_DIM), D ** -0.5, 0.1875, ((1, 4),))
    value_weight = bell_draw(keys[8], (D, HEADS * HEAD_DIM), D ** -0.5, 0.1875, ((1, 4),))
    output_weight = bell_draw(keys[9], (HEADS * HEAD_DIM, D), (HEADS * HEAD_DIM // 64) ** -0.5, 1.5, ((0, 4),))
    second_gain = jnp.clip(1.0 + 0.15 * jax.random.normal(keys[10], (D,), jnp.float32), 0.25, 1.75)
    up_weight = bell_draw(keys[11], (D, FF), D ** -0.5, 0.1875, ((1, 4),))
    down_weight = bell_draw(keys[12], (FF, D), FF ** -0.5, 0.09375, ((0, 4),))
    return dict(tokens=tokens, cotangent=cotangent, routed=routed, valid_mask=valid_mask, w_router=w_router, first_gain=first_gain, query_weight=query_weight, key_weight=key_weight, value_weight=value_weight, output_weight=output_weight, second_gain=second_gain, up_weight=up_weight, down_weight=down_weight)


@jax.custom_vjp
def low(v):
    return lax.optimization_barrier(v.astype(jnp.bfloat16)).astype(jnp.float32)

@jax.custom_vjp
def low_back(v):
    return v

def low_keep(v):
    return (low(v), None)

def low_pass(kept, grad):
    return (grad,)

def back_keep(v):
    return (v, None)

def back_low(kept, grad):
    return (low(grad),)
low.defvjp(low_keep, low_pass)
low_back.defvjp(back_keep, back_low)

def rms_norm(value, gain):
    factor = lax.rsqrt(lax.optimization_barrier(jnp.mean(value * value, axis=-1, keepdims=True)) + 1e-06)
    return value * factor * gain

def matmul(left, right):
    return jnp.dot(left, right, precision=lax.Precision.HIGHEST)

def forward(token_rows, weights, routed_rows, valid_rows):
    w_router, first_gain, query_weight, key_weight, value_weight, output_weight, second_gain, up_weight, down_weight = weights
    chosen = jnp.take(token_rows, routed_rows, axis=0)
    chosen_valid = jnp.take(valid_rows, routed_rows, axis=0).astype(jnp.float32)
    gate_value = matmul(chosen, w_router) * chosen_valid
    normed = low(rms_norm(chosen, first_gain))
    query_rows = low(low_back(matmul(normed, query_weight))).reshape(ROUTED, HEADS, HEAD_DIM)
    key_rows = low(low_back(matmul(normed, key_weight))).reshape(ROUTED, HEADS, HEAD_DIM)
    value_rows = low(low_back(matmul(normed, value_weight))).reshape(ROUTED, HEADS, HEAD_DIM)
    raw_scores = jnp.einsum('qhe,khe->hqk', query_rows, key_rows, precision=lax.Precision.HIGHEST) * HEAD_DIM ** (-0.5)
    rank_order = jnp.arange(ROUTED)
    causal = rank_order[:, None] >= rank_order[None, :]
    scores = jnp.where(causal[None], low_back(raw_scores), -1e+30)
    attention = jax.nn.softmax(scores, axis=-1)
    context = jnp.einsum('hqk,khe->qhe', low(attention), value_rows, precision=lax.Precision.HIGHEST)
    context = low(low_back(context)).reshape(ROUTED, N_MP, HEADS * HEAD_DIM // N_MP)
    attn_parts = jnp.einsum('kgc,gcd->gkd', context, output_weight.reshape(N_MP, HEADS * HEAD_DIM // N_MP, D), precision=lax.Precision.HIGHEST)
    attended = low_back(lax.optimization_barrier(jnp.sum(low(attn_parts), axis=0)))
    mixed_rows = chosen + attended
    normed_two = low(rms_norm(mixed_rows, second_gain))
    upward = low_back(matmul(normed_two, up_weight))
    active = low(jax.nn.gelu(upward, approximate=False)).reshape(ROUTED, N_MP, FF // N_MP)
    down_parts = jnp.einsum('kgf,gfd->gkd', active, down_weight.reshape(N_MP, FF // N_MP, D), precision=lax.Precision.HIGHEST)
    feed = low_back(lax.optimization_barrier(jnp.sum(low(down_parts), axis=0)))
    update = gate_value[:, None] * (attended + feed)
    result = token_rows.at[routed_rows].add(update)
    return (result, jnp.sum(update * update))

def reference(tokens, cotangent, routed, valid_mask, w_router, first_gain, query_weight, key_weight, value_weight, output_weight, second_gain, up_weight, down_weight):
    params = tuple((weight.astype(jnp.float32) for weight in (w_router, first_gain, query_weight, key_weight, value_weight, output_weight, second_gain, up_weight, down_weight)))

    def one_sequence(totals, items):
        token_rows, cot_rows, routed_rows, valid_rows = items

        def run(token_float, *weights):
            return forward(token_float, weights, routed_rows, valid_rows)
        result, pull_back, squares = jax.vjp(run, token_rows.astype(jnp.float32), *params, has_aux=True)
        grads = pull_back(cot_rows.astype(jnp.float32))
        count = jnp.sum(valid_rows.astype(jnp.float32))
        sublayer = jnp.sqrt(squares / (D * jnp.maximum(count, 1.0)))
        totals = jax.tree.map(jnp.add, totals, tuple(grads[1:]))
        return (totals, (result.astype(jnp.bfloat16), grads[0].astype(jnp.bfloat16), sublayer))
    start_sums = tuple((jnp.zeros_like(weight) for weight in params))
    sums, outputs = lax.scan(one_sequence, start_sums, (tokens, cotangent, routed, valid_mask))
    residual, grad_tokens, sublayer_rms = outputs
    return (residual, grad_tokens, sublayer_rms, sums[0], sums[1], sums[2], sums[3], sums[4], sums[5], sums[6], sums[7], sums[8])
```

```python
import functools
import math

import jax
import jax.numpy as jnp
from jax import lax
from jax.experimental import pallas as pl
from jax.experimental.pallas import tpu as pltpu
from jax.sharding import PartitionSpec as P

HEADS = 16
HEAD_DIM = 64
EPS = 1e-06
F32 = jnp.float32
BF16 = jnp.bfloat16
TILE = 64


def mm(left, right):
    return jnp.dot(left, right, preferred_element_type=F32)


def mm_nt(left, right):
    return lax.dot_general(left, right, (((1,), (1,)), ((), ())), preferred_element_type=F32)


def mm_tn(left, right):
    return lax.dot_general(left, right, (((0,), (0,)), ((), ())), preferred_element_type=F32)


def row_tiles(rows, body, init=0):
    def step(index, carry):
        return body(pl.ds(pl.multiple_of(index * TILE, TILE), TILE), carry)

    return lax.fori_loop(0, rows // TILE, step, init)


def fold_rows(value):
    return jnp.sum(value.reshape(-1, 8, value.shape[-1]), axis=0)


def gelu_both(value):
    cdf = 0.5 * (1.0 + lax.erf(value * math.sqrt(0.5)))
    density = jnp.exp(-0.5 * value * value) * (1.0 / math.sqrt(2.0 * math.pi))
    return value * cdf, cdf + value * density


def block_kernel(size, *refs):
    shards, ybit, rows, width, length = size["S"], size["ybit"], size["R"], size["D"], size["L"]
    heads, narrow, hidden, cut = size["hh"], size["n"], size["f"], size["DB"]
    joined = size["joined"]
    quarter = 2 * cut
    refs = list(refs)

    def take(count):
        taken, refs[:count] = refs[:count], []
        return taken

    tokens, cotangent, routed, valid, w_router, first_gain, second_gain = take(7)
    qkv_in = take(1 if joined else 3)
    out_in, up_in, down_in = take(3)
    rows_res, rows_grad, rms_out, small_out, attn_out, feed_out = take(6)
    w_qkv, w_out, w_up, w_down = take(4)
    h1, dfeed, h2, datt, turn_a, turn_b = take(6)
    qkv, ctx, prob, act, dup = take(5)
    dqkv = take(1)[0] if joined else act.at[0, :, 0 : 3 * narrow]
    total, wide, sent, got = take(4)
    own_z, own_c, attended, dmixed, feed_own, columns = take(6)
    lane = lax.broadcasted_iota(jnp.int32, (1, 128), 1)

    def column(k, at):
        return columns[at][:, k : k + 1]

    def set_column(k, at, value):
        columns[at] = jnp.where(lane == k, value, columns[at])

    gate, live, dscore = (functools.partial(column, k) for k in range(3))
    grads, core_f, y_f, z_f, core_a, y_a, z_a, swap_f, swap_a = take(9)
    small_send, small_got = take(2)
    load_sem, tok_sem = take(2)
    wz_s, wz_r, wy_s, wy_r, wc_s, wc_r = take(6)
    x_s, x_r = take(2)
    gc_s, gc_r, gy_s, gy_r, gz_s, gz_r, gx_s, gx_r = take(8)
    sm_s, sm_r = take(2)

    dp = lax.axis_index("dp")
    z = lax.axis_index("mp")
    core = lax.rem(dp, 2)
    x = lax.rem(lax.div(dp, 2), 2)
    y = lax.rem(lax.div(dp, ybit), 2)
    core_dev = (dp + 1 - 2 * core, z)
    x_dev = (dp + 2 * (1 - 2 * x), z)
    y_dev = (dp + ybit * (1 - 2 * y), z)
    up_dev = (dp, z + 1)
    down_dev = (dp, z - 1)
    z_bits = [1 << k for k in range(int(math.log2(shards)))]
    z_partners = [(dp, z + bit * (1 - 2 * lax.rem(lax.div(z, bit), 2))) for bit in z_bits]

    def remote(src, dst, send, recv, device):
        return pltpu.make_async_remote_copy(
            src_ref=src,
            dst_ref=dst,
            send_sem=send,
            recv_sem=recv,
            device_id=device,
            device_id_type=pl.DeviceIdType.MESH,
        )

    barrier = pltpu.get_barrier_semaphore()

    def greet(device):
        pl.semaphore_signal(barrier, inc=1, device_id=device, device_id_type=pl.DeviceIdType.MESH)

    for device in [core_dev, x_dev, y_dev] + z_partners[1:]:
        greet(device)

    @pl.when(z > 0)
    def _():
        greet(down_dev)

    @pl.when(z < shards - 1)
    def _():
        greet(up_dev)

    ends = jnp.where(z == 0, 1, 0) + jnp.where(z == shards - 1, 1, 0)
    pl.semaphore_wait(barrier, 4 + len(z_partners) - ends)

    def order(j):
        high = lax.div(z, shards // 2)
        base = z + high * (shards - 1 - 2 * z)
        odd = lax.rem(j, 2)
        near = base + lax.div(j + 1, 2) * (2 * odd - 1)
        pick = jnp.where(j <= 2 * base, near, j)
        return pick + high * (shards - 1 - 2 * pick)

    attn_mats = list(range(len(qkv_in) + 1))
    feed_mats = [len(attn_mats), len(attn_mats) + 1]
    out_at, up_at = attn_mats[-1], feed_mats[0]

    def span(qy, qc):
        return pl.ds(pl.multiple_of((2 * qy + qc) * quarter, quarter), quarter)

    def lanes(count):
        return pl.ds(pl.multiple_of(x * count, count), count)

    def held(i, s, qy, qc):
        if i < out_at:
            part = w_qkv if joined else w_qkv.at[:, :, i * narrow : (i + 1) * narrow]
            return part.at[s, span(qy, qc)]
        if i == out_at:
            return w_out.at[s, :, span(qy, qc)]
        if i == up_at:
            return w_up.at[s, qy, qc]
        return w_down.at[s, :, span(qy, qc)]

    def own_piece(i):
        if i < out_at:
            part = qkv_in[i].at[span(y, core)]
            return part if joined else part.at[:, lanes(narrow)]
        if i == out_at:
            return out_in.at[lanes(narrow), span(y, core)]
        if i == up_at:
            return up_in.at[y, core, :, :, lanes(hidden)]
        return down_in.at[lanes(hidden), span(y, core)]

    def load_own(i):
        if i < out_at:
            if joined:
                src, dst = qkv_in[i], w_qkv.at[z]
            else:
                src, dst = qkv_in[i].at[:, lanes(narrow)], w_qkv.at[z, :, i * narrow : (i + 1) * narrow]
        elif i == out_at:
            src, dst = out_in.at[lanes(narrow), :], w_out.at[z]
        elif i == up_at:
            src, dst = up_in.at[:, :, :, :, lanes(hidden)], w_up.at[z]
        else:
            src, dst = down_in.at[lanes(hidden), :], w_down.at[z]
        return pltpu.make_async_copy(src, dst, load_sem.at[i])

    def own_up(i):
        return remote(own_piece(i), held(i, z, y, core), wz_s.at[i, z], wz_r.at[i, z], up_dev)

    def own_down(i):
        return remote(own_piece(i), held(i, z, y, core), wz_s.at[i, shards], wz_r.at[i, z], down_dev)

    def pass_on(i, s, device):
        piece = held(i, s, y, core)
        return remote(piece, piece, wz_s.at[i, s], wz_r.at[i, s], device)

    def across_y(i, s, qy):
        piece = held(i, s, qy, core)
        return remote(piece, piece, wy_s.at[i, s], wy_r.at[i, s], y_dev)

    def across_core(i, s, qy, qc, slot):
        piece = held(i, s, qy, qc)
        return remote(piece, piece, wc_s.at[i, slot, s], wc_r.at[i, slot, s], core_dev)

    def send_own(mats):
        @pl.when(z < shards - 1)
        def _():
            for i in mats:
                own_up(i).start()

        @pl.when(z > 0)
        def _():
            for i in mats:
                own_down(i).start()

    def passing(s, action):
        @pl.when((s < z) & (z < shards - 1))
        def _():
            action(up_dev)

        @pl.when((s > z) & (z > 0))
        def _():
            action(down_dev)

    def arrive(mats, j):
        s = order(j)
        for i in mats:
            pass_on(i, s, up_dev).wait_recv()
            passing(s, lambda device: pass_on(i, s, device).start())
            across_y(i, s, y).start()
            across_core(i, s, y, core, 0).start()

    def complete(mats, j):
        s = order(j)
        for i in mats:
            across_y(i, s, 1 - y).wait_recv()
            across_core(i, s, 1 - y, core, 1).start()
        for i in mats:
            across_core(i, s, y, 1 - core, 0).wait_recv()
            across_core(i, s, 1 - y, 1 - core, 1).wait_recv()

    def drain(mats):
        @pl.when(z < shards - 1)
        def _():
            for i in mats:
                own_up(i).wait_send()

        @pl.when(z > 0)
        def _():
            for i in mats:
                own_down(i).wait_send()

        def step(j, carry):
            s = order(j)
            for i in mats:
                passing(s, lambda device: pass_on(i, s, device).wait_send())
                across_y(i, s, y).wait_send()
                across_core(i, s, y, core, 0).wait_send()
                across_core(i, s, 1 - y, core, 1).wait_send()
            return carry

        lax.fori_loop(1, shards, step, 0)

    def exchange(slot, src, dst):
        return remote(src, dst, x_s.at[slot], x_r.at[slot], x_dev)

    x_h1 = exchange(0, h1.at[0], h1.at[1])
    x_dfeed = exchange(1, dfeed.at[0], dfeed.at[1])
    x_att = exchange(2, sent.at[0], got.at[0])
    x_h2 = exchange(3, h2.at[0], h2.at[1])
    x_dh2 = exchange(4, sent.at[0], got.at[0])
    x_feed = exchange(5, sent.at[1], got.at[1])
    x_datt = exchange(6, datt.at[0], datt.at[1])
    x_dh1 = exchange(7, sent.at[0], got.at[0])

    send_own(attn_mats)
    steps = length // rows

    def block_loads(t):
        slot = lax.rem(t, 2)
        where = pl.ds(pl.multiple_of(t * rows, rows), rows)
        return (
            pltpu.make_async_copy(tokens.at[0, where], got.at[slot], tok_sem.at[0, slot]),
            pltpu.make_async_copy(cotangent.at[0, where], sent.at[slot], tok_sem.at[1, slot]),
        )

    for copy in block_loads(0):
        copy.start()
    for i in attn_mats + feed_mats:
        load_own(i).start()

    as_rows = jnp.broadcast_to(routed[...].astype(F32), (8, rows))
    position = jnp.transpose(as_rows)[:, 0:1].astype(jnp.int32)
    total[...] = jnp.zeros_like(total)

    def gather(t, flags):
        @pl.when(t + 1 < steps)
        def _():
            for copy in block_loads(t + 1):
                copy.start()

        slot = lax.rem(t, 2)
        for copy in block_loads(t):
            copy.wait()
        hit = position == t * rows + lax.broadcasted_iota(jnp.int32, (rows, rows), 1)
        chosen = jnp.where(hit, 1.0, 0.0)
        pick = chosen.astype(BF16)
        total[0] += mm(pick, got[slot])
        total[1] += mm(pick, sent[slot])
        mask = valid[:, pl.ds(pl.multiple_of(t * rows, rows), rows)].astype(F32)
        return flags + jnp.sum(chosen * mask, axis=1, keepdims=True)

    flags = lax.fori_loop(0, steps, gather, jnp.zeros((rows, 1), F32))
    columns[...] = jnp.broadcast_to(flags, columns.shape)

    def prepare(at, carry):
        row, cot = total[0, at], total[1, at]
        own_z[at] = row.astype(BF16)
        own_c[at] = cot.astype(BF16)
        gate_here = jnp.sum(row * w_router[...], axis=1, keepdims=True) * live(at)
        set_column(0, at, gate_here)
        factor = lax.rsqrt(jnp.mean(row * row, axis=1, keepdims=True) + EPS)
        h1[0, at] = (row * factor * first_gain[...]).astype(BF16)
        dfeed[0, at] = (gate_here * cot).astype(BF16)
        return carry

    row_tiles(rows, prepare)
    x_h1.start()

    lane_head = lax.div(lax.broadcasted_iota(jnp.int32, (1, narrow), 1), HEAD_DIM)
    masks = [jnp.where(lane_head == h, 1.0, 0.0) for h in range(heads)]
    masks_low = [mask.astype(BF16) for mask in masks]

    def stacked(value):
        return jnp.concatenate([value * mask for mask in masks_low], axis=0) if heads > 1 else value

    def unstacked(value):
        if heads == 1:
            return value
        picked = value[0:rows] * masks[0]
        for h in range(1, heads):
            picked = picked + value[h * rows : (h + 1) * rows] * masks[h]
        return picked

    score_shape = (heads * rows, rows)
    causal = lax.rem(lax.broadcasted_iota(jnp.int32, score_shape, 0), rows) >= lax.broadcasted_iota(
        jnp.int32, score_shape, 1
    )

    for i in attn_mats:
        load_own(i).wait()
    x_h1.wait_recv()
    x_dfeed.start()

    def attend(j, carry):
        s = order(j)

        @pl.when(j + 1 < shards)
        def _():
            arrive(attn_mats, j + 1)

        @pl.when(j + 1 == shards)
        def _():
            send_own(feed_mats)

        @pl.when(j > 0)
        def _():
            complete(attn_mats, j)

        low = mm(h1[...].reshape(2 * rows, width), w_qkv[s]).astype(BF16)
        query = low[:, 0:narrow] * jnp.asarray(HEAD_DIM**-0.5, BF16)
        qkv[s] = jnp.concatenate([query, low[:, narrow:]], axis=1).reshape(2, rows, 3 * narrow)
        for half in range(2):
            query = qkv[s, half, :, 0:narrow]
            key = qkv[s, half, :, narrow : 2 * narrow]
            value = qkv[s, half, :, 2 * narrow : 3 * narrow]
            scores = jnp.where(causal, mm_nt(stacked(query), key), -1e30)
            raised = jnp.exp(scores - jnp.max(scores, axis=1, keepdims=True))
            weights = (raised / jnp.sum(raised, axis=1, keepdims=True)).astype(BF16)
            prob[s, half] = weights
            ctx[s, half * rows : (half + 1) * rows] = unstacked(mm(weights, value)).astype(BF16)
        return carry

    lax.fori_loop(0, shards, attend, 0)

    def project_out(half):
        parts = [ctx[s, half * rows : (half + 1) * rows] for s in range(shards)]
        return mm(jnp.concatenate(parts, axis=1), w_out[...].reshape(shards * narrow, width))

    sent[0] = project_out(1).astype(BF16)
    x_att.start()
    attended[...] = project_out(0)
    arrive(feed_mats, 1)
    x_att.wait()

    def mix(at, carry):
        att = attended[at] + got[0, at].astype(F32)
        attended[at] = att
        mixed = own_z[at].astype(F32) + att
        factor = lax.rsqrt(jnp.mean(mixed * mixed, axis=1, keepdims=True) + EPS)
        h2[0, at] = (mixed * factor * second_gain[...]).astype(BF16)
        return carry

    row_tiles(rows, mix)
    x_h2.start()
    x_dfeed.wait_recv()
    arrive(feed_mats, 2)
    x_h2.wait_recv()

    total[...] = jnp.zeros_like(total)
    for i in feed_mats:
        load_own(i).wait()

    def feed_step(j, carry):
        s = order(j)

        @pl.when((j > 0) & (j + 2 < shards))
        def _():
            arrive(feed_mats, j + 2)

        @pl.when(j > 0)
        def _():
            complete(feed_mats, j)

        up_here = w_up[s].reshape(width, hidden)
        wide[0] = mm(h2[...].reshape(2 * rows, width), up_here)
        wide[1] = mm_nt(dfeed[...].reshape(2 * rows, width), w_down[s])

        def turn(at, inner):
            active, slope = gelu_both(wide[0, at])
            act[s, at] = active.astype(BF16)
            dup[s, at] = (wide[1, at] * slope).astype(BF16)
            return inner

        row_tiles(2 * rows, turn)
        total[...] += mm_nt(dup[s], up_here).reshape(2, rows, width)
        return carry

    lax.fori_loop(0, shards, feed_step, 0)
    sent[0] = total[1].astype(BF16)
    x_dh2.start()

    def feed_rows(half):
        value = mm(act[0, half * rows : (half + 1) * rows], w_down[0])
        for s in range(1, shards):
            value += mm(act[s, half * rows : (half + 1) * rows], w_down[s])
        return value

    sent[1] = feed_rows(1).astype(BF16)
    feed_own[...] = feed_rows(0)

    def core_send(group, buf, into, s, at=None):
        src = buf.at[s, :, :, 1 - core]
        return remote(src, into.at[s], gc_s.at[group, s], gc_r.at[group, s], core_dev)

    def y_send(group, buf, into, s):
        return remote(buf.at[s, 1 - y, :, core], into.at[s], gy_s.at[group, s], gy_r.at[group, s], y_dev)

    def z_send(group, buf, into, s, device, slot):
        src = buf.at[s, y, :, core]
        return remote(src, into.at[slot], gz_s.at[group, s], gz_r.at[group, slot], device)

    def add_into(ref, *others):
        value = ref[...].astype(F32)
        for other in others:
            value = value + other[...].astype(F32)
        ref[...] = value.astype(BF16)

    def stage_core(group, buf, core_got, y_got, s):
        core_send(group, buf, core_got, s).wait_recv()
        for a in range(2):
            for b in range(2):
                add_into(buf.at[s, a, b, core], core_got.at[s, a, b])
        y_send(group, buf, y_got, s).start()

    def stage_y(group, buf, y_got, s):
        y_send(group, buf, y_got, s).wait_recv()
        for b in range(2):
            add_into(buf.at[s, y, b, core], y_got.at[s, b])

    def line_in(group, buf, z_got, s, slot):
        z_send(group, buf, z_got, s, up_dev, slot).wait_recv()
        for b in range(2):
            add_into(buf.at[s, y, b, core], z_got.at[slot, b])

    def stage_z(group, buf, z_got, s, action):
        @pl.when(s > z)
        def _():
            if action == "start":

                @pl.when(z > 0)
                def _():
                    line_in(group, buf, z_got, s, s)

            copy = z_send(group, buf, z_got, s, up_dev, s)
            copy.start() if action == "start" else copy.wait_send()

        @pl.when(s < z)
        def _():
            if action == "start":

                @pl.when(z < shards - 1)
                def _():
                    line_in(group, buf, z_got, s, s)

            slot = jnp.where(s == z - 1, shards, s)
            copy = z_send(group, buf, z_got, s, down_dev, slot)
            copy.start() if action == "start" else copy.wait_send()

    def swap(group, pair):
        return remote(pair.at[0], pair.at[1], gx_s.at[group], gx_r.at[group], x_dev)

    def stage_last(group, buf, z_got, pair, out):
        for b in range(2):
            out[b] = buf[z, y, b, core].astype(F32)

        @pl.when(z > 0)
        def _():
            z_send(group, buf, z_got, z, up_dev, z).wait_recv()
            out[...] += z_got[z].astype(F32)

        @pl.when(z < shards - 1)
        def _():
            z_send(group, buf, z_got, z, up_dev, shards).wait_recv()
            out[...] += z_got[shards].astype(F32)

        pair[0] = out[1 - x].astype(BF16)
        swap(group, pair).start()

    def stage_out(group, pair, out):
        swap(group, pair).wait_recv()
        out[1 - x] = pair[1].astype(F32)

    def reversed_order(k):
        return order(shards - 1 - k)

    def store_grads(buf, s, left, right, lo, count):
        for a in range(2):
            for b in range(2):
                start = (2 * a + b) * quarter
                value = mm(left[start : start + quarter, :], right).astype(BF16)
                buf[s, a, b, :, :, lo : lo + count] = value.reshape(2, cut, count)

    turn_a[...] = jnp.transpose(h2[...].reshape(2 * rows, width))
    turn_b[...] = jnp.transpose(dfeed[...].reshape(2 * rows, width))

    def feed_grads(k, carry):
        s = reversed_order(k)
        store_grads(grads, s, turn_a, dup[s], 0, hidden)
        store_grads(grads, s, turn_b, act[s], hidden, hidden)
        core_send(0, grads, core_f, s).start()

        @pl.when(k > 0)
        def _():
            stage_core(0, grads, core_f, y_f, reversed_order(k - 1))

        return carry

    x_dh2.wait()

    def second_back(at, carry):
        dh2 = total[0, at] + got[0, at].astype(F32)
        mixed = own_z[at].astype(F32) + attended[at]
        factor = lax.rsqrt(jnp.mean(mixed * mixed, axis=1, keepdims=True) + EPS)
        scaled = dh2 * second_gain[...]
        back = factor * scaled - mixed * (factor**3 * jnp.mean(mixed * scaled, axis=1, keepdims=True))
        dmixed[at] = back
        datt[0, at] = (gate(at) * own_c[at].astype(F32) + back).astype(BF16)
        return carry + fold_rows(dh2 * mixed * factor)

    second_sum = row_tiles(rows, second_back, jnp.zeros((8, width), F32))
    x_datt.start()
    x_feed.start()

    lax.fori_loop(0, shards, feed_grads, 0)
    stage_core(0, grads, core_f, y_f, z)
    x_datt.wait_recv()

    drain(feed_mats)
    turn_a[...] = jnp.transpose(h1[...].reshape(2 * rows, width))
    turn_b[...] = jnp.transpose(datt[...].reshape(2 * rows, width))
    total[...] = jnp.zeros_like(total)

    def attend_back(k, carry):
        s = reversed_order(k)
        dctx = mm_nt(datt[...].reshape(2 * rows, width), w_out[s]).astype(BF16)
        for half in range(2):
            query = qkv[s, half, :, 0:narrow]
            key = qkv[s, half, :, narrow : 2 * narrow]
            value = qkv[s, half, :, 2 * narrow : 3 * narrow]
            weights = prob[s, half]
            dhead = stacked(dctx[half * rows : (half + 1) * rows])
            dweights = mm_nt(dhead, value)
            full = weights.astype(F32)
            dscores = full * (dweights - jnp.sum(dweights * full, axis=1, keepdims=True))
            dscores = dscores.astype(BF16)
            dquery = unstacked(mm(dscores, key)) * HEAD_DIM**-0.5
            dkey = mm_tn(dscores, stacked(query))
            dvalue = mm_tn(weights, dhead)
            dqkv[half * rows : (half + 1) * rows] = jnp.concatenate([dquery, dkey, dvalue], axis=1).astype(BF16)
        total[...] += mm_nt(dqkv[...], w_qkv[s]).reshape(2, rows, width)
        store_grads(w_up, s, turn_a, dqkv[...], 0, 3 * narrow)
        store_grads(w_up, s, turn_b, ctx[s], 3 * narrow, narrow)
        core_send(1, w_up, core_a, s).start()
        return carry

    lax.fori_loop(0, shards, attend_back, 0)
    sent[0] = total[1].astype(BF16)
    x_dh1.start()

    x_feed.wait()

    def finish_forward(at, squares):
        branch = attended[at] + feed_own[at] + got[1, at].astype(F32)
        update = gate(at) * branch
        rows_res[at] = (own_z[at].astype(F32) + update).astype(BF16)
        dgate = jnp.sum(own_c[at].astype(F32) * branch, axis=1, keepdims=True)
        set_column(2, at, dgate * live(at))
        return squares + fold_rows(update * update)

    squares = row_tiles(rows, finish_forward, jnp.zeros((8, width), F32))
    count = jnp.sum(valid[...].astype(F32), axis=1, keepdims=True)
    energy = jnp.sum(jnp.sum(squares, axis=0, keepdims=True), axis=1, keepdims=True)
    rms_out[...] = jnp.broadcast_to(jnp.sqrt(energy / (width * jnp.maximum(count, 1.0))), rms_out.shape)

    def feed_line(k, carry):
        s = reversed_order(k)
        stage_y(0, grads, y_f, s)
        stage_z(0, grads, z_f, s, "start")
        return carry

    lax.fori_loop(0, shards - 1, feed_line, 0)
    stage_y(0, grads, y_f, z)
    stage_last(0, grads, z_f, swap_f, feed_out)

    def attn_core(k, carry):
        stage_core(1, w_up, core_a, y_a, reversed_order(k))
        return carry

    lax.fori_loop(0, shards, attn_core, 0)

    x_dh1.wait()

    def first_back(at, sums):
        dh1 = total[0, at] + got[0, at].astype(F32)
        row = own_z[at].astype(F32)
        factor = lax.rsqrt(jnp.mean(row * row, axis=1, keepdims=True) + EPS)
        scaled = dh1 * first_gain[...]
        back = factor * scaled - row * (factor**3 * jnp.mean(row * scaled, axis=1, keepdims=True))
        back = back + dmixed[at] + dscore(at) * w_router[...]
        rows_grad[at] = (own_c[at].astype(F32) + back).astype(BF16)
        return sums[0] + fold_rows(dscore(at) * row), sums[1] + fold_rows(dh1 * row * factor)

    zero = jnp.zeros((8, width), F32)
    router_sum, first_sum = row_tiles(rows, first_back, (zero, zero))
    parts = [jnp.sum(part, axis=0, keepdims=True) for part in (router_sum, first_sum, second_sum)]
    small = jnp.concatenate(parts + [jnp.zeros((5, width), F32)], axis=0)
    for k, device in enumerate([core_dev, x_dev, y_dev] + z_partners):
        small_send[k] = small
        copy = remote(small_send.at[k], small_got.at[k], sm_s.at[k], sm_r.at[k], device)
        copy.start()
        copy.wait()
        small = small + small_got[k]
    small_out[...] = small

    def attn_line(k, carry):
        s = reversed_order(k)
        stage_y(1, w_up, y_a, s)
        stage_z(1, w_up, z_a, s, "start")
        return carry

    lax.fori_loop(0, shards - 1, attn_line, 0)
    stage_y(1, w_up, y_a, z)
    stage_last(1, w_up, z_a, swap_a, attn_out)
    stage_out(0, swap_f, feed_out)
    stage_out(1, swap_a, attn_out)

    drain(attn_mats)
    for copy in (x_h1, x_dfeed, x_h2, x_datt):
        copy.wait_send()

    def drain_grads(k, carry):
        s = reversed_order(k)
        for group, buf, core_got, y_got, z_got in (
            (0, grads, core_f, y_f, z_f),
            (1, w_up, core_a, y_a, z_a),
        ):
            core_send(group, buf, core_got, s).wait_send()
            y_send(group, buf, y_got, s).wait_send()
            stage_z(group, buf, z_got, s, "wait")
        return carry

    lax.fori_loop(0, shards, drain_grads, 0)
    swap(0, swap_f).wait_send()
    swap(1, swap_a).wait_send()


def run_block(size, operands):
    shards, rows, width = size["S"], size["R"], size["D"]
    heads, narrow, hidden, cut = size["hh"], size["n"], size["f"], size["DB"]
    mats = (2 if size["joined"] else 4) + 2
    stages = 3 + int(math.log2(shards))
    attn, feed = 4 * narrow, 2 * hidden
    dma = pltpu.SemaphoreType.DMA
    vmem = lambda *shape: pltpu.VMEM(shape, BF16)
    full = lambda *shape: pltpu.VMEM(shape, F32)
    scratch = [
        vmem(shards, width, 3 * narrow),
        vmem(shards, narrow, width),
        vmem(shards, 2, 2, 2, cut, hidden),
        vmem(shards, hidden, width),
        *[vmem(2, rows, width) for _ in range(4)],
        *[vmem(width, 2 * rows) for _ in range(2)],
        vmem(shards, 2, rows, 3 * narrow),
        vmem(shards, 2 * rows, narrow),
        vmem(shards, 2, heads * rows, rows),
        vmem(shards, 2 * rows, hidden),
        vmem(shards, 2 * rows, hidden),
        *([vmem(2 * rows, 3 * narrow)] if size["joined"] else []),
        full(2, rows, width),
        full(2, 2 * rows, hidden),
        vmem(2, rows, width),
        vmem(2, rows, width),
        vmem(rows, width),
        vmem(rows, width),
        *[full(rows, width) for _ in range(3)],
        full(rows, 128),
        vmem(shards, 2, 2, 2, cut, feed),
        vmem(shards, 2, 2, cut, feed),
        vmem(shards, 2, cut, feed),
        vmem(shards + 1, 2, cut, feed),
        vmem(shards, 2, 2, cut, attn),
        vmem(shards, 2, cut, attn),
        vmem(shards + 1, 2, cut, attn),
        vmem(2, cut, feed),
        vmem(2, cut, attn),
        full(stages, 8, width),
        full(stages, 8, width),
        dma((mats,)),
        dma((2, 2)),
        dma((mats, shards + 1)),
        dma((mats, shards)),
        dma((mats, shards)),
        dma((mats, shards)),
        dma((mats, 2, shards)),
        dma((mats, 2, shards)),
        dma((8,)),
        dma((8,)),
        *[dma((2, shards)) for _ in range(5)],
        dma((2, shards + 1)),
        dma((2,)),
        dma((2,)),
        dma((stages,)),
        dma((stages,)),
    ]
    near = pl.BlockSpec(memory_space=pltpu.VMEM)
    far = pl.BlockSpec(memory_space=pl.ANY)
    outs = [
        jax.ShapeDtypeStruct((rows, width), BF16),
        jax.ShapeDtypeStruct((rows, width), BF16),
        jax.ShapeDtypeStruct((8, 128), F32),
        jax.ShapeDtypeStruct((8, width), F32),
        jax.ShapeDtypeStruct((2, cut, attn), F32),
        jax.ShapeDtypeStruct((2, cut, feed), F32),
    ]
    return pl.pallas_call(
        functools.partial(block_kernel, size),
        out_shape=outs,
        in_specs=[far, far] + [near] * 5 + [far] * (len(operands) - 7),
        out_specs=[near] * len(outs),
        scratch_shapes=scratch,
        compiler_params=pltpu.CompilerParams(
            collective_id=0, has_side_effects=True, vmem_limit_bytes=64 * 2**20 - 65536
        ),
    )(*operands)


def place_kernel(size, assemble, routed, tok, cot, rows_res, rows_grad, attn, feed, *outs):
    block, count = tok.shape[0], routed.shape[1]
    step = pl.program_id(0)
    line = step * block + lax.broadcasted_iota(jnp.int32, (block, count), 0)
    chosen = jnp.where(line == routed[...], 1.0, 0.0)
    taken = jnp.sum(chosen, axis=1, keepdims=True) > 0.0
    pick = chosen.astype(BF16)
    outs[0][...] = jnp.where(taken, mm(pick, rows_res[...]), tok[...].astype(F32)).astype(BF16)
    outs[1][...] = jnp.where(taken, mm(pick, rows_grad[...]), cot[...].astype(F32)).astype(BF16)
    if assemble:

        @pl.when(step == 0)
        def _():
            for ref, value in zip(outs[2:], weight_outputs(size, attn, feed)):
                ref[...] = value


def weight_outputs(size, attn, feed):
    narrow, hidden = size["n"], size["f"]

    def side_by_side(ref, lo, count):
        return jnp.concatenate([ref[0, :, lo : lo + count], ref[1, :, lo : lo + count]], axis=1)

    return (
        side_by_side(attn, 0, narrow),
        side_by_side(attn, narrow, narrow),
        side_by_side(attn, 2 * narrow, narrow),
        side_by_side(attn, 3 * narrow, narrow).T,
        side_by_side(feed, 0, hidden),
        side_by_side(feed, hidden, hidden).T,
    )


def place_rows(size, routed, tokens, cotangent, rows_res, rows_grad, attn, feed, assemble):
    length, width, rows = size["L"], size["D"], size["R"]
    block = 256
    cut, narrow, hidden = size["DB"], size["n"], size["f"]
    whole = lambda *shape: pl.BlockSpec(shape, lambda i: (0,) * len(shape))
    moving = pl.BlockSpec((block, width), lambda i: (i, 0))
    outs = [jax.ShapeDtypeStruct((length, width), BF16)] * 2
    out_specs = [moving] * 2
    if assemble:
        shapes = [(cut, 2 * narrow)] * 3 + [(2 * narrow, cut), (cut, 2 * hidden), (2 * hidden, cut)]
        outs = outs + [jax.ShapeDtypeStruct(shape, F32) for shape in shapes]
        out_specs = out_specs + [whole(*shape) for shape in shapes]
    return pl.pallas_call(
        functools.partial(place_kernel, size, assemble),
        grid=(length // block,),
        out_shape=outs,
        in_specs=[
            whole(1, rows),
            moving,
            moving,
            whole(rows, width),
            whole(rows, width),
            whole(*attn.shape),
            whole(*feed.shape),
        ],
        out_specs=out_specs,
        compiler_params=pltpu.CompilerParams(vmem_limit_bytes=48 * 2**20),
    )(routed, tokens, cotangent, rows_res, rows_grad, attn, feed)


def shards_of(
    groups,
    tokens,
    cotangent,
    routed,
    valid_mask,
    w_router,
    first_gain,
    query_weight,
    key_weight,
    value_weight,
    output_weight,
    second_gain,
    up_weight,
    down_weight,
):
    shards, data = lax.axis_size("mp"), lax.axis_size("dp")
    _, length, width = tokens.shape
    rows = routed.shape[1]
    narrow = query_weight.shape[1] // 2
    hidden = up_weight.shape[1] // 2
    cut = width // 8
    chips_x = 1 << ((data // 2).bit_length() - 1) // 2
    size = dict(
        S=shards, ybit=2 * chips_x, R=rows, D=width, L=length, hh=narrow // HEAD_DIM,
        n=narrow, f=hidden, DB=cut, joined=narrow % 128 != 0,
    )
    dp = lax.axis_index("dp")
    x, y = (dp // 2) % 2, (dp // size["ybit"]) % 2
    qkv = (query_weight, key_weight, value_weight)
    if size["joined"]:
        halves = [lax.dynamic_slice_in_dim(weight, x * narrow, narrow, 1) for weight in qkv]
        qkv = (jnp.concatenate(halves, axis=1),)
    row = lambda vector: vector.reshape(1, width)
    operands = (
        tokens, cotangent, routed, valid_mask, row(w_router), row(first_gain), row(second_gain),
        *qkv, output_weight, up_weight.reshape(2, 2, 2, cut, 2 * hidden), down_weight,
    )
    rows_res, rows_grad, rms, small, attn, feed = run_block(size, operands)
    whole_group = data == 8
    if not whole_group:
        block = 4 * y + 2 * x + dp % 2

        def over_groups(part):
            base = jnp.zeros((2, width, part.shape[2]), F32)
            placed = lax.dynamic_update_slice_in_dim(base, part, block * cut, 1)
            return lax.psum_scatter(placed, "dp", scatter_dimension=1, tiled=True)

        attn, feed = over_groups(attn), over_groups(feed)
        small = lax.psum(small, "dp") / 8.0
    placed = place_rows(size, routed, tokens[0], cotangent[0], rows_res, rows_grad, attn, feed, whole_group)
    residual, grad_tokens = placed[:2]
    weights = placed[2:] if whole_group else weight_outputs(size, attn, feed)
    grad_query, grad_key, grad_value, grad_output, grad_up, grad_down = weights
    return (
        residual[None],
        grad_tokens[None],
        rms[0, 0:1],
        small[0],
        small[1],
        grad_query,
        grad_key,
        grad_value,
        grad_output,
        small[2],
        grad_up,
        grad_down,
    )


def solution(mesh):
    in_specs = (
        P(("dp", "mp"), None, None),
        P(("dp", "mp"), None, None),
        P(("dp", "mp"), None),
        P(("dp", "mp"), None),
        P(),
        P(),
        P(None, "mp"),
        P(None, "mp"),
        P(None, "mp"),
        P("mp", None),
        P(),
        P(None, "mp"),
        P("mp", None),
    )
    out_specs = (
        P(("dp", "mp"), None, None),
        P(("dp", "mp"), None, None),
        P(("dp", "mp")),
        P(),
        P(),
        P("dp", "mp"),
        P("dp", "mp"),
        P("dp", "mp"),
        P("mp", "dp"),
        P(),
        P("dp", "mp"),
        P("mp", "dp"),
    )
    body = functools.partial(shards_of, mesh.shape["dp"] // 8)
    return jax.shard_map(body, mesh=mesh, in_specs=in_specs, out_specs=out_specs, check_vma=False)
```

```python
import functools
import math

import jax
import jax.numpy as jnp
from jax import lax
from jax.experimental import pallas as pl
from jax.experimental.pallas import tpu as pltpu
from jax.sharding import PartitionSpec as P

HEADS = 16
HEAD_DIM = 64
EPS = 1e-06
F32 = jnp.float32
BF16 = jnp.bfloat16
TILE = 64


def mm(left, right):
    return jnp.dot(left, right, preferred_element_type=F32)


def mm_nt(left, right):
    return lax.dot_general(left, right, (((1,), (1,)), ((), ())), preferred_element_type=F32)


def mm_tn(left, right):
    return lax.dot_general(left, right, (((0,), (0,)), ((), ())), preferred_element_type=F32)


def row_tiles(rows, body, init=0):
    def step(index, carry):
        return body(pl.ds(pl.multiple_of(index * TILE, TILE), TILE), carry)

    return lax.fori_loop(0, rows // TILE, step, init)


def fold_rows(value):
    return jnp.sum(value.reshape(-1, 8, value.shape[-1]), axis=0)


def gelu_both(value):
    cdf = 0.5 * (1.0 + lax.erf(value * math.sqrt(0.5)))
    density = jnp.exp(-0.5 * value * value) * (1.0 / math.sqrt(2.0 * math.pi))
    return value * cdf, cdf + value * density


def block_kernel(size, *refs):
    shards, ybit, rows, width, length = size["S"], size["ybit"], size["R"], size["D"], size["L"]
    heads, narrow, hidden, cut = size["hh"], size["n"], size["f"], size["DB"]
    joined = size["joined"]
    quarter = 2 * cut
    refs = list(refs)

    def take(count):
        taken, refs[:count] = refs[:count], []
        return taken

    tokens, cotangent, routed, valid, w_router, first_gain, second_gain = take(7)
    qkv_in = take(1 if joined else 3)
    out_in, up_in, down_in = take(3)
    outputs = take(5)
    w_qkv, w_out, w_up, w_down = take(4)
    h1, dfeed, h2, datt, turn_a, turn_b = take(6)
    qkv, ctx, prob, act, dup = take(5)
    total, wide, sent, got = take(4)
    own_z, own_c, attended, dmixed, feed_own, columns = take(6)
    lane = lax.broadcasted_iota(jnp.int32, (1, 128), 1)

    def column(k, at):
        return columns[at][:, k : k + 1]

    def set_column(k, at, value):
        columns[at] = jnp.where(lane == k, value, columns[at])

    gate, live, dscore = (functools.partial(column, k) for k in range(3))
    grads, core_f, y_f, z_f, core_a, y_a, z_a, swap_f, swap_a = take(9)
    attn_out, feed_out = take(2)
    small_send, small_got = take(2)
    load_sem, tok_sem, out_sem = take(3)
    wz_s, wz_r, wy_s, wy_r, wc_s, wc_r = take(6)
    x_s, x_r = take(2)
    gc_s, gc_r, gy_s, gy_r, gz_s, gz_r, gx_s, gx_r = take(8)
    sm_s, sm_r = take(2)

    dp = lax.axis_index("dp")
    z = lax.axis_index("mp")
    core = lax.rem(dp, 2)
    x = lax.rem(lax.div(dp, 2), 2)
    y = lax.rem(lax.div(dp, ybit), 2)
    core_dev = (dp + 1 - 2 * core, z)
    x_dev = (dp + 2 * (1 - 2 * x), z)
    y_dev = (dp + ybit * (1 - 2 * y), z)
    up_dev = (dp, z + 1)
    down_dev = (dp, z - 1)
    x_dp = dp + 2 * (1 - 2 * x)
    z_bits = [1 << k for k in range(int(math.log2(shards)))]
    small_devices = [core_dev, x_dev, (x_dp + ybit * (1 - 2 * y), z)]
    small_devices += [(x_dp, z + bit * (1 - 2 * lax.rem(lax.div(z, bit), 2))) for bit in z_bits]

    def remote(src, dst, send, recv, device):
        return pltpu.make_async_remote_copy(
            src_ref=src,
            dst_ref=dst,
            send_sem=send,
            recv_sem=recv,
            device_id=device,
            device_id_type=pl.DeviceIdType.MESH,
        )

    def order(j):
        high = lax.div(z, shards // 2)
        base = z + high * (shards - 1 - 2 * z)
        odd = lax.rem(j, 2)
        near = base + lax.div(j + 1, 2) * (2 * odd - 1)
        pick = jnp.where(j <= 2 * base, near, j)
        return pick + high * (shards - 1 - 2 * pick)

    attn_mats = list(range(len(qkv_in) + 1))
    feed_mats = [len(attn_mats), len(attn_mats) + 1]
    out_at, up_at = attn_mats[-1], feed_mats[0]

    def span(qy, qc):
        return pl.ds(pl.multiple_of((2 * qy + qc) * quarter, quarter), quarter)

    def lanes(count):
        return pl.ds(pl.multiple_of(x * count, count), count)

    def held(i, s, qy, qc):
        if i < out_at:
            part = w_qkv if joined else w_qkv.at[:, :, i * narrow : (i + 1) * narrow]
            return part.at[s, span(qy, qc)]
        if i == out_at:
            return w_out.at[s, :, span(qy, qc)]
        if i == up_at:
            return w_up.at[s, qy, qc]
        return w_down.at[s, :, span(qy, qc)]

    def own_piece(i):
        if i < out_at:
            part = qkv_in[i].at[span(y, core)]
            return part if joined else part.at[:, lanes(narrow)]
        if i == out_at:
            return out_in.at[lanes(narrow), span(y, core)]
        if i == up_at:
            return up_in.at[y, core, :, :, lanes(hidden)]
        return down_in.at[lanes(hidden), span(y, core)]

    def load_own(i):
        if i < out_at:
            if joined:
                src, dst = qkv_in[i], w_qkv.at[z]
            else:
                src, dst = qkv_in[i].at[:, lanes(narrow)], w_qkv.at[z, :, i * narrow : (i + 1) * narrow]
        elif i == out_at:
            src, dst = out_in.at[lanes(narrow), :], w_out.at[z]
        elif i == up_at:
            src, dst = up_in.at[:, :, :, :, lanes(hidden)], w_up.at[z]
        else:
            src, dst = down_in.at[lanes(hidden), :], w_down.at[z]
        return pltpu.make_async_copy(src, dst, load_sem.at[i])

    def own_up(i):
        return remote(own_piece(i), held(i, z, y, core), wz_s.at[i, z], wz_r.at[i, z], up_dev)

    def own_down(i):
        return remote(own_piece(i), held(i, z, y, core), wz_s.at[i, shards], wz_r.at[i, z], down_dev)

    def pass_on(i, s, device):
        piece = held(i, s, y, core)
        return remote(piece, piece, wz_s.at[i, s], wz_r.at[i, s], device)

    def across_y(i, s, qy):
        piece = held(i, s, qy, core)
        return remote(piece, piece, wy_s.at[i, s], wy_r.at[i, s], y_dev)

    def across_core(i, s, qy, qc, slot):
        piece = held(i, s, qy, qc)
        return remote(piece, piece, wc_s.at[i, slot, s], wc_r.at[i, slot, s], core_dev)

    def send_own_up(mats):
        for i in mats:
            own_up(i).start()

    def send_own_down(mats):
        for i in mats:
            own_down(i).start()

    def passing(s, action):
        @pl.when((s < z) & (z < shards - 1))
        def _():
            action(up_dev)

        @pl.when((s > z) & (z > 0))
        def _():
            action(down_dev)

    def arrive(mats, j):
        s = order(j)
        for i in mats:
            pass_on(i, s, up_dev).wait_recv()
            passing(s, lambda device: pass_on(i, s, device).start())
            across_y(i, s, y).start()
            across_core(i, s, y, core, 0).start()

    def arrive_attn(j):
        arrive(attn_mats, j)
        s = order(j)

        @pl.when((s == 0) & (z < shards - 1))
        def _():
            send_own_up(feed_mats)

        @pl.when((s == shards - 1) & (z > 0))
        def _():
            send_own_down(feed_mats)

    def relay(mats, j):
        s = order(j)
        for i in mats:
            across_y(i, s, 1 - y).wait_recv()
            across_core(i, s, 1 - y, core, 1).start()

    def settle(mats, j):
        s = order(j)
        for i in mats:
            across_core(i, s, y, 1 - core, 0).wait_recv()
            across_core(i, s, 1 - y, 1 - core, 1).wait_recv()

    def drain(mats):
        @pl.when(z < shards - 1)
        def _():
            for i in mats:
                own_up(i).wait_send()

        @pl.when(z > 0)
        def _():
            for i in mats:
                own_down(i).wait_send()

        def step(j, carry):
            s = order(j)
            for i in mats:
                passing(s, lambda device: pass_on(i, s, device).wait_send())
                across_y(i, s, y).wait_send()
                across_core(i, s, y, core, 0).wait_send()
                across_core(i, s, 1 - y, core, 1).wait_send()
            return carry

        lax.fori_loop(1, shards, step, 0)

    def exchange(slot, src, dst):
        return remote(src, dst, x_s.at[slot], x_r.at[slot], x_dev)

    x_h1 = exchange(0, h1.at[0], h1.at[1])
    x_dfeed = exchange(1, dfeed.at[0], dfeed.at[1])
    x_att = exchange(2, sent.at[0], got.at[0])
    x_h2 = exchange(3, h2.at[0], h2.at[1])
    x_dh2 = exchange(4, sent.at[0], got.at[0])
    x_feed = exchange(5, sent.at[1], got.at[1])
    x_datt = exchange(6, datt.at[0], datt.at[1])
    x_dh1 = exchange(7, sent.at[0], got.at[0])

    def put(k, src):
        return pltpu.make_async_copy(src, outputs[k], out_sem.at[k])

    steps = length // (2 * rows)
    stages = ((got, sent), (h2, datt))

    def block_loads(t):
        copies = []
        for k, (array, buf) in enumerate(zip((tokens, cotangent), stages[t % 2])):
            for half in range(2):
                src = array.at[0, (2 * t + half) * rows : (2 * t + half + 1) * rows]
                copies.append(pltpu.make_async_copy(src, buf.at[half], tok_sem.at[t % 2, k, half]))
        return copies

    for t in range(2):
        for copy in block_loads(t):
            copy.start()
    for i in attn_mats + feed_mats:
        load_own(i).start()

    barrier = pltpu.get_barrier_semaphore()

    def greet(device):
        pl.semaphore_signal(barrier, inc=1, device_id=device, device_id_type=pl.DeviceIdType.MESH)

    for device in [y_dev] + small_devices:
        greet(device)

    @pl.when(z > 0)
    def _():
        greet(down_dev)

    @pl.when(z < shards - 1)
    def _():
        greet(up_dev)

    ends = jnp.where(z == 0, 1, 0) + jnp.where(z == shards - 1, 1, 0)
    pl.semaphore_wait(barrier, 3 + len(small_devices) - ends)

    @pl.when(z < shards - 1)
    def _():
        send_own_up(attn_mats)

    @pl.when(z > 0)
    def _():
        send_own_down(attn_mats)

    @pl.when(z == 0)
    def _():
        send_own_up(feed_mats)

    @pl.when(z == shards - 1)
    def _():
        send_own_down(feed_mats)

    as_rows = jnp.broadcast_to(routed[...].astype(F32), (8, rows))
    position = jnp.transpose(as_rows)[:, 0:1].astype(jnp.int32)
    flags = jnp.zeros((rows, 1), F32)
    for t in range(steps):
        for copy in block_loads(t):
            copy.wait()
        hit = position == 2 * t * rows + lax.broadcasted_iota(jnp.int32, (rows, 2 * rows), 1)
        chosen = jnp.where(hit, 1.0, 0.0)
        pick = chosen.astype(BF16)
        for k, buf in enumerate(stages[t % 2]):
            picked = mm(pick, buf[...].reshape(2 * rows, width))
            total[k] = picked if t == 0 else total[k] + picked
        if t + 2 < steps:
            for copy in block_loads(t + 2):
                copy.start()
        mask = valid[:, 2 * t * rows : 2 * (t + 1) * rows].astype(F32)
        flags = flags + jnp.sum(chosen * mask, axis=1, keepdims=True)
    columns[...] = jnp.broadcast_to(flags, columns.shape)

    def prepare(at, carry):
        row, cot = total[0, at], total[1, at]
        own_z[at] = row.astype(BF16)
        own_c[at] = cot.astype(BF16)
        gate_here = jnp.sum(row * w_router[...], axis=1, keepdims=True) * live(at)
        set_column(0, at, gate_here)
        factor = lax.rsqrt(jnp.mean(row * row, axis=1, keepdims=True) + EPS)
        h1[0, at] = (row * factor * first_gain[...]).astype(BF16)
        dfeed[0, at] = (gate_here * cot).astype(BF16)
        return carry

    row_tiles(rows, prepare)
    x_h1.start()
    x_dfeed.start()

    lane_head = lax.div(lax.broadcasted_iota(jnp.int32, (1, narrow), 1), HEAD_DIM)
    masks = [jnp.where(lane_head == h, 1.0, 0.0) for h in range(heads)]
    masks_low = [mask.astype(BF16) for mask in masks]

    def stacked(value):
        return jnp.concatenate([value * mask for mask in masks_low], axis=0) if heads > 1 else value

    def unstacked(value):
        if heads == 1:
            return value
        picked = value[0:rows] * masks[0]
        for h in range(1, heads):
            picked = picked + value[h * rows : (h + 1) * rows] * masks[h]
        return picked

    score_shape = (heads * rows, rows)
    causal = lax.rem(lax.broadcasted_iota(jnp.int32, score_shape, 0), rows) >= lax.broadcasted_iota(
        jnp.int32, score_shape, 1
    )

    for i in attn_mats:
        load_own(i).wait()
    arrive_attn(1)
    for j in range(2, shards):
        arrive_attn(j)
        relay(attn_mats, j - 1)
    x_h1.wait_recv()

    def attend(j, carry):
        s = order(j)

        @pl.when(j + 1 == shards)
        def _():
            arrive(feed_mats[:1], 1)
            relay(attn_mats, j)

        @pl.when(j > 0)
        def _():
            settle(attn_mats, j)

        low = mm(h1[...].reshape(2 * rows, width), w_qkv[s]).astype(BF16)
        query = low[:, 0:narrow] * jnp.asarray(HEAD_DIM**-0.5, BF16)
        qkv[s] = jnp.concatenate([query, low[:, narrow:]], axis=1).reshape(2, rows, 3 * narrow)
        for half in range(2):
            query = qkv[s, half, :, 0:narrow]
            key = qkv[s, half, :, narrow : 2 * narrow]
            value = qkv[s, half, :, 2 * narrow : 3 * narrow]
            scores = jnp.where(causal, mm_nt(stacked(query), key), -1e30)
            raised = jnp.exp(scores - jnp.max(scores, axis=1, keepdims=True))
            weights = (raised / jnp.sum(raised, axis=1, keepdims=True)).astype(BF16)
            prob[s, half] = weights
            ctx[s, half * rows : (half + 1) * rows] = unstacked(mm(weights, value)).astype(BF16)
        return carry

    lax.fori_loop(0, shards, attend, 0)

    def project_out(half):
        parts = [ctx[s, half * rows : (half + 1) * rows] for s in range(shards)]
        return mm(jnp.concatenate(parts, axis=1), w_out[...].reshape(shards * narrow, width))

    sent[0] = project_out(1).astype(BF16)
    x_att.start()
    attended[...] = project_out(0)
    arrive(feed_mats[1:], 1)
    arrive(feed_mats[:1], 2)
    x_att.wait()

    def mix(at, carry):
        att = attended[at] + got[0, at].astype(F32)
        attended[at] = att
        mixed = own_z[at].astype(F32) + att
        factor = lax.rsqrt(jnp.mean(mixed * mixed, axis=1, keepdims=True) + EPS)
        h2[0, at] = (mixed * factor * second_gain[...]).astype(BF16)
        return carry

    row_tiles(rows, mix)
    x_h2.start()
    arrive(feed_mats[1:], 2)
    x_dfeed.wait_recv()

    def core_send(group, buf, into, s, at=None):
        src = buf.at[s, :, :, 1 - core]
        return remote(src, into.at[s], gc_s.at[group, s], gc_r.at[group, s], core_dev)

    def y_send(group, buf, into, s):
        return remote(buf.at[s, 1 - y, :, core], into.at[s], gy_s.at[group, s], gy_r.at[group, s], y_dev)

    def z_send(group, buf, into, s, device, slot):
        src = buf.at[s, y, :, core]
        return remote(src, into.at[slot], gz_s.at[group, s], gz_r.at[group, slot], device)

    def add_into(ref, *others):
        value = ref[...].astype(F32)
        for other in others:
            value = value + other[...].astype(F32)
        ref[...] = value.astype(BF16)

    def stage_core(group, buf, core_got, y_got, s):
        core_send(group, buf, core_got, s).wait_recv()
        for a in range(2):
            for b in range(2):
                add_into(buf.at[s, a, b, core], core_got.at[s, a, b])
        y_send(group, buf, y_got, s).start()

    def stage_y(group, buf, y_got, s):
        y_send(group, buf, y_got, s).wait_recv()
        for b in range(2):
            add_into(buf.at[s, y, b, core], y_got.at[s, b])

    def line_in(group, buf, z_got, s, slot):
        z_send(group, buf, z_got, s, up_dev, slot).wait_recv()
        for b in range(2):
            add_into(buf.at[s, y, b, core], z_got.at[slot, b])

    def stage_z(group, buf, z_got, s, action):
        @pl.when(s > z)
        def _():
            if action == "start":

                @pl.when(z > 0)
                def _():
                    line_in(group, buf, z_got, s, s)

            copy = z_send(group, buf, z_got, s, up_dev, s)
            copy.start() if action == "start" else copy.wait_send()

        @pl.when(s < z)
        def _():
            if action == "start":

                @pl.when(z < shards - 1)
                def _():
                    line_in(group, buf, z_got, s, s)

            slot = jnp.where(s == z - 1, shards, s)
            copy = z_send(group, buf, z_got, s, down_dev, slot)
            copy.start() if action == "start" else copy.wait_send()

    def swap(group, pair):
        return remote(pair.at[0], pair.at[1], gx_s.at[group], gx_r.at[group], x_dev)

    def stage_last(group, buf, z_got, pair, out):
        for b in range(2):
            out[b] = buf[z, y, b, core].astype(F32)

        @pl.when(z > 0)
        def _():
            z_send(group, buf, z_got, z, up_dev, z).wait_recv()
            out[...] += z_got[z].astype(F32)

        @pl.when(z < shards - 1)
        def _():
            z_send(group, buf, z_got, z, up_dev, shards).wait_recv()
            out[...] += z_got[shards].astype(F32)

        pair[0] = out[1 - x].astype(BF16)
        swap(group, pair).start()

    def stage_out(group, pair, out):
        swap(group, pair).wait_recv()
        out[1 - x] = pair[1].astype(F32)

    def reversed_order(k):
        return order(shards - 1 - k)

    def store_grads(buf, s, left, right, lo, count):
        for a in range(2):
            value = mm(left[2 * a * quarter : 2 * (a + 1) * quarter, :], right).astype(BF16)
            buf[s, a, :, :, :, lo : lo + count] = value.reshape(2, 2, cut, count)

    total[...] = jnp.zeros_like(total)
    for i in feed_mats:
        load_own(i).wait()
    def feed_grads(s):
        store_grads(grads, s, turn_a, dup[s], 0, hidden)
        store_grads(grads, s, turn_b, act[s], hidden, hidden)
        core_send(0, grads, core_f, s).start()

    def feed_chunk(s, half):
        part = pl.ds(pl.multiple_of(half * rows, rows), rows)
        up_here = w_up[s].reshape(width, hidden)
        wide[0] = mm(h2[half], up_here)
        wide[1] = mm_nt(dfeed[half], w_down[s])

        def turn(at, inner):
            active, slope = gelu_both(wide[0, at])
            out = pl.ds(pl.multiple_of(half * rows + at.start, TILE), TILE)
            act[s, out] = active.astype(BF16)
            dup[s, out] = (wide[1, at] * slope).astype(BF16)
            return inner

        row_tiles(rows, turn)
        total[half] += mm_nt(dup[s, part], up_here)

    def own_step(j, carry):
        @pl.when(j > 0)
        def _():
            settle(feed_mats, j)

        feed_chunk(order(j), 0)

        @pl.when((j > 0) & (j + 2 < shards))
        def _():
            arrive(feed_mats[1:], j + 2)

        @pl.when(j + 2 < shards)
        def _():
            relay(feed_mats, j + 1)

        @pl.when(j + 3 < shards)
        def _():
            arrive(feed_mats[:1], j + 3)

        return carry

    lax.fori_loop(0, shards - 1, own_step, 0)
    x_h2.wait_recv()
    turn_a[...] = jnp.transpose(h2[...].reshape(2 * rows, width))
    turn_b[...] = jnp.transpose(dfeed[...].reshape(2 * rows, width))

    def other_step(j, carry):
        feed_chunk(order(j), 1)

        @pl.when(j == 0)
        def _():
            feed_grads(z)

        @pl.when(j == 1)
        def _():
            stage_core(0, grads, core_f, y_f, z)

        return carry

    lax.fori_loop(0, shards - 1, other_step, 0)
    relay(feed_mats, shards - 1)
    settle(feed_mats, shards - 1)

    def last_step(k, carry):
        feed_chunk(order(shards - 1), 1 - k)

        @pl.when(k == 0)
        def _():
            sent[0] = total[1].astype(BF16)
            x_dh2.start()

        return carry

    lax.fori_loop(0, 2, last_step, 0)

    def feed_grads_step(k, carry):
        feed_grads(reversed_order(k))

        @pl.when(k > 0)
        def _():
            stage_core(0, grads, core_f, y_f, reversed_order(k - 1))

        return carry

    lax.fori_loop(0, shards - 1, feed_grads_step, 0)
    stage_core(0, grads, core_f, y_f, order(1))

    def feed_rows(half):
        value = mm(act[0, half * rows : (half + 1) * rows], w_down[0])
        for s in range(1, shards):
            value += mm(act[s, half * rows : (half + 1) * rows], w_down[s])
        return value

    sent[1] = feed_rows(1).astype(BF16)
    feed_own[...] = feed_rows(0)
    x_dh2.wait()

    def second_back(at, carry):
        dh2 = total[0, at] + got[0, at].astype(F32)
        mixed = own_z[at].astype(F32) + attended[at]
        factor = lax.rsqrt(jnp.mean(mixed * mixed, axis=1, keepdims=True) + EPS)
        scaled = dh2 * second_gain[...]
        back = factor * scaled - mixed * (factor**3 * jnp.mean(mixed * scaled, axis=1, keepdims=True))
        dmixed[at] = back
        datt[0, at] = (gate(at) * own_c[at].astype(F32) + back).astype(BF16)
        return carry + fold_rows(dh2 * mixed * factor)

    second_sum = row_tiles(rows, second_back, jnp.zeros((8, width), F32))
    x_datt.start()
    x_feed.start()

    def attend_back(half):
        part = slice(half * rows, (half + 1) * rows)

        def step(k, carry):
            s = reversed_order(k)
            dctx = mm_nt(datt[half], w_out[s]).astype(BF16)
            query = qkv[s, half, :, 0:narrow]
            key = qkv[s, half, :, narrow : 2 * narrow]
            value = qkv[s, half, :, 2 * narrow : 3 * narrow]
            weights = prob[s, half]
            dhead = stacked(dctx)
            dweights = mm_nt(dhead, value)
            full = weights.astype(F32)
            dscores = full * (dweights - jnp.sum(dweights * full, axis=1, keepdims=True))
            dscores = dscores.astype(BF16)
            dquery = unstacked(mm(dscores, key)) * HEAD_DIM**-0.5
            dkey = mm_tn(dscores, stacked(query))
            dvalue = mm_tn(weights, dhead)
            act[s, part, 0 : 3 * narrow] = jnp.concatenate([dquery, dkey, dvalue], axis=1).astype(BF16)
            return carry

        lax.fori_loop(0, shards, step, 0)

    def dh1_rows(half):
        part = slice(half * rows, (half + 1) * rows)
        value = mm_nt(act[0, part, 0 : 3 * narrow], w_qkv[0])
        for s in range(1, shards):
            value += mm_nt(act[s, part, 0 : 3 * narrow], w_qkv[s])
        return value

    attend_back(0)
    total[0] = dh1_rows(0)
    turn_a[...] = jnp.transpose(h1[...].reshape(2 * rows, width))
    drain(feed_mats)
    edge = (z == 0) | (z == shards - 1)

    @pl.when(edge)
    def _():
        far = reversed_order(0)
        stage_y(0, grads, y_f, far)
        stage_z(0, grads, z_f, far, "start")

    x_datt.wait_recv()
    turn_b[...] = jnp.transpose(datt[...].reshape(2 * rows, width))
    attend_back(1)
    sent[0] = dh1_rows(1).astype(BF16)
    x_dh1.start()

    def attn_grads(k, carry):
        s = reversed_order(k)
        store_grads(w_up, s, turn_a, act[s, :, 0 : 3 * narrow], 0, 3 * narrow)
        store_grads(w_up, s, turn_b, ctx[s], 3 * narrow, narrow)
        core_send(1, w_up, core_a, s).start()

        @pl.when(k > 0)
        def _():
            stage_core(1, w_up, core_a, y_a, reversed_order(k - 1))

        return carry

    @pl.when(edge)
    def _():
        near = reversed_order(1)
        stage_y(0, grads, y_f, near)
        stage_z(0, grads, z_f, near, "start")

    lax.fori_loop(0, shards, attn_grads, 0)
    stage_core(1, w_up, core_a, y_a, z)

    def line_step(group, buf, y_got, z_got):
        def step(k, carry):
            s = reversed_order(k)
            stage_y(group, buf, y_got, s)
            stage_z(group, buf, z_got, s, "start")
            return carry

        return step

    feed_line = line_step(0, grads, y_f, z_f)
    attn_line = line_step(1, w_up, y_a, z_a)
    x_feed.wait()

    def finish_forward(at, squares):
        branch = attended[at] + feed_own[at] + got[1, at].astype(F32)
        update = gate(at) * branch
        sent[1, at] = (own_z[at].astype(F32) + update).astype(BF16)
        dgate = jnp.sum(own_c[at].astype(F32) * branch, axis=1, keepdims=True)
        set_column(2, at, dgate * live(at))
        return squares + fold_rows(update * update)

    squares = row_tiles(rows, finish_forward, jnp.zeros((8, width), F32))
    put(0, sent.at[1]).start()
    count = jnp.sum(valid[...].astype(F32), axis=1, keepdims=True)
    energy = jnp.sum(jnp.sum(squares, axis=0, keepdims=True), axis=1, keepdims=True)
    rms = jnp.sqrt(energy / (width * jnp.maximum(count, 1.0)))

    lax.fori_loop(jnp.where(edge, 2, 0), shards - 1, feed_line, 0)

    @pl.when(edge)
    def _():
        attn_line(0, 0)

    x_dh1.wait()

    def first_back(at, sums):
        dh1 = total[0, at] + got[0, at].astype(F32)
        row = own_z[at].astype(F32)
        factor = lax.rsqrt(jnp.mean(row * row, axis=1, keepdims=True) + EPS)
        scaled = dh1 * first_gain[...]
        back = factor * scaled - row * (factor**3 * jnp.mean(row * scaled, axis=1, keepdims=True))
        back = back + dmixed[at] + dscore(at) * w_router[...]
        got[1, at] = (own_c[at].astype(F32) + back).astype(BF16)
        return sums[0] + fold_rows(dscore(at) * row), sums[1] + fold_rows(dh1 * row * factor)

    zero = jnp.zeros((8, width), F32)
    router_sum, first_sum = row_tiles(rows, first_back, (zero, zero))
    put(1, got.at[1]).start()
    parts = [jnp.sum(part, axis=0, keepdims=True) for part in (router_sum, first_sum, second_sum)]
    small = jnp.concatenate(parts + [jnp.zeros((5, width), F32)], axis=0)

    def small_copy(k):
        return remote(small_send.at[k], small_got.at[k], sm_s.at[k], sm_r.at[k], small_devices[k])

    for k in range(len(small_devices)):
        small_send[k] = small
        small_copy(k).start()
        small_copy(k).wait()
        small = small + small_got[k]
    row_at = lax.broadcasted_iota(jnp.int32, (8, 1), 0)
    small_send[0] = jnp.where(row_at == 3, rms, small)
    put(2, small_send.at[0]).start()
    lax.fori_loop(jnp.where(edge, 1, 0), shards - 1, attn_line, 0)
    stage_y(0, grads, y_f, z)
    stage_last(0, grads, z_f, swap_f, feed_out)
    stage_y(1, w_up, y_a, z)
    stage_last(1, w_up, z_a, swap_a, attn_out)
    stage_out(0, swap_f, feed_out)
    put(4, feed_out).start()
    stage_out(1, swap_a, attn_out)
    put(3, attn_out).start()

    drain(attn_mats)
    for copy in (x_h1, x_dfeed, x_h2, x_datt):
        copy.wait_send()

    def drain_grads(k, carry):
        s = reversed_order(k)
        for group, buf, core_got, y_got, z_got in (
            (0, grads, core_f, y_f, z_f),
            (1, w_up, core_a, y_a, z_a),
        ):
            core_send(group, buf, core_got, s).wait_send()
            y_send(group, buf, y_got, s).wait_send()
            stage_z(group, buf, z_got, s, "wait")
        return carry

    lax.fori_loop(0, shards, drain_grads, 0)
    swap(0, swap_f).wait_send()
    swap(1, swap_a).wait_send()
    for k, src in enumerate((sent.at[1], got.at[1], small_send.at[0], attn_out, feed_out)):
        put(k, src).wait()


def run_block(size, operands):
    shards, rows, width = size["S"], size["R"], size["D"]
    heads, narrow, hidden, cut = size["hh"], size["n"], size["f"], size["DB"]
    mats = (2 if size["joined"] else 4) + 2
    stages = 3 + int(math.log2(shards))
    attn, feed = 4 * narrow, 2 * hidden
    dma = pltpu.SemaphoreType.DMA
    vmem = lambda *shape: pltpu.VMEM(shape, BF16)
    full = lambda *shape: pltpu.VMEM(shape, F32)
    scratch = [
        vmem(shards, width, 3 * narrow),
        vmem(shards, narrow, width),
        vmem(shards, 2, 2, 2, cut, hidden),
        vmem(shards, hidden, width),
        *[vmem(2, rows, width) for _ in range(4)],
        *[vmem(width, 2 * rows) for _ in range(2)],
        vmem(shards, 2, rows, 3 * narrow),
        vmem(shards, 2 * rows, narrow),
        vmem(shards, 2, heads * rows, rows),
        vmem(shards, 2 * rows, hidden),
        vmem(shards, 2 * rows, hidden),
        full(2, rows, width),
        full(2, rows, hidden),
        vmem(2, rows, width),
        vmem(2, rows, width),
        vmem(rows, width),
        vmem(rows, width),
        *[full(rows, width) for _ in range(3)],
        full(rows, 128),
        vmem(shards, 2, 2, 2, cut, feed),
        vmem(shards, 2, 2, cut, feed),
        vmem(shards, 2, cut, feed),
        vmem(shards + 1, 2, cut, feed),
        vmem(shards, 2, 2, cut, attn),
        vmem(shards, 2, cut, attn),
        vmem(shards + 1, 2, cut, attn),
        vmem(2, cut, feed),
        vmem(2, cut, attn),
        full(2, cut, attn),
        full(2, cut, feed),
        full(stages, 8, width),
        full(stages, 8, width),
        dma((mats,)),
        dma((2, 2, 2)),
        dma((5,)),
        dma((mats, shards + 1)),
        dma((mats, shards)),
        dma((mats, shards)),
        dma((mats, shards)),
        dma((mats, 2, shards)),
        dma((mats, 2, shards)),
        dma((8,)),
        dma((8,)),
        *[dma((2, shards)) for _ in range(5)],
        dma((2, shards + 1)),
        dma((2,)),
        dma((2,)),
        dma((stages,)),
        dma((stages,)),
    ]
    near = pl.BlockSpec(memory_space=pltpu.VMEM)
    far = pl.BlockSpec(memory_space=pl.ANY)
    outs = [
        jax.ShapeDtypeStruct((rows, width), BF16),
        jax.ShapeDtypeStruct((rows, width), BF16),
        jax.ShapeDtypeStruct((8, width), F32),
        jax.ShapeDtypeStruct((2, cut, attn), F32),
        jax.ShapeDtypeStruct((2, cut, feed), F32),
    ]
    return pl.pallas_call(
        functools.partial(block_kernel, size),
        out_shape=outs,
        in_specs=[far, far] + [near] * 5 + [far] * (len(operands) - 7),
        out_specs=[pl.BlockSpec(memory_space=pltpu.HBM)] * len(outs),
        scratch_shapes=scratch,
        compiler_params=pltpu.CompilerParams(
            collective_id=0, has_side_effects=True, vmem_limit_bytes=64 * 2**20 - 65536
        ),
    )(*operands)


def place_kernel(size, assemble, routed, tok, cot, rows_res, rows_grad, small, attn, feed, *outs):
    block, count = tok.shape[0], routed.shape[1]
    step = pl.program_id(0)
    line = step * block + lax.broadcasted_iota(jnp.int32, (block, count), 0)
    chosen = jnp.where(line == routed[...], 1.0, 0.0)
    keep = (1.0 - jnp.sum(chosen, axis=1, keepdims=True)).astype(BF16)
    pick = chosen.astype(BF16)
    outs[0][...] = mm(pick, rows_res[...]).astype(BF16) + tok[...] * keep
    outs[1][...] = mm(pick, rows_grad[...]).astype(BF16) + cot[...] * keep
    if assemble:

        @pl.when(step == 0)
        def _():
            for ref, value in zip(outs[2:], weight_outputs(size, attn, feed)):
                ref[...] = value
            for k in range(3):
                outs[8 + k][...] = small[k : k + 1, :]
            outs[11][...] = small[3:4, 0:1]


def weight_outputs(size, attn, feed):
    narrow, hidden = size["n"], size["f"]

    def side_by_side(ref, lo, count):
        return jnp.concatenate([ref[0, :, lo : lo + count], ref[1, :, lo : lo + count]], axis=1)

    return (
        side_by_side(attn, 0, narrow),
        side_by_side(attn, narrow, narrow),
        side_by_side(attn, 2 * narrow, narrow),
        side_by_side(attn, 3 * narrow, narrow).T,
        side_by_side(feed, 0, hidden),
        side_by_side(feed, hidden, hidden).T,
    )


def place_rows(size, routed, tokens, cotangent, rows_res, rows_grad, small, attn, feed, assemble):
    length, width, rows = size["L"], size["D"], size["R"]
    block = 256
    cut, narrow, hidden = size["DB"], size["n"], size["f"]
    whole = lambda *shape: pl.BlockSpec(shape, lambda i: (0,) * len(shape))
    moving = pl.BlockSpec((block, width), lambda i: (i, 0))
    outs = [jax.ShapeDtypeStruct((length, width), BF16)] * 2
    out_specs = [moving] * 2
    if assemble:
        shapes = [(cut, 2 * narrow)] * 3 + [(2 * narrow, cut), (cut, 2 * hidden), (2 * hidden, cut)]
        shapes += [(1, width)] * 3 + [(1, 1)]
        outs = outs + [jax.ShapeDtypeStruct(shape, F32) for shape in shapes]
        out_specs = out_specs + [whole(*shape) for shape in shapes]
    return pl.pallas_call(
        functools.partial(place_kernel, size, assemble),
        grid=(length // block,),
        out_shape=outs,
        in_specs=[
            whole(1, rows),
            moving,
            moving,
            whole(rows, width),
            whole(rows, width),
            whole(*small.shape),
            whole(*attn.shape),
            whole(*feed.shape),
        ],
        out_specs=out_specs,
        compiler_params=pltpu.CompilerParams(vmem_limit_bytes=48 * 2**20),
    )(routed, tokens, cotangent, rows_res, rows_grad, small, attn, feed)


def shards_of(
    groups,
    tokens,
    cotangent,
    routed,
    valid_mask,
    w_router,
    first_gain,
    query_weight,
    key_weight,
    value_weight,
    output_weight,
    second_gain,
    up_weight,
    down_weight,
):
    shards, data = lax.axis_size("mp"), lax.axis_size("dp")
    _, length, width = tokens.shape
    rows = routed.shape[1]
    narrow = query_weight.shape[1] // 2
    hidden = up_weight.shape[1] // 2
    cut = width // 8
    chips_x = 1 << ((data // 2).bit_length() - 1) // 2
    size = dict(
        S=shards, ybit=2 * chips_x, R=rows, D=width, L=length, hh=narrow // HEAD_DIM,
        n=narrow, f=hidden, DB=cut, joined=narrow % 128 != 0,
    )
    dp = lax.axis_index("dp")
    x, y = (dp // 2) % 2, (dp // size["ybit"]) % 2
    qkv = (query_weight, key_weight, value_weight)
    if size["joined"]:
        halves = [lax.dynamic_slice_in_dim(weight, x * narrow, narrow, 1) for weight in qkv]
        qkv = (jnp.concatenate(halves, axis=1),)
    row = lambda vector: vector.reshape(1, width)
    operands = (
        tokens, cotangent, routed, valid_mask, row(w_router), row(first_gain), row(second_gain),
        *qkv, output_weight, up_weight.reshape(2, 2, 2, cut, 2 * hidden), down_weight,
    )
    rows_res, rows_grad, small, attn, feed = run_block(size, operands)
    whole_group = data == 8
    rms = small[3, 0:1]
    if not whole_group:
        block = 4 * y + 2 * x + dp % 2

        def over_groups(part):
            base = jnp.zeros((2, width, part.shape[2]), F32)
            placed = lax.dynamic_update_slice_in_dim(base, part, block * cut, 1)
            return lax.psum_scatter(placed, "dp", scatter_dimension=1, tiled=True)

        attn, feed = over_groups(attn), over_groups(feed)
        small = lax.psum(small, "dp") / 8.0
    placed = place_rows(size, routed, tokens[0], cotangent[0], rows_res, rows_grad, small, attn, feed, whole_group)
    residual, grad_tokens = placed[:2]
    if whole_group:
        vectors = [vector.reshape(width) for vector in placed[8:11]]
        weights, rms = placed[2:8], placed[11].reshape(1)
    else:
        vectors, weights = [small[k] for k in range(3)], weight_outputs(size, attn, feed)
    grad_query, grad_key, grad_value, grad_output, grad_up, grad_down = weights
    return (
        residual[None],
        grad_tokens[None],
        rms,
        vectors[0],
        vectors[1],
        grad_query,
        grad_key,
        grad_value,
        grad_output,
        vectors[2],
        grad_up,
        grad_down,
    )


def solution(mesh):
    in_specs = (
        P(("dp", "mp"), None, None),
        P(("dp", "mp"), None, None),
        P(("dp", "mp"), None),
        P(("dp", "mp"), None),
        P(),
        P(),
        P(None, "mp"),
        P(None, "mp"),
        P(None, "mp"),
        P("mp", None),
        P(),
        P(None, "mp"),
        P("mp", None),
    )
    out_specs = (
        P(("dp", "mp"), None, None),
        P(("dp", "mp"), None, None),
        P(("dp", "mp")),
        P(),
        P(),
        P("dp", "mp"),
        P("dp", "mp"),
        P("dp", "mp"),
        P("mp", "dp"),
        P(),
        P("dp", "mp"),
        P("mp", "dp"),
    )
    body = functools.partial(shards_of, mesh.shape["dp"] // 8)
    return jax.shard_map(body, mesh=mesh, in_specs=in_specs, out_specs=out_specs, check_vma=False)
```

```python
import functools
import math

import jax
import jax.numpy as jnp
from jax import lax
from jax.experimental import pallas as pl
from jax.experimental.pallas import tpu as pltpu
from jax.sharding import PartitionSpec as P

HEADS = 16
HEAD_DIM = 64
EPS = 1e-06
F32 = jnp.float32
BF16 = jnp.bfloat16
TILE = 64


def mm(left, right):
    return jnp.dot(left, right, preferred_element_type=F32)


def mm_nt(left, right):
    return lax.dot_general(left, right, (((1,), (1,)), ((), ())), preferred_element_type=F32)


def mm_tn(left, right):
    return lax.dot_general(left, right, (((0,), (0,)), ((), ())), preferred_element_type=F32)


def row_tiles(rows, body, init=0):
    def step(index, carry):
        return body(pl.ds(pl.multiple_of(index * TILE, TILE), TILE), carry)

    return lax.fori_loop(0, rows // TILE, step, init)


def fold_rows(value):
    return jnp.sum(value.reshape(-1, 8, value.shape[-1]), axis=0)


def gelu_both(value):
    cdf = 0.5 * (1.0 + lax.erf(value * math.sqrt(0.5)))
    density = jnp.exp(-0.5 * value * value) * (1.0 / math.sqrt(2.0 * math.pi))
    return value * cdf, cdf + value * density


def block_kernel(size, *refs):
    shards, ybit, rows, width, length = size["S"], size["ybit"], size["R"], size["D"], size["L"]
    heads, narrow, hidden, cut = size["hh"], size["n"], size["f"], size["DB"]
    joined = size["joined"]
    quarter = 2 * cut
    refs = list(refs)

    def take(count):
        taken, refs[:count] = refs[:count], []
        return taken

    tokens, cotangent, routed, valid, w_router, first_gain, second_gain = take(7)
    qkv_in = take(1 if joined else 3)
    out_in, up_in, down_in = take(3)
    outputs = take(5)
    w_qkv, w_out, w_up, w_down = take(4)
    h1, dfeed, h2, datt, turn_a, turn_b = take(6)
    qkv, ctx, prob, act, dup = take(5)
    total, wide, sent, got = take(4)
    own_z, own_c, attended, dmixed, feed_own, columns = take(6)
    lane = lax.broadcasted_iota(jnp.int32, (1, 128), 1)

    def column(k, at):
        return columns[at][:, k : k + 1]

    def set_column(k, at, value):
        columns[at] = jnp.where(lane == k, value, columns[at])

    gate, live, dscore = (functools.partial(column, k) for k in range(3))
    grads, core_f, y_f, z_f, core_a, y_a, z_a, swap_f, swap_a = take(9)
    attn_out, feed_out = take(2)
    small_send, small_got = take(2)
    load_sem, tok_sem, out_sem = take(3)
    wz_s, wz_r, wy_s, wy_r, wc_s, wc_r = take(6)
    x_s, x_r = take(2)
    gc_s, gc_r, gy_s, gy_r, gz_s, gz_r, gx_s, gx_r = take(8)
    sm_s, sm_r = take(2)

    dp = lax.axis_index("dp")
    z = lax.axis_index("mp")
    core = lax.rem(dp, 2)
    x = lax.rem(lax.div(dp, 2), 2)
    y = lax.rem(lax.div(dp, ybit), 2)
    core_dev = (dp + 1 - 2 * core, z)
    x_dev = (dp + 2 * (1 - 2 * x), z)
    y_dev = (dp + ybit * (1 - 2 * y), z)
    up_dev = (dp, z + 1)
    down_dev = (dp, z - 1)
    small_devices = [core_dev, x_dev, (dp + 2 * (1 - 2 * x) + ybit * (1 - 2 * y), z)]

    def remote(src, dst, send, recv, device):
        return pltpu.make_async_remote_copy(
            src_ref=src,
            dst_ref=dst,
            send_sem=send,
            recv_sem=recv,
            device_id=device,
            device_id_type=pl.DeviceIdType.MESH,
        )

    def order(j):
        high = lax.div(z, shards // 2)
        base = z + high * (shards - 1 - 2 * z)
        odd = lax.rem(j, 2)
        near = base + lax.div(j + 1, 2) * (2 * odd - 1)
        pick = jnp.where(j <= 2 * base, near, j)
        return pick + high * (shards - 1 - 2 * pick)

    attn_mats = list(range(len(qkv_in) + 1))
    feed_mats = [len(attn_mats), len(attn_mats) + 1]
    out_at, up_at = attn_mats[-1], feed_mats[0]

    def span(qy, qc):
        return pl.ds(pl.multiple_of((2 * qy + qc) * quarter, quarter), quarter)

    def lanes(count):
        return pl.ds(pl.multiple_of(x * count, count), count)

    def held(i, s, qy, qc):
        if i < out_at:
            part = w_qkv if joined else w_qkv.at[:, :, i * narrow : (i + 1) * narrow]
            return part.at[s, span(qy, qc)]
        if i == out_at:
            return w_out.at[s, :, span(qy, qc)]
        if i == up_at:
            return w_up.at[s, qy, qc]
        return w_down.at[s, :, span(qy, qc)]

    def own_piece(i):
        if i < out_at:
            part = qkv_in[i].at[span(y, core)]
            return part if joined else part.at[:, lanes(narrow)]
        if i == out_at:
            return out_in.at[lanes(narrow), span(y, core)]
        if i == up_at:
            return up_in.at[y, core, :, :, lanes(hidden)]
        return down_in.at[lanes(hidden), span(y, core)]

    def load_own(i):
        if i < out_at:
            if joined:
                src, dst = qkv_in[i], w_qkv.at[z]
            else:
                src, dst = qkv_in[i].at[:, lanes(narrow)], w_qkv.at[z, :, i * narrow : (i + 1) * narrow]
        elif i == out_at:
            src, dst = out_in.at[lanes(narrow), :], w_out.at[z]
        elif i == up_at:
            src, dst = up_in.at[:, :, :, :, lanes(hidden)], w_up.at[z]
        else:
            src, dst = down_in.at[lanes(hidden), :], w_down.at[z]
        return pltpu.make_async_copy(src, dst, load_sem.at[i])

    def group_of(i):
        return 0 if i <= out_at else 1

    def own_up(i):
        return remote(own_piece(i), held(i, z, y, core), wz_s.at[group_of(i), z], wz_r.at[i, z], up_dev)

    def own_down(i):
        return remote(own_piece(i), held(i, z, y, core), wz_s.at[group_of(i), shards], wz_r.at[i, z], down_dev)

    def pass_on(i, s, device):
        piece = held(i, s, y, core)
        return remote(piece, piece, wz_s.at[group_of(i), s], wz_r.at[i, s], device)

    def across_y(i, s, qy):
        piece = held(i, s, qy, core)
        return remote(piece, piece, wy_s.at[group_of(i)], wy_r.at[i, s], y_dev)

    def across_core(i, s, qy, qc):
        piece = held(i, s, qy, qc)
        group = group_of(i)
        return remote(piece, piece, wc_s.at[group], wc_r.at[group, s], core_dev)

    def await_pieces(group, sem, count, receiving=False):
        mats = attn_mats if group == 0 else feed_mats
        if joined:
            refs = [held(i, 0, 0, 0) for i in mats] * count
        else:
            flat = w_up.at[0, 0, 0] if group == 0 else w_up.at[0, 0]
            if count == 2:
                flat = w_up.at[0, 0] if group == 0 else w_up.at[0]
            elif count == shards - 1:
                flat = w_up.at[0 : shards - 1, 0, 0] if group == 0 else w_up.at[0 : shards - 1, 0]
            elif count == 2 * (shards - 1):
                flat = w_up.at[0 : shards - 1, 0] if group == 0 else w_up.at[0 : shards - 1]
            refs = [flat]
        for ref in refs:
            if receiving:
                remote(ref, ref, wc_s.at[group], sem, core_dev).wait_recv()
            else:
                remote(ref, ref, sem, wc_r.at[group, 0], core_dev).wait_send()

    def send_own_up(mats):
        for i in mats:
            own_up(i).start()

    def send_own_down(mats):
        for i in mats:
            own_down(i).start()

    def passing(s, action):
        @pl.when((s < z) & (z < shards - 1))
        def _():
            action(up_dev)

        @pl.when((s > z) & (z > 0))
        def _():
            action(down_dev)

    edge = (z == 0) | (z == shards - 1)
    inner = jnp.logical_not(edge)

    def arrive_one(i, j):
        s = order(j)
        pass_on(i, s, up_dev).wait_recv()
        passing(s, lambda device: pass_on(i, s, device).start())
        across_y(i, s, y).start()
        across_core(i, s, y, core).start()

    def arrive(mats, j):
        for i in mats:
            arrive_one(i, j)

    def follow(j):
        s = order(j)

        @pl.when((s == 0) & (z < shards - 1))
        def _():
            send_own_up(feed_mats)

        @pl.when((s == shards - 1) & (z > 0))
        def _():
            send_own_down(feed_mats)

    def relay(mats, j):
        s = order(j)
        for i in mats:
            across_y(i, s, 1 - y).wait_recv()
            across_core(i, s, 1 - y, core).start()

    def settle(group, j):
        await_pieces(group, wc_r.at[group, order(j)], 2, True)

    def drain(group):
        @pl.when(z < shards - 1)
        def _():
            await_pieces(group, wz_s.at[group, z], 1)

        @pl.when(z > 0)
        def _():
            await_pieces(group, wz_s.at[group, shards], 1)

        def step(j, carry):
            s = order(j)
            passing(s, lambda device: await_pieces(group, wz_s.at[group, s], 1))
            return carry

        lax.fori_loop(1, shards, step, 0)
        await_pieces(group, wy_s.at[group], shards - 1)
        await_pieces(group, wc_s.at[group], 2 * (shards - 1))

    def exchange(slot, src, dst):
        return remote(src, dst, x_s.at[slot], x_r.at[slot], x_dev)

    x_h1 = exchange(0, h1.at[0], h1.at[1])
    x_dfeed = exchange(1, dfeed.at[0], dfeed.at[1])
    x_att = exchange(2, sent.at[0], got.at[0])
    x_h2 = exchange(3, h2.at[0], h2.at[1])
    x_dh2 = exchange(4, sent.at[0], got.at[0])
    x_feed = exchange(5, sent.at[1], got.at[1])
    x_datt = exchange(6, datt.at[0], datt.at[1])
    x_dh1 = exchange(7, sent.at[0], got.at[0])

    def put(k, src):
        return pltpu.make_async_copy(src, outputs[k], out_sem.at[k])

    steps = length // (2 * rows)
    stages = ((got, sent), (h2, datt))

    def block_loads(t):
        copies = []
        for k, (array, buf) in enumerate(zip((tokens, cotangent), stages[t % 2])):
            copies.append(pltpu.make_async_copy(array.at[2 * t : 2 * t + 2], buf, tok_sem.at[t % 2, k]))
        return copies

    barrier = pltpu.get_barrier_semaphore()

    def greet(device):
        pl.semaphore_signal(barrier, inc=1, device_id=device, device_id_type=pl.DeviceIdType.MESH)

    for device in (core_dev, x_dev, y_dev):
        greet(device)

    @pl.when(z > 0)
    def _():
        greet(down_dev)

    @pl.when(z < shards - 1)
    def _():
        greet(up_dev)

    for t in range(2):
        for copy in block_loads(t):
            copy.start()
    for i in attn_mats + feed_mats:
        load_own(i).start()

    def begin():
        ends = jnp.where(z == 0, 1, 0) + jnp.where(z == shards - 1, 1, 0)
        pl.semaphore_wait(barrier, 5 - ends)

        @pl.when(z < shards - 1)
        def _():
            send_own_up(attn_mats)

        @pl.when(z > 0)
        def _():
            send_own_down(attn_mats)

        @pl.when(z == 0)
        def _():
            send_own_up(feed_mats)

        @pl.when(z == shards - 1)
        def _():
            send_own_down(feed_mats)

    as_rows = jnp.broadcast_to(routed[...].astype(F32), (8, rows))
    position = jnp.transpose(as_rows)[:, 0:1].astype(jnp.int32)
    flags = jnp.zeros((rows, 1), F32)
    for t in range(steps):
        for copy in block_loads(t):
            copy.wait()
        hit = position == 2 * t * rows + lax.broadcasted_iota(jnp.int32, (rows, 2 * rows), 1)
        chosen = jnp.where(hit, 1.0, 0.0)
        pick = chosen.astype(BF16)
        for k, buf in enumerate(stages[t % 2]):
            picked = mm(pick, buf[...].reshape(2 * rows, width))
            total[k] = picked if t == 0 else total[k] + picked
        if t + 2 < steps:
            for copy in block_loads(t + 2):
                copy.start()
        mask = valid[:, 2 * t * rows : 2 * (t + 1) * rows].astype(F32)
        flags = flags + jnp.sum(chosen * mask, axis=1, keepdims=True)
        if t == steps // 2 - 1:
            begin()
    columns[...] = jnp.broadcast_to(flags, columns.shape)

    def prepare(at, carry):
        row, cot = total[0, at], total[1, at]
        own_z[at] = row.astype(BF16)
        own_c[at] = cot.astype(BF16)
        gate_here = jnp.sum(row * w_router[...], axis=1, keepdims=True) * live(at)
        set_column(0, at, gate_here)
        factor = lax.rsqrt(jnp.mean(row * row, axis=1, keepdims=True) + EPS)
        h1[0, at] = (row * factor * first_gain[...]).astype(BF16)
        dfeed[0, at] = (gate_here * cot).astype(BF16)
        return carry

    row_tiles(rows, prepare)
    x_h1.start()
    x_dfeed.start()

    lane_head = lax.div(lax.broadcasted_iota(jnp.int32, (1, narrow), 1), HEAD_DIM)
    masks = [jnp.where(lane_head == h, 1.0, 0.0) for h in range(heads)]
    masks_low = [mask.astype(BF16) for mask in masks]

    def stacked(value):
        return jnp.concatenate([value * mask for mask in masks_low], axis=0) if heads > 1 else value

    def unstacked(value):
        if heads == 1:
            return value
        picked = value[0:rows] * masks[0]
        for h in range(1, heads):
            picked = picked + value[h * rows : (h + 1) * rows] * masks[h]
        return picked

    score_shape = (heads * rows, rows)
    causal = lax.rem(lax.broadcasted_iota(jnp.int32, score_shape, 0), rows) >= lax.broadcasted_iota(
        jnp.int32, score_shape, 1
    )

    for i in attn_mats:
        load_own(i).wait()

    @pl.when(edge)
    def _():
        for j in range(1, shards):
            arrive(attn_mats, j)
            follow(j)
            if j > 1:
                relay(attn_mats, j - 1)

    @pl.when(inner)
    def _():
        for i in attn_mats:
            for j in (1, 2):
                arrive_one(i, j)
        for j in (1, 2):
            follow(j)
        for j in range(3, shards):
            arrive(attn_mats, j)
            follow(j)
        for j in range(1, shards - 1):
            relay(attn_mats, j)

    x_h1.wait_recv()

    def attend(j, carry):
        s = order(j)

        @pl.when(j + 1 == shards)
        def _():
            relay(attn_mats, j)
            arrive(feed_mats[:1], 1)

        @pl.when(j > 0)
        def _():
            settle(0, j)

        low = mm(h1[...].reshape(2 * rows, width), w_qkv[s]).astype(BF16)
        query = low[:, 0:narrow] * jnp.asarray(HEAD_DIM**-0.5, BF16)
        qkv[s] = jnp.concatenate([query, low[:, narrow:]], axis=1).reshape(2, rows, 3 * narrow)
        for half in range(2):
            query = qkv[s, half, :, 0:narrow]
            key = qkv[s, half, :, narrow : 2 * narrow]
            value = qkv[s, half, :, 2 * narrow : 3 * narrow]
            scores = jnp.where(causal, mm_nt(stacked(query), key), -1e30)
            raised = jnp.exp(scores - jnp.max(scores, axis=1, keepdims=True))
            weights = (raised / jnp.sum(raised, axis=1, keepdims=True)).astype(BF16)
            prob[s, half] = weights
            ctx[s, half * rows : (half + 1) * rows] = unstacked(mm(weights, value)).astype(BF16)
        return carry

    lax.fori_loop(0, shards, attend, 0)

    def project_out(half):
        parts = [ctx[s, half * rows : (half + 1) * rows] for s in range(shards)]
        return mm(jnp.concatenate(parts, axis=1), w_out[...].reshape(shards * narrow, width))

    sent[0] = project_out(1).astype(BF16)
    x_att.start()
    attended[...] = project_out(0)
    arrive(feed_mats[1:], 1)
    arrive(feed_mats[:1], 2)

    @pl.when(inner)
    def _():
        arrive(feed_mats[1:], 2)

    x_att.wait()

    def mix(at, carry):
        att = attended[at] + got[0, at].astype(F32)
        attended[at] = att
        mixed = own_z[at].astype(F32) + att
        factor = lax.rsqrt(jnp.mean(mixed * mixed, axis=1, keepdims=True) + EPS)
        h2[0, at] = (mixed * factor * second_gain[...]).astype(BF16)
        return carry

    row_tiles(rows, mix)
    x_h2.start()

    @pl.when(edge)
    def _():
        arrive(feed_mats[1:], 2)

    x_dfeed.wait_recv()

    def core_send(group, buf, into, s, at=None):
        src = buf.at[s, :, :, 1 - core]
        return remote(src, into.at[s], gc_s.at[group], gc_r.at[group, s], core_dev)

    def y_send(group, buf, into, s):
        return remote(buf.at[s, 1 - y, :, core], into.at[s], gy_s.at[group], gy_r.at[group, s], y_dev)

    def z_send(group, buf, into, s, device, slot):
        src = buf.at[s, y, :, core]
        return remote(src, into.at[slot], gz_s.at[group], gz_r.at[group, slot], device)

    def add_into(ref, *others):
        value = ref[...].astype(F32)
        for other in others:
            value = value + other[...].astype(F32)
        ref[...] = value.astype(BF16)

    def stage_core(group, buf, core_got, y_got, s):
        core_send(group, buf, core_got, s).wait_recv()
        for a in range(2):
            for b in range(2):
                add_into(buf.at[s, a, b, core], core_got.at[s, a, b])
        y_send(group, buf, y_got, s).start()

    def stage_y(group, buf, y_got, s):
        y_send(group, buf, y_got, s).wait_recv()
        for b in range(2):
            add_into(buf.at[s, y, b, core], y_got.at[s, b])

    def line_in(group, buf, z_got, s, slot):
        z_send(group, buf, z_got, s, up_dev, slot).wait_recv()
        for b in range(2):
            add_into(buf.at[s, y, b, core], z_got.at[slot, b])

    def stage_z(group, buf, z_got, s):
        @pl.when(s > z)
        def _():
            @pl.when(z > 0)
            def _():
                line_in(group, buf, z_got, s, s)

            z_send(group, buf, z_got, s, up_dev, s).start()

        @pl.when(s < z)
        def _():
            @pl.when(z < shards - 1)
            def _():
                line_in(group, buf, z_got, s, s)

            slot = jnp.where(s == z - 1, shards, s)
            z_send(group, buf, z_got, s, down_dev, slot).start()

    def swap(group, pair):
        return remote(pair.at[0], pair.at[1], gx_s.at[group], gx_r.at[group], x_dev)

    def stage_last(group, buf, z_got, pair, out):
        for b in range(2):
            out[b] = buf[z, y, b, core].astype(F32)

        @pl.when(z > 0)
        def _():
            z_send(group, buf, z_got, z, up_dev, z).wait_recv()
            out[...] += z_got[z].astype(F32)

        @pl.when(z < shards - 1)
        def _():
            z_send(group, buf, z_got, z, up_dev, shards).wait_recv()
            out[...] += z_got[shards].astype(F32)

        pair[0] = out[1 - x].astype(BF16)
        swap(group, pair).start()

    def stage_out(group, pair, out):
        swap(group, pair).wait_recv()
        out[1 - x] = pair[1].astype(F32)

    def reversed_order(k):
        return order(shards - 1 - k)

    def store_grads(buf, s, left, right, lo, count):
        for a in range(2):
            value = mm(left[2 * a * quarter : 2 * (a + 1) * quarter, :], right).astype(BF16)
            buf[s, a, :, :, :, lo : lo + count] = value.reshape(2, 2, cut, count)

    def line_step(group, buf, y_got, z_got, j):
        s = order(j)
        stage_y(group, buf, y_got, s)
        stage_z(group, buf, z_got, s)

    def feed_line(j):
        line_step(0, grads, y_f, z_f, j)

    def attn_line(j):
        line_step(1, w_up, y_a, z_a, j)

    total[...] = jnp.zeros_like(total)
    for i in feed_mats:
        load_own(i).wait()

    def feed_grads(s):
        store_grads(grads, s, turn_a, dup[s], 0, hidden)
        store_grads(grads, s, turn_b, act[s], hidden, hidden)
        core_send(0, grads, core_f, s).start()

    def feed_core(s):
        stage_core(0, grads, core_f, y_f, s)

    def feed_chunk(s, half):
        part = pl.ds(pl.multiple_of(half * rows, rows), rows)
        up_here = w_up[s].reshape(width, hidden)
        wide[0] = mm(h2[half], up_here)
        wide[1] = mm_nt(dfeed[half], w_down[s])

        def turn(at, inside):
            active, slope = gelu_both(wide[0, at])
            out = pl.ds(pl.multiple_of(half * rows + at.start, TILE), TILE)
            act[s, out] = active.astype(BF16)
            dup[s, out] = (wide[1, at] * slope).astype(BF16)
            return inside

        row_tiles(rows, turn)
        total[half] += mm_nt(dup[s, part], up_here)

    def own_step(j, carry):
        @pl.when(j > 0)
        def _():
            settle(1, j)

        feed_chunk(order(j), 0)

        @pl.when((j > 0) & (j + 2 < shards))
        def _():
            arrive(feed_mats[1:], j + 2)

        relay(feed_mats, j + 1)

        @pl.when(j + 3 < shards)
        def _():
            arrive(feed_mats[:1], j + 3)

        return carry

    lax.fori_loop(0, shards - 2, own_step, 0)
    x_h2.wait_recv()
    turn_a[...] = jnp.transpose(h2[...].reshape(2 * rows, width))
    turn_b[...] = jnp.transpose(dfeed[...].reshape(2 * rows, width))

    quick = shards == 4

    def leaving(k):
        if not quick:
            return shards - 1 - k
        ends, middle = jnp.where(edge, 2, 1), jnp.where(edge, 1, 2)
        return jnp.where(k == 0, ends, jnp.where(k == 1, 3, jnp.where(k == 2, middle, 0)))

    def other_step(k, carry):
        late = jnp.where(quick & edge, 0, shards - 2)
        mine = k == late

        @pl.when(mine)
        def _():
            settle(1, shards - 2)

        plain = jnp.where(k < late, k, shards - 2)
        if quick:
            plain = jnp.where(edge, jnp.where(k < 2, 2, k - 2), jnp.where(k < 2, 1 - k, 2))
        feed_chunk(order(plain), jnp.where(mine, 0, 1))
        if quick:

            @pl.when(k == jnp.where(edge, 1, 0))
            def _():
                feed_grads(order(leaving(0)))

            @pl.when(k == jnp.where(edge, 2, 1))
            def _():
                feed_core(order(leaving(0)))

        return carry

    lax.fori_loop(0, shards, other_step, 0)
    relay(feed_mats, shards - 1)
    settle(1, shards - 1)

    def last_step(k, carry):
        feed_chunk(order(shards - 1), 1 - k)

        @pl.when(k == 0)
        def _():
            sent[0] = total[1].astype(BF16)
            x_dh2.start()

        return carry

    lax.fori_loop(0, 2, last_step, 0)
    first_left = 1 if quick else 0

    def feed_grads_step(k, carry):
        if quick:

            @pl.when((k == shards - 1) & edge)
            def _():
                feed_line(leaving(0))

        feed_grads(order(leaving(k)))

        @pl.when(k > first_left)
        def _():
            feed_core(order(leaving(k - 1)))

        return carry

    lax.fori_loop(first_left, shards, feed_grads_step, 0)
    feed_core(z)

    def feed_rows(half):
        value = mm(act[0, half * rows : (half + 1) * rows], w_down[0])
        for s in range(1, shards):
            value += mm(act[s, half * rows : (half + 1) * rows], w_down[s])
        return value

    sent[1] = feed_rows(1).astype(BF16)
    feed_own[...] = feed_rows(0)
    x_dh2.wait()

    def second_back(at, carry):
        dh2 = total[0, at] + got[0, at].astype(F32)
        mixed = own_z[at].astype(F32) + attended[at]
        factor = lax.rsqrt(jnp.mean(mixed * mixed, axis=1, keepdims=True) + EPS)
        scaled = dh2 * second_gain[...]
        back = factor * scaled - mixed * (factor**3 * jnp.mean(mixed * scaled, axis=1, keepdims=True))
        dmixed[at] = back
        datt[0, at] = (gate(at) * own_c[at].astype(F32) + back).astype(BF16)
        return carry + fold_rows(dh2 * mixed * factor)

    second_sum = row_tiles(rows, second_back, jnp.zeros((8, width), F32))
    x_datt.start()
    x_feed.start()

    def attend_back(half):
        part = slice(half * rows, (half + 1) * rows)

        def step(k, carry):
            s = reversed_order(k)
            dctx = mm_nt(datt[half], w_out[s]).astype(BF16)
            query = qkv[s, half, :, 0:narrow]
            key = qkv[s, half, :, narrow : 2 * narrow]
            value = qkv[s, half, :, 2 * narrow : 3 * narrow]
            weights = prob[s, half]
            dhead = stacked(dctx)
            dweights = mm_nt(dhead, value)
            full = weights.astype(F32)
            dscores = full * (dweights - jnp.sum(dweights * full, axis=1, keepdims=True))
            dscores = dscores.astype(BF16)
            dquery = unstacked(mm(dscores, key)) * HEAD_DIM**-0.5
            dkey = mm_tn(dscores, stacked(query))
            dvalue = mm_tn(weights, dhead)
            act[s, part, 0 : 3 * narrow] = jnp.concatenate([dquery, dkey, dvalue], axis=1).astype(BF16)
            return carry

        lax.fori_loop(0, shards, step, 0)

    def dh1_rows(half):
        part = slice(half * rows, (half + 1) * rows)
        value = mm_nt(act[0, part, 0 : 3 * narrow], w_qkv[0])
        for s in range(1, shards):
            value += mm_nt(act[s, part, 0 : 3 * narrow], w_qkv[s])
        return value

    attend_back(0)
    if quick:
        feed_line(jnp.where(edge, leaving(1), leaving(0)))
    total[0] = dh1_rows(0)
    turn_a[...] = jnp.transpose(h1[...].reshape(2 * rows, width))
    drain(1)
    x_datt.wait_recv()
    turn_b[...] = jnp.transpose(datt[...].reshape(2 * rows, width))

    if quick:
        feed_line(jnp.where(edge, leaving(2), leaving(1)))
    attend_back(1)
    sent[0] = dh1_rows(1).astype(BF16)
    x_dh1.start()

    def attn_grads(k, carry):
        s = reversed_order(k)
        store_grads(w_up, s, turn_a, act[s, :, 0 : 3 * narrow], 0, 3 * narrow)
        store_grads(w_up, s, turn_b, ctx[s], 3 * narrow, narrow)
        core_send(1, w_up, core_a, s).start()

        @pl.when(k > 0)
        def _():
            stage_core(1, w_up, core_a, y_a, reversed_order(k - 1))

        return carry

    lax.fori_loop(0, shards, attn_grads, 0)
    stage_core(1, w_up, core_a, y_a, z)

    x_feed.wait()

    def finish_forward(at, squares):
        branch = attended[at] + feed_own[at] + got[1, at].astype(F32)
        update = gate(at) * branch
        sent[1, at] = (own_z[at].astype(F32) + update).astype(BF16)
        dgate = jnp.sum(own_c[at].astype(F32) * branch, axis=1, keepdims=True)
        set_column(2, at, dgate * live(at))
        return squares + fold_rows(update * update)

    squares = row_tiles(rows, finish_forward, jnp.zeros((8, width), F32))
    put(0, sent.at[1]).start()
    count = jnp.sum(valid[...].astype(F32), axis=1, keepdims=True)
    energy = jnp.sum(jnp.sum(squares, axis=0, keepdims=True), axis=1, keepdims=True)
    rms = jnp.sqrt(energy / (width * jnp.maximum(count, 1.0)))

    def feed_rest(k, carry):
        feed_line(leaving(k))
        return carry

    lax.fori_loop(jnp.where(edge, 3, 2) if quick else 0, shards - 1, feed_rest, 0)

    @pl.when(edge)
    def _():
        attn_line(shards - 1)

    x_dh1.wait()

    def first_back(at, sums):
        dh1 = total[0, at] + got[0, at].astype(F32)
        row = own_z[at].astype(F32)
        factor = lax.rsqrt(jnp.mean(row * row, axis=1, keepdims=True) + EPS)
        scaled = dh1 * first_gain[...]
        back = factor * scaled - row * (factor**3 * jnp.mean(row * scaled, axis=1, keepdims=True))
        back = back + dmixed[at] + dscore(at) * w_router[...]
        got[1, at] = (own_c[at].astype(F32) + back).astype(BF16)
        return sums[0] + fold_rows(dscore(at) * row), sums[1] + fold_rows(dh1 * row * factor)

    zero = jnp.zeros((8, width), F32)
    router_sum, first_sum = row_tiles(rows, first_back, (zero, zero))
    put(1, got.at[1]).start()
    parts = [jnp.sum(part, axis=0, keepdims=True) for part in (router_sum, first_sum, second_sum)]
    small = jnp.concatenate(parts + [jnp.zeros((5, width), F32)], axis=0)

    def small_copy(k):
        return remote(small_send.at[k], small_got.at[k], sm_s.at[k], sm_r.at[k], small_devices[k])

    hops = len(small_devices)
    for k in range(hops):
        small_send[k] = small
        small_copy(k).start()
        small_copy(k).wait()
        small = small + small_got[k]
        if k == 0:

            @pl.when(edge)
            def _():
                attn_line(shards - 2)

            @pl.when(inner)
            def _():
                attn_line(shards - 1)

    def small_spread(far, source):
        slot = hops + source
        return remote(
            small_send.at[hops], small_got.at[slot], sm_s.at[hops + far - 1], sm_r.at[slot], (dp, lax.rem(z + far, shards))
        )

    small_send[hops] = small
    small_got[hops + z] = small
    for far in range(1, shards):
        small_spread(far, z).start()

    def attn_rest(k, carry):
        attn_line(shards - 2 - k)
        return carry

    lax.fori_loop(jnp.where(edge, 1, 0), shards - 2, attn_rest, 0)
    stage_y(0, grads, y_f, z)
    stage_last(0, grads, z_f, swap_f, feed_out)
    for far in range(1, shards):
        small_spread(far, lax.rem(z + shards - far, shards)).wait_recv()
        small_spread(far, z).wait_send()
    small = small_got[hops]
    for k in range(1, shards):
        small = small + small_got[hops + k]
    row_at = lax.broadcasted_iota(jnp.int32, (8, 1), 0)
    small_send[0] = jnp.where(row_at == 3, rms, small)
    put(2, small_send.at[0]).start()
    stage_y(1, w_up, y_a, z)
    stage_last(1, w_up, z_a, swap_a, attn_out)
    stage_out(0, swap_f, feed_out)
    put(4, feed_out).start()
    stage_out(1, swap_a, attn_out)
    put(3, attn_out).start()

    drain(0)
    for copy in (x_h1, x_dfeed, x_h2, x_datt):
        copy.wait_send()

    for group, core_got, y_got, z_got in ((0, core_f, y_f, z_f), (1, core_a, y_a, z_a)):
        remote(core_got, core_got, gc_s.at[group], gc_r.at[group, 0], core_dev).wait_send()
        remote(y_got, y_got, gy_s.at[group], gy_r.at[group, 0], y_dev).wait_send()
        moved = z_got.at[0 : shards - 1]
        remote(moved, moved, gz_s.at[group], gz_r.at[group, 0], up_dev).wait_send()

    swap(0, swap_f).wait_send()
    swap(1, swap_a).wait_send()
    for k, src in enumerate((sent.at[1], got.at[1], small_send.at[0], attn_out, feed_out)):
        put(k, src).wait()


def run_block(size, operands):
    shards, rows, width = size["S"], size["R"], size["D"]
    heads, narrow, hidden, cut = size["hh"], size["n"], size["f"], size["DB"]
    mats = (2 if size["joined"] else 4) + 2
    stages = 3 + shards
    attn, feed = 4 * narrow, 2 * hidden
    dma = pltpu.SemaphoreType.DMA
    vmem = lambda *shape: pltpu.VMEM(shape, BF16)
    full = lambda *shape: pltpu.VMEM(shape, F32)
    scratch = [
        vmem(shards, width, 3 * narrow),
        vmem(shards, narrow, width),
        vmem(shards, 2, 2, 2, cut, hidden),
        vmem(shards, hidden, width),
        *[vmem(2, rows, width) for _ in range(4)],
        *[vmem(width, 2 * rows) for _ in range(2)],
        vmem(shards, 2, rows, 3 * narrow),
        vmem(shards, 2 * rows, narrow),
        vmem(shards, 2, heads * rows, rows),
        vmem(shards, 2 * rows, hidden),
        vmem(shards, 2 * rows, hidden),
        full(2, rows, width),
        full(2, rows, hidden),
        vmem(2, rows, width),
        vmem(2, rows, width),
        vmem(rows, width),
        vmem(rows, width),
        *[full(rows, width) for _ in range(3)],
        full(rows, 128),
        vmem(shards, 2, 2, 2, cut, feed),
        vmem(shards, 2, 2, cut, feed),
        vmem(shards, 2, cut, feed),
        vmem(shards + 1, 2, cut, feed),
        vmem(shards, 2, 2, cut, attn),
        vmem(shards, 2, cut, attn),
        vmem(shards + 1, 2, cut, attn),
        vmem(2, cut, feed),
        vmem(2, cut, attn),
        full(2, cut, attn),
        full(2, cut, feed),
        full(stages, 8, width),
        full(stages, 8, width),
        dma((mats,)),
        dma((2, 2)),
        dma((5,)),
        dma((2, shards + 1)),
        dma((mats, shards)),
        dma((2,)),
        dma((mats, shards)),
        dma((2,)),
        dma((2, shards)),
        dma((8,)),
        dma((8,)),
        dma((2,)),
        dma((2, shards)),
        dma((2,)),
        dma((2, shards)),
        dma((2,)),
        dma((2, shards + 1)),
        dma((2,)),
        dma((2,)),
        dma((stages,)),
        dma((stages,)),
    ]
    near = pl.BlockSpec(memory_space=pltpu.VMEM)
    far = pl.BlockSpec(memory_space=pl.ANY)
    outs = [
        jax.ShapeDtypeStruct((rows, width), BF16),
        jax.ShapeDtypeStruct((rows, width), BF16),
        jax.ShapeDtypeStruct((8, width), F32),
        jax.ShapeDtypeStruct((2, cut, attn), F32),
        jax.ShapeDtypeStruct((2, cut, feed), F32),
    ]
    return pl.pallas_call(
        functools.partial(block_kernel, size),
        out_shape=outs,
        in_specs=[far, far] + [near] * 5 + [far] * (len(operands) - 7),
        out_specs=[pl.BlockSpec(memory_space=pltpu.HBM)] * len(outs),
        scratch_shapes=scratch,
        compiler_params=pltpu.CompilerParams(
            collective_id=0, has_side_effects=True, vmem_limit_bytes=64 * 2**20 - 65536
        ),
    )(*operands)


def place_kernel(size, assemble, routed, small, tokens, cotangent, *refs):
    length, width, rows = size["L"], size["D"], size["R"]
    gathered, refs = refs[: 4 if assemble else 2], refs[4 if assemble else 2 :]
    outs, refs = refs[: 12 if assemble else 2], refs[12 if assemble else 2 :]
    bases, staged, refs = refs[:2], refs[2 : 2 + len(gathered)], refs[2 + len(gathered) :]
    finals, (pick, keep, in_sem, out_sem, part_sem, final_sem) = refs[:-6], refs[-6:]
    block = 512
    steps = width // block

    def moving(src, dst, sem, k, b):
        at = (slice(None), pl.ds(b * block, block))
        return pltpu.make_async_copy(src[k].at[at], dst[k].at[at], sem.at[k, b])

    sources = (tokens, cotangent)
    parts = [pltpu.make_async_copy(src, dst, part_sem.at[k]) for k, (src, dst) in enumerate(zip(gathered, staged))]
    for copy in parts[:2]:
        copy.start()
    for b in range(steps):
        for k in range(2):
            moving(sources, bases, in_sem, k, b).start()
    for copy in parts[2:]:
        copy.start()
    line = lax.broadcasted_iota(jnp.int32, (length, rows), 0)
    chosen = jnp.where(line == routed[...], 1.0, 0.0)
    pick[...] = chosen.astype(BF16)
    keep[...] = jnp.broadcast_to((1.0 - jnp.sum(chosen, axis=1, keepdims=True)).astype(BF16), keep.shape)
    for copy in parts[:2]:
        copy.wait()
    for b in range(steps):
        for k in range(2):
            at = slice(b * block, (b + 1) * block)
            moving(sources, bases, in_sem, k, b).wait()
            kept = jnp.concatenate([keep[...]] * (block // 128), axis=1)
            bases[k][:, at] = mm(pick[...], staged[k][:, at]).astype(BF16) + bases[k][:, at] * kept
            moving(bases, outs, out_sem, k, b).start()
    last = []
    if assemble:
        for copy in parts[2:]:
            copy.wait()
        for k, value in enumerate(weight_outputs(size, *staged[2:])):
            finals[k][...] = value
            last.append(pltpu.make_async_copy(finals[k], outs[2 + k], final_sem.at[k]))
            last[-1].start()
        for k in range(3):
            outs[8 + k][...] = small[k : k + 1, :]
        outs[11][...] = small[3:4, 0:1]
    for b in range(steps):
        for k in range(2):
            moving(bases, outs, out_sem, k, b).wait()
    for copy in last:
        copy.wait()


def weight_outputs(size, attn, feed):
    narrow, hidden = size["n"], size["f"]

    def side_by_side(ref, lo, count):
        return jnp.concatenate([ref[0, :, lo : lo + count], ref[1, :, lo : lo + count]], axis=1)

    return (
        side_by_side(attn, 0, narrow),
        side_by_side(attn, narrow, narrow),
        side_by_side(attn, 2 * narrow, narrow),
        side_by_side(attn, 3 * narrow, narrow).T,
        side_by_side(feed, 0, hidden),
        side_by_side(feed, hidden, hidden).T,
    )


def place_rows(size, routed, tokens, cotangent, rows_res, rows_grad, small, attn, feed, assemble):
    length, width, rows = size["L"], size["D"], size["R"]
    cut, narrow, hidden = size["DB"], size["n"], size["f"]
    whole = lambda *shape: pl.BlockSpec(shape, lambda i: (0,) * len(shape))
    far = pl.BlockSpec(memory_space=pltpu.HBM)
    outs, out_specs = [jax.ShapeDtypeStruct((length, width), BF16)] * 2, [far] * 2
    gathered, finals = [rows_res, rows_grad], []
    if assemble:
        gathered += [attn, feed]
        finals = [(cut, 2 * narrow)] * 3 + [(2 * narrow, cut), (cut, 2 * hidden), (2 * hidden, cut)]
        tiny = [(1, width)] * 3 + [(1, 1)]
        outs = outs + [jax.ShapeDtypeStruct(shape, F32) for shape in finals + tiny]
        out_specs = out_specs + [far] * len(finals) + [whole(*shape) for shape in tiny]
    dma = pltpu.SemaphoreType.DMA
    return pl.pallas_call(
        functools.partial(place_kernel, size, assemble),
        grid=(1,),
        out_shape=outs,
        in_specs=[whole(1, rows), whole(*small.shape)] + [far] * (2 + len(gathered)),
        out_specs=out_specs,
        scratch_shapes=[
            *[pltpu.VMEM((length, width), BF16) for _ in range(2)],
            *[pltpu.VMEM(part.shape, part.dtype) for part in gathered],
            *[pltpu.VMEM(shape, F32) for shape in finals],
            pltpu.VMEM((length, rows), BF16),
            pltpu.VMEM((length, 128), BF16),
            dma((2, width // 512)),
            dma((2, width // 512)),
            dma((4,)),
            dma((6,)),
        ],
        compiler_params=pltpu.CompilerParams(vmem_limit_bytes=60 * 2**20),
    )(routed, small, tokens, cotangent, *gathered)


def shards_of(
    groups,
    tokens,
    cotangent,
    routed,
    valid_mask,
    w_router,
    first_gain,
    query_weight,
    key_weight,
    value_weight,
    output_weight,
    second_gain,
    up_weight,
    down_weight,
):
    shards, data = lax.axis_size("mp"), lax.axis_size("dp")
    _, length, width = tokens.shape
    rows = routed.shape[1]
    narrow = query_weight.shape[1] // 2
    hidden = up_weight.shape[1] // 2
    cut = width // 8
    chips_x = 1 << ((data // 2).bit_length() - 1) // 2
    size = dict(
        S=shards, ybit=2 * chips_x, R=rows, D=width, L=length, hh=narrow // HEAD_DIM,
        n=narrow, f=hidden, DB=cut, joined=narrow % 128 != 0,
    )
    dp = lax.axis_index("dp")
    x, y = (dp // 2) % 2, (dp // size["ybit"]) % 2
    qkv = (query_weight, key_weight, value_weight)
    if size["joined"]:
        halves = [lax.dynamic_slice_in_dim(weight, x * narrow, narrow, 1) for weight in qkv]
        qkv = (jnp.concatenate(halves, axis=1),)
    row = lambda vector: vector.reshape(1, width)
    operands = (
        tokens.reshape(-1, rows, width), cotangent.reshape(-1, rows, width), routed, valid_mask, row(w_router), row(first_gain), row(second_gain),
        *qkv, output_weight, up_weight.reshape(2, 2, 2, cut, 2 * hidden), down_weight,
    )
    rows_res, rows_grad, small, attn, feed = run_block(size, operands)
    whole_group = data == 8
    rms = small[3, 0:1]
    if not whole_group:
        block = 4 * y + 2 * x + dp % 2

        def over_groups(part):
            base = jnp.zeros((2, width, part.shape[2]), F32)
            placed = lax.dynamic_update_slice_in_dim(base, part, block * cut, 1)
            return lax.psum_scatter(placed, "dp", scatter_dimension=1, tiled=True)

        attn, feed = over_groups(attn), over_groups(feed)
        small = lax.psum(small, "dp") / 8.0
    placed = place_rows(size, routed, tokens[0], cotangent[0], rows_res, rows_grad, small, attn, feed, whole_group)
    residual, grad_tokens = placed[:2]
    if whole_group:
        vectors = [vector.reshape(width) for vector in placed[8:11]]
        weights, rms = placed[2:8], placed[11].reshape(1)
    else:
        vectors, weights = [small[k] for k in range(3)], weight_outputs(size, attn, feed)
    grad_query, grad_key, grad_value, grad_output, grad_up, grad_down = weights
    return (
        residual[None],
        grad_tokens[None],
        rms,
        vectors[0],
        vectors[1],
        grad_query,
        grad_key,
        grad_value,
        grad_output,
        vectors[2],
        grad_up,
        grad_down,
    )


def solution(mesh):
    in_specs = (
        P(("dp", "mp"), None, None),
        P(("dp", "mp"), None, None),
        P(("dp", "mp"), None),
        P(("dp", "mp"), None),
        P(),
        P(),
        P(None, "mp"),
        P(None, "mp"),
        P(None, "mp"),
        P("mp", None),
        P(),
        P(None, "mp"),
        P("mp", None),
    )
    out_specs = (
        P(("dp", "mp"), None, None),
        P(("dp", "mp"), None, None),
        P(("dp", "mp")),
        P(),
        P(),
        P("dp", "mp"),
        P("dp", "mp"),
        P("dp", "mp"),
        P("mp", "dp"),
        P(),
        P("dp", "mp"),
        P("mp", "dp"),
    )
    body = functools.partial(shards_of, mesh.shape["dp"] // 8)
    return jax.shard_map(body, mesh=mesh, in_specs=in_specs, out_specs=out_specs, check_vma=False)
```

```python
import functools
import math

import jax
import jax.numpy as jnp
from jax import lax
from jax.experimental import pallas as pl
from jax.experimental.pallas import tpu as pltpu
from jax.sharding import PartitionSpec as P

HEADS = 16
HEAD_DIM = 64
EPS = 1e-06
F32 = jnp.float32
BF16 = jnp.bfloat16
TILE = 64


def mm(left, right):
    return jnp.dot(left, right, preferred_element_type=F32)


def mm_nt(left, right):
    return lax.dot_general(left, right, (((1,), (1,)), ((), ())), preferred_element_type=F32)


def mm_tn(left, right):
    return lax.dot_general(left, right, (((0,), (0,)), ((), ())), preferred_element_type=F32)


def row_tiles(rows, body, init=0):
    def step(index, carry):
        return body(pl.ds(pl.multiple_of(index * TILE, TILE), TILE), carry)

    return lax.fori_loop(0, rows // TILE, step, init)


def fold_rows(value):
    return jnp.sum(value.reshape(-1, 8, value.shape[-1]), axis=0)


def gelu_both(value):
    cdf = 0.5 * (1.0 + lax.erf(value * math.sqrt(0.5)))
    density = jnp.exp(-0.5 * value * value) * (1.0 / math.sqrt(2.0 * math.pi))
    return value * cdf, cdf + value * density


def block_kernel(size, *refs):
    shards, ybit, rows, width, length = size["S"], size["ybit"], size["R"], size["D"], size["L"]
    heads, narrow, hidden, cut = size["hh"], size["n"], size["f"], size["DB"]
    joined = size["joined"]
    quarter = 2 * cut
    refs = list(refs)

    def take(count):
        taken, refs[:count] = refs[:count], []
        return taken

    tokens, cotangent, routed, valid, w_router, first_gain, second_gain = take(7)
    qkv_in = take(1 if joined else 3)
    out_in, up_in, down_in = take(3)
    outputs = take(5)
    w_qkv, w_out, w_up, w_down = take(4)
    h1, dfeed, h2, datt, turn_a, turn_b = take(6)
    qkv, ctx, prob, act, dup = take(5)
    total, wide, sent, got = take(4)
    own_z, own_c, attended, dmixed, feed_own, columns = take(6)
    lane = lax.broadcasted_iota(jnp.int32, (1, 128), 1)

    def column(k, at):
        return columns[at][:, k : k + 1]

    def set_column(k, at, value):
        columns[at] = jnp.where(lane == k, value, columns[at])

    gate, live, dscore = (functools.partial(column, k) for k in range(3))
    grads, core_f, y_f, z_f, core_a, y_a, z_a, swap_f, swap_a = take(9)
    attn_out, feed_out = take(2)
    small_send, small_got = take(2)
    load_sem, tok_sem, out_sem = take(3)
    wz_s, wz_r, wy_s, wy_r, wc_s, wc_r = take(6)
    x_s, x_r = take(2)
    gc_s, gc_r, gy_s, gy_r, gz_s, gz_r, gx_s, gx_r = take(8)
    sm_s, sm_r = take(2)

    dp = lax.axis_index("dp")
    z = lax.axis_index("mp")
    core = lax.rem(dp, 2)
    x = lax.rem(lax.div(dp, 2), 2)
    y = lax.rem(lax.div(dp, ybit), 2)
    core_dev = (dp + 1 - 2 * core, z)
    x_dev = (dp + 2 * (1 - 2 * x), z)
    y_dev = (dp + ybit * (1 - 2 * y), z)
    up_dev = (dp, z + 1)
    down_dev = (dp, z - 1)
    small_devices = [core_dev, x_dev, (dp + 2 * (1 - 2 * x) + ybit * (1 - 2 * y), z)]

    def remote(src, dst, send, recv, device):
        return pltpu.make_async_remote_copy(
            src_ref=src,
            dst_ref=dst,
            send_sem=send,
            recv_sem=recv,
            device_id=device,
            device_id_type=pl.DeviceIdType.MESH,
        )

    def order(j):
        high = lax.div(z, shards // 2)
        base = z + high * (shards - 1 - 2 * z)
        odd = lax.rem(j, 2)
        near = base + lax.div(j + 1, 2) * (2 * odd - 1)
        pick = jnp.where(j <= 2 * base, near, j)
        return pick + high * (shards - 1 - 2 * pick)

    attn_mats = list(range(len(qkv_in) + 1))
    feed_mats = [len(attn_mats), len(attn_mats) + 1]
    out_at, up_at = attn_mats[-1], feed_mats[0]

    def span(qy, qc):
        return pl.ds(pl.multiple_of((2 * qy + qc) * quarter, quarter), quarter)

    def lanes(count):
        return pl.ds(pl.multiple_of(x * count, count), count)

    def held(i, s, qy, qc):
        if i < out_at:
            part = w_qkv if joined else w_qkv.at[:, :, i * narrow : (i + 1) * narrow]
            return part.at[s, span(qy, qc)]
        if i == out_at:
            return w_out.at[s, :, span(qy, qc)]
        if i == up_at:
            return w_up.at[s, qy, qc]
        return w_down.at[s, :, span(qy, qc)]

    def own_piece(i):
        if i < out_at:
            part = qkv_in[i].at[span(y, core)]
            return part if joined else part.at[:, lanes(narrow)]
        if i == out_at:
            return out_in.at[lanes(narrow), span(y, core)]
        if i == up_at:
            return up_in.at[y, core, :, :, lanes(hidden)]
        return down_in.at[lanes(hidden), span(y, core)]

    def load_own(i):
        if i < out_at:
            if joined:
                src, dst = qkv_in[i], w_qkv.at[z]
            else:
                src, dst = qkv_in[i].at[:, lanes(narrow)], w_qkv.at[z, :, i * narrow : (i + 1) * narrow]
        elif i == out_at:
            src, dst = out_in.at[lanes(narrow), :], w_out.at[z]
        elif i == up_at:
            src, dst = up_in.at[:, :, :, :, lanes(hidden)], w_up.at[z]
        else:
            src, dst = down_in.at[lanes(hidden), :], w_down.at[z]
        return pltpu.make_async_copy(src, dst, load_sem.at[i])

    def group_of(i):
        return 0 if i <= out_at else 1

    def own_up(i):
        return remote(own_piece(i), held(i, z, y, core), wz_s.at[group_of(i), z], wz_r.at[i, z], up_dev)

    def own_down(i):
        return remote(own_piece(i), held(i, z, y, core), wz_s.at[group_of(i), shards], wz_r.at[i, z], down_dev)

    def pass_on(i, s, device):
        piece = held(i, s, y, core)
        return remote(piece, piece, wz_s.at[group_of(i), s], wz_r.at[i, s], device)

    def across_y(i, s, qy):
        piece = held(i, s, qy, core)
        return remote(piece, piece, wy_s.at[group_of(i)], wy_r.at[i, s], y_dev)

    def across_core(i, s, qy, qc):
        piece = held(i, s, qy, qc)
        group = group_of(i)
        return remote(piece, piece, wc_s.at[group], wc_r.at[group, s], core_dev)

    def await_pieces(group, sem, count, receiving=False):
        mats = attn_mats if group == 0 else feed_mats
        if joined:
            refs = [held(i, 0, 0, 0) for i in mats] * count
        else:
            flat = w_up.at[0, 0, 0] if group == 0 else w_up.at[0, 0]
            if count == 2:
                flat = w_up.at[0, 0] if group == 0 else w_up.at[0]
            elif count == shards - 1:
                flat = w_up.at[0 : shards - 1, 0, 0] if group == 0 else w_up.at[0 : shards - 1, 0]
            elif count == 2 * (shards - 1):
                flat = w_up.at[0 : shards - 1, 0] if group == 0 else w_up.at[0 : shards - 1]
            refs = [flat]
        for ref in refs:
            if receiving:
                remote(ref, ref, wc_s.at[group], sem, core_dev).wait_recv()
            else:
                remote(ref, ref, sem, wc_r.at[group, 0], core_dev).wait_send()

    def send_own_up(mats):
        for i in mats:
            own_up(i).start()

    def send_own_down(mats):
        for i in mats:
            own_down(i).start()

    def passing(s, action):
        @pl.when((s < z) & (z < shards - 1))
        def _():
            action(up_dev)

        @pl.when((s > z) & (z > 0))
        def _():
            action(down_dev)

    edge = (z == 0) | (z == shards - 1)
    inner = jnp.logical_not(edge)

    def arrive_one(i, j):
        s = order(j)
        pass_on(i, s, up_dev).wait_recv()
        passing(s, lambda device: pass_on(i, s, device).start())
        across_y(i, s, y).start()
        across_core(i, s, y, core).start()

    def arrive(mats, j):
        for i in mats:
            arrive_one(i, j)

    def follow(j):
        s = order(j)

        @pl.when((s == 0) & (z < shards - 1))
        def _():
            send_own_up(feed_mats)

        @pl.when((s == shards - 1) & (z > 0))
        def _():
            send_own_down(feed_mats)

    def relay(mats, j):
        s = order(j)
        for i in mats:
            across_y(i, s, 1 - y).wait_recv()
            across_core(i, s, 1 - y, core).start()

    def settle(group, j):
        await_pieces(group, wc_r.at[group, order(j)], 2, True)

    def drain(group):
        @pl.when(z < shards - 1)
        def _():
            await_pieces(group, wz_s.at[group, z], 1)

        @pl.when(z > 0)
        def _():
            await_pieces(group, wz_s.at[group, shards], 1)

        def step(j, carry):
            s = order(j)
            passing(s, lambda device: await_pieces(group, wz_s.at[group, s], 1))
            return carry

        lax.fori_loop(1, shards, step, 0)
        await_pieces(group, wy_s.at[group], shards - 1)
        await_pieces(group, wc_s.at[group], 2 * (shards - 1))

    def exchange(slot, src, dst):
        return remote(src, dst, x_s.at[slot], x_r.at[slot], x_dev)

    x_h1 = exchange(0, h1.at[0], h1.at[1])
    x_dfeed = exchange(1, dfeed.at[0], dfeed.at[1])
    x_att = exchange(2, sent.at[0], got.at[0])
    x_h2 = exchange(3, h2.at[0], h2.at[1])
    x_dh2 = exchange(4, sent.at[0], got.at[0])
    x_feed = exchange(5, sent.at[1], got.at[1])
    x_datt = exchange(6, datt.at[0], datt.at[1])
    x_dh1 = exchange(7, sent.at[0], got.at[0])

    def put(k, src):
        return pltpu.make_async_copy(src, outputs[k], out_sem.at[k])

    steps = length // (2 * rows)
    stages = ((got, sent), (h2, datt))

    def block_loads(t):
        copies = []
        for k, (array, buf) in enumerate(zip((tokens, cotangent), stages[t % 2])):
            copies.append(pltpu.make_async_copy(array.at[2 * t : 2 * t + 2], buf, tok_sem.at[t % 2, k]))
        return copies

    barrier = pltpu.get_barrier_semaphore()

    def greet(device):
        pl.semaphore_signal(barrier, inc=1, device_id=device, device_id_type=pl.DeviceIdType.MESH)

    for device in (core_dev, x_dev, y_dev):
        greet(device)

    @pl.when(z > 0)
    def _():
        greet(down_dev)

    @pl.when(z < shards - 1)
    def _():
        greet(up_dev)

    for t in range(2):
        for copy in block_loads(t):
            copy.start()
    for i in attn_mats + feed_mats:
        load_own(i).start()

    def begin():
        ends = jnp.where(z == 0, 1, 0) + jnp.where(z == shards - 1, 1, 0)
        pl.semaphore_wait(barrier, 5 - ends)

        @pl.when(z < shards - 1)
        def _():
            send_own_up(attn_mats)

        @pl.when(z > 0)
        def _():
            send_own_down(attn_mats)

        @pl.when(z == 0)
        def _():
            send_own_up(feed_mats)

        @pl.when(z == shards - 1)
        def _():
            send_own_down(feed_mats)

    as_rows = jnp.broadcast_to(routed[...].astype(F32), (8, rows))
    position = jnp.transpose(as_rows)[:, 0:1].astype(jnp.int32)
    flags = jnp.zeros((rows, 1), F32)
    for t in range(steps):
        for copy in block_loads(t):
            copy.wait()
        hit = position == 2 * t * rows + lax.broadcasted_iota(jnp.int32, (rows, 2 * rows), 1)
        chosen = jnp.where(hit, 1.0, 0.0)
        pick = chosen.astype(BF16)
        for k, buf in enumerate(stages[t % 2]):
            picked = mm(pick, buf[...].reshape(2 * rows, width))
            total[k] = picked if t == 0 else total[k] + picked
        if t + 2 < steps:
            for copy in block_loads(t + 2):
                copy.start()
        mask = valid[:, 2 * t * rows : 2 * (t + 1) * rows].astype(F32)
        flags = flags + jnp.sum(chosen * mask, axis=1, keepdims=True)
        if t == steps // 2 - 1:
            begin()
    columns[...] = jnp.broadcast_to(flags, columns.shape)

    def prepare(at, carry):
        row, cot = total[0, at], total[1, at]
        own_z[at] = row.astype(BF16)
        own_c[at] = cot.astype(BF16)
        gate_here = jnp.sum(row * w_router[...], axis=1, keepdims=True) * live(at)
        set_column(0, at, gate_here)
        factor = lax.rsqrt(jnp.mean(row * row, axis=1, keepdims=True) + EPS)
        h1[0, at] = (row * factor * first_gain[...]).astype(BF16)
        dfeed[0, at] = (gate_here * cot).astype(BF16)
        return carry

    row_tiles(rows, prepare)
    x_h1.start()
    x_dfeed.start()

    lane_head = lax.div(lax.broadcasted_iota(jnp.int32, (1, narrow), 1), HEAD_DIM)
    masks = [jnp.where(lane_head == h, 1.0, 0.0) for h in range(heads)]
    masks_low = [mask.astype(BF16) for mask in masks]

    def stacked(value):
        return jnp.concatenate([value * mask for mask in masks_low], axis=0) if heads > 1 else value

    def unstacked(value):
        if heads == 1:
            return value
        picked = value[0:rows] * masks[0]
        for h in range(1, heads):
            picked = picked + value[h * rows : (h + 1) * rows] * masks[h]
        return picked

    score_shape = (heads * rows, rows)
    causal = lax.rem(lax.broadcasted_iota(jnp.int32, score_shape, 0), rows) >= lax.broadcasted_iota(
        jnp.int32, score_shape, 1
    )

    for i in attn_mats:
        load_own(i).wait()

    @pl.when(edge)
    def _():
        for j in range(1, shards):
            arrive(attn_mats, j)
            follow(j)
            if j > 1:
                relay(attn_mats, j - 1)

    @pl.when(inner)
    def _():
        for i in attn_mats:
            for j in (1, 2):
                arrive_one(i, j)
        for j in (1, 2):
            follow(j)
        for j in range(3, shards):
            arrive(attn_mats, j)
            follow(j)
        for j in range(1, shards - 1):
            relay(attn_mats, j)

    x_h1.wait_recv()

    def attend(j, carry):
        s = order(j)

        @pl.when(j + 1 == shards)
        def _():
            relay(attn_mats, j)
            arrive(feed_mats[:1], 1)

        @pl.when(j > 0)
        def _():
            settle(0, j)

        low = mm(h1[...].reshape(2 * rows, width), w_qkv[s]).astype(BF16)
        query = low[:, 0:narrow] * jnp.asarray(HEAD_DIM**-0.5, BF16)
        qkv[s] = jnp.concatenate([query, low[:, narrow:]], axis=1).reshape(2, rows, 3 * narrow)
        for half in range(2):
            query = qkv[s, half, :, 0:narrow]
            key = qkv[s, half, :, narrow : 2 * narrow]
            value = qkv[s, half, :, 2 * narrow : 3 * narrow]
            scores = jnp.where(causal, mm_nt(stacked(query), key), -1e30)
            raised = jnp.exp(scores - jnp.max(scores, axis=1, keepdims=True))
            weights = (raised / jnp.sum(raised, axis=1, keepdims=True)).astype(BF16)
            prob[s, half] = weights
            ctx[s, half * rows : (half + 1) * rows] = unstacked(mm(weights, value)).astype(BF16)
        return carry

    lax.fori_loop(0, shards, attend, 0)

    def project_out(half):
        parts = [ctx[s, half * rows : (half + 1) * rows] for s in range(shards)]
        return mm(jnp.concatenate(parts, axis=1), w_out[...].reshape(shards * narrow, width))

    sent[0] = project_out(1).astype(BF16)
    x_att.start()
    attended[...] = project_out(0)
    arrive(feed_mats[1:], 1)
    arrive(feed_mats[:1], 2)

    @pl.when(inner)
    def _():
        arrive(feed_mats[1:], 2)

    x_att.wait()

    def mix(at, carry):
        att = attended[at] + got[0, at].astype(F32)
        attended[at] = att
        mixed = own_z[at].astype(F32) + att
        factor = lax.rsqrt(jnp.mean(mixed * mixed, axis=1, keepdims=True) + EPS)
        h2[0, at] = (mixed * factor * second_gain[...]).astype(BF16)
        return carry

    row_tiles(rows, mix)
    x_h2.start()

    @pl.when(edge)
    def _():
        arrive(feed_mats[1:], 2)

    x_dfeed.wait_recv()

    def core_send(group, buf, into, s, at=None):
        src = buf.at[s, :, :, 1 - core]
        return remote(src, into.at[s], gc_s.at[group], gc_r.at[group, s], core_dev)

    halves = (1 - x, x)

    def y_send(group, buf, into, s, b):
        src = buf.at[s, 1 - y, b, core]
        return remote(src, into.at[s, b], gy_s.at[group], gy_r.at[group, s, b], y_dev)

    def z_send(group, buf, into, s, device, slot, b):
        src = buf.at[s, y, b, core]
        return remote(src, into.at[slot, b], gz_s.at[group], gz_r.at[group, slot, b], device)

    def add_into(ref, other):
        ref[...] = (ref[...].astype(F32) + other[...].astype(F32)).astype(BF16)

    def stage_core(group, buf, core_got, y_got, s):
        core_send(group, buf, core_got, s).wait_recv()
        for b in halves:
            add_into(buf.at[s, 1 - y, b, core], core_got.at[s, 1 - y, b])
            y_send(group, buf, y_got, s, b).start()
        for b in range(2):
            add_into(buf.at[s, y, b, core], core_got.at[s, y, b])

    def stage_y(group, buf, y_got, s, b):
        y_send(group, buf, y_got, s, b).wait_recv()
        add_into(buf.at[s, y, b, core], y_got.at[s, b])

    def line_in(group, buf, z_got, s, slot, b):
        z_send(group, buf, z_got, s, up_dev, slot, b).wait_recv()
        add_into(buf.at[s, y, b, core], z_got.at[slot, b])

    def stage_z(group, buf, z_got, s, b):
        @pl.when(s > z)
        def _():
            @pl.when(z > 0)
            def _():
                line_in(group, buf, z_got, s, s, b)

            z_send(group, buf, z_got, s, up_dev, s, b).start()

        @pl.when(s < z)
        def _():
            @pl.when(z < shards - 1)
            def _():
                line_in(group, buf, z_got, s, s, b)

            slot = jnp.where(s == z - 1, shards, s)
            z_send(group, buf, z_got, s, down_dev, slot, b).start()

    def swap(group, pair):
        return remote(pair.at[0], pair.at[1], gx_s.at[group], gx_r.at[group], x_dev)

    def stage_last(group, buf, y_got, z_got, pair, out):
        for b in halves:
            stage_y(group, buf, y_got, z, b)
            out[b] = buf[z, y, b, core].astype(F32)

            @pl.when(z > 0)
            def _():
                z_send(group, buf, z_got, z, up_dev, z, b).wait_recv()
                out[b] += z_got[z, b].astype(F32)

            @pl.when(z < shards - 1)
            def _():
                z_send(group, buf, z_got, z, up_dev, shards, b).wait_recv()
                out[b] += z_got[shards, b].astype(F32)

            if b is halves[0]:
                pair[0] = out[b].astype(BF16)
                swap(group, pair).start()

    def stage_out(group, pair, out):
        swap(group, pair).wait_recv()
        out[1 - x] = pair[1].astype(F32)

    def reversed_order(k):
        return order(shards - 1 - k)

    def store_grads(buf, s, left, right, lo, count):
        for a in range(2):
            value = mm(left[2 * a * quarter : 2 * (a + 1) * quarter, :], right).astype(BF16)
            buf[s, a, :, :, :, lo : lo + count] = value.reshape(2, 2, cut, count)

    def line_half(group, buf, y_got, z_got, s, m):
        b = jnp.where(lax.rem(m, 2) == 0, 1 - x, x)
        stage_y(group, buf, y_got, s, b)
        stage_z(group, buf, z_got, s, b)

    def feed_half(m):
        line_half(0, grads, y_f, z_f, order(leaving(lax.div(m, 2))), m)

    def attn_half(m):
        line_half(1, w_up, y_a, z_a, reversed_order(lax.div(m, 2)), m)

    def run_halves(step, first, last):
        def body(m, carry):
            step(m)
            return carry

        lax.fori_loop(first, last, body, 0)

    total_halves = 2 * (shards - 1)

    quick = shards == 4

    def leaving(k):
        if not quick:
            return shards - 1 - k
        ends, middle = jnp.where(edge, 2, 1), jnp.where(edge, 1, 2)
        return jnp.where(k == 0, ends, jnp.where(k == 1, 3, jnp.where(k == 2, middle, 0)))

    def feed_point(ends, middle):
        if quick and ends is not None:

            @pl.when(edge)
            def _():
                run_halves(feed_half, *ends)

        if quick and middle is not None:

            @pl.when(inner)
            def _():
                run_halves(feed_half, *middle)

    total[...] = jnp.zeros_like(total)
    for i in feed_mats:
        load_own(i).wait()

    def feed_grads(s):
        store_grads(grads, s, turn_a, dup[s], 0, hidden)
        store_grads(grads, s, turn_b, act[s], hidden, hidden)
        core_send(0, grads, core_f, s).start()

    def feed_core(s):
        stage_core(0, grads, core_f, y_f, s)

    def feed_chunk(s, half):
        part = pl.ds(pl.multiple_of(half * rows, rows), rows)
        up_here = w_up[s].reshape(width, hidden)
        wide[0] = mm(h2[half], up_here)
        wide[1] = mm_nt(dfeed[half], w_down[s])

        def turn(at, inside):
            active, slope = gelu_both(wide[0, at])
            out = pl.ds(pl.multiple_of(half * rows + at.start, TILE), TILE)
            act[s, out] = active.astype(BF16)
            dup[s, out] = (wide[1, at] * slope).astype(BF16)
            return inside

        row_tiles(rows, turn)
        total[half] += mm_nt(dup[s, part], up_here)

    def own_step(j, carry):
        @pl.when(j > 0)
        def _():
            settle(1, j)

        feed_chunk(order(j), 0)

        @pl.when((j > 1) & (j + 1 < shards))
        def _():
            arrive(feed_mats[1:], j + 1)

        @pl.when(j + 2 < shards)
        def _():
            relay(feed_mats, j + 1)

        @pl.when(j + 3 < shards)
        def _():
            arrive(feed_mats[:1], j + 3)

        return carry

    lax.fori_loop(0, shards - 1, own_step, 0)
    x_h2.wait_recv()
    turn_a[...] = jnp.transpose(h2[...].reshape(2 * rows, width))
    turn_b[...] = jnp.transpose(dfeed[...].reshape(2 * rows, width))

    def other_step(k, carry):
        j = k
        if quick:
            j = jnp.where(edge, jnp.where(k == 0, 2, k - 1), jnp.where(k < 2, 1 - k, k))
        feed_chunk(order(j), 1)
        if quick:

            @pl.when(k == 0)
            def _():
                feed_grads(order(leaving(0)))

            @pl.when(k == 1)
            def _():
                feed_core(order(leaving(0)))

        return carry

    lax.fori_loop(0, shards - 1, other_step, 0)
    relay(feed_mats, shards - 1)
    settle(1, shards - 1)

    def last_step(k, carry):
        feed_chunk(order(shards - 1), 1 - k)

        @pl.when(k == 0)
        def _():
            sent[0] = total[1].astype(BF16)
            x_dh2.start()

        return carry

    lax.fori_loop(0, 2, last_step, 0)
    first_left = 1 if quick else 0

    def feed_grads_step(k, carry):
        if quick:

            @pl.when((k == 2) & edge)
            def _():
                feed_half(0)

        feed_grads(order(leaving(k)))

        @pl.when(k > first_left)
        def _():
            feed_core(order(leaving(k - 1)))

        return carry

    lax.fori_loop(first_left, shards, feed_grads_step, 0)
    feed_point((1, 2), None)
    feed_core(z)

    def feed_rows(half):
        value = mm(act[0, half * rows : (half + 1) * rows], w_down[0])
        for s in range(1, shards):
            value += mm(act[s, half * rows : (half + 1) * rows], w_down[s])
        return value

    x_dh2.wait()

    def second_back(at, carry):
        dh2 = total[0, at] + got[0, at].astype(F32)
        mixed = own_z[at].astype(F32) + attended[at]
        factor = lax.rsqrt(jnp.mean(mixed * mixed, axis=1, keepdims=True) + EPS)
        scaled = dh2 * second_gain[...]
        back = factor * scaled - mixed * (factor**3 * jnp.mean(mixed * scaled, axis=1, keepdims=True))
        dmixed[at] = back
        datt[0, at] = (gate(at) * own_c[at].astype(F32) + back).astype(BF16)
        return carry + fold_rows(dh2 * mixed * factor)

    second_sum = row_tiles(rows, second_back, jnp.zeros((8, width), F32))
    x_datt.start()
    sent[1] = feed_rows(1).astype(BF16)
    x_feed.start()
    feed_point((2, 3), (0, 1))
    feed_own[...] = feed_rows(0)

    def attend_back(half):
        part = slice(half * rows, (half + 1) * rows)

        def step(k, carry):
            s = reversed_order(k)
            dctx = mm_nt(datt[half], w_out[s]).astype(BF16)
            query = qkv[s, half, :, 0:narrow]
            key = qkv[s, half, :, narrow : 2 * narrow]
            value = qkv[s, half, :, 2 * narrow : 3 * narrow]
            weights = prob[s, half]
            dhead = stacked(dctx)
            dweights = mm_nt(dhead, value)
            full = weights.astype(F32)
            dscores = full * (dweights - jnp.sum(dweights * full, axis=1, keepdims=True))
            dscores = dscores.astype(BF16)
            dquery = unstacked(mm(dscores, key)) * HEAD_DIM**-0.5
            dkey = mm_tn(dscores, stacked(query))
            dvalue = mm_tn(weights, dhead)
            act[s, part, 0 : 3 * narrow] = jnp.concatenate([dquery, dkey, dvalue], axis=1).astype(BF16)
            return carry

        lax.fori_loop(0, shards, step, 0)

    def dh1_rows(half):
        part = slice(half * rows, (half + 1) * rows)
        value = mm_nt(act[0, part, 0 : 3 * narrow], w_qkv[0])
        for s in range(1, shards):
            value += mm_nt(act[s, part, 0 : 3 * narrow], w_qkv[s])
        return value

    attend_back(0)
    feed_point((3, 4), (1, 2))
    total[0] = dh1_rows(0)
    turn_a[...] = jnp.transpose(h1[...].reshape(2 * rows, width))
    drain(1)
    feed_point(None, (2, 3))
    x_datt.wait_recv()
    turn_b[...] = jnp.transpose(datt[...].reshape(2 * rows, width))

    feed_point((4, 5), None)
    attend_back(1)
    sent[0] = dh1_rows(1).astype(BF16)
    x_dh1.start()
    feed_point((5, 6), (3, 5))

    def attn_grads(k, carry):
        s = reversed_order(k)
        store_grads(w_up, s, turn_a, act[s, :, 0 : 3 * narrow], 0, 3 * narrow)
        store_grads(w_up, s, turn_b, ctx[s], 3 * narrow, narrow)
        core_send(1, w_up, core_a, s).start()

        @pl.when(k > 0)
        def _():
            stage_core(1, w_up, core_a, y_a, reversed_order(k - 1))

        return carry

    lax.fori_loop(0, shards, attn_grads, 0)
    stage_core(1, w_up, core_a, y_a, z)

    x_feed.wait()

    def finish_forward(at, squares):
        branch = attended[at] + feed_own[at] + got[1, at].astype(F32)
        update = gate(at) * branch
        sent[1, at] = (own_z[at].astype(F32) + update).astype(BF16)
        dgate = jnp.sum(own_c[at].astype(F32) * branch, axis=1, keepdims=True)
        set_column(2, at, dgate * live(at))
        return squares + fold_rows(update * update)

    squares = row_tiles(rows, finish_forward, jnp.zeros((8, width), F32))
    put(0, sent.at[1]).start()
    count = jnp.sum(valid[...].astype(F32), axis=1, keepdims=True)
    energy = jnp.sum(jnp.sum(squares, axis=0, keepdims=True), axis=1, keepdims=True)
    rms = jnp.sqrt(energy / (width * jnp.maximum(count, 1.0)))

    if quick:
        feed_point(None, (5, 6))
    else:
        run_halves(feed_half, 0, total_halves)
    ahead = jnp.where(edge, 2, 1)
    run_halves(attn_half, 0, ahead)
    x_dh1.wait()

    def first_back(at, sums):
        dh1 = total[0, at] + got[0, at].astype(F32)
        row = own_z[at].astype(F32)
        factor = lax.rsqrt(jnp.mean(row * row, axis=1, keepdims=True) + EPS)
        scaled = dh1 * first_gain[...]
        back = factor * scaled - row * (factor**3 * jnp.mean(row * scaled, axis=1, keepdims=True))
        back = back + dmixed[at] + dscore(at) * w_router[...]
        got[1, at] = (own_c[at].astype(F32) + back).astype(BF16)
        return sums[0] + fold_rows(dscore(at) * row), sums[1] + fold_rows(dh1 * row * factor)

    zero = jnp.zeros((8, width), F32)
    router_sum, first_sum = row_tiles(rows, first_back, (zero, zero))
    put(1, got.at[1]).start()
    parts = [jnp.sum(part, axis=0, keepdims=True) for part in (router_sum, first_sum, second_sum)]
    small = jnp.concatenate(parts + [jnp.zeros((5, width), F32)], axis=0)

    def small_copy(k):
        return remote(small_send.at[k], small_got.at[k], sm_s.at[k], sm_r.at[k], small_devices[k])

    hops = len(small_devices)
    for k in range(hops):
        small_send[k] = small
        small_copy(k).start()
        if k > 0:
            attn_half(ahead + k)
        small_copy(k).wait()
        small = small + small_got[k]
        if k == 0:
            attn_half(ahead)
    stage_last(0, grads, y_f, z_f, swap_f, feed_out)

    def small_spread(far, source):
        slot = hops + source
        return remote(
            small_send.at[hops], small_got.at[slot], sm_s.at[hops + far - 1], sm_r.at[slot], (dp, lax.rem(z + far, shards))
        )

    small_send[hops] = small
    small_got[hops + z] = small
    for far in range(1, shards):
        small_spread(far, z).start()

    run_halves(attn_half, ahead + hops, total_halves)
    stage_last(1, w_up, y_a, z_a, swap_a, attn_out)
    for far in range(1, shards):
        small_spread(far, lax.rem(z + shards - far, shards)).wait_recv()
        small_spread(far, z).wait_send()
    small = small_got[hops]
    for k in range(1, shards):
        small = small + small_got[hops + k]
    row_at = lax.broadcasted_iota(jnp.int32, (8, 1), 0)
    small_send[0] = jnp.where(row_at == 3, rms, small)
    put(2, small_send.at[0]).start()
    stage_out(0, swap_f, feed_out)
    put(4, feed_out).start()
    stage_out(1, swap_a, attn_out)
    put(3, attn_out).start()

    drain(0)
    for copy in (x_h1, x_dfeed, x_h2, x_datt):
        copy.wait_send()

    for group, core_got, y_got, z_got in ((0, core_f, y_f, z_f), (1, core_a, y_a, z_a)):
        remote(core_got, core_got, gc_s.at[group], gc_r.at[group, 0], core_dev).wait_send()
        remote(y_got, y_got, gy_s.at[group], gy_r.at[group, 0, 0], y_dev).wait_send()
        moved = z_got.at[0 : shards - 1]
        remote(moved, moved, gz_s.at[group], gz_r.at[group, 0, 0], up_dev).wait_send()

    swap(0, swap_f).wait_send()
    swap(1, swap_a).wait_send()
    for k, src in enumerate((sent.at[1], got.at[1], small_send.at[0], attn_out, feed_out)):
        put(k, src).wait()


def run_block(size, operands):
    shards, rows, width = size["S"], size["R"], size["D"]
    heads, narrow, hidden, cut = size["hh"], size["n"], size["f"], size["DB"]
    mats = (2 if size["joined"] else 4) + 2
    stages = 3 + shards
    attn, feed = 4 * narrow, 2 * hidden
    dma = pltpu.SemaphoreType.DMA
    vmem = lambda *shape: pltpu.VMEM(shape, BF16)
    full = lambda *shape: pltpu.VMEM(shape, F32)
    scratch = [
        vmem(shards, width, 3 * narrow),
        vmem(shards, narrow, width),
        vmem(shards, 2, 2, 2, cut, hidden),
        vmem(shards, hidden, width),
        *[vmem(2, rows, width) for _ in range(4)],
        *[vmem(width, 2 * rows) for _ in range(2)],
        vmem(shards, 2, rows, 3 * narrow),
        vmem(shards, 2 * rows, narrow),
        vmem(shards, 2, heads * rows, rows),
        vmem(shards, 2 * rows, hidden),
        vmem(shards, 2 * rows, hidden),
        full(2, rows, width),
        full(2, rows, hidden),
        vmem(2, rows, width),
        vmem(2, rows, width),
        vmem(rows, width),
        vmem(rows, width),
        *[full(rows, width) for _ in range(3)],
        full(rows, 128),
        vmem(shards, 2, 2, 2, cut, feed),
        vmem(shards, 2, 2, cut, feed),
        vmem(shards, 2, cut, feed),
        vmem(shards + 1, 2, cut, feed),
        vmem(shards, 2, 2, cut, attn),
        vmem(shards, 2, cut, attn),
        vmem(shards + 1, 2, cut, attn),
        vmem(2, cut, feed),
        vmem(2, cut, attn),
        full(2, cut, attn),
        full(2, cut, feed),
        full(stages, 8, width),
        full(stages, 8, width),
        dma((mats,)),
        dma((2, 2)),
        dma((5,)),
        dma((2, shards + 1)),
        dma((mats, shards)),
        dma((2,)),
        dma((mats, shards)),
        dma((2,)),
        dma((2, shards)),
        dma((8,)),
        dma((8,)),
        dma((2,)),
        dma((2, shards)),
        dma((2,)),
        dma((2, shards, 2)),
        dma((2,)),
        dma((2, shards + 1, 2)),
        dma((2,)),
        dma((2,)),
        dma((stages,)),
        dma((stages,)),
    ]
    near = pl.BlockSpec(memory_space=pltpu.VMEM)
    far = pl.BlockSpec(memory_space=pl.ANY)
    outs = [
        jax.ShapeDtypeStruct((rows, width), BF16),
        jax.ShapeDtypeStruct((rows, width), BF16),
        jax.ShapeDtypeStruct((8, width), F32),
        jax.ShapeDtypeStruct((2, cut, attn), F32),
        jax.ShapeDtypeStruct((2, cut, feed), F32),
    ]
    return pl.pallas_call(
        functools.partial(block_kernel, size),
        out_shape=outs,
        in_specs=[far, far] + [near] * 5 + [far] * (len(operands) - 7),
        out_specs=[pl.BlockSpec(memory_space=pltpu.HBM)] * len(outs),
        scratch_shapes=scratch,
        compiler_params=pltpu.CompilerParams(
            collective_id=0, has_side_effects=True, vmem_limit_bytes=64 * 2**20 - 65536
        ),
    )(*operands)


def place_kernel(size, assemble, routed, small, tokens, cotangent, *refs):
    length, width, rows = size["L"], size["D"], size["R"]
    gathered, refs = refs[: 4 if assemble else 2], refs[4 if assemble else 2 :]
    outs, refs = refs[: 12 if assemble else 2], refs[12 if assemble else 2 :]
    bases, staged, refs = refs[:2], refs[2 : 2 + len(gathered)], refs[2 + len(gathered) :]
    finals, (pick, keep, in_sem, out_sem, part_sem, final_sem) = refs[:-6], refs[-6:]
    block = 512
    steps = width // block

    def moving(src, dst, sem, k, b):
        at = (slice(None), pl.ds(b * block, block))
        return pltpu.make_async_copy(src[k].at[at], dst[k].at[at], sem.at[k, b])

    sources = (tokens, cotangent)
    parts = [pltpu.make_async_copy(src, dst, part_sem.at[k]) for k, (src, dst) in enumerate(zip(gathered, staged))]
    for copy in parts[:2]:
        copy.start()
    for b in range(steps):
        for k in range(2):
            moving(sources, bases, in_sem, k, b).start()
    for copy in parts[2:]:
        copy.start()
    line = lax.broadcasted_iota(jnp.int32, (length, rows), 0)
    chosen = jnp.where(line == routed[...], 1.0, 0.0)
    pick[...] = chosen.astype(BF16)
    keep[...] = jnp.broadcast_to((1.0 - jnp.sum(chosen, axis=1, keepdims=True)).astype(BF16), keep.shape)
    for copy in parts[:2]:
        copy.wait()
    for b in range(steps):
        for k in range(2):
            at = slice(b * block, (b + 1) * block)
            moving(sources, bases, in_sem, k, b).wait()
            kept = jnp.concatenate([keep[...]] * (block // 128), axis=1)
            bases[k][:, at] = mm(pick[...], staged[k][:, at]).astype(BF16) + bases[k][:, at] * kept
            moving(bases, outs, out_sem, k, b).start()
    last = []
    if assemble:
        for copy in parts[2:]:
            copy.wait()
        for k, value in enumerate(weight_outputs(size, *staged[2:])):
            finals[k][...] = value
            last.append(pltpu.make_async_copy(finals[k], outs[2 + k], final_sem.at[k]))
            last[-1].start()
        for k in range(3):
            outs[8 + k][...] = small[k : k + 1, :]
        outs[11][...] = small[3:4, 0:1]
    for b in range(steps):
        for k in range(2):
            moving(bases, outs, out_sem, k, b).wait()
    for copy in last:
        copy.wait()


def weight_outputs(size, attn, feed):
    narrow, hidden = size["n"], size["f"]

    def side_by_side(ref, lo, count):
        return jnp.concatenate([ref[0, :, lo : lo + count], ref[1, :, lo : lo + count]], axis=1)

    return (
        side_by_side(attn, 0, narrow),
        side_by_side(attn, narrow, narrow),
        side_by_side(attn, 2 * narrow, narrow),
        side_by_side(attn, 3 * narrow, narrow).T,
        side_by_side(feed, 0, hidden),
        side_by_side(feed, hidden, hidden).T,
    )


def place_rows(size, routed, tokens, cotangent, rows_res, rows_grad, small, attn, feed, assemble):
    length, width, rows = size["L"], size["D"], size["R"]
    cut, narrow, hidden = size["DB"], size["n"], size["f"]
    whole = lambda *shape: pl.BlockSpec(shape, lambda i: (0,) * len(shape))
    far = pl.BlockSpec(memory_space=pltpu.HBM)
    outs, out_specs = [jax.ShapeDtypeStruct((length, width), BF16)] * 2, [far] * 2
    gathered, finals = [rows_res, rows_grad], []
    if assemble:
        gathered += [attn, feed]
        finals = [(cut, 2 * narrow)] * 3 + [(2 * narrow, cut), (cut, 2 * hidden), (2 * hidden, cut)]
        tiny = [(1, width)] * 3 + [(1, 1)]
        outs = outs + [jax.ShapeDtypeStruct(shape, F32) for shape in finals + tiny]
        out_specs = out_specs + [far] * len(finals) + [whole(*shape) for shape in tiny]
    dma = pltpu.SemaphoreType.DMA
    return pl.pallas_call(
        functools.partial(place_kernel, size, assemble),
        grid=(1,),
        out_shape=outs,
        in_specs=[whole(1, rows), whole(*small.shape)] + [far] * (2 + len(gathered)),
        out_specs=out_specs,
        scratch_shapes=[
            *[pltpu.VMEM((length, width), BF16) for _ in range(2)],
            *[pltpu.VMEM(part.shape, part.dtype) for part in gathered],
            *[pltpu.VMEM(shape, F32) for shape in finals],
            pltpu.VMEM((length, rows), BF16),
            pltpu.VMEM((length, 128), BF16),
            dma((2, width // 512)),
            dma((2, width // 512)),
            dma((4,)),
            dma((6,)),
        ],
        compiler_params=pltpu.CompilerParams(vmem_limit_bytes=60 * 2**20),
    )(routed, small, tokens, cotangent, *gathered)


def shards_of(
    groups,
    tokens,
    cotangent,
    routed,
    valid_mask,
    w_router,
    first_gain,
    query_weight,
    key_weight,
    value_weight,
    output_weight,
    second_gain,
    up_weight,
    down_weight,
):
    shards, data = lax.axis_size("mp"), lax.axis_size("dp")
    _, length, width = tokens.shape
    rows = routed.shape[1]
    narrow = query_weight.shape[1] // 2
    hidden = up_weight.shape[1] // 2
    cut = width // 8
    chips_x = 1 << ((data // 2).bit_length() - 1) // 2
    size = dict(
        S=shards, ybit=2 * chips_x, R=rows, D=width, L=length, hh=narrow // HEAD_DIM,
        n=narrow, f=hidden, DB=cut, joined=narrow % 128 != 0,
    )
    dp = lax.axis_index("dp")
    x, y = (dp // 2) % 2, (dp // size["ybit"]) % 2
    qkv = (query_weight, key_weight, value_weight)
    if size["joined"]:
        halves = [lax.dynamic_slice_in_dim(weight, x * narrow, narrow, 1) for weight in qkv]
        qkv = (jnp.concatenate(halves, axis=1),)
    row = lambda vector: vector.reshape(1, width)
    operands = (
        tokens.reshape(-1, rows, width), cotangent.reshape(-1, rows, width), routed, valid_mask, row(w_router), row(first_gain), row(second_gain),
        *qkv, output_weight, up_weight.reshape(2, 2, 2, cut, 2 * hidden), down_weight,
    )
    rows_res, rows_grad, small, attn, feed = run_block(size, operands)
    whole_group = data == 8
    rms = small[3, 0:1]
    if not whole_group:
        block = 4 * y + 2 * x + dp % 2

        def over_groups(part):
            base = jnp.zeros((2, width, part.shape[2]), F32)
            placed = lax.dynamic_update_slice_in_dim(base, part, block * cut, 1)
            return lax.psum_scatter(placed, "dp", scatter_dimension=1, tiled=True)

        attn, feed = over_groups(attn), over_groups(feed)
        small = lax.psum(small, "dp") / 8.0
    placed = place_rows(size, routed, tokens[0], cotangent[0], rows_res, rows_grad, small, attn, feed, whole_group)
    residual, grad_tokens = placed[:2]
    if whole_group:
        vectors = [vector.reshape(width) for vector in placed[8:11]]
        weights, rms = placed[2:8], placed[11].reshape(1)
    else:
        vectors, weights = [small[k] for k in range(3)], weight_outputs(size, attn, feed)
    grad_query, grad_key, grad_value, grad_output, grad_up, grad_down = weights
    return (
        residual[None],
        grad_tokens[None],
        rms,
        vectors[0],
        vectors[1],
        grad_query,
        grad_key,
        grad_value,
        grad_output,
        vectors[2],
        grad_up,
        grad_down,
    )


def solution(mesh):
    in_specs = (
        P(("dp", "mp"), None, None),
        P(("dp", "mp"), None, None),
        P(("dp", "mp"), None),
        P(("dp", "mp"), None),
        P(),
        P(),
        P(None, "mp"),
        P(None, "mp"),
        P(None, "mp"),
        P("mp", None),
        P(),
        P(None, "mp"),
        P("mp", None),
    )
    out_specs = (
        P(("dp", "mp"), None, None),
        P(("dp", "mp"), None, None),
        P(("dp", "mp")),
        P(),
        P(),
        P("dp", "mp"),
        P("dp", "mp"),
        P("dp", "mp"),
        P("mp", "dp"),
        P(),
        P("dp", "mp"),
        P("mp", "dp"),
    )
    body = functools.partial(shards_of, mesh.shape["dp"] // 8)
    return jax.shard_map(body, mesh=mesh, in_specs=in_specs, out_specs=out_specs, check_vma=False)
```

```python
import functools
import math

import jax
import jax.numpy as jnp
from jax import lax
from jax.experimental import pallas as pl
from jax.experimental.pallas import tpu as pltpu
from jax.sharding import PartitionSpec as P

HEADS = 16
HEAD_DIM = 64
EPS = 1e-06
F32 = jnp.float32
BF16 = jnp.bfloat16
TILE = 64


def mm(left, right):
    return jnp.dot(left, right, preferred_element_type=F32)


def mm_nt(left, right):
    return lax.dot_general(left, right, (((1,), (1,)), ((), ())), preferred_element_type=F32)


def mm_tn(left, right):
    return lax.dot_general(left, right, (((0,), (0,)), ((), ())), preferred_element_type=F32)


def row_tiles(rows, body, init=0, first=0):
    def step(index, carry):
        return body(pl.ds(pl.multiple_of(first + index * TILE, TILE), TILE), carry)

    return lax.fori_loop(0, rows // TILE, step, init)


def fold_rows(value):
    return jnp.sum(value.reshape(-1, 8, value.shape[-1]), axis=0)


def gelu_both(value):
    cdf = 0.5 * (1.0 + lax.erf(value * math.sqrt(0.5)))
    density = jnp.exp(-0.5 * value * value) * (1.0 / math.sqrt(2.0 * math.pi))
    return value * cdf, cdf + value * density


def block_kernel(size, *refs):
    shards, ybit, rows, width, length = size["S"], size["ybit"], size["R"], size["D"], size["L"]
    heads, narrow, hidden, cut = size["hh"], size["n"], size["f"], size["DB"]
    joined = size["joined"]
    quarter = 2 * cut
    refs = list(refs)

    def take(count):
        taken, refs[:count] = refs[:count], []
        return taken

    tokens, cotangent, routed, valid, w_router, first_gain, second_gain = take(7)
    qkv_in = take(1 if joined else 3)
    out_in, up_in, down_in = take(3)
    outputs = take(5)
    w_qkv, w_out, w_up, w_down = take(4)
    h1, dfeed, h2, datt, turn_a, turn_b = take(6)
    qkv, ctx, prob, act, dup = take(5)
    total, wide, sent, got = take(4)
    own_z, own_c, attended, dmixed, feed_own, columns = take(6)
    lane = lax.broadcasted_iota(jnp.int32, (1, 128), 1)

    def column(k, at):
        return columns[at][:, k : k + 1]

    def set_column(k, at, value):
        columns[at] = jnp.where(lane == k, value, columns[at])

    gate, live, dscore = (functools.partial(column, k) for k in range(3))
    grads, core_f, y_f, z_f, core_a, y_a, z_a, swap_f, swap_a = take(9)
    attn_out, feed_out = take(2)
    small_send, small_got = take(2)
    load_sem, tok_sem, out_sem = take(3)
    wz_s, wz_r, wy_s, wy_r, wc_s, wc_r = take(6)
    x_s, x_r = take(2)
    gc_s, gc_r, gy_s, gy_r, gz_s, gz_r, gx_s, gx_r = take(8)
    sm_s, sm_r = take(2)

    dp = lax.axis_index("dp")
    z = lax.axis_index("mp")
    core = lax.rem(dp, 2)
    x = lax.rem(lax.div(dp, 2), 2)
    y = lax.rem(lax.div(dp, ybit), 2)
    core_dev = (dp + 1 - 2 * core, z)
    x_dev = (dp + 2 * (1 - 2 * x), z)
    y_dev = (dp + ybit * (1 - 2 * y), z)
    up_dev = (dp, z + 1)
    down_dev = (dp, z - 1)
    small_devices = [core_dev, x_dev, (dp + 2 * (1 - 2 * x) + ybit * (1 - 2 * y), z)]

    def remote(src, dst, send, recv, device):
        return pltpu.make_async_remote_copy(
            src_ref=src,
            dst_ref=dst,
            send_sem=send,
            recv_sem=recv,
            device_id=device,
            device_id_type=pl.DeviceIdType.MESH,
        )

    def order(j):
        high = lax.div(z, shards // 2)
        base = z + high * (shards - 1 - 2 * z)
        odd = lax.rem(j, 2)
        near = base + lax.div(j + 1, 2) * (2 * odd - 1)
        pick = jnp.where(j <= 2 * base, near, j)
        return pick + high * (shards - 1 - 2 * pick)

    attn_mats = list(range(len(qkv_in) + 1))
    up_mats = [len(attn_mats), len(attn_mats) + 1]
    down_mats = [len(attn_mats) + 2, len(attn_mats) + 3]
    feed_mats = up_mats + down_mats
    out_at, up_at, down_at = attn_mats[-1], up_mats[0], down_mats[0]

    def down_rows(i, start=0):
        return pl.ds(pl.multiple_of(start + (i - down_at) * (hidden // 2), hidden // 2), hidden // 2)

    def span(qy, qc):
        return pl.ds(pl.multiple_of((2 * qy + qc) * quarter, quarter), quarter)

    def lanes(count):
        return pl.ds(pl.multiple_of(x * count, count), count)

    def held(i, s, qy, qc):
        if i < out_at:
            part = w_qkv if joined else w_qkv.at[:, :, i * narrow : (i + 1) * narrow]
            return part.at[s, span(qy, qc)]
        if i == out_at:
            return w_out.at[s, :, span(qy, qc)]
        if i < down_at:
            return w_up.at[s, qy, qc, i - up_at]
        return w_down.at[s, down_rows(i), span(qy, qc)]

    def own_piece(i):
        if i < out_at:
            part = qkv_in[i].at[span(y, core)]
            return part if joined else part.at[:, lanes(narrow)]
        if i == out_at:
            return out_in.at[lanes(narrow), span(y, core)]
        if i < down_at:
            return up_in.at[y, core, i - up_at, :, lanes(hidden)]
        return down_in.at[down_rows(i, x * hidden), span(y, core)]

    def load_own(i):
        if i < out_at:
            if joined:
                src, dst = qkv_in[i], w_qkv.at[z]
            else:
                src, dst = qkv_in[i].at[:, lanes(narrow)], w_qkv.at[z, :, i * narrow : (i + 1) * narrow]
        elif i == out_at:
            src, dst = out_in.at[lanes(narrow), :], w_out.at[z]
        elif i < down_at:
            b = i - up_at
            src, dst = up_in.at[:, :, b, :, lanes(hidden)], w_up.at[z, :, :, b]
        else:
            src, dst = down_in.at[down_rows(i, x * hidden), :], w_down.at[z, down_rows(i)]
        return pltpu.make_async_copy(src, dst, load_sem.at[i])

    def group_of(i):
        return 0 if i <= out_at else 1

    def own_up(i):
        return remote(own_piece(i), held(i, z, y, core), wz_s.at[group_of(i), z], wz_r.at[i, z], up_dev)

    def own_down(i):
        return remote(own_piece(i), held(i, z, y, core), wz_s.at[group_of(i), shards], wz_r.at[i, z], down_dev)

    def pass_on(i, s, device):
        piece = held(i, s, y, core)
        return remote(piece, piece, wz_s.at[group_of(i), s], wz_r.at[i, s], device)

    def across_y(i, s, qy):
        piece = held(i, s, qy, core)
        return remote(piece, piece, wy_s.at[group_of(i)], wy_r.at[i, s], y_dev)

    def across_core(i, s, qy, qc):
        piece = held(i, s, qy, qc)
        group = group_of(i)
        return remote(piece, piece, wc_s.at[group], wc_r.at[group, s], core_dev)

    def await_pieces(group, sem, count, receiving=False):
        mats = attn_mats if group == 0 else feed_mats
        if joined:
            refs = [held(i, 0, 0, 0) for i in mats] * count
        else:
            flat = w_up.at[0, 0, 0] if group == 0 else w_up.at[0, 0]
            if count == 2:
                flat = w_up.at[0, 0] if group == 0 else w_up.at[0]
            elif count == shards - 1:
                flat = w_up.at[0 : shards - 1, 0, 0] if group == 0 else w_up.at[0 : shards - 1, 0]
            elif count == 2 * (shards - 1):
                flat = w_up.at[0 : shards - 1, 0] if group == 0 else w_up.at[0 : shards - 1]
            refs = [flat]
        for ref in refs:
            if receiving:
                remote(ref, ref, wc_s.at[group], sem, core_dev).wait_recv()
            else:
                remote(ref, ref, sem, wc_r.at[group, 0], core_dev).wait_send()

    def send_own_up(mats):
        for i in mats:
            own_up(i).start()

    def send_own_down(mats):
        for i in mats:
            own_down(i).start()

    def passing(s, action):
        @pl.when((s < z) & (z < shards - 1))
        def _():
            action(up_dev)

        @pl.when((s > z) & (z > 0))
        def _():
            action(down_dev)

    edge = (z == 0) | (z == shards - 1)
    inner = jnp.logical_not(edge)

    def arrive_one(i, j):
        s = order(j)
        pass_on(i, s, up_dev).wait_recv()
        passing(s, lambda device: pass_on(i, s, device).start())
        across_y(i, s, y).start()
        across_core(i, s, y, core).start()

    def arrive(mats, j):
        for i in mats:
            arrive_one(i, j)

    def follow(j):
        s = order(j)

        @pl.when((s == 0) & (z < shards - 1))
        def _():
            send_own_up(feed_mats)

        @pl.when((s == shards - 1) & (z > 0))
        def _():
            send_own_down(feed_mats)

    def relay(mats, j):
        s = order(j)
        for i in mats:
            across_y(i, s, 1 - y).wait_recv()
            across_core(i, s, 1 - y, core).start()

    def settle(group, j):
        await_pieces(group, wc_r.at[group, order(j)], 2, True)

    def drain(group):
        @pl.when(z < shards - 1)
        def _():
            await_pieces(group, wz_s.at[group, z], 1)

        @pl.when(z > 0)
        def _():
            await_pieces(group, wz_s.at[group, shards], 1)

        def step(j, carry):
            s = order(j)
            passing(s, lambda device: await_pieces(group, wz_s.at[group, s], 1))
            return carry

        lax.fori_loop(1, shards, step, 0)
        await_pieces(group, wy_s.at[group], shards - 1)
        await_pieces(group, wc_s.at[group], 2 * (shards - 1))

    def exchange(slot, src, dst):
        return remote(src, dst, x_s.at[slot], x_r.at[slot], x_dev)

    x_h1 = exchange(0, h1.at[0], h1.at[1])
    x_dfeed = exchange(1, dfeed.at[0], dfeed.at[1])
    upper, lower = slice(0, rows // 2), slice(rows // 2, rows)
    x_att = [exchange(2 + 6 * k, sent.at[0, part], got.at[0, part]) for k, part in enumerate((upper, lower))]
    x_h2 = [exchange(3 + 6 * k, h2.at[0, part], h2.at[1, part]) for k, part in enumerate((upper, lower))]
    x_dh2 = exchange(4, sent.at[0], got.at[0])
    x_feed = exchange(5, sent.at[1], got.at[1])
    x_datt = exchange(6, datt.at[0], datt.at[1])
    x_dh1 = exchange(7, sent.at[0], got.at[0])

    def put(k, src):
        return pltpu.make_async_copy(src, outputs[k], out_sem.at[k])

    steps = length // (2 * rows)
    stages = ((got, sent), (h2, datt))

    def block_loads(t):
        copies = []
        for k, (array, buf) in enumerate(zip((tokens, cotangent), stages[t % 2])):
            copies.append(pltpu.make_async_copy(array.at[2 * t : 2 * t + 2], buf, tok_sem.at[t % 2, k]))
        return copies

    barrier = pltpu.get_barrier_semaphore()

    def greet(device):
        pl.semaphore_signal(barrier, inc=1, device_id=device, device_id_type=pl.DeviceIdType.MESH)

    for device in (core_dev, x_dev, y_dev):
        greet(device)

    @pl.when(z > 0)
    def _():
        greet(down_dev)

    @pl.when(z < shards - 1)
    def _():
        greet(up_dev)

    for t in range(2):
        for copy in block_loads(t):
            copy.start()
    for i in attn_mats + feed_mats:
        load_own(i).start()

    def begin():
        ends = jnp.where(z == 0, 1, 0) + jnp.where(z == shards - 1, 1, 0)
        pl.semaphore_wait(barrier, 5 - ends)

        @pl.when(z < shards - 1)
        def _():
            send_own_up(attn_mats)

        @pl.when(z > 0)
        def _():
            send_own_down(attn_mats)

        @pl.when(z == 0)
        def _():
            send_own_up(feed_mats)

        @pl.when(z == shards - 1)
        def _():
            send_own_down(feed_mats)

    as_rows = jnp.broadcast_to(routed[...].astype(F32), (8, rows))
    position = jnp.transpose(as_rows)[:, 0:1].astype(jnp.int32)
    flags = jnp.zeros((rows, 1), F32)
    for t in range(steps):
        for copy in block_loads(t):
            copy.wait()
        hit = position == 2 * t * rows + lax.broadcasted_iota(jnp.int32, (rows, 2 * rows), 1)
        chosen = jnp.where(hit, 1.0, 0.0)
        pick = chosen.astype(BF16)
        for k, buf in enumerate(stages[t % 2]):
            picked = mm(pick, buf[...].reshape(2 * rows, width))
            total[k] = picked if t == 0 else total[k] + picked
        if t + 2 < steps:
            for copy in block_loads(t + 2):
                copy.start()
        mask = valid[:, 2 * t * rows : 2 * (t + 1) * rows].astype(F32)
        flags = flags + jnp.sum(chosen * mask, axis=1, keepdims=True)
        if t == steps // 2 - 1:
            begin()
    columns[...] = jnp.broadcast_to(flags, columns.shape)

    def prepare(at, carry):
        row, cot = total[0, at], total[1, at]
        own_z[at] = row.astype(BF16)
        own_c[at] = cot.astype(BF16)
        gate_here = jnp.sum(row * w_router[...], axis=1, keepdims=True) * live(at)
        set_column(0, at, gate_here)
        factor = lax.rsqrt(jnp.mean(row * row, axis=1, keepdims=True) + EPS)
        h1[0, at] = (row * factor * first_gain[...]).astype(BF16)
        dfeed[0, at] = (gate_here * cot).astype(BF16)
        return carry

    row_tiles(rows, prepare)
    x_h1.start()
    x_dfeed.start()

    lane_head = lax.div(lax.broadcasted_iota(jnp.int32, (1, narrow), 1), HEAD_DIM)
    masks = [jnp.where(lane_head == h, 1.0, 0.0) for h in range(heads)]
    masks_low = [mask.astype(BF16) for mask in masks]

    def stacked(value):
        return jnp.concatenate([value * mask for mask in masks_low], axis=0) if heads > 1 else value

    def unstacked(value):
        if heads == 1:
            return value
        picked = value[0:rows] * masks[0]
        for h in range(1, heads):
            picked = picked + value[h * rows : (h + 1) * rows] * masks[h]
        return picked

    score_shape = (heads * rows, rows)
    causal = lax.rem(lax.broadcasted_iota(jnp.int32, score_shape, 0), rows) >= lax.broadcasted_iota(
        jnp.int32, score_shape, 1
    )

    for i in attn_mats:
        load_own(i).wait()

    @pl.when(edge)
    def _():
        for j in range(1, shards):
            arrive(attn_mats, j)
            follow(j)
            if j > 1:
                relay(attn_mats, j - 1)

    @pl.when(inner)
    def _():
        for i in attn_mats:
            for j in (1, 2):
                arrive_one(i, j)
        for j in (1, 2):
            follow(j)
        for j in range(3, shards):
            arrive(attn_mats, j)
            follow(j)
        for j in range(1, shards - 1):
            relay(attn_mats, j)

    x_h1.wait_recv()

    def attend(j, carry):
        s = order(j)

        @pl.when(j + 1 == shards)
        def _():
            relay(attn_mats, j)
            arrive(up_mats, 1)

        @pl.when(j > 0)
        def _():
            settle(0, j)

        low = mm(h1[...].reshape(2 * rows, width), w_qkv[s]).astype(BF16)
        query = low[:, 0:narrow] * jnp.asarray(HEAD_DIM**-0.5, BF16)
        qkv[s] = jnp.concatenate([query, low[:, narrow:]], axis=1).reshape(2, rows, 3 * narrow)
        for half in range(2):
            query = qkv[s, half, :, 0:narrow]
            key = qkv[s, half, :, narrow : 2 * narrow]
            value = qkv[s, half, :, 2 * narrow : 3 * narrow]
            scores = jnp.where(causal, mm_nt(stacked(query), key), -1e30)
            raised = jnp.exp(scores - jnp.max(scores, axis=1, keepdims=True))
            weights = (raised / jnp.sum(raised, axis=1, keepdims=True)).astype(BF16)
            prob[s, half] = weights
            ctx[s, half * rows : (half + 1) * rows] = unstacked(mm(weights, value)).astype(BF16)
        return carry

    lax.fori_loop(0, shards, attend, 0)

    def project_out(half):
        parts = [ctx[s, half * rows : (half + 1) * rows] for s in range(shards)]
        return mm(jnp.concatenate(parts, axis=1), w_out[...].reshape(shards * narrow, width))

    sent[0] = project_out(1).astype(BF16)
    for copy in x_att:
        copy.start()
    attended[...] = project_out(0)
    arrive(down_mats, 1)
    arrive(up_mats, 2)

    @pl.when(inner)
    def _():
        arrive(down_mats, 2)
        for j in range(3, shards):
            arrive(feed_mats, j)

    def mix(at, carry):
        att = attended[at] + got[0, at].astype(F32)
        attended[at] = att
        mixed = own_z[at].astype(F32) + att
        factor = lax.rsqrt(jnp.mean(mixed * mixed, axis=1, keepdims=True) + EPS)
        h2[0, at] = (mixed * factor * second_gain[...]).astype(BF16)
        return carry

    for k in range(2):
        x_att[k].wait()
        row_tiles(rows // 2, mix, first=k * (rows // 2))
        x_h2[k].start()

    @pl.when(edge)
    def _():
        arrive(down_mats, 2)

    x_dfeed.wait_recv()

    parts_of = (1 - y, y)

    def core_send(group, buf, into, s, a):
        src = buf.at[s, a, :, 1 - core]
        return remote(src, into.at[s, a], gc_s.at[group], gc_r.at[group, s, a], core_dev)

    halves = (1 - x, x)

    def y_send(group, buf, into, s, b):
        src = buf.at[s, 1 - y, b, core]
        return remote(src, into.at[s, b], gy_s.at[group], gy_r.at[group, s, b], y_dev)

    def z_send(group, buf, into, s, device, slot, b):
        src = buf.at[s, y, b, core]
        return remote(src, into.at[slot, b], gz_s.at[group], gz_r.at[group, slot, b], device)

    def add_into(ref, other):
        ref[...] = (ref[...].astype(F32) + other[...].astype(F32)).astype(BF16)

    def stage_core(group, buf, core_got, y_got, s):
        core_send(group, buf, core_got, s, 1 - y).wait_recv()
        for b in halves:
            add_into(buf.at[s, 1 - y, b, core], core_got.at[s, 1 - y, b])
            y_send(group, buf, y_got, s, b).start()
        core_send(group, buf, core_got, s, y).wait_recv()
        for b in range(2):
            add_into(buf.at[s, y, b, core], core_got.at[s, y, b])

    def stage_y(group, buf, y_got, s, b):
        y_send(group, buf, y_got, s, b).wait_recv()
        add_into(buf.at[s, y, b, core], y_got.at[s, b])

    def line_in(group, buf, z_got, s, slot, b):
        z_send(group, buf, z_got, s, up_dev, slot, b).wait_recv()
        add_into(buf.at[s, y, b, core], z_got.at[slot, b])

    def stage_z(group, buf, z_got, s, b):
        @pl.when(s > z)
        def _():
            @pl.when(z > 0)
            def _():
                line_in(group, buf, z_got, s, s, b)

            z_send(group, buf, z_got, s, up_dev, s, b).start()

        @pl.when(s < z)
        def _():
            @pl.when(z < shards - 1)
            def _():
                line_in(group, buf, z_got, s, s, b)

            slot = jnp.where(s == z - 1, shards, s)
            z_send(group, buf, z_got, s, down_dev, slot, b).start()

    def swap(group, pair):
        return remote(pair.at[0], pair.at[1], gx_s.at[group], gx_r.at[group], x_dev)

    def stage_last(group, buf, y_got, z_got, pair, out):
        for b in halves:
            stage_y(group, buf, y_got, z, b)
            out[b] = buf[z, y, b, core].astype(F32)

            @pl.when(z > 0)
            def _():
                z_send(group, buf, z_got, z, up_dev, z, b).wait_recv()
                out[b] += z_got[z, b].astype(F32)

            @pl.when(z < shards - 1)
            def _():
                z_send(group, buf, z_got, z, up_dev, shards, b).wait_recv()
                out[b] += z_got[shards, b].astype(F32)

            if b is halves[0]:
                pair[0] = out[b].astype(BF16)
                swap(group, pair).start()

    def stage_out(group, pair, out):
        swap(group, pair).wait_recv()
        out[1 - x] = pair[1].astype(F32)

    def reversed_order(k):
        return order(shards - 1 - k)

    def store_grads(buf, s, a, left, right, lo, count):
        part = pl.ds(pl.multiple_of(2 * a * quarter, 2 * quarter), 2 * quarter)
        value = mm(left[part, :], right).astype(BF16)
        buf[s, a, :, :, :, lo : lo + count] = value.reshape(2, 2, cut, count)

    def line_half(group, buf, y_got, z_got, s, m):
        b = jnp.where(lax.rem(m, 2) == 0, 1 - x, x)
        stage_y(group, buf, y_got, s, b)
        stage_z(group, buf, z_got, s, b)

    def feed_half(m):
        line_half(0, grads, y_f, z_f, order(leaving(lax.div(m, 2))), m)

    def attn_half(m):
        line_half(1, w_up, y_a, z_a, reversed_order(lax.div(m, 2)), m)

    def run_halves(step, first, last):
        def body(m, carry):
            step(m)
            return carry

        lax.fori_loop(first, last, body, 0)

    total_halves = 2 * (shards - 1)

    quick = shards == 4

    def leaving(k):
        if not quick:
            return shards - 1 - k
        ends, middle = jnp.where(edge, 2, 1), jnp.where(edge, 1, 2)
        return jnp.where(k == 0, ends, jnp.where(k == 1, 3, jnp.where(k == 2, middle, 0)))

    def feed_point(ends, middle):
        if quick and ends is not None:

            @pl.when(edge)
            def _():
                run_halves(feed_half, *ends)

        if quick and middle is not None:

            @pl.when(inner)
            def _():
                run_halves(feed_half, *middle)

    total[...] = jnp.zeros_like(total)
    turn_a[:, 0:rows] = jnp.transpose(h2[0])
    turn_b[...] = jnp.transpose(dfeed[...].reshape(2 * rows, width))
    for i in feed_mats:
        load_own(i).wait()

    def feed_grads(s):
        for a in parts_of:
            store_grads(grads, s, a, turn_a, dup[s], 0, hidden)
            store_grads(grads, s, a, turn_b, act[s], hidden, hidden)
            core_send(0, grads, core_f, s, a).start()

    def feed_core(s):
        stage_core(0, grads, core_f, y_f, s)

    def feed_chunk(s, half):
        part = pl.ds(pl.multiple_of(half * rows, rows), rows)
        up_here = w_up[s].reshape(width, hidden)
        wide[0] = mm(h2[half], up_here)
        wide[1] = mm_nt(dfeed[half], w_down[s])

        def turn(at, inside):
            active, slope = gelu_both(wide[0, at])
            out = pl.ds(pl.multiple_of(half * rows + at.start, TILE), TILE)
            act[s, out] = active.astype(BF16)
            dup[s, out] = (wide[1, at] * slope).astype(BF16)
            return inside

        row_tiles(rows, turn)
        total[half] += mm_nt(dup[s, part], up_here)

    def own_step(j, carry):
        @pl.when(j > 0)
        def _():
            settle(1, j)

        feed_chunk(order(j), 0)

        @pl.when(edge & (j > 1) & (j + 1 < shards))
        def _():
            arrive(down_mats, j + 1)

        @pl.when(j + 2 < shards)
        def _():
            relay(feed_mats, j + 1)

        @pl.when(edge & (j + 3 < shards))
        def _():
            arrive(up_mats, j + 3)

        return carry

    lax.fori_loop(0, shards - 1, own_step, 0)
    for copy in x_h2:
        copy.wait_recv()
    turn_a[:, rows : 2 * rows] = jnp.transpose(h2[1])

    def other_step(k, carry):
        j = k
        if quick:
            j = jnp.where(edge, jnp.where(k == 0, 2, k - 1), jnp.where(k < 2, 1 - k, k))
        feed_chunk(order(j), 1)
        if quick:

            @pl.when(k == 0)
            def _():
                feed_grads(order(leaving(0)))

            @pl.when(k == 1)
            def _():
                feed_core(order(leaving(0)))

        return carry

    lax.fori_loop(0, shards - 1, other_step, 0)
    relay(feed_mats, shards - 1)
    settle(1, shards - 1)

    def last_step(k, carry):
        feed_chunk(order(shards - 1), 1 - k)

        @pl.when(k == 0)
        def _():
            sent[0] = total[1].astype(BF16)
            x_dh2.start()

        return carry

    lax.fori_loop(0, 2, last_step, 0)
    first_left = 1 if quick else 0

    def feed_grads_step(k, carry):
        if quick:

            @pl.when((k == 2) & edge)
            def _():
                feed_half(0)

        feed_grads(order(leaving(k)))

        @pl.when(k > first_left)
        def _():
            feed_core(order(leaving(k - 1)))

        return carry

    lax.fori_loop(first_left, shards, feed_grads_step, 0)
    feed_point((1, 2), None)
    feed_core(z)

    def feed_rows(half):
        value = mm(act[0, half * rows : (half + 1) * rows], w_down[0])
        for s in range(1, shards):
            value += mm(act[s, half * rows : (half + 1) * rows], w_down[s])
        return value

    x_dh2.wait()

    def second_back(at, carry):
        dh2 = total[0, at] + got[0, at].astype(F32)
        mixed = own_z[at].astype(F32) + attended[at]
        factor = lax.rsqrt(jnp.mean(mixed * mixed, axis=1, keepdims=True) + EPS)
        scaled = dh2 * second_gain[...]
        back = factor * scaled - mixed * (factor**3 * jnp.mean(mixed * scaled, axis=1, keepdims=True))
        dmixed[at] = back
        datt[0, at] = (gate(at) * own_c[at].astype(F32) + back).astype(BF16)
        return carry + fold_rows(dh2 * mixed * factor)

    second_sum = row_tiles(rows, second_back, jnp.zeros((8, width), F32))
    x_datt.start()
    sent[1] = feed_rows(1).astype(BF16)
    x_feed.start()
    feed_point((2, 3), (0, 1))
    feed_own[...] = feed_rows(0)

    def attend_back(half):
        part = slice(half * rows, (half + 1) * rows)

        def step(k, carry):
            s = reversed_order(k)
            dctx = mm_nt(datt[half], w_out[s]).astype(BF16)
            query = qkv[s, half, :, 0:narrow]
            key = qkv[s, half, :, narrow : 2 * narrow]
            value = qkv[s, half, :, 2 * narrow : 3 * narrow]
            weights = prob[s, half]
            dhead = stacked(dctx)
            dweights = mm_nt(dhead, value)
            full = weights.astype(F32)
            dscores = full * (dweights - jnp.sum(dweights * full, axis=1, keepdims=True))
            dscores = dscores.astype(BF16)
            dquery = unstacked(mm(dscores, key)) * HEAD_DIM**-0.5
            dkey = mm_tn(dscores, stacked(query))
            dvalue = mm_tn(weights, dhead)
            act[s, part, 0 : 3 * narrow] = jnp.concatenate([dquery, dkey, dvalue], axis=1).astype(BF16)
            return carry

        lax.fori_loop(0, shards, step, 0)

    def dh1_rows(half):
        part = slice(half * rows, (half + 1) * rows)
        value = mm_nt(act[0, part, 0 : 3 * narrow], w_qkv[0])
        for s in range(1, shards):
            value += mm_nt(act[s, part, 0 : 3 * narrow], w_qkv[s])
        return value

    attend_back(0)
    feed_point((3, 4), (1, 2))
    total[0] = dh1_rows(0)
    turn_a[...] = jnp.transpose(h1[...].reshape(2 * rows, width))
    drain(1)
    feed_point(None, (2, 3))
    x_datt.wait_recv()
    turn_b[...] = jnp.transpose(datt[...].reshape(2 * rows, width))

    feed_point((4, 5), None)
    attend_back(1)
    sent[0] = dh1_rows(1).astype(BF16)
    x_dh1.start()
    feed_point((5, 6), (3, 5))

    def attn_grads(k, carry):
        s = reversed_order(k)
        for a in parts_of:
            store_grads(w_up, s, a, turn_a, act[s, :, 0 : 3 * narrow], 0, 3 * narrow)
            store_grads(w_up, s, a, turn_b, ctx[s], 3 * narrow, narrow)
            core_send(1, w_up, core_a, s, a).start()

        @pl.when(k > 0)
        def _():
            stage_core(1, w_up, core_a, y_a, reversed_order(k - 1))

        return carry

    lax.fori_loop(0, shards, attn_grads, 0)
    stage_core(1, w_up, core_a, y_a, z)

    x_feed.wait()

    def finish_forward(at, squares):
        branch = attended[at] + feed_own[at] + got[1, at].astype(F32)
        update = gate(at) * branch
        sent[1, at] = (own_z[at].astype(F32) + update).astype(BF16)
        dgate = jnp.sum(own_c[at].astype(F32) * branch, axis=1, keepdims=True)
        set_column(2, at, dgate * live(at))
        return squares + fold_rows(update * update)

    squares = row_tiles(rows, finish_forward, jnp.zeros((8, width), F32))
    put(0, sent.at[1]).start()
    count = jnp.sum(valid[...].astype(F32), axis=1, keepdims=True)
    energy = jnp.sum(jnp.sum(squares, axis=0, keepdims=True), axis=1, keepdims=True)
    rms = jnp.sqrt(energy / (width * jnp.maximum(count, 1.0)))

    if quick:
        feed_point(None, (5, 6))
    else:
        run_halves(feed_half, 0, total_halves)
    ahead = jnp.where(edge, 2, 1)
    run_halves(attn_half, 0, ahead)
    x_dh1.wait()

    def first_back(at, sums):
        dh1 = total[0, at] + got[0, at].astype(F32)
        row = own_z[at].astype(F32)
        factor = lax.rsqrt(jnp.mean(row * row, axis=1, keepdims=True) + EPS)
        scaled = dh1 * first_gain[...]
        back = factor * scaled - row * (factor**3 * jnp.mean(row * scaled, axis=1, keepdims=True))
        back = back + dmixed[at] + dscore(at) * w_router[...]
        got[1, at] = (own_c[at].astype(F32) + back).astype(BF16)
        return sums[0] + fold_rows(dscore(at) * row), sums[1] + fold_rows(dh1 * row * factor)

    zero = jnp.zeros((8, width), F32)
    router_sum, first_sum = row_tiles(rows, first_back, (zero, zero))
    put(1, got.at[1]).start()
    parts = [jnp.sum(part, axis=0, keepdims=True) for part in (router_sum, first_sum, second_sum)]
    small = jnp.concatenate(parts + [jnp.zeros((5, width), F32)], axis=0)

    def small_copy(k):
        return remote(small_send.at[k], small_got.at[k], sm_s.at[k], sm_r.at[k], small_devices[k])

    hops = len(small_devices)
    for k in range(hops):
        small_send[k] = small
        small_copy(k).start()
        if k > 0:
            attn_half(ahead + k)
        small_copy(k).wait()
        small = small + small_got[k]
        if k == 0:
            attn_half(ahead)
    stage_last(0, grads, y_f, z_f, swap_f, feed_out)

    def small_spread(far, source):
        slot = hops + source
        return remote(
            small_send.at[hops], small_got.at[slot], sm_s.at[hops + far - 1], sm_r.at[slot], (dp, lax.rem(z + far, shards))
        )

    small_send[hops] = small
    small_got[hops + z] = small
    for far in range(1, shards):
        small_spread(far, z).start()

    run_halves(attn_half, ahead + hops, total_halves)
    stage_last(1, w_up, y_a, z_a, swap_a, attn_out)
    for far in range(1, shards):
        small_spread(far, lax.rem(z + shards - far, shards)).wait_recv()
        small_spread(far, z).wait_send()
    small = small_got[hops]
    for k in range(1, shards):
        small = small + small_got[hops + k]
    row_at = lax.broadcasted_iota(jnp.int32, (8, 1), 0)
    small_send[0] = jnp.where(row_at == 3, rms, small)
    put(2, small_send.at[0]).start()
    stage_out(0, swap_f, feed_out)
    put(4, feed_out).start()
    stage_out(1, swap_a, attn_out)
    put(3, attn_out).start()

    drain(0)
    for copy in (x_h1, x_dfeed, *x_h2, x_datt):
        copy.wait_send()

    for group, core_got, y_got, z_got in ((0, core_f, y_f, z_f), (1, core_a, y_a, z_a)):
        remote(core_got, core_got, gc_s.at[group], gc_r.at[group, 0, 0], core_dev).wait_send()
        remote(y_got, y_got, gy_s.at[group], gy_r.at[group, 0, 0], y_dev).wait_send()
        moved = z_got.at[0 : shards - 1]
        remote(moved, moved, gz_s.at[group], gz_r.at[group, 0, 0], up_dev).wait_send()

    swap(0, swap_f).wait_send()
    swap(1, swap_a).wait_send()
    for k, src in enumerate((sent.at[1], got.at[1], small_send.at[0], attn_out, feed_out)):
        put(k, src).wait()


def run_block(size, operands):
    shards, rows, width = size["S"], size["R"], size["D"]
    heads, narrow, hidden, cut = size["hh"], size["n"], size["f"], size["DB"]
    mats = (2 if size["joined"] else 4) + 4
    stages = 3 + shards
    attn, feed = 4 * narrow, 2 * hidden
    dma = pltpu.SemaphoreType.DMA
    vmem = lambda *shape: pltpu.VMEM(shape, BF16)
    full = lambda *shape: pltpu.VMEM(shape, F32)
    scratch = [
        vmem(shards, width, 3 * narrow),
        vmem(shards, narrow, width),
        vmem(shards, 2, 2, 2, cut, hidden),
        vmem(shards, hidden, width),
        *[vmem(2, rows, width) for _ in range(4)],
        *[vmem(width, 2 * rows) for _ in range(2)],
        vmem(shards, 2, rows, 3 * narrow),
        vmem(shards, 2 * rows, narrow),
        vmem(shards, 2, heads * rows, rows),
        vmem(shards, 2 * rows, hidden),
        vmem(shards, 2 * rows, hidden),
        full(2, rows, width),
        full(2, rows, hidden),
        vmem(2, rows, width),
        vmem(2, rows, width),
        vmem(rows, width),
        vmem(rows, width),
        *[full(rows, width) for _ in range(3)],
        full(rows, 128),
        vmem(shards, 2, 2, 2, cut, feed),
        vmem(shards, 2, 2, cut, feed),
        vmem(shards, 2, cut, feed),
        vmem(shards + 1, 2, cut, feed),
        vmem(shards, 2, 2, cut, attn),
        vmem(shards, 2, cut, attn),
        vmem(shards + 1, 2, cut, attn),
        vmem(2, cut, feed),
        vmem(2, cut, attn),
        full(2, cut, attn),
        full(2, cut, feed),
        full(stages, 8, width),
        full(stages, 8, width),
        dma((mats,)),
        dma((2, 2)),
        dma((5,)),
        dma((2, shards + 1)),
        dma((mats, shards)),
        dma((2,)),
        dma((mats, shards)),
        dma((2,)),
        dma((2, shards)),
        dma((10,)),
        dma((10,)),
        dma((2,)),
        dma((2, shards, 2)),
        dma((2,)),
        dma((2, shards, 2)),
        dma((2,)),
        dma((2, shards + 1, 2)),
        dma((2,)),
        dma((2,)),
        dma((stages,)),
        dma((stages,)),
    ]
    near = pl.BlockSpec(memory_space=pltpu.VMEM)
    far = pl.BlockSpec(memory_space=pl.ANY)
    outs = [
        jax.ShapeDtypeStruct((rows, width), BF16),
        jax.ShapeDtypeStruct((rows, width), BF16),
        jax.ShapeDtypeStruct((8, width), F32),
        jax.ShapeDtypeStruct((2, cut, attn), F32),
        jax.ShapeDtypeStruct((2, cut, feed), F32),
    ]
    return pl.pallas_call(
        functools.partial(block_kernel, size),
        out_shape=outs,
        in_specs=[far, far] + [near] * 5 + [far] * (len(operands) - 7),
        out_specs=[pl.BlockSpec(memory_space=pltpu.HBM)] * len(outs),
        scratch_shapes=scratch,
        compiler_params=pltpu.CompilerParams(
            collective_id=0, has_side_effects=True, vmem_limit_bytes=64 * 2**20 - 65536
        ),
    )(*operands)


def place_kernel(size, assemble, routed, small, tokens, cotangent, *refs):
    length, width, rows = size["L"], size["D"], size["R"]
    gathered, refs = refs[: 4 if assemble else 2], refs[4 if assemble else 2 :]
    outs, refs = refs[: 12 if assemble else 2], refs[12 if assemble else 2 :]
    bases, staged, refs = refs[:2], refs[2 : 2 + len(gathered)], refs[2 + len(gathered) :]
    finals, (pick, keep, in_sem, out_sem, part_sem, final_sem) = refs[:-6], refs[-6:]
    block = 512
    steps = width // block

    def moving(src, dst, sem, k, b):
        at = (slice(None), pl.ds(b * block, block))
        return pltpu.make_async_copy(src[k].at[at], dst[k].at[at], sem.at[k, b])

    sources = (tokens, cotangent)
    parts = [pltpu.make_async_copy(src, dst, part_sem.at[k]) for k, (src, dst) in enumerate(zip(gathered, staged))]
    for copy in parts[:2]:
        copy.start()
    for b in range(steps):
        for k in range(2):
            moving(sources, bases, in_sem, k, b).start()
    for copy in parts[2:]:
        copy.start()
    line = lax.broadcasted_iota(jnp.int32, (length, rows), 0)
    chosen = jnp.where(line == routed[...], 1.0, 0.0)
    pick[...] = chosen.astype(BF16)
    keep[...] = jnp.broadcast_to((1.0 - jnp.sum(chosen, axis=1, keepdims=True)).astype(BF16), keep.shape)
    for copy in parts[:2]:
        copy.wait()
    for b in range(steps):
        for k in range(2):
            at = slice(b * block, (b + 1) * block)
            moving(sources, bases, in_sem, k, b).wait()
            kept = jnp.concatenate([keep[...]] * (block // 128), axis=1)
            bases[k][:, at] = mm(pick[...], staged[k][:, at]).astype(BF16) + bases[k][:, at] * kept
            moving(bases, outs, out_sem, k, b).start()
    last = []
    if assemble:
        for copy in parts[2:]:
            copy.wait()
        for k, value in enumerate(weight_outputs(size, *staged[2:])):
            finals[k][...] = value
            last.append(pltpu.make_async_copy(finals[k], outs[2 + k], final_sem.at[k]))
            last[-1].start()
        for k in range(3):
            outs[8 + k][...] = small[k : k + 1, :]
        outs[11][...] = small[3:4, 0:1]
    for b in range(steps):
        for k in range(2):
            moving(bases, outs, out_sem, k, b).wait()
    for copy in last:
        copy.wait()


def weight_outputs(size, attn, feed):
    narrow, hidden = size["n"], size["f"]

    def side_by_side(ref, lo, count):
        return jnp.concatenate([ref[0, :, lo : lo + count], ref[1, :, lo : lo + count]], axis=1)

    return (
        side_by_side(attn, 0, narrow),
        side_by_side(attn, narrow, narrow),
        side_by_side(attn, 2 * narrow, narrow),
        side_by_side(attn, 3 * narrow, narrow).T,
        side_by_side(feed, 0, hidden),
        side_by_side(feed, hidden, hidden).T,
    )


def place_rows(size, routed, tokens, cotangent, rows_res, rows_grad, small, attn, feed, assemble):
    length, width, rows = size["L"], size["D"], size["R"]
    cut, narrow, hidden = size["DB"], size["n"], size["f"]
    whole = lambda *shape: pl.BlockSpec(shape, lambda i: (0,) * len(shape))
    far = pl.BlockSpec(memory_space=pltpu.HBM)
    outs, out_specs = [jax.ShapeDtypeStruct((length, width), BF16)] * 2, [far] * 2
    gathered, finals = [rows_res, rows_grad], []
    if assemble:
        gathered += [attn, feed]
        finals = [(cut, 2 * narrow)] * 3 + [(2 * narrow, cut), (cut, 2 * hidden), (2 * hidden, cut)]
        tiny = [(1, width)] * 3 + [(1, 1)]
        outs = outs + [jax.ShapeDtypeStruct(shape, F32) for shape in finals + tiny]
        out_specs = out_specs + [far] * len(finals) + [whole(*shape) for shape in tiny]
    dma = pltpu.SemaphoreType.DMA
    return pl.pallas_call(
        functools.partial(place_kernel, size, assemble),
        grid=(1,),
        out_shape=outs,
        in_specs=[whole(1, rows), whole(*small.shape)] + [far] * (2 + len(gathered)),
        out_specs=out_specs,
        scratch_shapes=[
            *[pltpu.VMEM((length, width), BF16) for _ in range(2)],
            *[pltpu.VMEM(part.shape, part.dtype) for part in gathered],
            *[pltpu.VMEM(shape, F32) for shape in finals],
            pltpu.VMEM((length, rows), BF16),
            pltpu.VMEM((length, 128), BF16),
            dma((2, width // 512)),
            dma((2, width // 512)),
            dma((4,)),
            dma((6,)),
        ],
        compiler_params=pltpu.CompilerParams(vmem_limit_bytes=60 * 2**20),
    )(routed, small, tokens, cotangent, *gathered)


def shards_of(
    groups,
    tokens,
    cotangent,
    routed,
    valid_mask,
    w_router,
    first_gain,
    query_weight,
    key_weight,
    value_weight,
    output_weight,
    second_gain,
    up_weight,
    down_weight,
):
    shards, data = lax.axis_size("mp"), lax.axis_size("dp")
    _, length, width = tokens.shape
    rows = routed.shape[1]
    narrow = query_weight.shape[1] // 2
    hidden = up_weight.shape[1] // 2
    cut = width // 8
    chips_x = 1 << ((data // 2).bit_length() - 1) // 2
    size = dict(
        S=shards, ybit=2 * chips_x, R=rows, D=width, L=length, hh=narrow // HEAD_DIM,
        n=narrow, f=hidden, DB=cut, joined=narrow % 128 != 0,
    )
    dp = lax.axis_index("dp")
    x, y = (dp // 2) % 2, (dp // size["ybit"]) % 2
    qkv = (query_weight, key_weight, value_weight)
    if size["joined"]:
        halves = [lax.dynamic_slice_in_dim(weight, x * narrow, narrow, 1) for weight in qkv]
        qkv = (jnp.concatenate(halves, axis=1),)
    row = lambda vector: vector.reshape(1, width)
    operands = (
        tokens.reshape(-1, rows, width), cotangent.reshape(-1, rows, width), routed, valid_mask, row(w_router), row(first_gain), row(second_gain),
        *qkv, output_weight, up_weight.reshape(2, 2, 2, cut, 2 * hidden), down_weight,
    )
    rows_res, rows_grad, small, attn, feed = run_block(size, operands)
    whole_group = data == 8
    rms = small[3, 0:1]
    if not whole_group:
        block = 4 * y + 2 * x + dp % 2

        def over_groups(part):
            base = jnp.zeros((2, width, part.shape[2]), F32)
            placed = lax.dynamic_update_slice_in_dim(base, part, block * cut, 1)
            return lax.psum_scatter(placed, "dp", scatter_dimension=1, tiled=True)

        attn, feed = over_groups(attn), over_groups(feed)
        small = lax.psum(small, "dp") / 8.0
    placed = place_rows(size, routed, tokens[0], cotangent[0], rows_res, rows_grad, small, attn, feed, whole_group)
    residual, grad_tokens = placed[:2]
    if whole_group:
        vectors = [vector.reshape(width) for vector in placed[8:11]]
        weights, rms = placed[2:8], placed[11].reshape(1)
    else:
        vectors, weights = [small[k] for k in range(3)], weight_outputs(size, attn, feed)
    grad_query, grad_key, grad_value, grad_output, grad_up, grad_down = weights
    return (
        residual[None],
        grad_tokens[None],
        rms,
        vectors[0],
        vectors[1],
        grad_query,
        grad_key,
        grad_value,
        grad_output,
        vectors[2],
        grad_up,
        grad_down,
    )


def solution(mesh):
    in_specs = (
        P(("dp", "mp"), None, None),
        P(("dp", "mp"), None, None),
        P(("dp", "mp"), None),
        P(("dp", "mp"), None),
        P(),
        P(),
        P(None, "mp"),
        P(None, "mp"),
        P(None, "mp"),
        P("mp", None),
        P(),
        P(None, "mp"),
        P("mp", None),
    )
    out_specs = (
        P(("dp", "mp"), None, None),
        P(("dp", "mp"), None, None),
        P(("dp", "mp")),
        P(),
        P(),
        P("dp", "mp"),
        P("dp", "mp"),
        P("dp", "mp"),
        P("mp", "dp"),
        P(),
        P("dp", "mp"),
        P("mp", "dp"),
    )
    body = functools.partial(shards_of, mesh.shape["dp"] // 8)
    return jax.shard_map(body, mesh=mesh, in_specs=in_specs, out_specs=out_specs, check_vma=False)
```

```python
import functools
import math

import jax
import jax.numpy as jnp
from jax import lax
from jax.experimental import pallas as pl
from jax.experimental.pallas import tpu as pltpu
from jax.sharding import PartitionSpec as P

HEADS = 16
HEAD_DIM = 64
EPS = 1e-06
F32 = jnp.float32
BF16 = jnp.bfloat16
TILE = 64


def mm(left, right):
    return jnp.dot(left, right, preferred_element_type=F32)


def mm_nt(left, right):
    return lax.dot_general(left, right, (((1,), (1,)), ((), ())), preferred_element_type=F32)


def mm_tn(left, right):
    return lax.dot_general(left, right, (((0,), (0,)), ((), ())), preferred_element_type=F32)


def row_tiles(rows, body, init=0, first=0):
    def step(index, carry):
        return body(pl.ds(pl.multiple_of(first + index * TILE, TILE), TILE), carry)

    return lax.fori_loop(0, rows // TILE, step, init)


def fold_rows(value):
    return jnp.sum(value.reshape(-1, 8, value.shape[-1]), axis=0)


def gelu_both(value):
    cdf = 0.5 * (1.0 + lax.erf(value * math.sqrt(0.5)))
    density = jnp.exp(-0.5 * value * value) * (1.0 / math.sqrt(2.0 * math.pi))
    return value * cdf, cdf + value * density


def block_kernel(size, *refs):
    shards, ybit, rows, width, length = size["S"], size["ybit"], size["R"], size["D"], size["L"]
    heads, narrow, hidden, cut = size["hh"], size["n"], size["f"], size["DB"]
    joined = size["joined"]
    quarter = 2 * cut
    refs = list(refs)

    def take(count):
        taken, refs[:count] = refs[:count], []
        return taken

    tokens, cotangent = take(2)
    small_in = take(5)
    qkv_in = take(1 if joined else 3)
    out_in, up_in, down_in = take(3)
    outputs = take(5)
    w_qkv, w_out, w_up, w_down = take(4)
    h1, dfeed, h2, datt, turn_a, turn_b = take(6)
    qkv, ctx, prob, act, dup = take(5)
    total, wide, sent, got = take(4)
    own_z, own_c, attended, dmixed, feed_own, columns = take(6)
    lane = lax.broadcasted_iota(jnp.int32, (1, 128), 1)

    def column(k, at):
        return columns[at][:, k : k + 1]

    def set_column(k, at, value):
        columns[at] = jnp.where(lane == k, value, columns[at])

    gate, live, dscore = (functools.partial(column, k) for k in range(3))
    grads, core_f, y_f, z_f, core_a, y_a, z_a, swap_f, swap_a = take(9)
    attn_out, feed_out = take(2)
    small_send, small_got = take(2)
    routed, valid, w_router, first_gain, second_gain = small_held = take(5)
    load_sem, tok_sem, out_sem, small_sem = take(4)
    wz_s, wz_r, wy_s, wy_r, wc_s, wc_r = take(6)
    x_s, x_r = take(2)
    gc_s, gc_r, gy_s, gy_r, gz_s, gz_r, gx_s, gx_r = take(8)
    sm_s, sm_r = take(2)
    ex_sem = take(1)[0]

    dp = lax.axis_index("dp")
    z = lax.axis_index("mp")
    core = lax.rem(dp, 2)
    x = lax.rem(lax.div(dp, 2), 2)
    y = lax.rem(lax.div(dp, ybit), 2)
    core_dev = (dp + 1 - 2 * core, z)
    x_dev = (dp + 2 * (1 - 2 * x), z)
    y_dev = (dp + ybit * (1 - 2 * y), z)
    up_dev = (dp, z + 1)
    down_dev = (dp, z - 1)
    small_devices = [core_dev, x_dev, (dp + 2 * (1 - 2 * x) + ybit * (1 - 2 * y), z)]

    def remote(src, dst, send, recv, device):
        return pltpu.make_async_remote_copy(
            src_ref=src,
            dst_ref=dst,
            send_sem=send,
            recv_sem=recv,
            device_id=device,
            device_id_type=pl.DeviceIdType.MESH,
        )

    def order(j):
        high = lax.div(z, shards // 2)
        base = z + high * (shards - 1 - 2 * z)
        odd = lax.rem(j, 2)
        near = base + lax.div(j + 1, 2) * (2 * odd - 1)
        pick = jnp.where(j <= 2 * base, near, j)
        return pick + high * (shards - 1 - 2 * pick)

    attn_mats = list(range(len(qkv_in) + 1))
    up_mats = [len(attn_mats), len(attn_mats) + 1]
    down_mats = [len(attn_mats) + 2, len(attn_mats) + 3]
    feed_mats = up_mats + down_mats
    out_at, up_at, down_at = attn_mats[-1], up_mats[0], down_mats[0]

    def down_rows(i, start=0):
        return pl.ds(pl.multiple_of(start + (i - down_at) * (hidden // 2), hidden // 2), hidden // 2)

    def span(qy, qc):
        return pl.ds(pl.multiple_of((2 * qy + qc) * quarter, quarter), quarter)

    def lanes(count):
        return pl.ds(pl.multiple_of(x * count, count), count)

    def held(i, s, qy, qc):
        if i < out_at:
            part = w_qkv if joined else w_qkv.at[:, :, i * narrow : (i + 1) * narrow]
            return part.at[s, span(qy, qc)]
        if i == out_at:
            return w_out.at[s, :, span(qy, qc)]
        if i < down_at:
            return w_up.at[s, qy, qc, i - up_at]
        return w_down.at[s, down_rows(i), span(qy, qc)]

    def own_piece(i):
        if i < out_at:
            part = qkv_in[i].at[span(y, core)]
            return part if joined else part.at[:, lanes(narrow)]
        if i == out_at:
            return out_in.at[lanes(narrow), span(y, core)]
        if i < down_at:
            return up_in.at[y, core, i - up_at, :, lanes(hidden)]
        return down_in.at[down_rows(i, x * hidden), span(y, core)]

    def load_own(i):
        if i < out_at:
            if joined:
                src, dst = qkv_in[i], w_qkv.at[z]
            else:
                src, dst = qkv_in[i].at[:, lanes(narrow)], w_qkv.at[z, :, i * narrow : (i + 1) * narrow]
        elif i == out_at:
            src, dst = out_in.at[lanes(narrow), :], w_out.at[z]
        elif i < down_at:
            b = i - up_at
            src, dst = up_in.at[:, :, b, :, lanes(hidden)], w_up.at[z, :, :, b]
        else:
            src, dst = down_in.at[down_rows(i, x * hidden), :], w_down.at[z, down_rows(i)]
        return pltpu.make_async_copy(src, dst, load_sem.at[i])

    def group_of(i):
        return 0 if i <= out_at else 1

    def y_group(i):
        return 0 if i <= out_at else 1 if i < down_at else 2 + i - down_at

    def own_up(i):
        return remote(own_piece(i), held(i, z, y, core), wz_s.at[group_of(i), z], wz_r.at[i, z], up_dev)

    def own_down(i):
        return remote(own_piece(i), held(i, z, y, core), wz_s.at[group_of(i), shards], wz_r.at[i, z], down_dev)

    def pass_on(i, s, device):
        piece = held(i, s, y, core)
        return remote(piece, piece, wz_s.at[group_of(i), s], wz_r.at[i, s], device)

    def across_y(i, s, qy):
        piece = held(i, s, qy, core)
        return remote(piece, piece, wy_s.at[y_group(i)], wy_r.at[i, s], y_dev)

    def across_core(i, s, qy, qc):
        piece = held(i, s, qy, qc)
        group = group_of(i)
        return remote(piece, piece, wc_s.at[group], wc_r.at[group, s], core_dev)

    def await_pieces(group, sem, count, receiving=False):
        mats = attn_mats if group == 0 else feed_mats
        if joined:
            refs = [held(i, 0, 0, 0) for i in mats] * count
        else:
            flat = w_up.at[0, 0, 0] if group == 0 else w_up.at[0, 0]
            if count == 2:
                flat = w_up.at[0, 0] if group == 0 else w_up.at[0]
            elif count == shards - 1:
                flat = w_up.at[0 : shards - 1, 0, 0] if group == 0 else w_up.at[0 : shards - 1, 0]
            elif count == 2 * (shards - 1):
                flat = w_up.at[0 : shards - 1, 0] if group == 0 else w_up.at[0 : shards - 1]
            refs = [flat]
        for ref in refs:
            if receiving:
                remote(ref, ref, wc_s.at[group], sem, core_dev).wait_recv()
            else:
                remote(ref, ref, sem, wc_r.at[group, 0], core_dev).wait_send()

    def send_own_up(mats):
        for i in mats:
            own_up(i).start()

    def send_own_down(mats):
        for i in mats:
            own_down(i).start()

    def passing(s, action):
        @pl.when((s < z) & (z < shards - 1))
        def _():
            action(up_dev)

        @pl.when((s > z) & (z > 0))
        def _():
            action(down_dev)

    edge = (z == 0) | (z == shards - 1)
    inner = jnp.logical_not(edge)

    def by_z_here(i, j):
        return quick and i == by_z and isinstance(j, int) and j == 1

    def arrive_one(i, j):
        s = order(j)
        pass_on(i, s, up_dev).wait_recv()
        passing(s, lambda device: pass_on(i, s, device).start())
        if by_z_here(i, j):

            @pl.when(inner)
            def _():
                across_y(i, s, y).start()

        else:
            across_y(i, s, y).start()
        across_core(i, s, y, core).start()

    def arrive(mats, j):
        for i in mats:
            arrive_one(i, j)

    def follow(j):
        s = order(j)

        @pl.when((s == 0) & (z < shards - 1))
        def _():
            send_own_up(feed_mats)

        @pl.when((s == shards - 1) & (z > 0))
        def _():
            send_own_down(feed_mats)

    def relay(mats, j):
        s = order(j)
        for i in mats:
            if by_z_here(i, j):

                @pl.when(edge)
                def _():
                    bypass(s, up_dev).wait_recv()

                @pl.when(inner)
                def _():
                    across_y(i, s, 1 - y).wait_recv()

            else:
                across_y(i, s, 1 - y).wait_recv()
            across_core(i, s, 1 - y, core).start()

    def settle(group, j):
        await_pieces(group, wc_r.at[group, order(j)], 2, True)

    def await_y(index, blocks, count):
        flat = w_up.at[0:count, 0, 0] if blocks == 2 else w_up.at[0:count, 0, 0, 0]
        remote(flat, flat, wy_s.at[index], wy_r.at[0, 0], y_dev).wait_send()

    quick = shards == 4
    by_z = down_mats[-1]

    def bypass(s, device):
        src = down_in.at[down_rows(by_z, x * hidden), span(1 - y, core)]
        return remote(src, held(by_z, s, 1 - y, core), ex_sem.at[0], ex_sem.at[1], device)

    def drain(group):
        @pl.when(z < shards - 1)
        def _():
            await_pieces(group, wz_s.at[group, z], 1)

        @pl.when(z > 0)
        def _():
            await_pieces(group, wz_s.at[group, shards], 1)

        def step(j, carry):
            s = order(j)
            passing(s, lambda device: await_pieces(group, wz_s.at[group, s], 1))
            return carry

        lax.fori_loop(1, shards, step, 0)
        if group == 0:
            await_pieces(0, wy_s.at[0], shards - 1)
        else:
            await_y(1, 2, shards - 1)
            await_y(2, 1, shards - 1)
            if not quick:
                await_y(3, 1, shards - 1)
            else:

                @pl.when(edge)
                def _():
                    await_y(3, 1, shards - 2)

                @pl.when(inner)
                def _():
                    await_y(3, 1, shards - 1)
                    bypass(z, up_dev).wait_send()

        await_pieces(group, wc_s.at[group], 2 * (shards - 1))

    def exchange(slot, src, dst):
        return remote(src, dst, x_s.at[slot], x_r.at[slot], x_dev)

    x_h1 = exchange(0, h1.at[0], h1.at[1])
    x_dfeed = exchange(1, dfeed.at[0], dfeed.at[1])
    upper, lower = slice(0, rows // 2), slice(rows // 2, rows)
    x_att = [exchange(2 + 6 * k, sent.at[0, part], got.at[0, part]) for k, part in enumerate((upper, lower))]
    x_h2 = [exchange(3 + 6 * k, h2.at[0, part], h2.at[1, part]) for k, part in enumerate((upper, lower))]
    x_dh2 = [exchange(4 + 6 * k, sent.at[0, part], got.at[0, part]) for k, part in enumerate((upper, lower))]
    x_feed = exchange(5, sent.at[1], got.at[1])
    x_datt = [exchange(6 + 5 * k, datt.at[0, part], datt.at[1, part]) for k, part in enumerate((upper, lower))]
    x_dh1 = exchange(7, sent.at[0], got.at[0])

    def put(k, src):
        return pltpu.make_async_copy(src, outputs[k], out_sem.at[k])

    steps = length // (2 * rows)
    stages = ((got, sent), (h2, datt))

    def block_loads(t):
        copies = []
        for k, (array, buf) in enumerate(zip((tokens, cotangent), stages[t % 2])):
            copies.append(pltpu.make_async_copy(array.at[2 * t : 2 * t + 2], buf, tok_sem.at[t % 2, k]))
        return copies

    barrier = pltpu.get_barrier_semaphore()

    def greet(device):
        pl.semaphore_signal(barrier, inc=1, device_id=device, device_id_type=pl.DeviceIdType.MESH)

    for device in (core_dev, x_dev, y_dev):
        greet(device)

    @pl.when(z > 0)
    def _():
        greet(down_dev)

    @pl.when(z < shards - 1)
    def _():
        greet(up_dev)

    small_loads = [pltpu.make_async_copy(src, dst, small_sem.at[k]) for k, (src, dst) in enumerate(zip(small_in, small_held))]
    for copy in small_loads:
        copy.start()
    for t in range(2):
        for copy in block_loads(t):
            copy.start()
    for i in attn_mats + feed_mats:
        load_own(i).start()

    def begin():
        ends = jnp.where(z == 0, 1, 0) + jnp.where(z == shards - 1, 1, 0)
        pl.semaphore_wait(barrier, 5 - ends)

        @pl.when(z < shards - 1)
        def _():
            send_own_up(attn_mats)

        @pl.when(z > 0)
        def _():
            send_own_down(attn_mats)

        @pl.when(z == 0)
        def _():
            send_own_up(feed_mats)

        @pl.when(z == shards - 1)
        def _():
            send_own_down(feed_mats)

    for copy in small_loads:
        copy.wait()
    as_rows = jnp.broadcast_to(routed[...].astype(F32), (8, rows))
    position = jnp.transpose(as_rows)[:, 0:1].astype(jnp.int32)
    flags = jnp.zeros((rows, 1), F32)
    for t in range(steps):
        for copy in block_loads(t):
            copy.wait()
        hit = position == 2 * t * rows + lax.broadcasted_iota(jnp.int32, (rows, 2 * rows), 1)
        chosen = jnp.where(hit, 1.0, 0.0)
        pick = chosen.astype(BF16)
        for k, buf in enumerate(stages[t % 2]):
            picked = mm(pick, buf[...].reshape(2 * rows, width))
            total[k] = picked if t == 0 else total[k] + picked
        if t + 2 < steps:
            for copy in block_loads(t + 2):
                copy.start()
        mask = valid[:, 2 * t * rows : 2 * (t + 1) * rows].astype(F32)
        flags = flags + jnp.sum(chosen * mask, axis=1, keepdims=True)
        if t == steps // 2 - 1:
            begin()
    columns[...] = jnp.broadcast_to(flags, columns.shape)

    def prepare(at, carry):
        row, cot = total[0, at], total[1, at]
        own_z[at] = row.astype(BF16)
        own_c[at] = cot.astype(BF16)
        gate_here = jnp.sum(row * w_router[...], axis=1, keepdims=True) * live(at)
        set_column(0, at, gate_here)
        factor = lax.rsqrt(jnp.mean(row * row, axis=1, keepdims=True) + EPS)
        h1[0, at] = (row * factor * first_gain[...]).astype(BF16)
        dfeed[0, at] = (gate_here * cot).astype(BF16)
        return carry

    row_tiles(rows, prepare)
    x_h1.start()
    x_dfeed.start()

    lane_head = lax.div(lax.broadcasted_iota(jnp.int32, (1, narrow), 1), HEAD_DIM)
    masks = [jnp.where(lane_head == h, 1.0, 0.0) for h in range(heads)]
    masks_low = [mask.astype(BF16) for mask in masks]

    def stacked(value):
        return jnp.concatenate([value * mask for mask in masks_low], axis=0) if heads > 1 else value

    def unstacked(value):
        if heads == 1:
            return value
        picked = value[0:rows] * masks[0]
        for h in range(1, heads):
            picked = picked + value[h * rows : (h + 1) * rows] * masks[h]
        return picked

    score_shape = (heads * rows, rows)
    causal = lax.rem(lax.broadcasted_iota(jnp.int32, score_shape, 0), rows) >= lax.broadcasted_iota(
        jnp.int32, score_shape, 1
    )

    for i in attn_mats:
        load_own(i).wait()

    @pl.when(edge)
    def _():
        for j in range(1, shards):
            arrive(attn_mats, j)
            follow(j)
            if j > 1:
                relay(attn_mats, j - 1)

    @pl.when(inner)
    def _():
        for i in attn_mats:
            for j in (1, 2):
                arrive_one(i, j)
        for j in (1, 2):
            follow(j)
        for j in range(3, shards):
            arrive(attn_mats, j)
            follow(j)
        for j in range(1, shards - 1):
            relay(attn_mats, j)

    x_h1.wait_recv()

    def attend(j, carry):
        s = order(j)

        @pl.when(j + 1 == shards)
        def _():
            relay(attn_mats, j)
            arrive(up_mats, 1)

        @pl.when(j > 0)
        def _():
            settle(0, j)

        low = mm(h1[...].reshape(2 * rows, width), w_qkv[s]).astype(BF16)
        query = low[:, 0:narrow] * jnp.asarray(HEAD_DIM**-0.5, BF16)
        qkv[s] = jnp.concatenate([query, low[:, narrow:]], axis=1).reshape(2, rows, 3 * narrow)
        for half in range(2):
            query = qkv[s, half, :, 0:narrow]
            key = qkv[s, half, :, narrow : 2 * narrow]
            value = qkv[s, half, :, 2 * narrow : 3 * narrow]
            scores = jnp.where(causal, mm_nt(stacked(query), key), -1e30)
            raised = jnp.exp(scores - jnp.max(scores, axis=1, keepdims=True))
            weights = (raised / jnp.sum(raised, axis=1, keepdims=True)).astype(BF16)
            prob[s, half] = weights
            ctx[s, half * rows : (half + 1) * rows] = unstacked(mm(weights, value)).astype(BF16)
        return carry

    lax.fori_loop(0, shards, attend, 0)

    def project_out(half):
        parts = [ctx[s, half * rows : (half + 1) * rows] for s in range(shards)]
        return mm(jnp.concatenate(parts, axis=1), w_out[...].reshape(shards * narrow, width))

    sent[0] = project_out(1).astype(BF16)
    for copy in x_att:
        copy.start()
    attended[...] = project_out(0)
    arrive(down_mats, 1)
    arrive(up_mats, 2)

    @pl.when(inner)
    def _():
        arrive(down_mats, 2)
        for j in range(3, shards):
            arrive(feed_mats, j)
        if quick:

            @pl.when(z == 1)
            def _():
                bypass(z, down_dev).start()

            @pl.when(z == shards - 2)
            def _():
                bypass(z, up_dev).start()

    def mix(at, carry):
        att = attended[at] + got[0, at].astype(F32)
        attended[at] = att
        mixed = own_z[at].astype(F32) + att
        factor = lax.rsqrt(jnp.mean(mixed * mixed, axis=1, keepdims=True) + EPS)
        h2[0, at] = (mixed * factor * second_gain[...]).astype(BF16)
        return carry

    for k in range(2):
        x_att[k].wait()
        row_tiles(rows // 2, mix, first=k * (rows // 2))
        x_h2[k].start()

        @pl.when(edge)
        def _():
            arrive(down_mats[k : k + 1], 2)


    x_dfeed.wait_recv()

    parts_of = (1 - y, y)

    def core_send(group, buf, into, s, a):
        src = buf.at[s, a, :, 1 - core]
        return remote(src, into.at[s, a], gc_s.at[group], gc_r.at[group, s, a], core_dev)

    halves = (1 - x, x)

    def columns_of(group, c):
        return slice(c * 2 * narrow, (c + 1) * 2 * narrow) if group == 1 else slice(0, 2 * hidden)

    def pieces(group):
        return range(2) if group == 1 else range(1)

    def sem_at(group, b, c):
        return 2 + 2 * b + c if group == 1 else b

    def y_send(group, buf, into, s, b, c):
        cols = columns_of(group, c)
        src = buf.at[s, 1 - y, b, core, :, cols]
        recv = gy_r.at[s, sem_at(group, b, c)]
        return remote(src, into.at[s, b, :, cols], gy_s.at[group], recv, y_dev)

    def z_send(group, buf, into, s, device, slot, b, c):
        cols = columns_of(group, c)
        src = buf.at[s, y, b, core, :, cols]
        recv = gz_r.at[slot, sem_at(group, b, c)]
        return remote(src, into.at[slot, b, :, cols], gz_s.at[group], recv, device)

    def add_into(ref, other):
        ref[...] = (ref[...].astype(F32) + other[...].astype(F32)).astype(BF16)

    def stage_core(group, buf, core_got, y_got, s):
        core_send(group, buf, core_got, s, 1 - y).wait_recv()
        for b in halves:
            add_into(buf.at[s, 1 - y, b, core], core_got.at[s, 1 - y, b])
            for c in pieces(group):
                y_send(group, buf, y_got, s, b, c).start()
        core_send(group, buf, core_got, s, y).wait_recv()
        for b in range(2):
            add_into(buf.at[s, y, b, core], core_got.at[s, y, b])

    def stage_y(group, buf, y_got, s, b, c):
        y_send(group, buf, y_got, s, b, c).wait_recv()
        cols = columns_of(group, c)
        add_into(buf.at[s, y, b, core, :, cols], y_got.at[s, b, :, cols])

    def line_in(group, buf, z_got, s, slot, b, c):
        z_send(group, buf, z_got, s, up_dev, slot, b, c).wait_recv()
        cols = columns_of(group, c)
        add_into(buf.at[s, y, b, core, :, cols], z_got.at[slot, b, :, cols])

    def stage_z(group, buf, z_got, s, b, c):
        @pl.when(s > z)
        def _():
            @pl.when(z > 0)
            def _():
                line_in(group, buf, z_got, s, s, b, c)

            z_send(group, buf, z_got, s, up_dev, s, b, c).start()

        @pl.when(s < z)
        def _():
            @pl.when(z < shards - 1)
            def _():
                line_in(group, buf, z_got, s, s, b, c)

            slot = jnp.where(s == z - 1, shards, s)
            z_send(group, buf, z_got, s, down_dev, slot, b, c).start()

    def swap(group, pair, c):
        cols = columns_of(group, c)
        index = 1 + c if group == 1 else 0
        return remote(pair.at[0, :, cols], pair.at[1, :, cols], gx_s.at[index], gx_r.at[index], x_dev)

    def stage_last(group, buf, y_got, z_got, pair, out):
        for b in halves:
            for c in pieces(group):
                cols = columns_of(group, c)
                stage_y(group, buf, y_got, z, b, c)
                out[b, :, cols] = buf[z, y, b, core, :, cols].astype(F32)

                @pl.when(z > 0)
                def _():
                    z_send(group, buf, z_got, z, up_dev, z, b, c).wait_recv()
                    out[b, :, cols] += z_got[z, b, :, cols].astype(F32)

                @pl.when(z < shards - 1)
                def _():
                    z_send(group, buf, z_got, z, up_dev, shards, b, c).wait_recv()
                    out[b, :, cols] += z_got[shards, b, :, cols].astype(F32)

                if b is halves[0]:
                    pair[0, :, cols] = out[b, :, cols].astype(BF16)
                    swap(group, pair, c).start()

    def stage_out(group, pair, out):
        for c in pieces(group):
            swap(group, pair, c).wait_recv()
        out[1 - x] = pair[1].astype(F32)

    def reversed_order(k):
        return order(shards - 1 - k)

    def store_grads(buf, s, a, left, right, lo, count):
        part = pl.ds(pl.multiple_of(2 * a * quarter, 2 * quarter), 2 * quarter)
        value = mm(left[part, :], right).astype(BF16)
        buf[s, a, :, :, :, lo : lo + count] = value.reshape(2, 2, cut, count)

    def line_half(group, buf, y_got, z_got, s, m):
        b = jnp.where(lax.rem(m, 2) == 0, 1 - x, x)
        for c in pieces(group):
            stage_y(group, buf, y_got, s, b, c)
            stage_z(group, buf, z_got, s, b, c)

    def feed_half(m):
        line_half(0, grads, y_f, z_f, order(leaving(lax.div(m, 2))), m)

    def attn_half(m):
        line_half(1, w_up, y_a, z_a, reversed_order(lax.div(m, 2)), m)

    def run_halves(step, first, last):
        def body(m, carry):
            step(m)
            return carry

        lax.fori_loop(first, last, body, 0)

    total_halves = 2 * (shards - 1)

    def leaving(k):
        if not quick:
            return shards - 1 - k
        ends, middle = jnp.where(edge, 2, 1), jnp.where(edge, 1, 2)
        return jnp.where(k == 0, ends, jnp.where(k == 1, 3, jnp.where(k == 2, middle, 0)))

    def feed_point(ends, middle):
        if quick and ends is not None:

            @pl.when(edge)
            def _():
                run_halves(feed_half, *ends)

        if quick and middle is not None:

            @pl.when(inner)
            def _():
                run_halves(feed_half, *middle)

    total[...] = jnp.zeros_like(total)
    turn_a[:, 0:rows] = jnp.transpose(h2[0])
    turn_b[...] = jnp.transpose(dfeed[...].reshape(2 * rows, width))
    for i in feed_mats:
        load_own(i).wait()

    def feed_grads(s):
        for a in parts_of:
            store_grads(grads, s, a, turn_a, dup[s], 0, hidden)
            store_grads(grads, s, a, turn_b, act[s], hidden, hidden)
            core_send(0, grads, core_f, s, a).start()

    def feed_core(s):
        stage_core(0, grads, core_f, y_f, s)

    def feed_chunk(s, half):
        part = pl.ds(pl.multiple_of(half * rows, rows), rows)
        up_here = w_up[s].reshape(width, hidden)
        wide[0] = mm(h2[half], up_here)
        wide[1] = mm_nt(dfeed[half], w_down[s])

        def turn(at, inside):
            active, slope = gelu_both(wide[0, at])
            out = pl.ds(pl.multiple_of(half * rows + at.start, TILE), TILE)
            act[s, out] = active.astype(BF16)
            dup[s, out] = (wide[1, at] * slope).astype(BF16)
            return inside

        row_tiles(rows, turn)
        total[half] += mm_nt(dup[s, part], up_here)

    def own_step(i, carry):
        j = jnp.where(edge, 2 * i, i) if quick else i
        active = inner | (i < 2) if quick else i >= 0

        @pl.when(active & (i > 0))
        def _():
            settle(1, j)

        @pl.when(active)
        def _():
            feed_chunk(order(j), 0)

        if quick:

            @pl.when(edge & (i == 0))
            def _():
                relay(feed_mats[:-1], 1)
                arrive(up_mats, 3)
                relay(feed_mats, 2)

            @pl.when(edge & (i == 1))
            def _():
                arrive(down_mats, 3)
                relay(up_mats, 3)

            @pl.when(inner & (i == 0))
            def _():
                relay(feed_mats, 1)

            @pl.when(inner & (i == 1))
            def _():
                relay(feed_mats, 2)

        else:

            @pl.when(edge & (j > 1) & (j + 1 < shards))
            def _():
                arrive(down_mats, j + 1)

            @pl.when(j + 2 < shards)
            def _():
                relay(feed_mats, j + 1)

            @pl.when(edge & (j + 3 < shards))
            def _():
                arrive(up_mats, j + 3)

        return carry

    lax.fori_loop(0, shards - 1, own_step, 0)
    for copy in x_h2:
        copy.wait_recv()
    turn_a[:, rows : 2 * rows] = jnp.transpose(h2[1])

    def other_step(k, carry):
        j, active = k, k >= 0
        if quick:
            j = jnp.where(edge, 2 - 2 * k, jnp.where(k < 2, 1 - k, 2))
            active = inner | (k < 2)

        @pl.when(active)
        def _():
            feed_chunk(order(j), 1)

        if quick:

            @pl.when(k == 0)
            def _():
                feed_grads(order(leaving(0)))
                feed_core(order(leaving(0)))

        return carry

    lax.fori_loop(0, shards - 1, other_step, 0)

    def last_step(k, carry):
        j, half, final = shards - 1, 1 - k, 0
        if quick:
            j = jnp.where(edge & (lax.rem(k, 2) == 1), 1, shards - 1)
            half = jnp.where(edge, jnp.where(k < 2, 1, 0), 1 - k)
            final = jnp.where(edge, 1, 0)

            @pl.when(inner & (k == 0))
            def _():
                relay(up_mats, shards - 1)

        @pl.when(k == 0)
        def _():
            relay(down_mats if quick else feed_mats, shards - 1)

        if quick:

            @pl.when(edge & (k == 0))
            def _():
                relay([by_z], 1)

        @pl.when(k <= final)
        def _():
            settle(1, j)

        feed_chunk(order(j), half)

        @pl.when(k == final)
        def _():
            sent[0] = total[1].astype(BF16)
            for copy in x_dh2:
                copy.start()

        if quick:

            @pl.when(edge & (k == 2))
            def _():
                feed_grads(order(leaving(1)))

            @pl.when(edge & (k == 3))
            def _():
                feed_core(order(leaving(1)))

        return carry

    lax.fori_loop(0, jnp.where(edge, 4, 2) if quick else 2, last_step, 0)
    first_left = jnp.where(edge, 2, 1) if quick else 0

    def feed_grads_step(k, carry):
        if quick:

            @pl.when((k == 2) & edge)
            def _():
                feed_half(0)

        feed_grads(order(leaving(k)))

        @pl.when(k > first_left)
        def _():
            feed_core(order(leaving(k - 1)))

        return carry

    lax.fori_loop(first_left, shards, feed_grads_step, 0)
    feed_point((1, 2), None)
    feed_core(z)

    def feed_rows(half):
        value = mm(act[0, half * rows : (half + 1) * rows], w_down[0])
        for s in range(1, shards):
            value += mm(act[s, half * rows : (half + 1) * rows], w_down[s])
        return value

    def second_back(at, carry):
        dh2 = total[0, at] + got[0, at].astype(F32)
        mixed = own_z[at].astype(F32) + attended[at]
        factor = lax.rsqrt(jnp.mean(mixed * mixed, axis=1, keepdims=True) + EPS)
        scaled = dh2 * second_gain[...]
        back = factor * scaled - mixed * (factor**3 * jnp.mean(mixed * scaled, axis=1, keepdims=True))
        dmixed[at] = back
        datt[0, at] = (gate(at) * own_c[at].astype(F32) + back).astype(BF16)
        return carry + fold_rows(dh2 * mixed * factor)

    second_sum = jnp.zeros((8, width), F32)
    for k in range(2):
        x_dh2[k].wait()
        second_sum = row_tiles(rows // 2, second_back, second_sum, first=k * (rows // 2))
        x_datt[k].start()
    sent[1] = feed_rows(1).astype(BF16)
    x_feed.start()
    feed_point((2, 3), (0, 1))
    feed_own[...] = feed_rows(0)

    def attend_back(half):
        part = slice(half * rows, (half + 1) * rows)

        def step(k, carry):
            s = reversed_order(k)
            dctx = mm_nt(datt[half], w_out[s]).astype(BF16)
            query = qkv[s, half, :, 0:narrow]
            key = qkv[s, half, :, narrow : 2 * narrow]
            value = qkv[s, half, :, 2 * narrow : 3 * narrow]
            weights = prob[s, half]
            dhead = stacked(dctx)
            dweights = mm_nt(dhead, value)
            full = weights.astype(F32)
            dscores = full * (dweights - jnp.sum(dweights * full, axis=1, keepdims=True))
            dscores = dscores.astype(BF16)
            dquery = unstacked(mm(dscores, key)) * HEAD_DIM**-0.5
            dkey = mm_tn(dscores, stacked(query))
            dvalue = mm_tn(weights, dhead)
            act[s, part, 0 : 3 * narrow] = jnp.concatenate([dquery, dkey, dvalue], axis=1).astype(BF16)
            return carry

        lax.fori_loop(0, shards, step, 0)

    def dh1_rows(half):
        part = slice(half * rows, (half + 1) * rows)
        value = mm_nt(act[0, part, 0 : 3 * narrow], w_qkv[0])
        for s in range(1, shards):
            value += mm_nt(act[s, part, 0 : 3 * narrow], w_qkv[s])
        return value

    attend_back(0)
    feed_point((3, 4), (1, 2))
    total[0] = dh1_rows(0)
    turn_a[...] = jnp.transpose(h1[...].reshape(2 * rows, width))
    drain(1)
    feed_point(None, (2, 3))
    for copy in x_datt:
        copy.wait_recv()
    turn_b[...] = jnp.transpose(datt[...].reshape(2 * rows, width))

    feed_point((4, 5), None)
    attend_back(1)
    sent[0] = dh1_rows(1).astype(BF16)
    x_dh1.start()
    feed_point((5, 6), (3, 5))

    def attn_grads(k, carry):
        s = reversed_order(k)
        for a in parts_of:
            store_grads(w_up, s, a, turn_a, act[s, :, 0 : 3 * narrow], 0, 3 * narrow)
            store_grads(w_up, s, a, turn_b, ctx[s], 3 * narrow, narrow)
            core_send(1, w_up, core_a, s, a).start()

        @pl.when(k > 0)
        def _():
            stage_core(1, w_up, core_a, y_a, reversed_order(k - 1))

        return carry

    lax.fori_loop(0, shards, attn_grads, 0)
    stage_core(1, w_up, core_a, y_a, z)

    x_feed.wait()

    def finish_forward(at, squares):
        branch = attended[at] + feed_own[at] + got[1, at].astype(F32)
        update = gate(at) * branch
        sent[1, at] = (own_z[at].astype(F32) + update).astype(BF16)
        dgate = jnp.sum(own_c[at].astype(F32) * branch, axis=1, keepdims=True)
        set_column(2, at, dgate * live(at))
        return squares + fold_rows(update * update)

    squares = row_tiles(rows, finish_forward, jnp.zeros((8, width), F32))
    put(0, sent.at[1]).start()
    count = jnp.sum(valid[...].astype(F32), axis=1, keepdims=True)
    energy = jnp.sum(jnp.sum(squares, axis=0, keepdims=True), axis=1, keepdims=True)
    rms = jnp.sqrt(energy / (width * jnp.maximum(count, 1.0)))

    if quick:
        feed_point(None, (5, 6))
    else:
        run_halves(feed_half, 0, total_halves)
    ahead = jnp.where(edge, 2, 1)
    run_halves(attn_half, 0, ahead)
    x_dh1.wait()

    def first_back(at, sums):
        dh1 = total[0, at] + got[0, at].astype(F32)
        row = own_z[at].astype(F32)
        factor = lax.rsqrt(jnp.mean(row * row, axis=1, keepdims=True) + EPS)
        scaled = dh1 * first_gain[...]
        back = factor * scaled - row * (factor**3 * jnp.mean(row * scaled, axis=1, keepdims=True))
        back = back + dmixed[at] + dscore(at) * w_router[...]
        got[1, at] = (own_c[at].astype(F32) + back).astype(BF16)
        return sums[0] + fold_rows(dscore(at) * row), sums[1] + fold_rows(dh1 * row * factor)

    zero = jnp.zeros((8, width), F32)
    router_sum, first_sum = row_tiles(rows, first_back, (zero, zero))
    put(1, got.at[1]).start()
    parts = [jnp.sum(part, axis=0, keepdims=True) for part in (router_sum, first_sum, second_sum)]
    small = jnp.concatenate(parts + [jnp.zeros((5, width), F32)], axis=0)

    def small_copy(k):
        return remote(small_send.at[k], small_got.at[k], sm_s.at[k], sm_r.at[k], small_devices[k])

    hops = len(small_devices)
    for k in range(hops):
        small_send[k] = small
        small_copy(k).start()
        if k > 0:
            attn_half(ahead + k)
        small_copy(k).wait()
        small = small + small_got[k]
        if k == 0:
            attn_half(ahead)
    stage_last(0, grads, y_f, z_f, swap_f, feed_out)

    def small_spread(far, source):
        slot = hops + source
        return remote(
            small_send.at[hops], small_got.at[slot], sm_s.at[hops + far - 1], sm_r.at[slot], (dp, lax.rem(z + far, shards))
        )

    small_send[hops] = small
    small_got[hops + z] = small
    for far in range(1, shards):
        small_spread(far, z).start()

    run_halves(attn_half, ahead + hops, total_halves)
    stage_last(1, w_up, y_a, z_a, swap_a, attn_out)
    for far in range(1, shards):
        small_spread(far, lax.rem(z + shards - far, shards)).wait_recv()
        small_spread(far, z).wait_send()
    small = small_got[hops]
    for k in range(1, shards):
        small = small + small_got[hops + k]
    row_at = lax.broadcasted_iota(jnp.int32, (8, 1), 0)
    small_send[0] = jnp.where(row_at == 3, rms, small)
    put(2, small_send.at[0]).start()
    stage_out(0, swap_f, feed_out)
    put(4, feed_out).start()
    stage_out(1, swap_a, attn_out)
    put(3, attn_out).start()

    drain(0)
    for copy in (x_h1, x_dfeed, *x_h2, *x_datt):
        copy.wait_send()

    for group, core_got, y_got, z_got in ((0, core_f, y_f, z_f), (1, core_a, y_a, z_a)):
        remote(core_got, core_got, gc_s.at[group], gc_r.at[group, 0, 0], core_dev).wait_send()
        remote(y_got, y_got, gy_s.at[group], gy_r.at[0, 0], y_dev).wait_send()
        moved = z_got.at[0 : shards - 1]
        remote(moved, moved, gz_s.at[group], gz_r.at[0, 0], up_dev).wait_send()

    swap(0, swap_f, 0).wait_send()
    for c in pieces(1):
        swap(1, swap_a, c).wait_send()
    for k, src in enumerate((sent.at[1], got.at[1], small_send.at[0], attn_out, feed_out)):
        put(k, src).wait()


def run_block(size, operands):
    shards, rows, width = size["S"], size["R"], size["D"]
    heads, narrow, hidden, cut = size["hh"], size["n"], size["f"], size["DB"]
    mats = (2 if size["joined"] else 4) + 4
    stages = 3 + shards
    attn, feed = 4 * narrow, 2 * hidden
    dma = pltpu.SemaphoreType.DMA
    vmem = lambda *shape: pltpu.VMEM(shape, BF16)
    full = lambda *shape: pltpu.VMEM(shape, F32)
    scratch = [
        vmem(shards, width, 3 * narrow),
        vmem(shards, narrow, width),
        vmem(shards, 2, 2, 2, cut, hidden),
        vmem(shards, hidden, width),
        *[vmem(2, rows, width) for _ in range(4)],
        *[vmem(width, 2 * rows) for _ in range(2)],
        vmem(shards, 2, rows, 3 * narrow),
        vmem(shards, 2 * rows, narrow),
        vmem(shards, 2, heads * rows, rows),
        vmem(shards, 2 * rows, hidden),
        vmem(shards, 2 * rows, hidden),
        full(2, rows, width),
        full(2, rows, hidden),
        vmem(2, rows, width),
        vmem(2, rows, width),
        vmem(rows, width),
        vmem(rows, width),
        *[full(rows, width) for _ in range(3)],
        full(rows, 128),
        vmem(shards, 2, 2, 2, cut, feed),
        vmem(shards, 2, 2, cut, feed),
        vmem(shards, 2, cut, feed),
        vmem(shards + 1, 2, cut, feed),
        vmem(shards, 2, 2, cut, attn),
        vmem(shards, 2, cut, attn),
        vmem(shards + 1, 2, cut, attn),
        vmem(2, cut, feed),
        vmem(2, cut, attn),
        full(2, cut, attn),
        full(2, cut, feed),
        full(stages, 8, width),
        full(stages, 8, width),
        pltpu.VMEM((1, rows), jnp.int32),
        pltpu.VMEM((1, size["L"]), jnp.int32),
        *[full(1, width) for _ in range(3)],
        dma((mats,)),
        dma((2, 2)),
        dma((5,)),
        dma((5,)),
        dma((2, shards + 1)),
        dma((mats, shards)),
        dma((4,)),
        dma((mats, shards)),
        dma((2,)),
        dma((2, shards)),
        dma((12,)),
        dma((12,)),
        dma((2,)),
        dma((2, shards, 2)),
        dma((2,)),
        dma((shards, 6)),
        dma((2,)),
        dma((shards + 1, 6)),
        dma((3,)),
        dma((3,)),
        dma((stages,)),
        dma((stages,)),
        dma((2,)),
    ]
    far = pl.BlockSpec(memory_space=pl.ANY)
    outs = [
        jax.ShapeDtypeStruct((rows, width), BF16),
        jax.ShapeDtypeStruct((rows, width), BF16),
        jax.ShapeDtypeStruct((8, width), F32),
        jax.ShapeDtypeStruct((2, cut, attn), F32),
        jax.ShapeDtypeStruct((2, cut, feed), F32),
    ]
    return pl.pallas_call(
        functools.partial(block_kernel, size),
        out_shape=outs,
        in_specs=[far] * len(operands),
        out_specs=[pl.BlockSpec(memory_space=pltpu.HBM)] * len(outs),
        scratch_shapes=scratch,
        compiler_params=pltpu.CompilerParams(
            collective_id=0, has_side_effects=True, vmem_limit_bytes=64 * 2**20 - 65536
        ),
    )(*operands)


def place_kernel(size, assemble, routed, small, tokens, cotangent, *refs):
    length, width, rows = size["L"], size["D"], size["R"]
    gathered, refs = refs[: 4 if assemble else 2], refs[4 if assemble else 2 :]
    outs, refs = refs[: 12 if assemble else 2], refs[12 if assemble else 2 :]
    bases, staged, refs = refs[:2], refs[2 : 2 + len(gathered)], refs[2 + len(gathered) :]
    finals, (pick, keep, in_sem, out_sem, part_sem, final_sem) = refs[:-6], refs[-6:]
    block = 512
    steps = width // block

    def moving(src, dst, sem, k, b):
        at = (slice(None), pl.ds(b * block, block))
        return pltpu.make_async_copy(src[k].at[at], dst[k].at[at], sem.at[k, b])

    sources = (tokens, cotangent)
    parts = [pltpu.make_async_copy(src, dst, part_sem.at[k]) for k, (src, dst) in enumerate(zip(gathered, staged))]
    for copy in parts[:2]:
        copy.start()
    for b in range(steps):
        for k in range(2):
            moving(sources, bases, in_sem, k, b).start()
    for copy in parts[2:]:
        copy.start()
    line = lax.broadcasted_iota(jnp.int32, (length, rows), 0)
    chosen = jnp.where(line == routed[...], 1.0, 0.0)
    pick[...] = chosen.astype(BF16)
    keep[...] = jnp.broadcast_to((1.0 - jnp.sum(chosen, axis=1, keepdims=True)).astype(BF16), keep.shape)
    for copy in parts[:2]:
        copy.wait()
    for b in range(steps):
        for k in range(2):
            at = slice(b * block, (b + 1) * block)
            moving(sources, bases, in_sem, k, b).wait()
            kept = jnp.concatenate([keep[...]] * (block // 128), axis=1)
            bases[k][:, at] = mm(pick[...], staged[k][:, at]).astype(BF16) + bases[k][:, at] * kept
            moving(bases, outs, out_sem, k, b).start()
    last = []
    if assemble:
        for copy in parts[2:]:
            copy.wait()
        for k, value in enumerate(weight_outputs(size, *staged[2:])):
            finals[k][...] = value
            last.append(pltpu.make_async_copy(finals[k], outs[2 + k], final_sem.at[k]))
            last[-1].start()
        for k in range(3):
            outs[8 + k][...] = small[k : k + 1, :]
        outs[11][...] = small[3:4, 0:1]
    for b in range(steps):
        for k in range(2):
            moving(bases, outs, out_sem, k, b).wait()
    for copy in last:
        copy.wait()


def weight_outputs(size, attn, feed):
    narrow, hidden = size["n"], size["f"]

    def side_by_side(ref, lo, count):
        return jnp.concatenate([ref[0, :, lo : lo + count], ref[1, :, lo : lo + count]], axis=1)

    return (
        side_by_side(attn, 0, narrow),
        side_by_side(attn, narrow, narrow),
        side_by_side(attn, 2 * narrow, narrow),
        side_by_side(attn, 3 * narrow, narrow).T,
        side_by_side(feed, 0, hidden),
        side_by_side(feed, hidden, hidden).T,
    )


def place_rows(size, routed, tokens, cotangent, rows_res, rows_grad, small, attn, feed, assemble):
    length, width, rows = size["L"], size["D"], size["R"]
    cut, narrow, hidden = size["DB"], size["n"], size["f"]
    whole = lambda *shape: pl.BlockSpec(shape, lambda i: (0,) * len(shape))
    far = pl.BlockSpec(memory_space=pltpu.HBM)
    outs, out_specs = [jax.ShapeDtypeStruct((length, width), BF16)] * 2, [far] * 2
    gathered, finals = [rows_res, rows_grad], []
    if assemble:
        gathered += [attn, feed]
        finals = [(cut, 2 * narrow)] * 3 + [(2 * narrow, cut), (cut, 2 * hidden), (2 * hidden, cut)]
        tiny = [(1, width)] * 3 + [(1, 1)]
        outs = outs + [jax.ShapeDtypeStruct(shape, F32) for shape in finals + tiny]
        out_specs = out_specs + [far] * len(finals) + [whole(*shape) for shape in tiny]
    dma = pltpu.SemaphoreType.DMA
    return pl.pallas_call(
        functools.partial(place_kernel, size, assemble),
        grid=(1,),
        out_shape=outs,
        in_specs=[whole(1, rows), whole(*small.shape)] + [far] * (2 + len(gathered)),
        out_specs=out_specs,
        scratch_shapes=[
            *[pltpu.VMEM((length, width), BF16) for _ in range(2)],
            *[pltpu.VMEM(part.shape, part.dtype) for part in gathered],
            *[pltpu.VMEM(shape, F32) for shape in finals],
            pltpu.VMEM((length, rows), BF16),
            pltpu.VMEM((length, 128), BF16),
            dma((2, width // 512)),
            dma((2, width // 512)),
            dma((4,)),
            dma((6,)),
        ],
        compiler_params=pltpu.CompilerParams(vmem_limit_bytes=60 * 2**20),
    )(routed, small, tokens, cotangent, *gathered)


def shards_of(
    groups,
    tokens,
    cotangent,
    routed,
    valid_mask,
    w_router,
    first_gain,
    query_weight,
    key_weight,
    value_weight,
    output_weight,
    second_gain,
    up_weight,
    down_weight,
):
    shards, data = lax.axis_size("mp"), lax.axis_size("dp")
    _, length, width = tokens.shape
    rows = routed.shape[1]
    narrow = query_weight.shape[1] // 2
    hidden = up_weight.shape[1] // 2
    cut = width // 8
    chips_x = 1 << ((data // 2).bit_length() - 1) // 2
    size = dict(
        S=shards, ybit=2 * chips_x, R=rows, D=width, L=length, hh=narrow // HEAD_DIM,
        n=narrow, f=hidden, DB=cut, joined=narrow % 128 != 0,
    )
    dp = lax.axis_index("dp")
    x, y = (dp // 2) % 2, (dp // size["ybit"]) % 2
    qkv = (query_weight, key_weight, value_weight)
    if size["joined"]:
        halves = [lax.dynamic_slice_in_dim(weight, x * narrow, narrow, 1) for weight in qkv]
        qkv = (jnp.concatenate(halves, axis=1),)
    row = lambda vector: vector.reshape(1, width)
    operands = (
        tokens.reshape(-1, rows, width), cotangent.reshape(-1, rows, width), routed, valid_mask, row(w_router), row(first_gain), row(second_gain),
        *qkv, output_weight, up_weight.reshape(2, 2, 2, cut, 2 * hidden), down_weight,
    )
    rows_res, rows_grad, small, attn, feed = run_block(size, operands)
    whole_group = data == 8
    rms = small[3, 0:1]
    if not whole_group:
        block = 4 * y + 2 * x + dp % 2

        def over_groups(part):
            base = jnp.zeros((2, width, part.shape[2]), F32)
            placed = lax.dynamic_update_slice_in_dim(base, part, block * cut, 1)
            return lax.psum_scatter(placed, "dp", scatter_dimension=1, tiled=True)

        attn, feed = over_groups(attn), over_groups(feed)
        small = lax.psum(small, "dp") / 8.0
    placed = place_rows(size, routed, tokens[0], cotangent[0], rows_res, rows_grad, small, attn, feed, whole_group)
    residual, grad_tokens = placed[:2]
    if whole_group:
        vectors = [vector.reshape(width) for vector in placed[8:11]]
        weights, rms = placed[2:8], placed[11].reshape(1)
    else:
        vectors, weights = [small[k] for k in range(3)], weight_outputs(size, attn, feed)
    grad_query, grad_key, grad_value, grad_output, grad_up, grad_down = weights
    return (
        residual[None],
        grad_tokens[None],
        rms,
        vectors[0],
        vectors[1],
        grad_query,
        grad_key,
        grad_value,
        grad_output,
        vectors[2],
        grad_up,
        grad_down,
    )


def solution(mesh):
    in_specs = (
        P(("dp", "mp"), None, None),
        P(("dp", "mp"), None, None),
        P(("dp", "mp"), None),
        P(("dp", "mp"), None),
        P(),
        P(),
        P(None, "mp"),
        P(None, "mp"),
        P(None, "mp"),
        P("mp", None),
        P(),
        P(None, "mp"),
        P("mp", None),
    )
    out_specs = (
        P(("dp", "mp"), None, None),
        P(("dp", "mp"), None, None),
        P(("dp", "mp")),
        P(),
        P(),
        P("dp", "mp"),
        P("dp", "mp"),
        P("dp", "mp"),
        P("mp", "dp"),
        P(),
        P("dp", "mp"),
        P("mp", "dp"),
    )
    body = functools.partial(shards_of, mesh.shape["dp"] // 8)
    return jax.shard_map(body, mesh=mesh, in_specs=in_specs, out_specs=out_specs, check_vma=False)
```

```python
import functools
import math

import jax
import jax.numpy as jnp
from jax import lax
from jax.experimental import pallas as pl
from jax.experimental.pallas import tpu as pltpu
from jax.sharding import PartitionSpec as P

HEADS = 16
HEAD_DIM = 64
EPS = 1e-06
F32 = jnp.float32
BF16 = jnp.bfloat16
TILE = 64


def mm(left, right):
    return jnp.dot(left, right, preferred_element_type=F32)


def mm_nt(left, right):
    return lax.dot_general(left, right, (((1,), (1,)), ((), ())), preferred_element_type=F32)


def mm_tn(left, right):
    return lax.dot_general(left, right, (((0,), (0,)), ((), ())), preferred_element_type=F32)


def row_tiles(rows, body, init=0, first=0):
    def step(index, carry):
        return body(pl.ds(pl.multiple_of(first + index * TILE, TILE), TILE), carry)

    return lax.fori_loop(0, rows // TILE, step, init)


def fold_rows(value):
    return jnp.sum(value.reshape(-1, 8, value.shape[-1]), axis=0)


def gelu_both(value):
    cdf = 0.5 * (1.0 + lax.erf(value * math.sqrt(0.5)))
    density = jnp.exp(-0.5 * value * value) * (1.0 / math.sqrt(2.0 * math.pi))
    return value * cdf, cdf + value * density


def block_kernel(size, *refs):
    shards, ybit, rows, width, length = size["S"], size["ybit"], size["R"], size["D"], size["L"]
    heads, narrow, hidden, cut = size["hh"], size["n"], size["f"], size["DB"]
    joined = size["joined"]
    quarter = 2 * cut
    refs = list(refs)

    def take(count):
        taken, refs[:count] = refs[:count], []
        return taken

    tokens, cotangent = take(2)
    small_in = take(5)
    qkv_in = take(1 if joined else 3)
    out_in, up_in, down_in = take(3)
    outputs = take(5)
    w_qkv, w_out, w_up, w_down = take(4)
    h1, dfeed, h2, datt, turn_a, turn_b = take(6)
    qkv, ctx, prob, act, dup = take(5)
    total, wide, sent, got = take(4)
    own_z, own_c, attended, dmixed, feed_own, columns = take(6)
    lane = lax.broadcasted_iota(jnp.int32, (1, 128), 1)

    def column(k, at):
        return columns[at][:, k : k + 1]

    def set_column(k, at, value):
        columns[at] = jnp.where(lane == k, value, columns[at])

    gate, live, dscore = (functools.partial(column, k) for k in range(3))
    grads, core_f, y_f, z_f, core_a, y_a, z_a, swap_f, swap_a = take(9)
    attn_out, feed_out = take(2)
    small_send, small_got = take(2)
    routed, valid, w_router, first_gain, second_gain = small_held = take(5)
    load_sem, tok_sem, out_sem, small_sem = take(4)
    wz_s, wz_r, wy_s, wy_r, wc_s, wc_r = take(6)
    x_s, x_r = take(2)
    gc_s, gc_r, gy_s, gy_r, gz_s, gz_r, gx_s, gx_r = take(8)
    sm_s, sm_r = take(2)
    ex_sem = take(1)[0]

    dp = lax.axis_index("dp")
    z = lax.axis_index("mp")
    core = lax.rem(dp, 2)
    x = lax.rem(lax.div(dp, 2), 2)
    y = lax.rem(lax.div(dp, ybit), 2)
    core_dev = (dp + 1 - 2 * core, z)
    x_dev = (dp + 2 * (1 - 2 * x), z)
    y_dev = (dp + ybit * (1 - 2 * y), z)
    up_dev = (dp, z + 1)
    down_dev = (dp, z - 1)
    small_devices = [core_dev, x_dev, (dp + 2 * (1 - 2 * x) + ybit * (1 - 2 * y), z)]

    def remote(src, dst, send, recv, device):
        return pltpu.make_async_remote_copy(
            src_ref=src,
            dst_ref=dst,
            send_sem=send,
            recv_sem=recv,
            device_id=device,
            device_id_type=pl.DeviceIdType.MESH,
        )

    def order(j):
        high = lax.div(z, shards // 2)
        base = z + high * (shards - 1 - 2 * z)
        odd = lax.rem(j, 2)
        near = base + lax.div(j + 1, 2) * (2 * odd - 1)
        pick = jnp.where(j <= 2 * base, near, j)
        return pick + high * (shards - 1 - 2 * pick)

    attn_mats = list(range(len(qkv_in) + 1))
    up_mats = [len(attn_mats), len(attn_mats) + 1]
    down_mats = [len(attn_mats) + 2, len(attn_mats) + 3]
    feed_mats = up_mats + down_mats
    out_at, up_at, down_at = attn_mats[-1], up_mats[0], down_mats[0]

    def down_rows(i, start=0):
        return pl.ds(pl.multiple_of(start + (i - down_at) * (hidden // 2), hidden // 2), hidden // 2)

    def span(qy, qc):
        return pl.ds(pl.multiple_of((2 * qy + qc) * quarter, quarter), quarter)

    def lanes(count):
        return pl.ds(pl.multiple_of(x * count, count), count)

    def held(i, s, qy, qc):
        if i < out_at:
            part = w_qkv if joined else w_qkv.at[:, :, i * narrow : (i + 1) * narrow]
            return part.at[s, span(qy, qc)]
        if i == out_at:
            return w_out.at[s, :, span(qy, qc)]
        if i < down_at:
            return w_up.at[s, qy, qc, i - up_at]
        return w_down.at[s, down_rows(i), span(qy, qc)]

    def own_piece(i):
        if i < out_at:
            part = qkv_in[i].at[span(y, core)]
            return part if joined else part.at[:, lanes(narrow)]
        if i == out_at:
            return out_in.at[lanes(narrow), span(y, core)]
        if i < down_at:
            return up_in.at[y, core, i - up_at, :, lanes(hidden)]
        return down_in.at[down_rows(i, x * hidden), span(y, core)]

    def load_own(i):
        if i < out_at:
            if joined:
                src, dst = qkv_in[i], w_qkv.at[z]
            else:
                src, dst = qkv_in[i].at[:, lanes(narrow)], w_qkv.at[z, :, i * narrow : (i + 1) * narrow]
        elif i == out_at:
            src, dst = out_in.at[lanes(narrow), :], w_out.at[z]
        elif i < down_at:
            b = i - up_at
            src, dst = up_in.at[:, :, b, :, lanes(hidden)], w_up.at[z, :, :, b]
        else:
            src, dst = down_in.at[down_rows(i, x * hidden), :], w_down.at[z, down_rows(i)]
        return pltpu.make_async_copy(src, dst, load_sem.at[i])

    def group_of(i):
        return 0 if i <= out_at else 1

    def y_group(i):
        return 0 if i <= out_at else 1 if i < down_at else 2 + i - down_at

    def own_up(i):
        return remote(own_piece(i), held(i, z, y, core), wz_s.at[group_of(i), z], wz_r.at[i, z], up_dev)

    def own_down(i):
        return remote(own_piece(i), held(i, z, y, core), wz_s.at[group_of(i), shards], wz_r.at[i, z], down_dev)

    def pass_on(i, s, device):
        piece = held(i, s, y, core)
        return remote(piece, piece, wz_s.at[group_of(i), s], wz_r.at[i, s], device)

    def across_y(i, s, qy):
        piece = held(i, s, qy, core)
        return remote(piece, piece, wy_s.at[y_group(i)], wy_r.at[i, s], y_dev)

    def across_core(i, s, qy, qc):
        piece = held(i, s, qy, qc)
        group = group_of(i)
        return remote(piece, piece, wc_s.at[group], wc_r.at[group, s], core_dev)

    def await_pieces(group, sem, count, receiving=False):
        mats = attn_mats if group == 0 else feed_mats
        if joined:
            refs = [held(i, 0, 0, 0) for i in mats] * count
        else:
            flat = w_up.at[0, 0, 0] if group == 0 else w_up.at[0, 0]
            if count == 2:
                flat = w_up.at[0, 0] if group == 0 else w_up.at[0]
            elif count == shards - 1:
                flat = w_up.at[0 : shards - 1, 0, 0] if group == 0 else w_up.at[0 : shards - 1, 0]
            elif count == 2 * (shards - 1):
                flat = w_up.at[0 : shards - 1, 0] if group == 0 else w_up.at[0 : shards - 1]
            refs = [flat]
        for ref in refs:
            if receiving:
                remote(ref, ref, wc_s.at[group], sem, core_dev).wait_recv()
            else:
                remote(ref, ref, sem, wc_r.at[group, 0], core_dev).wait_send()

    def send_own_up(mats):
        for i in mats:
            own_up(i).start()

    def send_own_down(mats):
        for i in mats:
            own_down(i).start()

    def passing(s, action):
        @pl.when((s < z) & (z < shards - 1))
        def _():
            action(up_dev)

        @pl.when((s > z) & (z > 0))
        def _():
            action(down_dev)

    edge = (z == 0) | (z == shards - 1)
    inner = jnp.logical_not(edge)

    def by_z_here(i, j):
        return quick and i == by_z and isinstance(j, int) and j == 1

    def arrive_one(i, j):
        s = order(j)
        pass_on(i, s, up_dev).wait_recv()
        passing(s, lambda device: pass_on(i, s, device).start())
        if by_z_here(i, j):

            @pl.when(inner)
            def _():
                across_y(i, s, y).start()

        else:
            across_y(i, s, y).start()
        across_core(i, s, y, core).start()

    def arrive(mats, j):
        for i in mats:
            arrive_one(i, j)

    def follow(j):
        s = order(j)

        @pl.when((s == 0) & (z < shards - 1))
        def _():
            send_own_up(feed_mats)

        @pl.when((s == shards - 1) & (z > 0))
        def _():
            send_own_down(feed_mats)

    def relay(mats, j):
        s = order(j)
        for i in mats:
            if by_z_here(i, j):

                @pl.when(edge)
                def _():
                    bypass(s, up_dev).wait_recv()

                @pl.when(inner)
                def _():
                    across_y(i, s, 1 - y).wait_recv()

            else:
                across_y(i, s, 1 - y).wait_recv()
            across_core(i, s, 1 - y, core).start()

    def settle(group, j):
        await_pieces(group, wc_r.at[group, order(j)], 2, True)

    def await_y(index, blocks, count):
        flat = w_up.at[0:count, 0, 0] if blocks == 2 else w_up.at[0:count, 0, 0, 0]
        remote(flat, flat, wy_s.at[index], wy_r.at[0, 0], y_dev).wait_send()

    quick = shards == 4
    by_z = down_mats[-1]

    def bypass(s, device):
        src = down_in.at[down_rows(by_z, x * hidden), span(1 - y, core)]
        return remote(src, held(by_z, s, 1 - y, core), ex_sem.at[0], ex_sem.at[1], device)

    def drain(group):
        @pl.when(z < shards - 1)
        def _():
            await_pieces(group, wz_s.at[group, z], 1)

        @pl.when(z > 0)
        def _():
            await_pieces(group, wz_s.at[group, shards], 1)

        def step(j, carry):
            s = order(j)
            passing(s, lambda device: await_pieces(group, wz_s.at[group, s], 1))
            return carry

        lax.fori_loop(1, shards, step, 0)
        if group == 0:
            await_pieces(0, wy_s.at[0], shards - 1)
        else:
            await_y(1, 2, shards - 1)
            await_y(2, 1, shards - 1)
            if not quick:
                await_y(3, 1, shards - 1)
            else:

                @pl.when(edge)
                def _():
                    await_y(3, 1, shards - 2)

                @pl.when(inner)
                def _():
                    await_y(3, 1, shards - 1)
                    bypass(z, up_dev).wait_send()

        await_pieces(group, wc_s.at[group], 2 * (shards - 1))

    def exchange(slot, src, dst):
        return remote(src, dst, x_s.at[slot], x_r.at[slot], x_dev)

    x_h1 = exchange(0, h1.at[0], h1.at[1])
    x_dfeed = exchange(1, dfeed.at[0], dfeed.at[1])
    upper, lower = slice(0, rows // 2), slice(rows // 2, rows)
    x_att = [exchange(2 + 6 * k, sent.at[0, part], got.at[0, part]) for k, part in enumerate((upper, lower))]
    x_h2 = [exchange(3 + 6 * k, h2.at[0, part], h2.at[1, part]) for k, part in enumerate((upper, lower))]
    x_dh2 = [exchange(4 + 6 * k, sent.at[0, part], got.at[0, part]) for k, part in enumerate((upper, lower))]
    x_feed = exchange(5, sent.at[1], got.at[1])
    x_datt = [exchange(6 + 5 * k, datt.at[0, part], datt.at[1, part]) for k, part in enumerate((upper, lower))]
    x_dh1 = exchange(7, sent.at[0], got.at[0])

    def put(k, src):
        return pltpu.make_async_copy(src, outputs[k], out_sem.at[k])

    steps = length // (2 * rows)
    stages = ((got, sent), (h2, datt))

    def block_loads(t):
        copies = []
        for k, (array, buf) in enumerate(zip((tokens, cotangent), stages[t % 2])):
            copies.append(pltpu.make_async_copy(array.at[2 * t : 2 * t + 2], buf, tok_sem.at[t % 2, k]))
        return copies

    barrier = pltpu.get_barrier_semaphore()

    def greet(device):
        pl.semaphore_signal(barrier, inc=1, device_id=device, device_id_type=pl.DeviceIdType.MESH)

    for device in (core_dev, x_dev, y_dev):
        greet(device)

    @pl.when(z > 0)
    def _():
        greet(down_dev)

    @pl.when(z < shards - 1)
    def _():
        greet(up_dev)

    small_loads = [pltpu.make_async_copy(src, dst, small_sem.at[k]) for k, (src, dst) in enumerate(zip(small_in, small_held))]
    for copy in small_loads:
        copy.start()
    for t in range(2):
        for copy in block_loads(t):
            copy.start()
    for i in attn_mats + feed_mats:
        load_own(i).start()

    def begin():
        ends = jnp.where(z == 0, 1, 0) + jnp.where(z == shards - 1, 1, 0)
        pl.semaphore_wait(barrier, 5 - ends)

        @pl.when(z < shards - 1)
        def _():
            send_own_up(attn_mats)

        @pl.when(z > 0)
        def _():
            send_own_down(attn_mats)

        @pl.when(z == 0)
        def _():
            send_own_up(feed_mats)

        @pl.when(z == shards - 1)
        def _():
            send_own_down(feed_mats)

    begin()

    for copy in small_loads:
        copy.wait()
    as_rows = jnp.broadcast_to(routed[...].astype(F32), (8, rows))
    position = jnp.transpose(as_rows)[:, 0:1].astype(jnp.int32)
    flags = jnp.zeros((rows, 1), F32)
    for t in range(steps):
        for copy in block_loads(t):
            copy.wait()
        hit = position == 2 * t * rows + lax.broadcasted_iota(jnp.int32, (rows, 2 * rows), 1)
        chosen = jnp.where(hit, 1.0, 0.0)
        pick = chosen.astype(BF16)
        for k, buf in enumerate(stages[t % 2]):
            picked = mm(pick, buf[...].reshape(2 * rows, width))
            total[k] = picked if t == 0 else total[k] + picked
        if t + 2 < steps:
            for copy in block_loads(t + 2):
                copy.start()
        mask = valid[:, 2 * t * rows : 2 * (t + 1) * rows].astype(F32)
        flags = flags + jnp.sum(chosen * mask, axis=1, keepdims=True)
    columns[...] = jnp.broadcast_to(flags, columns.shape)

    def prepare(at, carry):
        row, cot = total[0, at], total[1, at]
        own_z[at] = row.astype(BF16)
        own_c[at] = cot.astype(BF16)
        gate_here = jnp.sum(row * w_router[...], axis=1, keepdims=True) * live(at)
        set_column(0, at, gate_here)
        factor = lax.rsqrt(jnp.mean(row * row, axis=1, keepdims=True) + EPS)
        h1[0, at] = (row * factor * first_gain[...]).astype(BF16)
        dfeed[0, at] = (gate_here * cot).astype(BF16)
        return carry

    row_tiles(rows, prepare)
    x_h1.start()
    x_dfeed.start()

    lane_head = lax.div(lax.broadcasted_iota(jnp.int32, (1, narrow), 1), HEAD_DIM)
    masks = [jnp.where(lane_head == h, 1.0, 0.0) for h in range(heads)]
    masks_low = [mask.astype(BF16) for mask in masks]

    def stacked(value):
        return jnp.concatenate([value * mask for mask in masks_low], axis=0) if heads > 1 else value

    def unstacked(value):
        if heads == 1:
            return value
        picked = value[0:rows] * masks[0]
        for h in range(1, heads):
            picked = picked + value[h * rows : (h + 1) * rows] * masks[h]
        return picked

    score_shape = (heads * rows, rows)
    causal = lax.rem(lax.broadcasted_iota(jnp.int32, score_shape, 0), rows) >= lax.broadcasted_iota(
        jnp.int32, score_shape, 1
    )

    for i in attn_mats:
        load_own(i).wait()

    @pl.when(edge)
    def _():
        for j in range(1, shards):
            arrive(attn_mats, j)
            follow(j)
            if j > 1:
                relay(attn_mats, j - 1)

    @pl.when(inner)
    def _():
        for i in attn_mats:
            for j in (1, 2):
                arrive_one(i, j)
        for j in (1, 2):
            follow(j)
        for j in range(3, shards):
            arrive(attn_mats, j)
            follow(j)
        for j in range(1, shards - 1):
            relay(attn_mats, j)

    x_h1.wait_recv()

    def attend(j, carry):
        s = order(j)

        @pl.when(j + 1 == shards)
        def _():
            relay(attn_mats, j)
            arrive(up_mats, 1)

        @pl.when(j > 0)
        def _():
            settle(0, j)

        low = mm(h1[...].reshape(2 * rows, width), w_qkv[s]).astype(BF16)
        query = low[:, 0:narrow] * jnp.asarray(HEAD_DIM**-0.5, BF16)
        qkv[s] = jnp.concatenate([query, low[:, narrow:]], axis=1).reshape(2, rows, 3 * narrow)
        for half in range(2):
            query = qkv[s, half, :, 0:narrow]
            key = qkv[s, half, :, narrow : 2 * narrow]
            value = qkv[s, half, :, 2 * narrow : 3 * narrow]
            scores = jnp.where(causal, mm_nt(stacked(query), key), -1e30)
            raised = jnp.exp(scores - jnp.max(scores, axis=1, keepdims=True))
            weights = (raised / jnp.sum(raised, axis=1, keepdims=True)).astype(BF16)
            prob[s, half] = weights
            ctx[s, half * rows : (half + 1) * rows] = unstacked(mm(weights, value)).astype(BF16)
        return carry

    lax.fori_loop(0, shards, attend, 0)

    def project_out(half):
        parts = [ctx[s, half * rows : (half + 1) * rows] for s in range(shards)]
        return mm(jnp.concatenate(parts, axis=1), w_out[...].reshape(shards * narrow, width))

    sent[0] = project_out(1).astype(BF16)
    for copy in x_att:
        copy.start()
    attended[...] = project_out(0)
    arrive(down_mats, 1)
    arrive(up_mats, 2)

    @pl.when(inner)
    def _():
        arrive(down_mats, 2)
        for j in range(3, shards):
            arrive(feed_mats, j)
        if quick:

            @pl.when(z == 1)
            def _():
                bypass(z, down_dev).start()

            @pl.when(z == shards - 2)
            def _():
                bypass(z, up_dev).start()

    def mix(at, carry):
        att = attended[at] + got[0, at].astype(F32)
        attended[at] = att
        mixed = own_z[at].astype(F32) + att
        factor = lax.rsqrt(jnp.mean(mixed * mixed, axis=1, keepdims=True) + EPS)
        h2[0, at] = (mixed * factor * second_gain[...]).astype(BF16)
        return carry

    for k in range(2):
        x_att[k].wait()
        row_tiles(rows // 2, mix, first=k * (rows // 2))
        x_h2[k].start()

        @pl.when(edge)
        def _():
            arrive(down_mats[k : k + 1], 2)


    x_dfeed.wait_recv()

    parts_of = (1 - y, y)

    def core_send(group, buf, into, s, a):
        src = buf.at[s, a, :, 1 - core]
        return remote(src, into.at[s, a], gc_s.at[group], gc_r.at[group, s, a], core_dev)

    halves = (1 - x, x)

    def columns_of(group, c):
        return slice(c * 2 * narrow, (c + 1) * 2 * narrow) if group == 1 else slice(0, 2 * hidden)

    def pieces(group):
        return range(2) if group == 1 else range(1)

    def sem_at(group, b, c):
        return 2 + 2 * b + c if group == 1 else b

    def y_send(group, buf, into, s, b, c):
        cols = columns_of(group, c)
        src = buf.at[s, 1 - y, b, core, :, cols]
        recv = gy_r.at[s, sem_at(group, b, c)]
        return remote(src, into.at[s, b, :, cols], gy_s.at[group], recv, y_dev)

    def z_send(group, buf, into, s, device, slot, b, c):
        cols = columns_of(group, c)
        src = buf.at[s, y, b, core, :, cols]
        recv = gz_r.at[slot, sem_at(group, b, c)]
        return remote(src, into.at[slot, b, :, cols], gz_s.at[group], recv, device)

    def add_into(ref, other):
        ref[...] = (ref[...].astype(F32) + other[...].astype(F32)).astype(BF16)

    def stage_core(group, buf, core_got, y_got, s):
        core_send(group, buf, core_got, s, 1 - y).wait_recv()
        for b in halves:
            add_into(buf.at[s, 1 - y, b, core], core_got.at[s, 1 - y, b])
            for c in pieces(group):
                y_send(group, buf, y_got, s, b, c).start()
        core_send(group, buf, core_got, s, y).wait_recv()
        for b in range(2):
            add_into(buf.at[s, y, b, core], core_got.at[s, y, b])

    def stage_y(group, buf, y_got, s, b, c):
        y_send(group, buf, y_got, s, b, c).wait_recv()
        cols = columns_of(group, c)
        add_into(buf.at[s, y, b, core, :, cols], y_got.at[s, b, :, cols])

    def line_in(group, buf, z_got, s, slot, b, c):
        z_send(group, buf, z_got, s, up_dev, slot, b, c).wait_recv()
        cols = columns_of(group, c)
        add_into(buf.at[s, y, b, core, :, cols], z_got.at[slot, b, :, cols])

    def stage_z(group, buf, z_got, s, b, c):
        @pl.when(s > z)
        def _():
            @pl.when(z > 0)
            def _():
                line_in(group, buf, z_got, s, s, b, c)

            z_send(group, buf, z_got, s, up_dev, s, b, c).start()

        @pl.when(s < z)
        def _():
            @pl.when(z < shards - 1)
            def _():
                line_in(group, buf, z_got, s, s, b, c)

            slot = jnp.where(s == z - 1, shards, s)
            z_send(group, buf, z_got, s, down_dev, slot, b, c).start()

    def swap(group, pair, c):
        cols = columns_of(group, c)
        index = 1 + c if group == 1 else 0
        return remote(pair.at[0, :, cols], pair.at[1, :, cols], gx_s.at[index], gx_r.at[index], x_dev)

    def stage_last(group, buf, y_got, z_got, pair, out):
        for b in halves:
            for c in pieces(group):
                cols = columns_of(group, c)
                stage_y(group, buf, y_got, z, b, c)
                out[b, :, cols] = buf[z, y, b, core, :, cols].astype(F32)

                @pl.when(z > 0)
                def _():
                    z_send(group, buf, z_got, z, up_dev, z, b, c).wait_recv()
                    out[b, :, cols] += z_got[z, b, :, cols].astype(F32)

                @pl.when(z < shards - 1)
                def _():
                    z_send(group, buf, z_got, z, up_dev, shards, b, c).wait_recv()
                    out[b, :, cols] += z_got[shards, b, :, cols].astype(F32)

                if b is halves[0]:
                    pair[0, :, cols] = out[b, :, cols].astype(BF16)
                    swap(group, pair, c).start()

    def stage_out(group, pair, out):
        for c in pieces(group):
            swap(group, pair, c).wait_recv()
        out[1 - x] = pair[1].astype(F32)

    def reversed_order(k):
        return order(shards - 1 - k)

    def store_grads(buf, s, a, left, right, lo, count):
        part = pl.ds(pl.multiple_of(2 * a * quarter, 2 * quarter), 2 * quarter)
        value = mm(left[part, :], right).astype(BF16)
        buf[s, a, :, :, :, lo : lo + count] = value.reshape(2, 2, cut, count)

    def line_half(group, buf, y_got, z_got, s, m):
        b = jnp.where(lax.rem(m, 2) == 0, 1 - x, x)
        for c in pieces(group):
            stage_y(group, buf, y_got, s, b, c)
            stage_z(group, buf, z_got, s, b, c)

    def feed_half(m):
        line_half(0, grads, y_f, z_f, order(leaving(lax.div(m, 2))), m)

    def attn_half(m):
        line_half(1, w_up, y_a, z_a, reversed_order(lax.div(m, 2)), m)

    def run_halves(step, first, last):
        def body(m, carry):
            step(m)
            return carry

        lax.fori_loop(first, last, body, 0)

    total_halves = 2 * (shards - 1)

    def leaving(k):
        if not quick:
            return shards - 1 - k
        ends, middle = jnp.where(edge, 2, 1), jnp.where(edge, 1, 2)
        return jnp.where(k == 0, ends, jnp.where(k == 1, 3, jnp.where(k == 2, middle, 0)))

    def feed_point(ends, middle):
        if quick and ends is not None:

            @pl.when(edge)
            def _():
                run_halves(feed_half, *ends)

        if quick and middle is not None:

            @pl.when(inner)
            def _():
                run_halves(feed_half, *middle)

    total[...] = jnp.zeros_like(total)
    turn_a[:, 0:rows] = jnp.transpose(h2[0])
    turn_b[...] = jnp.transpose(dfeed[...].reshape(2 * rows, width))
    for i in feed_mats:
        load_own(i).wait()

    def feed_grads(s):
        for a in parts_of:
            store_grads(grads, s, a, turn_a, dup[s], 0, hidden)
            store_grads(grads, s, a, turn_b, act[s], hidden, hidden)
            core_send(0, grads, core_f, s, a).start()

    def feed_core(s):
        stage_core(0, grads, core_f, y_f, s)

    def feed_chunk(s, half):
        part = pl.ds(pl.multiple_of(half * rows, rows), rows)
        up_here = w_up[s].reshape(width, hidden)
        wide[0] = mm(h2[half], up_here)
        wide[1] = mm_nt(dfeed[half], w_down[s])

        def turn(at, inside):
            active, slope = gelu_both(wide[0, at])
            out = pl.ds(pl.multiple_of(half * rows + at.start, TILE), TILE)
            act[s, out] = active.astype(BF16)
            dup[s, out] = (wide[1, at] * slope).astype(BF16)
            return inside

        row_tiles(rows, turn)
        total[half] += mm_nt(dup[s, part], up_here)

    def own_step(i, carry):
        j = jnp.where(edge, 2 * i, i) if quick else i
        active = inner | (i < 2) if quick else i >= 0

        @pl.when(active & (i > 0))
        def _():
            settle(1, j)

        @pl.when(active)
        def _():
            feed_chunk(order(j), 0)

        if quick:

            @pl.when(edge & (i == 0))
            def _():
                relay(feed_mats[:-1], 1)
                arrive(up_mats, 3)
                relay(feed_mats, 2)

            @pl.when(edge & (i == 1))
            def _():
                arrive(down_mats, 3)
                relay(up_mats, 3)

            @pl.when(inner & (i == 0))
            def _():
                relay(feed_mats, 1)

            @pl.when(inner & (i == 1))
            def _():
                relay(feed_mats, 2)

        else:

            @pl.when(edge & (j > 1) & (j + 1 < shards))
            def _():
                arrive(down_mats, j + 1)

            @pl.when(j + 2 < shards)
            def _():
                relay(feed_mats, j + 1)

            @pl.when(edge & (j + 3 < shards))
            def _():
                arrive(up_mats, j + 3)

        return carry

    lax.fori_loop(0, shards - 1, own_step, 0)
    for copy in x_h2:
        copy.wait_recv()
    turn_a[:, rows : 2 * rows] = jnp.transpose(h2[1])

    def other_step(k, carry):
        j, active = k, k >= 0
        if quick:
            j = jnp.where(edge, 2 - 2 * k, jnp.where(k < 2, 1 - k, 2))
            active = inner | (k < 2)

        @pl.when(active)
        def _():
            feed_chunk(order(j), 1)

        if quick:

            @pl.when(k == 0)
            def _():
                feed_grads(order(leaving(0)))
                feed_core(order(leaving(0)))

        return carry

    lax.fori_loop(0, shards - 1, other_step, 0)

    def last_step(k, carry):
        j, half, final = shards - 1, 1 - k, 0
        if quick:
            j = jnp.where(edge & (lax.rem(k, 2) == 1), 1, shards - 1)
            half = jnp.where(edge, jnp.where(k < 2, 1, 0), 1 - k)
            final = jnp.where(edge, 1, 0)

            @pl.when(inner & (k == 0))
            def _():
                relay(up_mats, shards - 1)

        @pl.when(k == 0)
        def _():
            relay(down_mats if quick else feed_mats, shards - 1)

        if quick:

            @pl.when(edge & (k == 0))
            def _():
                relay([by_z], 1)

        @pl.when(k <= final)
        def _():
            settle(1, j)

        feed_chunk(order(j), half)

        @pl.when(k == final)
        def _():
            sent[0] = total[1].astype(BF16)
            for copy in x_dh2:
                copy.start()

        if quick:

            @pl.when(edge & (k == 2))
            def _():
                feed_grads(order(leaving(1)))

            @pl.when(edge & (k == 3))
            def _():
                feed_core(order(leaving(1)))

        return carry

    lax.fori_loop(0, jnp.where(edge, 4, 2) if quick else 2, last_step, 0)
    first_left = jnp.where(edge, 2, 1) if quick else 0

    def feed_grads_step(k, carry):
        if quick:

            @pl.when((k == 2) & edge)
            def _():
                feed_half(0)

        feed_grads(order(leaving(k)))

        @pl.when(k > first_left)
        def _():
            feed_core(order(leaving(k - 1)))

        return carry

    lax.fori_loop(first_left, shards, feed_grads_step, 0)
    feed_point((1, 2), None)
    feed_core(z)

    def feed_rows(half):
        value = mm(act[0, half * rows : (half + 1) * rows], w_down[0])
        for s in range(1, shards):
            value += mm(act[s, half * rows : (half + 1) * rows], w_down[s])
        return value

    def second_back(at, carry):
        dh2 = total[0, at] + got[0, at].astype(F32)
        mixed = own_z[at].astype(F32) + attended[at]
        factor = lax.rsqrt(jnp.mean(mixed * mixed, axis=1, keepdims=True) + EPS)
        scaled = dh2 * second_gain[...]
        back = factor * scaled - mixed * (factor**3 * jnp.mean(mixed * scaled, axis=1, keepdims=True))
        dmixed[at] = back
        datt[0, at] = (gate(at) * own_c[at].astype(F32) + back).astype(BF16)
        return carry + fold_rows(dh2 * mixed * factor)

    second_sum = jnp.zeros((8, width), F32)
    for k in range(2):
        x_dh2[k].wait()
        second_sum = row_tiles(rows // 2, second_back, second_sum, first=k * (rows // 2))
        x_datt[k].start()
    sent[1] = feed_rows(1).astype(BF16)
    x_feed.start()
    feed_point((2, 3), (0, 1))
    feed_own[...] = feed_rows(0)

    def attend_back(half):
        part = slice(half * rows, (half + 1) * rows)

        def step(k, carry):
            s = reversed_order(k)
            dctx = mm_nt(datt[half], w_out[s]).astype(BF16)
            query = qkv[s, half, :, 0:narrow]
            key = qkv[s, half, :, narrow : 2 * narrow]
            value = qkv[s, half, :, 2 * narrow : 3 * narrow]
            weights = prob[s, half]
            dhead = stacked(dctx)
            dweights = mm_nt(dhead, value)
            full = weights.astype(F32)
            dscores = full * (dweights - jnp.sum(dweights * full, axis=1, keepdims=True))
            dscores = dscores.astype(BF16)
            dquery = unstacked(mm(dscores, key)) * HEAD_DIM**-0.5
            dkey = mm_tn(dscores, stacked(query))
            dvalue = mm_tn(weights, dhead)
            act[s, part, 0 : 3 * narrow] = jnp.concatenate([dquery, dkey, dvalue], axis=1).astype(BF16)
            return carry

        lax.fori_loop(0, shards, step, 0)

    def dh1_rows(half):
        part = slice(half * rows, (half + 1) * rows)
        value = mm_nt(act[0, part, 0 : 3 * narrow], w_qkv[0])
        for s in range(1, shards):
            value += mm_nt(act[s, part, 0 : 3 * narrow], w_qkv[s])
        return value

    attend_back(0)
    feed_point((3, 4), (1, 2))
    total[0] = dh1_rows(0)
    turn_a[...] = jnp.transpose(h1[...].reshape(2 * rows, width))
    drain(1)
    feed_point(None, (2, 3))
    for copy in x_datt:
        copy.wait_recv()
    turn_b[...] = jnp.transpose(datt[...].reshape(2 * rows, width))

    feed_point((4, 5), None)
    attend_back(1)
    sent[0] = dh1_rows(1).astype(BF16)
    x_dh1.start()
    feed_point((5, 6), (3, 5))

    def attn_grads(k, carry):
        s = reversed_order(k)
        for a in parts_of:
            store_grads(w_up, s, a, turn_a, act[s, :, 0 : 3 * narrow], 0, 3 * narrow)
            store_grads(w_up, s, a, turn_b, ctx[s], 3 * narrow, narrow)
            core_send(1, w_up, core_a, s, a).start()

        @pl.when(k > 0)
        def _():
            stage_core(1, w_up, core_a, y_a, reversed_order(k - 1))

        return carry

    lax.fori_loop(0, shards, attn_grads, 0)
    stage_core(1, w_up, core_a, y_a, z)

    x_feed.wait()

    def finish_forward(at, squares):
        branch = attended[at] + feed_own[at] + got[1, at].astype(F32)
        update = gate(at) * branch
        sent[1, at] = (own_z[at].astype(F32) + update).astype(BF16)
        dgate = jnp.sum(own_c[at].astype(F32) * branch, axis=1, keepdims=True)
        set_column(2, at, dgate * live(at))
        return squares + fold_rows(update * update)

    squares = row_tiles(rows, finish_forward, jnp.zeros((8, width), F32))
    put(0, sent.at[1]).start()
    count = jnp.sum(valid[...].astype(F32), axis=1, keepdims=True)
    energy = jnp.sum(jnp.sum(squares, axis=0, keepdims=True), axis=1, keepdims=True)
    rms = jnp.sqrt(energy / (width * jnp.maximum(count, 1.0)))

    if quick:
        feed_point(None, (5, 6))
    else:
        run_halves(feed_half, 0, total_halves)
    ahead = jnp.where(edge, 2, 1)
    run_halves(attn_half, 0, ahead)
    x_dh1.wait()

    def first_back(at, sums):
        dh1 = total[0, at] + got[0, at].astype(F32)
        row = own_z[at].astype(F32)
        factor = lax.rsqrt(jnp.mean(row * row, axis=1, keepdims=True) + EPS)
        scaled = dh1 * first_gain[...]
        back = factor * scaled - row * (factor**3 * jnp.mean(row * scaled, axis=1, keepdims=True))
        back = back + dmixed[at] + dscore(at) * w_router[...]
        got[1, at] = (own_c[at].astype(F32) + back).astype(BF16)
        return sums[0] + fold_rows(dscore(at) * row), sums[1] + fold_rows(dh1 * row * factor)

    zero = jnp.zeros((8, width), F32)
    router_sum, first_sum = row_tiles(rows, first_back, (zero, zero))
    put(1, got.at[1]).start()
    parts = [jnp.sum(part, axis=0, keepdims=True) for part in (router_sum, first_sum, second_sum)]
    small = jnp.concatenate(parts + [jnp.zeros((5, width), F32)], axis=0)

    def small_copy(k):
        return remote(small_send.at[k], small_got.at[k], sm_s.at[k], sm_r.at[k], small_devices[k])

    hops = len(small_devices)
    for k in range(hops):
        small_send[k] = small
        small_copy(k).start()
        if k > 0:
            attn_half(ahead + k)
        small_copy(k).wait()
        small = small + small_got[k]
        if k == 0:
            attn_half(ahead)
    stage_last(0, grads, y_f, z_f, swap_f, feed_out)

    def small_spread(far, source):
        slot = hops + source
        return remote(
            small_send.at[hops], small_got.at[slot], sm_s.at[hops + far - 1], sm_r.at[slot], (dp, lax.rem(z + far, shards))
        )

    small_send[hops] = small
    small_got[hops + z] = small
    for far in range(1, shards):
        small_spread(far, z).start()

    run_halves(attn_half, ahead + hops, total_halves)
    stage_last(1, w_up, y_a, z_a, swap_a, attn_out)
    for far in range(1, shards):
        small_spread(far, lax.rem(z + shards - far, shards)).wait_recv()
        small_spread(far, z).wait_send()
    small = small_got[hops]
    for k in range(1, shards):
        small = small + small_got[hops + k]
    row_at = lax.broadcasted_iota(jnp.int32, (8, 1), 0)
    small_send[0] = jnp.where(row_at == 3, rms, small)
    put(2, small_send.at[0]).start()
    stage_out(0, swap_f, feed_out)
    put(4, feed_out).start()
    stage_out(1, swap_a, attn_out)
    put(3, attn_out).start()

    drain(0)
    for copy in (x_h1, x_dfeed, *x_h2, *x_datt):
        copy.wait_send()

    for group, core_got, y_got, z_got in ((0, core_f, y_f, z_f), (1, core_a, y_a, z_a)):
        remote(core_got, core_got, gc_s.at[group], gc_r.at[group, 0, 0], core_dev).wait_send()
        remote(y_got, y_got, gy_s.at[group], gy_r.at[0, 0], y_dev).wait_send()
        moved = z_got.at[0 : shards - 1]
        remote(moved, moved, gz_s.at[group], gz_r.at[0, 0], up_dev).wait_send()

    swap(0, swap_f, 0).wait_send()
    for c in pieces(1):
        swap(1, swap_a, c).wait_send()
    for k, src in enumerate((sent.at[1], got.at[1], small_send.at[0], attn_out, feed_out)):
        put(k, src).wait()


def run_block(size, operands):
    shards, rows, width = size["S"], size["R"], size["D"]
    heads, narrow, hidden, cut = size["hh"], size["n"], size["f"], size["DB"]
    mats = (2 if size["joined"] else 4) + 4
    stages = 3 + shards
    attn, feed = 4 * narrow, 2 * hidden
    dma = pltpu.SemaphoreType.DMA
    vmem = lambda *shape: pltpu.VMEM(shape, BF16)
    full = lambda *shape: pltpu.VMEM(shape, F32)
    scratch = [
        vmem(shards, width, 3 * narrow),
        vmem(shards, narrow, width),
        vmem(shards, 2, 2, 2, cut, hidden),
        vmem(shards, hidden, width),
        *[vmem(2, rows, width) for _ in range(4)],
        *[vmem(width, 2 * rows) for _ in range(2)],
        vmem(shards, 2, rows, 3 * narrow),
        vmem(shards, 2 * rows, narrow),
        vmem(shards, 2, heads * rows, rows),
        vmem(shards, 2 * rows, hidden),
        vmem(shards, 2 * rows, hidden),
        full(2, rows, width),
        full(2, rows, hidden),
        vmem(2, rows, width),
        vmem(2, rows, width),
        vmem(rows, width),
        vmem(rows, width),
        *[full(rows, width) for _ in range(3)],
        full(rows, 128),
        vmem(shards, 2, 2, 2, cut, feed),
        vmem(shards, 2, 2, cut, feed),
        vmem(shards, 2, cut, feed),
        vmem(shards + 1, 2, cut, feed),
        vmem(shards, 2, 2, cut, attn),
        vmem(shards, 2, cut, attn),
        vmem(shards + 1, 2, cut, attn),
        vmem(2, cut, feed),
        vmem(2, cut, attn),
        full(2, cut, attn),
        full(2, cut, feed),
        full(stages, 8, width),
        full(stages, 8, width),
        pltpu.VMEM((1, rows), jnp.int32),
        pltpu.VMEM((1, size["L"]), jnp.int32),
        *[full(1, width) for _ in range(3)],
        dma((mats,)),
        dma((2, 2)),
        dma((5,)),
        dma((5,)),
        dma((2, shards + 1)),
        dma((mats, shards)),
        dma((4,)),
        dma((mats, shards)),
        dma((2,)),
        dma((2, shards)),
        dma((12,)),
        dma((12,)),
        dma((2,)),
        dma((2, shards, 2)),
        dma((2,)),
        dma((shards, 6)),
        dma((2,)),
        dma((shards + 1, 6)),
        dma((3,)),
        dma((3,)),
        dma((stages,)),
        dma((stages,)),
        dma((2,)),
    ]
    far = pl.BlockSpec(memory_space=pl.ANY)
    outs = [
        jax.ShapeDtypeStruct((rows, width), BF16),
        jax.ShapeDtypeStruct((rows, width), BF16),
        jax.ShapeDtypeStruct((8, width), F32),
        jax.ShapeDtypeStruct((2, cut, attn), F32),
        jax.ShapeDtypeStruct((2, cut, feed), F32),
    ]
    return pl.pallas_call(
        functools.partial(block_kernel, size),
        out_shape=outs,
        in_specs=[far] * len(operands),
        out_specs=[pl.BlockSpec(memory_space=pltpu.HBM)] * len(outs),
        scratch_shapes=scratch,
        compiler_params=pltpu.CompilerParams(
            collective_id=0, has_side_effects=True, vmem_limit_bytes=64 * 2**20 - 65536
        ),
    )(*operands)


def place_kernel(size, assemble, routed, small, tokens, cotangent, *refs):
    length, width, rows = size["L"], size["D"], size["R"]
    gathered, refs = refs[: 4 if assemble else 2], refs[4 if assemble else 2 :]
    outs, refs = refs[: 12 if assemble else 2], refs[12 if assemble else 2 :]
    bases, staged, refs = refs[:2], refs[2 : 2 + len(gathered)], refs[2 + len(gathered) :]
    finals, (pick, keep, in_sem, out_sem, part_sem, final_sem) = refs[:-6], refs[-6:]
    block = 512
    steps = width // block

    def moving(src, dst, sem, k, b):
        at = (slice(None), pl.ds(b * block, block))
        return pltpu.make_async_copy(src[k].at[at], dst[k].at[at], sem.at[k, b])

    sources = (tokens, cotangent)
    parts = [pltpu.make_async_copy(src, dst, part_sem.at[k]) for k, (src, dst) in enumerate(zip(gathered, staged))]
    for copy in parts[:2]:
        copy.start()
    for b in range(steps):
        for k in range(2):
            moving(sources, bases, in_sem, k, b).start()
    for copy in parts[2:]:
        copy.start()
    line = lax.broadcasted_iota(jnp.int32, (length, rows), 0)
    chosen = jnp.where(line == routed[...], 1.0, 0.0)
    pick[...] = chosen.astype(BF16)
    keep[...] = jnp.broadcast_to((1.0 - jnp.sum(chosen, axis=1, keepdims=True)).astype(BF16), keep.shape)
    for copy in parts[:2]:
        copy.wait()
    for b in range(steps):
        for k in range(2):
            at = slice(b * block, (b + 1) * block)
            moving(sources, bases, in_sem, k, b).wait()
            kept = jnp.concatenate([keep[...]] * (block // 128), axis=1)
            bases[k][:, at] = mm(pick[...], staged[k][:, at]).astype(BF16) + bases[k][:, at] * kept
            moving(bases, outs, out_sem, k, b).start()
    last = []
    if assemble:
        for copy in parts[2:]:
            copy.wait()
        for k, value in enumerate(weight_outputs(size, *staged[2:])):
            finals[k][...] = value
            last.append(pltpu.make_async_copy(finals[k], outs[2 + k], final_sem.at[k]))
            last[-1].start()
        for k in range(3):
            outs[8 + k][...] = small[k : k + 1, :]
        outs[11][...] = small[3:4, 0:1]
    for b in range(steps):
        for k in range(2):
            moving(bases, outs, out_sem, k, b).wait()
    for copy in last:
        copy.wait()


def weight_outputs(size, attn, feed):
    narrow, hidden = size["n"], size["f"]

    def side_by_side(ref, lo, count):
        return jnp.concatenate([ref[0, :, lo : lo + count], ref[1, :, lo : lo + count]], axis=1)

    return (
        side_by_side(attn, 0, narrow),
        side_by_side(attn, narrow, narrow),
        side_by_side(attn, 2 * narrow, narrow),
        side_by_side(attn, 3 * narrow, narrow).T,
        side_by_side(feed, 0, hidden),
        side_by_side(feed, hidden, hidden).T,
    )


def place_rows(size, routed, tokens, cotangent, rows_res, rows_grad, small, attn, feed, assemble):
    length, width, rows = size["L"], size["D"], size["R"]
    cut, narrow, hidden = size["DB"], size["n"], size["f"]
    whole = lambda *shape: pl.BlockSpec(shape, lambda i: (0,) * len(shape))
    far = pl.BlockSpec(memory_space=pltpu.HBM)
    outs, out_specs = [jax.ShapeDtypeStruct((length, width), BF16)] * 2, [far] * 2
    gathered, finals = [rows_res, rows_grad], []
    if assemble:
        gathered += [attn, feed]
        finals = [(cut, 2 * narrow)] * 3 + [(2 * narrow, cut), (cut, 2 * hidden), (2 * hidden, cut)]
        tiny = [(1, width)] * 3 + [(1, 1)]
        outs = outs + [jax.ShapeDtypeStruct(shape, F32) for shape in finals + tiny]
        out_specs = out_specs + [far] * len(finals) + [whole(*shape) for shape in tiny]
    dma = pltpu.SemaphoreType.DMA
    return pl.pallas_call(
        functools.partial(place_kernel, size, assemble),
        grid=(1,),
        out_shape=outs,
        in_specs=[whole(1, rows), whole(*small.shape)] + [far] * (2 + len(gathered)),
        out_specs=out_specs,
        scratch_shapes=[
            *[pltpu.VMEM((length, width), BF16) for _ in range(2)],
            *[pltpu.VMEM(part.shape, part.dtype) for part in gathered],
            *[pltpu.VMEM(shape, F32) for shape in finals],
            pltpu.VMEM((length, rows), BF16),
            pltpu.VMEM((length, 128), BF16),
            dma((2, width // 512)),
            dma((2, width // 512)),
            dma((4,)),
            dma((6,)),
        ],
        compiler_params=pltpu.CompilerParams(vmem_limit_bytes=60 * 2**20),
    )(routed, small, tokens, cotangent, *gathered)


def shards_of(
    groups,
    tokens,
    cotangent,
    routed,
    valid_mask,
    w_router,
    first_gain,
    query_weight,
    key_weight,
    value_weight,
    output_weight,
    second_gain,
    up_weight,
    down_weight,
):
    shards, data = lax.axis_size("mp"), lax.axis_size("dp")
    _, length, width = tokens.shape
    rows = routed.shape[1]
    narrow = query_weight.shape[1] // 2
    hidden = up_weight.shape[1] // 2
    cut = width // 8
    chips_x = 1 << ((data // 2).bit_length() - 1) // 2
    size = dict(
        S=shards, ybit=2 * chips_x, R=rows, D=width, L=length, hh=narrow // HEAD_DIM,
        n=narrow, f=hidden, DB=cut, joined=narrow % 128 != 0,
    )
    dp = lax.axis_index("dp")
    x, y = (dp // 2) % 2, (dp // size["ybit"]) % 2
    qkv = (query_weight, key_weight, value_weight)
    if size["joined"]:
        halves = [lax.dynamic_slice_in_dim(weight, x * narrow, narrow, 1) for weight in qkv]
        qkv = (jnp.concatenate(halves, axis=1),)
    row = lambda vector: vector.reshape(1, width)
    operands = (
        tokens.reshape(-1, rows, width), cotangent.reshape(-1, rows, width), routed, valid_mask, row(w_router), row(first_gain), row(second_gain),
        *qkv, output_weight, up_weight.reshape(2, 2, 2, cut, 2 * hidden), down_weight,
    )
    rows_res, rows_grad, small, attn, feed = run_block(size, operands)
    whole_group = data == 8
    rms = small[3, 0:1]
    if not whole_group:
        block = 4 * y + 2 * x + dp % 2

        def over_groups(part):
            base = jnp.zeros((2, width, part.shape[2]), F32)
            placed = lax.dynamic_update_slice_in_dim(base, part, block * cut, 1)
            return lax.psum_scatter(placed, "dp", scatter_dimension=1, tiled=True)

        attn, feed = over_groups(attn), over_groups(feed)
        small = lax.psum(small, "dp") / 8.0
    placed = place_rows(size, routed, tokens[0], cotangent[0], rows_res, rows_grad, small, attn, feed, whole_group)
    residual, grad_tokens = placed[:2]
    if whole_group:
        vectors = [vector.reshape(width) for vector in placed[8:11]]
        weights, rms = placed[2:8], placed[11].reshape(1)
    else:
        vectors, weights = [small[k] for k in range(3)], weight_outputs(size, attn, feed)
    grad_query, grad_key, grad_value, grad_output, grad_up, grad_down = weights
    return (
        residual[None],
        grad_tokens[None],
        rms,
        vectors[0],
        vectors[1],
        grad_query,
        grad_key,
        grad_value,
        grad_output,
        vectors[2],
        grad_up,
        grad_down,
    )


def solution(mesh):
    in_specs = (
        P(("dp", "mp"), None, None),
        P(("dp", "mp"), None, None),
        P(("dp", "mp"), None),
        P(("dp", "mp"), None),
        P(),
        P(),
        P(None, "mp"),
        P(None, "mp"),
        P(None, "mp"),
        P("mp", None),
        P(),
        P(None, "mp"),
        P("mp", None),
    )
    out_specs = (
        P(("dp", "mp"), None, None),
        P(("dp", "mp"), None, None),
        P(("dp", "mp")),
        P(),
        P(),
        P("dp", "mp"),
        P("dp", "mp"),
        P("dp", "mp"),
        P("mp", "dp"),
        P(),
        P("dp", "mp"),
        P("mp", "dp"),
    )
    body = functools.partial(shards_of, mesh.shape["dp"] // 8)
    return jax.shard_map(body, mesh=mesh, in_specs=in_specs, out_specs=out_specs, check_vma=False)
```

```python
import functools
import math

import jax
import jax.numpy as jnp
from jax import lax
from jax.experimental import pallas as pl
from jax.experimental.pallas import tpu as pltpu
from jax.sharding import PartitionSpec as P

HEADS = 16
HEAD_DIM = 64
EPS = 1e-06
F32 = jnp.float32
BF16 = jnp.bfloat16
TILE = 64


def mm(left, right):
    return jnp.dot(left, right, preferred_element_type=F32)


def mm_nt(left, right):
    return lax.dot_general(left, right, (((1,), (1,)), ((), ())), preferred_element_type=F32)


def mm_tn(left, right):
    return lax.dot_general(left, right, (((0,), (0,)), ((), ())), preferred_element_type=F32)


def row_tiles(rows, body, init=0, first=0):
    def step(index, carry):
        return body(pl.ds(pl.multiple_of(first + index * TILE, TILE), TILE), carry)

    return lax.fori_loop(0, rows // TILE, step, init)


def fold_rows(value):
    return jnp.sum(value.reshape(-1, 8, value.shape[-1]), axis=0)


def gelu_both(value):
    cdf = 0.5 * (1.0 + lax.erf(value * math.sqrt(0.5)))
    density = jnp.exp(-0.5 * value * value) * (1.0 / math.sqrt(2.0 * math.pi))
    return value * cdf, cdf + value * density


def block_kernel(size, *refs):
    shards, ybit, rows, width, length = size["S"], size["ybit"], size["R"], size["D"], size["L"]
    heads, narrow, hidden, cut = size["hh"], size["n"], size["f"], size["DB"]
    joined = size["joined"]
    quarter = 2 * cut
    refs = list(refs)

    def take(count):
        taken, refs[:count] = refs[:count], []
        return taken

    tokens, cotangent = take(2)
    small_in = take(5)
    qkv_in = take(1 if joined else 3)
    out_in, up_in, down_in = take(3)
    outputs = take(5)
    w_qkv, w_out, w_up, w_down = take(4)
    h1, dfeed, h2, datt, turn_a, turn_b = take(6)
    qkv, ctx, prob, act, dup = take(5)
    total, wide, sent, got = take(4)
    own_z, own_c, attended, dmixed, feed_own, columns = take(6)
    lane = lax.broadcasted_iota(jnp.int32, (1, 128), 1)

    def column(k, at):
        return columns[at][:, k : k + 1]

    def set_column(k, at, value):
        columns[at] = jnp.where(lane == k, value, columns[at])

    gate, live, dscore = (functools.partial(column, k) for k in range(3))
    grads, core_f, y_f, z_f, core_a, y_a, z_a, swap_f, swap_a = take(9)
    attn_out, feed_out = take(2)
    small_send, small_got = take(2)
    routed, valid, w_router, first_gain, second_gain = small_held = take(5)
    load_sem, tok_sem, out_sem, small_sem = take(4)
    wz_s, wz_r, wy_s, wy_r, wc_s, wc_r = take(6)
    x_s, x_r = take(2)
    gc_s, gc_r, gy_s, gy_r, gz_s, gz_r, gx_s, gx_r = take(8)
    sm_s, sm_r = take(2)
    ex_sem = take(1)[0]

    dp = lax.axis_index("dp")
    z = lax.axis_index("mp")
    core = lax.rem(dp, 2)
    x = lax.rem(lax.div(dp, 2), 2)
    y = lax.rem(lax.div(dp, ybit), 2)
    core_dev = (dp + 1 - 2 * core, z)
    x_dev = (dp + 2 * (1 - 2 * x), z)
    y_dev = (dp + ybit * (1 - 2 * y), z)
    up_dev = (dp, z + 1)
    down_dev = (dp, z - 1)
    small_devices = [core_dev, x_dev, (dp + 2 * (1 - 2 * x) + ybit * (1 - 2 * y), z)]

    def remote(src, dst, send, recv, device):
        return pltpu.make_async_remote_copy(
            src_ref=src,
            dst_ref=dst,
            send_sem=send,
            recv_sem=recv,
            device_id=device,
            device_id_type=pl.DeviceIdType.MESH,
        )

    def order(j):
        high = lax.div(z, shards // 2)
        base = z + high * (shards - 1 - 2 * z)
        odd = lax.rem(j, 2)
        near = base + lax.div(j + 1, 2) * (2 * odd - 1)
        pick = jnp.where(j <= 2 * base, near, j)
        return pick + high * (shards - 1 - 2 * pick)

    attn_mats = list(range(len(qkv_in) + 1))
    up_mats = [len(attn_mats), len(attn_mats) + 1]
    down_mats = [len(attn_mats) + 2, len(attn_mats) + 3]
    feed_mats = up_mats + down_mats
    out_at, up_at, down_at = attn_mats[-1], up_mats[0], down_mats[0]

    def down_rows(i, start=0):
        return pl.ds(pl.multiple_of(start + (i - down_at) * (hidden // 2), hidden // 2), hidden // 2)

    def span(qy, qc):
        return pl.ds(pl.multiple_of((2 * qy + qc) * quarter, quarter), quarter)

    def lanes(count):
        return pl.ds(pl.multiple_of(x * count, count), count)

    def held(i, s, qy, qc):
        if i < out_at:
            part = w_qkv if joined else w_qkv.at[:, :, i * narrow : (i + 1) * narrow]
            return part.at[s, span(qy, qc)]
        if i == out_at:
            return w_out.at[s, :, span(qy, qc)]
        if i < down_at:
            return w_up.at[s, qy, qc, i - up_at]
        return w_down.at[s, down_rows(i), span(qy, qc)]

    def own_piece(i):
        if i < out_at:
            part = qkv_in[i].at[span(y, core)]
            return part if joined else part.at[:, lanes(narrow)]
        if i == out_at:
            return out_in.at[lanes(narrow), span(y, core)]
        if i < down_at:
            return up_in.at[y, core, i - up_at, :, lanes(hidden)]
        return down_in.at[down_rows(i, x * hidden), span(y, core)]

    def load_own(i):
        if i < out_at:
            if joined:
                src, dst = qkv_in[i], w_qkv.at[z]
            else:
                src, dst = qkv_in[i].at[:, lanes(narrow)], w_qkv.at[z, :, i * narrow : (i + 1) * narrow]
        elif i == out_at:
            src, dst = out_in.at[lanes(narrow), :], w_out.at[z]
        elif i < down_at:
            b = i - up_at
            src, dst = up_in.at[:, :, b, :, lanes(hidden)], w_up.at[z, :, :, b]
        else:
            src, dst = down_in.at[down_rows(i, x * hidden), :], w_down.at[z, down_rows(i)]
        return pltpu.make_async_copy(src, dst, load_sem.at[i])

    def group_of(i):
        return 0 if i <= out_at else 1

    def y_group(i):
        return 0 if i <= out_at else 1 if i < down_at else 2 + i - down_at

    def own_up(i):
        return remote(own_piece(i), held(i, z, y, core), wz_s.at[group_of(i), z], wz_r.at[i, z], up_dev)

    def own_down(i):
        return remote(own_piece(i), held(i, z, y, core), wz_s.at[group_of(i), shards], wz_r.at[i, z], down_dev)

    def pass_on(i, s, device):
        piece = held(i, s, y, core)
        return remote(piece, piece, wz_s.at[group_of(i), s], wz_r.at[i, s], device)

    def across_y(i, s, qy):
        piece = held(i, s, qy, core)
        return remote(piece, piece, wy_s.at[y_group(i)], wy_r.at[i, s], y_dev)

    def across_core(i, s, qy, qc):
        piece = held(i, s, qy, qc)
        group = group_of(i)
        return remote(piece, piece, wc_s.at[group], wc_r.at[group, s], core_dev)

    def await_pieces(group, sem, count, receiving=False):
        mats = attn_mats if group == 0 else feed_mats
        if joined:
            refs = [held(i, 0, 0, 0) for i in mats] * count
        else:
            flat = w_up.at[0, 0, 0] if group == 0 else w_up.at[0, 0]
            if count == 2:
                flat = w_up.at[0, 0] if group == 0 else w_up.at[0]
            elif count == shards - 1:
                flat = w_up.at[0 : shards - 1, 0, 0] if group == 0 else w_up.at[0 : shards - 1, 0]
            elif count == 2 * (shards - 1):
                flat = w_up.at[0 : shards - 1, 0] if group == 0 else w_up.at[0 : shards - 1]
            refs = [flat]
        for ref in refs:
            if receiving:
                remote(ref, ref, wc_s.at[group], sem, core_dev).wait_recv()
            else:
                remote(ref, ref, sem, wc_r.at[group, 0], core_dev).wait_send()

    def send_own_up(mats):
        for i in mats:
            own_up(i).start()

    def send_own_down(mats):
        for i in mats:
            own_down(i).start()

    def passing(s, action):
        @pl.when((s < z) & (z < shards - 1))
        def _():
            action(up_dev)

        @pl.when((s > z) & (z > 0))
        def _():
            action(down_dev)

    edge = (z == 0) | (z == shards - 1)
    inner = jnp.logical_not(edge)

    def by_z_here(i, j):
        return quick and i == by_z and isinstance(j, int) and j == 1

    def arrive_one(i, j):
        s = order(j)
        pass_on(i, s, up_dev).wait_recv()
        passing(s, lambda device: pass_on(i, s, device).start())
        if by_z_here(i, j):

            @pl.when(inner)
            def _():
                across_y(i, s, y).start()

        else:
            across_y(i, s, y).start()
        across_core(i, s, y, core).start()

    def arrive(mats, j):
        for i in mats:
            arrive_one(i, j)

    def follow(j):
        s = order(j)

        @pl.when((s == 0) & (z < shards - 1))
        def _():
            send_own_up(feed_mats)

        @pl.when((s == shards - 1) & (z > 0))
        def _():
            send_own_down(feed_mats)

    def relay(mats, j):
        s = order(j)
        for i in mats:
            if by_z_here(i, j):

                @pl.when(edge)
                def _():
                    bypass(s, up_dev).wait_recv()

                @pl.when(inner)
                def _():
                    across_y(i, s, 1 - y).wait_recv()

            else:
                across_y(i, s, 1 - y).wait_recv()
            across_core(i, s, 1 - y, core).start()

    def settle(group, j):
        await_pieces(group, wc_r.at[group, order(j)], 2, True)

    def await_y(index, blocks, count):
        flat = w_up.at[0:count, 0, 0] if blocks == 2 else w_up.at[0:count, 0, 0, 0]
        remote(flat, flat, wy_s.at[index], wy_r.at[0, 0], y_dev).wait_send()

    quick = shards == 4
    by_z = down_mats[-1]

    def bypass(s, device):
        src = down_in.at[down_rows(by_z, x * hidden), span(1 - y, core)]
        return remote(src, held(by_z, s, 1 - y, core), ex_sem.at[0], ex_sem.at[1], device)

    def drain(group):
        @pl.when(z < shards - 1)
        def _():
            await_pieces(group, wz_s.at[group, z], 1)

        @pl.when(z > 0)
        def _():
            await_pieces(group, wz_s.at[group, shards], 1)

        def step(j, carry):
            s = order(j)
            passing(s, lambda device: await_pieces(group, wz_s.at[group, s], 1))
            return carry

        lax.fori_loop(1, shards, step, 0)
        if group == 0:
            await_pieces(0, wy_s.at[0], shards - 1)
        else:
            await_y(1, 2, shards - 1)
            await_y(2, 1, shards - 1)
            if not quick:
                await_y(3, 1, shards - 1)
            else:

                @pl.when(edge)
                def _():
                    await_y(3, 1, shards - 2)

                @pl.when(inner)
                def _():
                    await_y(3, 1, shards - 1)
                    bypass(z, up_dev).wait_send()

        await_pieces(group, wc_s.at[group], 2 * (shards - 1))

    def exchange(slot, src, dst):
        return remote(src, dst, x_s.at[slot], x_r.at[slot], x_dev)

    x_h1 = exchange(0, h1.at[0], h1.at[1])
    x_dfeed = exchange(1, dfeed.at[0], dfeed.at[1])
    upper, lower = slice(0, rows // 2), slice(rows // 2, rows)
    x_att = [exchange(2 + 6 * k, sent.at[0, part], got.at[0, part]) for k, part in enumerate((upper, lower))]
    x_h2 = [exchange(3 + 6 * k, h2.at[0, part], h2.at[1, part]) for k, part in enumerate((upper, lower))]
    x_dh2 = [exchange(4 + 6 * k, sent.at[0, part], got.at[0, part]) for k, part in enumerate((upper, lower))]
    x_feed = exchange(5, sent.at[1], got.at[1])
    x_datt = [exchange(6 + 5 * k, datt.at[0, part], datt.at[1, part]) for k, part in enumerate((upper, lower))]
    x_dh1 = exchange(7, sent.at[0], got.at[0])

    def put(k, src):
        return pltpu.make_async_copy(src, outputs[k], out_sem.at[k])

    steps = length // (2 * rows)
    stages = ((got, sent), (h2, datt))

    def block_loads(t):
        copies = []
        for k, (array, buf) in enumerate(zip((tokens, cotangent), stages[t % 2])):
            copies.append(pltpu.make_async_copy(array.at[2 * t : 2 * t + 2], buf, tok_sem.at[t % 2, k]))
        return copies

    barrier = pltpu.get_barrier_semaphore()

    def greet(device):
        pl.semaphore_signal(barrier, inc=1, device_id=device, device_id_type=pl.DeviceIdType.MESH)

    for device in (core_dev, x_dev, y_dev):
        greet(device)

    @pl.when(z > 0)
    def _():
        greet(down_dev)

    @pl.when(z < shards - 1)
    def _():
        greet(up_dev)

    small_loads = [pltpu.make_async_copy(src, dst, small_sem.at[k]) for k, (src, dst) in enumerate(zip(small_in, small_held))]
    for copy in small_loads:
        copy.start()
    for t in range(2):
        for copy in block_loads(t):
            copy.start()
    for i in attn_mats + feed_mats:
        load_own(i).start()

    def begin():
        ends = jnp.where(z == 0, 1, 0) + jnp.where(z == shards - 1, 1, 0)
        pl.semaphore_wait(barrier, 5 - ends)

        @pl.when(z < shards - 1)
        def _():
            send_own_up(attn_mats)

        @pl.when(z > 0)
        def _():
            send_own_down(attn_mats)

        @pl.when(z == 0)
        def _():
            send_own_up(feed_mats)

        @pl.when(z == shards - 1)
        def _():
            send_own_down(feed_mats)

    begin()

    for copy in small_loads:
        copy.wait()
    as_rows = jnp.broadcast_to(routed[...].astype(F32), (8, rows))
    position = jnp.transpose(as_rows)[:, 0:1].astype(jnp.int32)
    flags = jnp.zeros((rows, 1), F32)
    for t in range(steps):
        for copy in block_loads(t):
            copy.wait()
        hit = position == 2 * t * rows + lax.broadcasted_iota(jnp.int32, (rows, 2 * rows), 1)
        chosen = jnp.where(hit, 1.0, 0.0)
        pick = chosen.astype(BF16)
        for k, buf in enumerate(stages[t % 2]):
            picked = mm(pick, buf[...].reshape(2 * rows, width))
            total[k] = picked if t == 0 else total[k] + picked
        if t + 2 < steps:
            for copy in block_loads(t + 2):
                copy.start()
        mask = valid[:, 2 * t * rows : 2 * (t + 1) * rows].astype(F32)
        flags = flags + jnp.sum(chosen * mask, axis=1, keepdims=True)
    columns[...] = jnp.broadcast_to(flags, columns.shape)

    def prepare(at, carry):
        row, cot = total[0, at], total[1, at]
        own_z[at] = row.astype(BF16)
        own_c[at] = cot.astype(BF16)
        gate_here = jnp.sum(row * w_router[...], axis=1, keepdims=True) * live(at)
        set_column(0, at, gate_here)
        factor = lax.rsqrt(jnp.mean(row * row, axis=1, keepdims=True) + EPS)
        h1[0, at] = (row * factor * first_gain[...]).astype(BF16)
        dfeed[0, at] = (gate_here * cot).astype(BF16)
        return carry

    row_tiles(rows, prepare)
    x_h1.start()
    x_dfeed.start()

    lane_head = lax.div(lax.broadcasted_iota(jnp.int32, (1, narrow), 1), HEAD_DIM)
    masks = [jnp.where(lane_head == h, 1.0, 0.0) for h in range(heads)]
    masks_low = [mask.astype(BF16) for mask in masks]

    def stacked(value):
        return jnp.concatenate([value * mask for mask in masks_low], axis=0) if heads > 1 else value

    def unstacked(value):
        if heads == 1:
            return value
        picked = value[0:rows] * masks[0]
        for h in range(1, heads):
            picked = picked + value[h * rows : (h + 1) * rows] * masks[h]
        return picked

    score_shape = (heads * rows, rows)
    causal = lax.rem(lax.broadcasted_iota(jnp.int32, score_shape, 0), rows) >= lax.broadcasted_iota(
        jnp.int32, score_shape, 1
    )

    for i in attn_mats:
        load_own(i).wait()

    @pl.when(edge)
    def _():
        for j in range(1, shards):
            arrive(attn_mats, j)
            follow(j)
            if j > 1:
                relay(attn_mats, j - 1)

    @pl.when(inner)
    def _():
        for i in attn_mats:
            for j in (1, 2):
                arrive_one(i, j)
        for j in (1, 2):
            follow(j)
        for j in range(3, shards):
            arrive(attn_mats, j)
            follow(j)
        for j in range(1, shards - 1):
            relay(attn_mats, j)

    x_h1.wait_recv()

    def attend(j, carry):
        s = order(j)

        @pl.when(j + 2 == shards)
        def _():
            arrive(up_mats[:1], 1)

        @pl.when(j + 1 == shards)
        def _():
            relay(attn_mats, j)
            arrive(up_mats[1:], 1)

        @pl.when(j > 0)
        def _():
            settle(0, j)

        low = mm(h1[...].reshape(2 * rows, width), w_qkv[s]).astype(BF16)
        query = low[:, 0:narrow] * jnp.asarray(HEAD_DIM**-0.5, BF16)
        qkv[s] = jnp.concatenate([query, low[:, narrow:]], axis=1).reshape(2, rows, 3 * narrow)
        for half in range(2):
            query = qkv[s, half, :, 0:narrow]
            key = qkv[s, half, :, narrow : 2 * narrow]
            value = qkv[s, half, :, 2 * narrow : 3 * narrow]
            scores = jnp.where(causal, mm_nt(stacked(query), key), -1e30)
            raised = jnp.exp(scores - jnp.max(scores, axis=1, keepdims=True))
            weights = (raised / jnp.sum(raised, axis=1, keepdims=True)).astype(BF16)
            prob[s, half] = weights
            ctx[s, half * rows : (half + 1) * rows] = unstacked(mm(weights, value)).astype(BF16)
        return carry

    lax.fori_loop(0, shards, attend, 0)

    def project_out(half):
        parts = [ctx[s, half * rows : (half + 1) * rows] for s in range(shards)]
        return mm(jnp.concatenate(parts, axis=1), w_out[...].reshape(shards * narrow, width))

    sent[0] = project_out(1).astype(BF16)
    for copy in x_att:
        copy.start()
    attended[...] = project_out(0)
    arrive(down_mats, 1)
    arrive(up_mats, 2)

    @pl.when(inner)
    def _():
        arrive(down_mats, 2)
        for j in range(3, shards):
            arrive(feed_mats, j)
        if quick:

            @pl.when(z == 1)
            def _():
                bypass(z, down_dev).start()

            @pl.when(z == shards - 2)
            def _():
                bypass(z, up_dev).start()

    def mix(at, carry):
        att = attended[at] + got[0, at].astype(F32)
        attended[at] = att
        mixed = own_z[at].astype(F32) + att
        factor = lax.rsqrt(jnp.mean(mixed * mixed, axis=1, keepdims=True) + EPS)
        h2[0, at] = (mixed * factor * second_gain[...]).astype(BF16)
        return carry

    for k in range(2):
        x_att[k].wait()
        row_tiles(rows // 2, mix, first=k * (rows // 2))
        x_h2[k].start()

        @pl.when(edge)
        def _():
            arrive(down_mats[k : k + 1], 2)


    x_dfeed.wait_recv()

    parts_of = (1 - y, y)

    def core_send(group, buf, into, s, a):
        src = buf.at[s, a, :, 1 - core]
        return remote(src, into.at[s, a], gc_s.at[group], gc_r.at[group, s, a], core_dev)

    halves = (1 - x, x)

    def columns_of(group, c):
        return slice(c * 2 * narrow, (c + 1) * 2 * narrow) if group == 1 else slice(0, 2 * hidden)

    def pieces(group):
        return range(2) if group == 1 else range(1)

    def sem_at(group, b, c):
        return 2 + 2 * b + c if group == 1 else b

    def y_send(group, buf, into, s, b, c):
        cols = columns_of(group, c)
        src = buf.at[s, 1 - y, b, core, :, cols]
        recv = gy_r.at[s, sem_at(group, b, c)]
        return remote(src, into.at[s, b, :, cols], gy_s.at[group], recv, y_dev)

    def z_send(group, buf, into, s, device, slot, b, c):
        cols = columns_of(group, c)
        src = buf.at[s, y, b, core, :, cols]
        recv = gz_r.at[slot, sem_at(group, b, c)]
        return remote(src, into.at[slot, b, :, cols], gz_s.at[group], recv, device)

    def add_into(ref, other):
        ref[...] = (ref[...].astype(F32) + other[...].astype(F32)).astype(BF16)

    def stage_core(group, buf, core_got, y_got, s):
        core_send(group, buf, core_got, s, 1 - y).wait_recv()
        for b in halves:
            add_into(buf.at[s, 1 - y, b, core], core_got.at[s, 1 - y, b])
            for c in pieces(group):
                y_send(group, buf, y_got, s, b, c).start()
        core_send(group, buf, core_got, s, y).wait_recv()
        for b in range(2):
            add_into(buf.at[s, y, b, core], core_got.at[s, y, b])

    def stage_y(group, buf, y_got, s, b, c):
        y_send(group, buf, y_got, s, b, c).wait_recv()
        cols = columns_of(group, c)
        add_into(buf.at[s, y, b, core, :, cols], y_got.at[s, b, :, cols])

    def line_in(group, buf, z_got, s, slot, b, c):
        z_send(group, buf, z_got, s, up_dev, slot, b, c).wait_recv()
        cols = columns_of(group, c)
        add_into(buf.at[s, y, b, core, :, cols], z_got.at[slot, b, :, cols])

    def stage_z(group, buf, z_got, s, b, c):
        @pl.when(s > z)
        def _():
            @pl.when(z > 0)
            def _():
                line_in(group, buf, z_got, s, s, b, c)

            z_send(group, buf, z_got, s, up_dev, s, b, c).start()

        @pl.when(s < z)
        def _():
            @pl.when(z < shards - 1)
            def _():
                line_in(group, buf, z_got, s, s, b, c)

            slot = jnp.where(s == z - 1, shards, s)
            z_send(group, buf, z_got, s, down_dev, slot, b, c).start()

    def swap(group, pair, c):
        cols = columns_of(group, c)
        index = 1 + c if group == 1 else 0
        return remote(pair.at[0, :, cols], pair.at[1, :, cols], gx_s.at[index], gx_r.at[index], x_dev)

    def stage_last(group, buf, y_got, z_got, pair, out):
        for b in halves:
            for c in pieces(group):
                cols = columns_of(group, c)
                stage_y(group, buf, y_got, z, b, c)
                out[b, :, cols] = buf[z, y, b, core, :, cols].astype(F32)

                @pl.when(z > 0)
                def _():
                    z_send(group, buf, z_got, z, up_dev, z, b, c).wait_recv()
                    out[b, :, cols] += z_got[z, b, :, cols].astype(F32)

                @pl.when(z < shards - 1)
                def _():
                    z_send(group, buf, z_got, z, up_dev, shards, b, c).wait_recv()
                    out[b, :, cols] += z_got[shards, b, :, cols].astype(F32)

                if b is halves[0]:
                    pair[0, :, cols] = out[b, :, cols].astype(BF16)
                    swap(group, pair, c).start()

    def stage_out(group, pair, out):
        for c in pieces(group):
            swap(group, pair, c).wait_recv()
        out[1 - x] = pair[1].astype(F32)

    def reversed_order(k):
        return order(shards - 1 - k)

    def store_grads(buf, s, a, left, right, lo, count):
        part = pl.ds(pl.multiple_of(2 * a * quarter, 2 * quarter), 2 * quarter)
        value = mm(left[part, :], right).astype(BF16)
        buf[s, a, :, :, :, lo : lo + count] = value.reshape(2, 2, cut, count)

    def line_half(group, buf, y_got, z_got, s, m):
        b = jnp.where(lax.rem(m, 2) == 0, 1 - x, x)
        for c in pieces(group):
            stage_y(group, buf, y_got, s, b, c)
            stage_z(group, buf, z_got, s, b, c)

    def feed_half(m):
        line_half(0, grads, y_f, z_f, order(leaving(lax.div(m, 2))), m)

    def attn_half(m):
        line_half(1, w_up, y_a, z_a, reversed_order(lax.div(m, 2)), m)

    def run_halves(step, first, last):
        def body(m, carry):
            step(m)
            return carry

        lax.fori_loop(first, last, body, 0)

    total_halves = 2 * (shards - 1)

    def leaving(k):
        if not quick:
            return shards - 1 - k
        ends, middle = jnp.where(edge, 2, 1), jnp.where(edge, 1, 2)
        return jnp.where(k == 0, ends, jnp.where(k == 1, 3, jnp.where(k == 2, middle, 0)))

    def feed_point(ends, middle):
        if quick and ends is not None:

            @pl.when(edge)
            def _():
                run_halves(feed_half, *ends)

        if quick and middle is not None:

            @pl.when(inner)
            def _():
                run_halves(feed_half, *middle)

    total[...] = jnp.zeros_like(total)
    turn_a[:, 0:rows] = jnp.transpose(h2[0])
    turn_b[...] = jnp.transpose(dfeed[...].reshape(2 * rows, width))
    for i in feed_mats:
        load_own(i).wait()

    def feed_grads(s):
        for a in parts_of:
            store_grads(grads, s, a, turn_a, dup[s], 0, hidden)
            store_grads(grads, s, a, turn_b, act[s], hidden, hidden)
            core_send(0, grads, core_f, s, a).start()

    def feed_core(s):
        stage_core(0, grads, core_f, y_f, s)

    def feed_chunk(s, half):
        part = pl.ds(pl.multiple_of(half * rows, rows), rows)
        up_here = w_up[s].reshape(width, hidden)
        wide[0] = mm(h2[half], up_here)
        wide[1] = mm_nt(dfeed[half], w_down[s])

        def turn(at, inside):
            active, slope = gelu_both(wide[0, at])
            out = pl.ds(pl.multiple_of(half * rows + at.start, TILE), TILE)
            act[s, out] = active.astype(BF16)
            dup[s, out] = (wide[1, at] * slope).astype(BF16)
            return inside

        row_tiles(rows, turn)
        total[half] += mm_nt(dup[s, part], up_here)

    def own_step(i, carry):
        j = jnp.where(edge, 2 * i, i) if quick else i
        active = inner | (i < 2) if quick else i >= 0

        @pl.when(active & (i > 0))
        def _():
            settle(1, j)

        @pl.when(active)
        def _():
            feed_chunk(order(j), 0)

        if quick:

            @pl.when(edge & (i == 0))
            def _():
                relay(feed_mats[:-1], 1)
                arrive(up_mats, 3)
                relay(feed_mats, 2)

            @pl.when(edge & (i == 1))
            def _():
                arrive(down_mats[:1], 3)

            @pl.when(inner & (i == 0))
            def _():
                relay(feed_mats, 1)

            @pl.when(inner & (i == 1))
            def _():
                relay(feed_mats, 2)

        else:

            @pl.when(edge & (j > 1) & (j + 1 < shards))
            def _():
                arrive(down_mats, j + 1)

            @pl.when(j + 2 < shards)
            def _():
                relay(feed_mats, j + 1)

            @pl.when(edge & (j + 3 < shards))
            def _():
                arrive(up_mats, j + 3)

        return carry

    lax.fori_loop(0, shards - 1, own_step, 0)
    for copy in x_h2:
        copy.wait_recv()
    turn_a[:, rows : 2 * rows] = jnp.transpose(h2[1])

    def other_step(k, carry):
        j, active = k, k >= 0
        if quick:
            j = jnp.where(edge, 2 - 2 * k, jnp.where(k < 2, 1 - k, 2))
            active = inner | (k < 2)

        @pl.when(active)
        def _():
            feed_chunk(order(j), 1)

        if quick:

            @pl.when(edge & (k == 0))
            def _():
                arrive(down_mats[1:], 3)

            @pl.when(k == 0)
            def _():
                feed_grads(order(leaving(0)))
                feed_core(order(leaving(0)))

            @pl.when(edge & (k == 0))
            def _():
                relay(up_mats, 3)

        return carry

    lax.fori_loop(0, shards - 1, other_step, 0)

    def last_step(k, carry):
        j, half, final = shards - 1, 1 - k, 0
        if quick:
            j = jnp.where(edge & (lax.rem(k, 2) == 1), 1, shards - 1)
            half = jnp.where(edge, jnp.where(k < 2, 1, 0), 1 - k)
            final = jnp.where(edge, 1, 0)

            @pl.when(inner & (k == 0))
            def _():
                relay(up_mats, shards - 1)

        @pl.when(k == 0)
        def _():
            relay(down_mats if quick else feed_mats, shards - 1)

        if quick:

            @pl.when(edge & (k == 0))
            def _():
                relay([by_z], 1)

        @pl.when(k <= final)
        def _():
            settle(1, j)

        feed_chunk(order(j), half)

        @pl.when(k == final)
        def _():
            sent[0] = total[1].astype(BF16)
            for copy in x_dh2:
                copy.start()

        if quick:

            @pl.when(edge & (k == 2))
            def _():
                feed_grads(order(leaving(1)))

            @pl.when(edge & (k == 3))
            def _():
                feed_core(order(leaving(1)))

        return carry

    lax.fori_loop(0, jnp.where(edge, 4, 2) if quick else 2, last_step, 0)
    first_left = jnp.where(edge, 2, 1) if quick else 0

    def feed_grads_step(k, carry):
        if quick:

            @pl.when((k == 2) & edge)
            def _():
                feed_half(0)

        feed_grads(order(leaving(k)))

        @pl.when(k > first_left)
        def _():
            feed_core(order(leaving(k - 1)))

        return carry

    lax.fori_loop(first_left, shards, feed_grads_step, 0)
    feed_point((1, 2), None)
    feed_core(z)

    def feed_rows(half):
        value = mm(act[0, half * rows : (half + 1) * rows], w_down[0])
        for s in range(1, shards):
            value += mm(act[s, half * rows : (half + 1) * rows], w_down[s])
        return value

    def second_back(at, carry):
        dh2 = total[0, at] + got[0, at].astype(F32)
        mixed = own_z[at].astype(F32) + attended[at]
        factor = lax.rsqrt(jnp.mean(mixed * mixed, axis=1, keepdims=True) + EPS)
        scaled = dh2 * second_gain[...]
        back = factor * scaled - mixed * (factor**3 * jnp.mean(mixed * scaled, axis=1, keepdims=True))
        dmixed[at] = back
        datt[0, at] = (gate(at) * own_c[at].astype(F32) + back).astype(BF16)
        return carry + fold_rows(dh2 * mixed * factor)

    second_sum = jnp.zeros((8, width), F32)
    for k in range(2):
        x_dh2[k].wait()
        second_sum = row_tiles(rows // 2, second_back, second_sum, first=k * (rows // 2))
        x_datt[k].start()
    sent[1] = feed_rows(1).astype(BF16)
    x_feed.start()
    feed_point((2, 3), (0, 1))
    feed_own[...] = feed_rows(0)

    def attend_back(half):
        part = slice(half * rows, (half + 1) * rows)

        def step(k, carry):
            s = reversed_order(k)
            dctx = mm_nt(datt[half], w_out[s]).astype(BF16)
            query = qkv[s, half, :, 0:narrow]
            key = qkv[s, half, :, narrow : 2 * narrow]
            value = qkv[s, half, :, 2 * narrow : 3 * narrow]
            weights = prob[s, half]
            dhead = stacked(dctx)
            dweights = mm_nt(dhead, value)
            full = weights.astype(F32)
            dscores = full * (dweights - jnp.sum(dweights * full, axis=1, keepdims=True))
            dscores = dscores.astype(BF16)
            dquery = unstacked(mm(dscores, key)) * HEAD_DIM**-0.5
            dkey = mm_tn(dscores, stacked(query))
            dvalue = mm_tn(weights, dhead)
            act[s, part, 0 : 3 * narrow] = jnp.concatenate([dquery, dkey, dvalue], axis=1).astype(BF16)
            return carry

        lax.fori_loop(0, shards, step, 0)

    def dh1_rows(half):
        part = slice(half * rows, (half + 1) * rows)
        value = mm_nt(act[0, part, 0 : 3 * narrow], w_qkv[0])
        for s in range(1, shards):
            value += mm_nt(act[s, part, 0 : 3 * narrow], w_qkv[s])
        return value

    attend_back(0)
    feed_point((3, 4), (1, 2))
    total[0] = dh1_rows(0)
    turn_a[...] = jnp.transpose(h1[...].reshape(2 * rows, width))
    drain(1)
    feed_point(None, (2, 3))
    for copy in x_datt:
        copy.wait_recv()
    turn_b[...] = jnp.transpose(datt[...].reshape(2 * rows, width))

    feed_point((4, 5), None)
    attend_back(1)
    sent[0] = dh1_rows(1).astype(BF16)
    x_dh1.start()
    feed_point((5, 6), (3, 5))

    def attn_grads(k, carry):
        s = reversed_order(k)
        for a in parts_of:
            store_grads(w_up, s, a, turn_a, act[s, :, 0 : 3 * narrow], 0, 3 * narrow)
            store_grads(w_up, s, a, turn_b, ctx[s], 3 * narrow, narrow)
            core_send(1, w_up, core_a, s, a).start()

        @pl.when(k > 0)
        def _():
            stage_core(1, w_up, core_a, y_a, reversed_order(k - 1))

        return carry

    lax.fori_loop(0, shards, attn_grads, 0)
    stage_core(1, w_up, core_a, y_a, z)

    x_feed.wait()

    def finish_forward(at, squares):
        branch = attended[at] + feed_own[at] + got[1, at].astype(F32)
        update = gate(at) * branch
        sent[1, at] = (own_z[at].astype(F32) + update).astype(BF16)
        dgate = jnp.sum(own_c[at].astype(F32) * branch, axis=1, keepdims=True)
        set_column(2, at, dgate * live(at))
        return squares + fold_rows(update * update)

    squares = row_tiles(rows, finish_forward, jnp.zeros((8, width), F32))
    put(0, sent.at[1]).start()
    count = jnp.sum(valid[...].astype(F32), axis=1, keepdims=True)
    energy = jnp.sum(jnp.sum(squares, axis=0, keepdims=True), axis=1, keepdims=True)
    rms = jnp.sqrt(energy / (width * jnp.maximum(count, 1.0)))

    if quick:
        feed_point(None, (5, 6))
    else:
        run_halves(feed_half, 0, total_halves)
    ahead = jnp.where(edge, 2, 1)
    run_halves(attn_half, 0, ahead)
    x_dh1.wait()

    def first_back(at, sums):
        dh1 = total[0, at] + got[0, at].astype(F32)
        row = own_z[at].astype(F32)
        factor = lax.rsqrt(jnp.mean(row * row, axis=1, keepdims=True) + EPS)
        scaled = dh1 * first_gain[...]
        back = factor * scaled - row * (factor**3 * jnp.mean(row * scaled, axis=1, keepdims=True))
        back = back + dmixed[at] + dscore(at) * w_router[...]
        got[1, at] = (own_c[at].astype(F32) + back).astype(BF16)
        return sums[0] + fold_rows(dscore(at) * row), sums[1] + fold_rows(dh1 * row * factor)

    zero = jnp.zeros((8, width), F32)
    router_sum, first_sum = row_tiles(rows, first_back, (zero, zero))
    put(1, got.at[1]).start()
    parts = [jnp.sum(part, axis=0, keepdims=True) for part in (router_sum, first_sum, second_sum)]
    small = jnp.concatenate(parts + [jnp.zeros((5, width), F32)], axis=0)

    def small_copy(k):
        return remote(small_send.at[k], small_got.at[k], sm_s.at[k], sm_r.at[k], small_devices[k])

    hops = len(small_devices)
    for k in range(hops):
        small_send[k] = small
        small_copy(k).start()
        if k > 0:
            attn_half(ahead + k)
        if k == hops - 1:

            @pl.when(inner)
            def _():
                attn_half(ahead + hops)

        small_copy(k).wait()
        small = small + small_got[k]
        if k == 0:
            attn_half(ahead)
    stage_last(0, grads, y_f, z_f, swap_f, feed_out)

    def small_spread(far, source):
        slot = hops + source
        return remote(
            small_send.at[hops], small_got.at[slot], sm_s.at[hops + far - 1], sm_r.at[slot], (dp, lax.rem(z + far, shards))
        )

    small_send[hops] = small
    small_got[hops + z] = small
    for far in range(1, shards):
        small_spread(far, z).start()

    run_halves(attn_half, ahead + hops + jnp.where(edge, 0, 1), total_halves)
    stage_last(1, w_up, y_a, z_a, swap_a, attn_out)
    for far in range(1, shards):
        small_spread(far, lax.rem(z + shards - far, shards)).wait_recv()
        small_spread(far, z).wait_send()
    small = small_got[hops]
    for k in range(1, shards):
        small = small + small_got[hops + k]
    row_at = lax.broadcasted_iota(jnp.int32, (8, 1), 0)
    small_send[0] = jnp.where(row_at == 3, rms, small)
    put(2, small_send.at[0]).start()
    stage_out(0, swap_f, feed_out)
    put(4, feed_out).start()
    stage_out(1, swap_a, attn_out)
    put(3, attn_out).start()

    drain(0)
    for copy in (x_h1, x_dfeed, *x_h2, *x_datt):
        copy.wait_send()

    for group, core_got, y_got, z_got in ((0, core_f, y_f, z_f), (1, core_a, y_a, z_a)):
        remote(core_got, core_got, gc_s.at[group], gc_r.at[group, 0, 0], core_dev).wait_send()
        remote(y_got, y_got, gy_s.at[group], gy_r.at[0, 0], y_dev).wait_send()
        moved = z_got.at[0 : shards - 1]
        remote(moved, moved, gz_s.at[group], gz_r.at[0, 0], up_dev).wait_send()

    swap(0, swap_f, 0).wait_send()
    for c in pieces(1):
        swap(1, swap_a, c).wait_send()
    for k, src in enumerate((sent.at[1], got.at[1], small_send.at[0], attn_out, feed_out)):
        put(k, src).wait()


def run_block(size, operands):
    shards, rows, width = size["S"], size["R"], size["D"]
    heads, narrow, hidden, cut = size["hh"], size["n"], size["f"], size["DB"]
    mats = (2 if size["joined"] else 4) + 4
    stages = 3 + shards
    attn, feed = 4 * narrow, 2 * hidden
    dma = pltpu.SemaphoreType.DMA
    vmem = lambda *shape: pltpu.VMEM(shape, BF16)
    full = lambda *shape: pltpu.VMEM(shape, F32)
    scratch = [
        vmem(shards, width, 3 * narrow),
        vmem(shards, narrow, width),
        vmem(shards, 2, 2, 2, cut, hidden),
        vmem(shards, hidden, width),
        *[vmem(2, rows, width) for _ in range(4)],
        *[vmem(width, 2 * rows) for _ in range(2)],
        vmem(shards, 2, rows, 3 * narrow),
        vmem(shards, 2 * rows, narrow),
        vmem(shards, 2, heads * rows, rows),
        vmem(shards, 2 * rows, hidden),
        vmem(shards, 2 * rows, hidden),
        full(2, rows, width),
        full(2, rows, hidden),
        vmem(2, rows, width),
        vmem(2, rows, width),
        vmem(rows, width),
        vmem(rows, width),
        *[full(rows, width) for _ in range(3)],
        full(rows, 128),
        vmem(shards, 2, 2, 2, cut, feed),
        vmem(shards, 2, 2, cut, feed),
        vmem(shards, 2, cut, feed),
        vmem(shards + 1, 2, cut, feed),
        vmem(shards, 2, 2, cut, attn),
        vmem(shards, 2, cut, attn),
        vmem(shards + 1, 2, cut, attn),
        vmem(2, cut, feed),
        vmem(2, cut, attn),
        full(2, cut, attn),
        full(2, cut, feed),
        full(stages, 8, width),
        full(stages, 8, width),
        pltpu.VMEM((1, rows), jnp.int32),
        pltpu.VMEM((1, size["L"]), jnp.int32),
        *[full(1, width) for _ in range(3)],
        dma((mats,)),
        dma((2, 2)),
        dma((5,)),
        dma((5,)),
        dma((2, shards + 1)),
        dma((mats, shards)),
        dma((4,)),
        dma((mats, shards)),
        dma((2,)),
        dma((2, shards)),
        dma((12,)),
        dma((12,)),
        dma((2,)),
        dma((2, shards, 2)),
        dma((2,)),
        dma((shards, 6)),
        dma((2,)),
        dma((shards + 1, 6)),
        dma((3,)),
        dma((3,)),
        dma((stages,)),
        dma((stages,)),
        dma((2,)),
    ]
    far = pl.BlockSpec(memory_space=pl.ANY)
    outs = [
        jax.ShapeDtypeStruct((rows, width), BF16),
        jax.ShapeDtypeStruct((rows, width), BF16),
        jax.ShapeDtypeStruct((8, width), F32),
        jax.ShapeDtypeStruct((2, cut, attn), F32),
        jax.ShapeDtypeStruct((2, cut, feed), F32),
    ]
    return pl.pallas_call(
        functools.partial(block_kernel, size),
        out_shape=outs,
        in_specs=[far] * len(operands),
        out_specs=[pl.BlockSpec(memory_space=pltpu.HBM)] * len(outs),
        scratch_shapes=scratch,
        compiler_params=pltpu.CompilerParams(
            collective_id=0, has_side_effects=True, vmem_limit_bytes=64 * 2**20 - 65536
        ),
    )(*operands)


def place_kernel(size, assemble, routed, small, tokens, cotangent, *refs):
    length, width, rows = size["L"], size["D"], size["R"]
    gathered, refs = refs[: 4 if assemble else 2], refs[4 if assemble else 2 :]
    outs, refs = refs[: 12 if assemble else 2], refs[12 if assemble else 2 :]
    bases, staged, refs = refs[:2], refs[2 : 2 + len(gathered)], refs[2 + len(gathered) :]
    finals, (pick, keep, in_sem, out_sem, part_sem, final_sem) = refs[:-6], refs[-6:]
    block = 512
    steps = width // block

    def moving(src, dst, sem, k, b):
        at = (slice(None), pl.ds(b * block, block))
        return pltpu.make_async_copy(src[k].at[at], dst[k].at[at], sem.at[k, b])

    sources = (tokens, cotangent)
    parts = [pltpu.make_async_copy(src, dst, part_sem.at[k]) for k, (src, dst) in enumerate(zip(gathered, staged))]
    for copy in parts[:2]:
        copy.start()
    for b in range(steps):
        for k in range(2):
            moving(sources, bases, in_sem, k, b).start()
    for copy in parts[2:]:
        copy.start()
    line = lax.broadcasted_iota(jnp.int32, (length, rows), 0)
    chosen = jnp.where(line == routed[...], 1.0, 0.0)
    pick[...] = chosen.astype(BF16)
    keep[...] = jnp.broadcast_to((1.0 - jnp.sum(chosen, axis=1, keepdims=True)).astype(BF16), keep.shape)
    for copy in parts[:2]:
        copy.wait()
    for b in range(steps):
        for k in range(2):
            at = slice(b * block, (b + 1) * block)
            moving(sources, bases, in_sem, k, b).wait()
            kept = jnp.concatenate([keep[...]] * (block // 128), axis=1)
            bases[k][:, at] = mm(pick[...], staged[k][:, at]).astype(BF16) + bases[k][:, at] * kept
            moving(bases, outs, out_sem, k, b).start()
    last = []
    if assemble:
        for copy in parts[2:]:
            copy.wait()
        for k, value in enumerate(weight_outputs(size, *staged[2:])):
            finals[k][...] = value
            last.append(pltpu.make_async_copy(finals[k], outs[2 + k], final_sem.at[k]))
            last[-1].start()
        for k in range(3):
            outs[8 + k][...] = small[k : k + 1, :]
        outs[11][...] = small[3:4, 0:1]
    for b in range(steps):
        for k in range(2):
            moving(bases, outs, out_sem, k, b).wait()
    for copy in last:
        copy.wait()


def weight_outputs(size, attn, feed):
    narrow, hidden = size["n"], size["f"]

    def side_by_side(ref, lo, count):
        return jnp.concatenate([ref[0, :, lo : lo + count], ref[1, :, lo : lo + count]], axis=1)

    return (
        side_by_side(attn, 0, narrow),
        side_by_side(attn, narrow, narrow),
        side_by_side(attn, 2 * narrow, narrow),
        side_by_side(attn, 3 * narrow, narrow).T,
        side_by_side(feed, 0, hidden),
        side_by_side(feed, hidden, hidden).T,
    )


def place_rows(size, routed, tokens, cotangent, rows_res, rows_grad, small, attn, feed, assemble):
    length, width, rows = size["L"], size["D"], size["R"]
    cut, narrow, hidden = size["DB"], size["n"], size["f"]
    whole = lambda *shape: pl.BlockSpec(shape, lambda i: (0,) * len(shape))
    far = pl.BlockSpec(memory_space=pltpu.HBM)
    outs, out_specs = [jax.ShapeDtypeStruct((length, width), BF16)] * 2, [far] * 2
    gathered, finals = [rows_res, rows_grad], []
    if assemble:
        gathered += [attn, feed]
        finals = [(cut, 2 * narrow)] * 3 + [(2 * narrow, cut), (cut, 2 * hidden), (2 * hidden, cut)]
        tiny = [(1, width)] * 3 + [(1, 1)]
        outs = outs + [jax.ShapeDtypeStruct(shape, F32) for shape in finals + tiny]
        out_specs = out_specs + [far] * len(finals) + [whole(*shape) for shape in tiny]
    dma = pltpu.SemaphoreType.DMA
    return pl.pallas_call(
        functools.partial(place_kernel, size, assemble),
        grid=(1,),
        out_shape=outs,
        in_specs=[whole(1, rows), whole(*small.shape)] + [far] * (2 + len(gathered)),
        out_specs=out_specs,
        scratch_shapes=[
            *[pltpu.VMEM((length, width), BF16) for _ in range(2)],
            *[pltpu.VMEM(part.shape, part.dtype) for part in gathered],
            *[pltpu.VMEM(shape, F32) for shape in finals],
            pltpu.VMEM((length, rows), BF16),
            pltpu.VMEM((length, 128), BF16),
            dma((2, width // 512)),
            dma((2, width // 512)),
            dma((4,)),
            dma((6,)),
        ],
        compiler_params=pltpu.CompilerParams(vmem_limit_bytes=60 * 2**20),
    )(routed, small, tokens, cotangent, *gathered)


def shards_of(
    groups,
    tokens,
    cotangent,
    routed,
    valid_mask,
    w_router,
    first_gain,
    query_weight,
    key_weight,
    value_weight,
    output_weight,
    second_gain,
    up_weight,
    down_weight,
):
    shards, data = lax.axis_size("mp"), lax.axis_size("dp")
    _, length, width = tokens.shape
    rows = routed.shape[1]
    narrow = query_weight.shape[1] // 2
    hidden = up_weight.shape[1] // 2
    cut = width // 8
    chips_x = 1 << ((data // 2).bit_length() - 1) // 2
    size = dict(
        S=shards, ybit=2 * chips_x, R=rows, D=width, L=length, hh=narrow // HEAD_DIM,
        n=narrow, f=hidden, DB=cut, joined=narrow % 128 != 0,
    )
    dp = lax.axis_index("dp")
    x, y = (dp // 2) % 2, (dp // size["ybit"]) % 2
    qkv = (query_weight, key_weight, value_weight)
    if size["joined"]:
        halves = [lax.dynamic_slice_in_dim(weight, x * narrow, narrow, 1) for weight in qkv]
        qkv = (jnp.concatenate(halves, axis=1),)
    row = lambda vector: vector.reshape(1, width)
    operands = (
        tokens.reshape(-1, rows, width), cotangent.reshape(-1, rows, width), routed, valid_mask, row(w_router), row(first_gain), row(second_gain),
        *qkv, output_weight, up_weight.reshape(2, 2, 2, cut, 2 * hidden), down_weight,
    )
    rows_res, rows_grad, small, attn, feed = run_block(size, operands)
    whole_group = data == 8
    rms = small[3, 0:1]
    if not whole_group:
        block = 4 * y + 2 * x + dp % 2

        def over_groups(part):
            base = jnp.zeros((2, width, part.shape[2]), F32)
            placed = lax.dynamic_update_slice_in_dim(base, part, block * cut, 1)
            return lax.psum_scatter(placed, "dp", scatter_dimension=1, tiled=True)

        attn, feed = over_groups(attn), over_groups(feed)
        small = lax.psum(small, "dp") / 8.0
    placed = place_rows(size, routed, tokens[0], cotangent[0], rows_res, rows_grad, small, attn, feed, whole_group)
    residual, grad_tokens = placed[:2]
    if whole_group:
        vectors = [vector.reshape(width) for vector in placed[8:11]]
        weights, rms = placed[2:8], placed[11].reshape(1)
    else:
        vectors, weights = [small[k] for k in range(3)], weight_outputs(size, attn, feed)
    grad_query, grad_key, grad_value, grad_output, grad_up, grad_down = weights
    return (
        residual[None],
        grad_tokens[None],
        rms,
        vectors[0],
        vectors[1],
        grad_query,
        grad_key,
        grad_value,
        grad_output,
        vectors[2],
        grad_up,
        grad_down,
    )


def solution(mesh):
    in_specs = (
        P(("dp", "mp"), None, None),
        P(("dp", "mp"), None, None),
        P(("dp", "mp"), None),
        P(("dp", "mp"), None),
        P(),
        P(),
        P(None, "mp"),
        P(None, "mp"),
        P(None, "mp"),
        P("mp", None),
        P(),
        P(None, "mp"),
        P("mp", None),
    )
    out_specs = (
        P(("dp", "mp"), None, None),
        P(("dp", "mp"), None, None),
        P(("dp", "mp")),
        P(),
        P(),
        P("dp", "mp"),
        P("dp", "mp"),
        P("dp", "mp"),
        P("mp", "dp"),
        P(),
        P("dp", "mp"),
        P("mp", "dp"),
    )
    body = functools.partial(shards_of, mesh.shape["dp"] // 8)
    return jax.shard_map(body, mesh=mesh, in_specs=in_specs, out_specs=out_specs, check_vma=False)
```

```python
import functools
import math

import jax
import jax.numpy as jnp
from jax import lax
from jax.experimental import pallas as pl
from jax.experimental.pallas import tpu as pltpu
from jax.sharding import PartitionSpec as P

HEADS = 16
HEAD_DIM = 64
EPS = 1e-06
F32 = jnp.float32
BF16 = jnp.bfloat16
TILE = 64


def mm(left, right):
    return jnp.dot(left, right, preferred_element_type=F32)


def mm_nt(left, right):
    return lax.dot_general(left, right, (((1,), (1,)), ((), ())), preferred_element_type=F32)


def mm_tn(left, right):
    return lax.dot_general(left, right, (((0,), (0,)), ((), ())), preferred_element_type=F32)


def row_tiles(rows, body, init=0, first=0):
    def step(index, carry):
        return body(pl.ds(pl.multiple_of(first + index * TILE, TILE), TILE), carry)

    return lax.fori_loop(0, rows // TILE, step, init)


def fold_rows(value):
    return jnp.sum(value.reshape(-1, 8, value.shape[-1]), axis=0)


def gelu_both(value):
    cdf = 0.5 * (1.0 + lax.erf(value * math.sqrt(0.5)))
    density = jnp.exp(-0.5 * value * value) * (1.0 / math.sqrt(2.0 * math.pi))
    return value * cdf, cdf + value * density


def block_kernel(size, *refs):
    shards, ybit, rows, width, length = size["S"], size["ybit"], size["R"], size["D"], size["L"]
    heads, narrow, hidden, cut = size["hh"], size["n"], size["f"], size["DB"]
    joined = size["joined"]
    quarter = 2 * cut
    refs = list(refs)

    def take(count):
        taken, refs[:count] = refs[:count], []
        return taken

    tokens, cotangent = take(2)
    small_in = take(5)
    qkv_in = take(1 if joined else 3)
    out_in, up_in, down_in = take(3)
    outputs = take(5)
    w_qkv, w_out, w_up, w_down = take(4)
    h1, dfeed, h2, datt, turn_a, turn_b = take(6)
    qkv, ctx, prob, act, dup = take(5)
    total, wide, sent, got = take(4)
    own_z, own_c, attended, dmixed, feed_own, columns = take(6)
    lane = lax.broadcasted_iota(jnp.int32, (1, 128), 1)

    def column(k, at):
        return columns[at][:, k : k + 1]

    def set_column(k, at, value):
        columns[at] = jnp.where(lane == k, value, columns[at])

    gate, live, dscore = (functools.partial(column, k) for k in range(3))
    grads, core_f, y_f, z_f, core_a, y_a, z_a, swap_f, swap_a = take(9)
    attn_out, feed_out = take(2)
    small_send, small_got = take(2)
    routed, valid, w_router, first_gain, second_gain = small_held = take(5)
    load_sem, tok_sem, out_sem, small_sem = take(4)
    wz_s, wz_r, wy_s, wy_r, wc_s, wc_r = take(6)
    x_s, x_r = take(2)
    gc_s, gc_r, gy_s, gy_r, gz_s, gz_r, gx_s, gx_r = take(8)
    sm_s, sm_r = take(2)
    ex_sem = take(1)[0]

    dp = lax.axis_index("dp")
    z = lax.axis_index("mp")
    core = lax.rem(dp, 2)
    x = lax.rem(lax.div(dp, 2), 2)
    y = lax.rem(lax.div(dp, ybit), 2)
    core_dev = (dp + 1 - 2 * core, z)
    x_dev = (dp + 2 * (1 - 2 * x), z)
    y_dev = (dp + ybit * (1 - 2 * y), z)
    up_dev = (dp, z + 1)
    down_dev = (dp, z - 1)
    small_devices = [core_dev, x_dev, (dp + 2 * (1 - 2 * x) + ybit * (1 - 2 * y), z)]

    def remote(src, dst, send, recv, device):
        return pltpu.make_async_remote_copy(
            src_ref=src,
            dst_ref=dst,
            send_sem=send,
            recv_sem=recv,
            device_id=device,
            device_id_type=pl.DeviceIdType.MESH,
        )

    def order(j):
        high = lax.div(z, shards // 2)
        base = z + high * (shards - 1 - 2 * z)
        odd = lax.rem(j, 2)
        near = base + lax.div(j + 1, 2) * (2 * odd - 1)
        pick = jnp.where(j <= 2 * base, near, j)
        return pick + high * (shards - 1 - 2 * pick)

    attn_mats = list(range(len(qkv_in) + 1))
    up_mats = [len(attn_mats), len(attn_mats) + 1]
    down_mats = [len(attn_mats) + 2, len(attn_mats) + 3]
    feed_mats = up_mats + down_mats
    out_at, up_at, down_at = attn_mats[-1], up_mats[0], down_mats[0]

    def down_rows(i, start=0):
        return pl.ds(pl.multiple_of(start + (i - down_at) * (hidden // 2), hidden // 2), hidden // 2)

    def span(qy, qc):
        return pl.ds(pl.multiple_of((2 * qy + qc) * quarter, quarter), quarter)

    def lanes(count):
        return pl.ds(pl.multiple_of(x * count, count), count)

    def held(i, s, qy, qc):
        if i < out_at:
            part = w_qkv if joined else w_qkv.at[:, :, i * narrow : (i + 1) * narrow]
            return part.at[s, span(qy, qc)]
        if i == out_at:
            return w_out.at[s, :, span(qy, qc)]
        if i < down_at:
            return w_up.at[s, qy, qc, i - up_at]
        return w_down.at[s, down_rows(i), span(qy, qc)]

    def own_piece(i):
        if i < out_at:
            part = qkv_in[i].at[span(y, core)]
            return part if joined else part.at[:, lanes(narrow)]
        if i == out_at:
            return out_in.at[lanes(narrow), span(y, core)]
        if i < down_at:
            return up_in.at[y, core, i - up_at, :, lanes(hidden)]
        return down_in.at[down_rows(i, x * hidden), span(y, core)]

    def load_own(i):
        if i < out_at:
            if joined:
                src, dst = qkv_in[i], w_qkv.at[z]
            else:
                src, dst = qkv_in[i].at[:, lanes(narrow)], w_qkv.at[z, :, i * narrow : (i + 1) * narrow]
        elif i == out_at:
            src, dst = out_in.at[lanes(narrow), :], w_out.at[z]
        elif i < down_at:
            b = i - up_at
            src, dst = up_in.at[:, :, b, :, lanes(hidden)], w_up.at[z, :, :, b]
        else:
            src, dst = down_in.at[down_rows(i, x * hidden), :], w_down.at[z, down_rows(i)]
        return pltpu.make_async_copy(src, dst, load_sem.at[i])

    def group_of(i):
        return 0 if i <= out_at else 1

    def y_group(i):
        return 0 if i <= out_at else 1 if i < down_at else 2 + i - down_at

    def own_up(i):
        return remote(own_piece(i), held(i, z, y, core), wz_s.at[group_of(i), z], wz_r.at[i, z], up_dev)

    def own_down(i):
        return remote(own_piece(i), held(i, z, y, core), wz_s.at[group_of(i), shards], wz_r.at[i, z], down_dev)

    def pass_on(i, s, device):
        piece = held(i, s, y, core)
        return remote(piece, piece, wz_s.at[group_of(i), s], wz_r.at[i, s], device)

    def across_y(i, s, qy):
        piece = held(i, s, qy, core)
        return remote(piece, piece, wy_s.at[y_group(i)], wy_r.at[i, s], y_dev)

    def across_core(i, s, qy, qc):
        piece = held(i, s, qy, qc)
        group = group_of(i)
        return remote(piece, piece, wc_s.at[group], wc_r.at[group, s], core_dev)

    def await_pieces(group, sem, count, receiving=False):
        mats = attn_mats if group == 0 else feed_mats
        if joined:
            refs = [held(i, 0, 0, 0) for i in mats] * count
        else:
            flat = w_up.at[0, 0, 0] if group == 0 else w_up.at[0, 0]
            if count == 2:
                flat = w_up.at[0, 0] if group == 0 else w_up.at[0]
            elif count == shards - 1:
                flat = w_up.at[0 : shards - 1, 0, 0] if group == 0 else w_up.at[0 : shards - 1, 0]
            elif count == 2 * (shards - 1):
                flat = w_up.at[0 : shards - 1, 0] if group == 0 else w_up.at[0 : shards - 1]
            refs = [flat]
        for ref in refs:
            if receiving:
                remote(ref, ref, wc_s.at[group], sem, core_dev).wait_recv()
            else:
                remote(ref, ref, sem, wc_r.at[group, 0], core_dev).wait_send()

    def send_own_up(mats):
        for i in mats:
            own_up(i).start()

    def send_own_down(mats):
        for i in mats:
            own_down(i).start()

    def passing(s, action):
        @pl.when((s < z) & (z < shards - 1))
        def _():
            action(up_dev)

        @pl.when((s > z) & (z > 0))
        def _():
            action(down_dev)

    edge = (z == 0) | (z == shards - 1)
    inner = jnp.logical_not(edge)

    def by_z_here(i, j):
        return quick and i == by_z and isinstance(j, int) and j == 1

    def arrive_one(i, j):
        s = order(j)
        pass_on(i, s, up_dev).wait_recv()
        passing(s, lambda device: pass_on(i, s, device).start())
        if by_z_here(i, j):

            @pl.when(inner)
            def _():
                across_y(i, s, y).start()

        else:
            across_y(i, s, y).start()
        across_core(i, s, y, core).start()

    def arrive(mats, j):
        for i in mats:
            arrive_one(i, j)

    def follow(j):
        s = order(j)

        @pl.when((s == 0) & (z < shards - 1))
        def _():
            send_own_up(feed_mats)

        @pl.when((s == shards - 1) & (z > 0))
        def _():
            send_own_down(feed_mats)

    def relay(mats, j):
        s = order(j)
        for i in mats:
            if by_z_here(i, j):

                @pl.when(edge)
                def _():
                    bypass(s, up_dev).wait_recv()

                @pl.when(inner)
                def _():
                    across_y(i, s, 1 - y).wait_recv()

            else:
                across_y(i, s, 1 - y).wait_recv()
            across_core(i, s, 1 - y, core).start()

    def settle(group, j):
        await_pieces(group, wc_r.at[group, order(j)], 2, True)

    def await_y(index, blocks, count):
        flat = w_up.at[0:count, 0, 0] if blocks == 2 else w_up.at[0:count, 0, 0, 0]
        remote(flat, flat, wy_s.at[index], wy_r.at[0, 0], y_dev).wait_send()

    quick = shards == 4
    by_z = down_mats[-1]

    def bypass(s, device):
        src = down_in.at[down_rows(by_z, x * hidden), span(1 - y, core)]
        return remote(src, held(by_z, s, 1 - y, core), ex_sem.at[0], ex_sem.at[1], device)

    def drain(group):
        @pl.when(z < shards - 1)
        def _():
            await_pieces(group, wz_s.at[group, z], 1)

        @pl.when(z > 0)
        def _():
            await_pieces(group, wz_s.at[group, shards], 1)

        def step(j, carry):
            s = order(j)
            passing(s, lambda device: await_pieces(group, wz_s.at[group, s], 1))
            return carry

        lax.fori_loop(1, shards, step, 0)
        if group == 0:
            await_pieces(0, wy_s.at[0], shards - 1)
        else:
            await_y(1, 2, shards - 1)
            await_y(2, 1, shards - 1)
            if not quick:
                await_y(3, 1, shards - 1)
            else:

                @pl.when(edge)
                def _():
                    await_y(3, 1, shards - 2)

                @pl.when(inner)
                def _():
                    await_y(3, 1, shards - 1)
                    bypass(z, up_dev).wait_send()

        await_pieces(group, wc_s.at[group], 2 * (shards - 1))

    def exchange(slot, src, dst):
        return remote(src, dst, x_s.at[slot], x_r.at[slot], x_dev)

    x_h1 = exchange(0, h1.at[0], h1.at[1])
    x_dfeed = exchange(1, dfeed.at[0], dfeed.at[1])
    upper, lower = slice(0, rows // 2), slice(rows // 2, rows)
    x_att = [exchange(2 + 6 * k, sent.at[0, part], got.at[0, part]) for k, part in enumerate((upper, lower))]
    x_h2 = [exchange(3 + 6 * k, h2.at[0, part], h2.at[1, part]) for k, part in enumerate((upper, lower))]
    x_dh2 = [exchange(4 + 6 * k, sent.at[0, part], got.at[0, part]) for k, part in enumerate((upper, lower))]
    x_feed = exchange(5, sent.at[1], got.at[1])
    x_datt = [exchange(6 + 5 * k, datt.at[0, part], datt.at[1, part]) for k, part in enumerate((upper, lower))]
    x_dh1 = exchange(7, sent.at[0], got.at[0])

    def put(k, src):
        return pltpu.make_async_copy(src, outputs[k], out_sem.at[k])

    def put_half(b, index):
        return pltpu.make_async_copy(attn_out.at[b], outputs[3].at[b], out_sem.at[5 + index])

    steps = length // (2 * rows)
    stages = ((got, sent), (h2, datt))

    def block_loads(t):
        copies = []
        for k, (array, buf) in enumerate(zip((tokens, cotangent), stages[t % 2])):
            copies.append(pltpu.make_async_copy(array.at[2 * t : 2 * t + 2], buf, tok_sem.at[t % 2, k]))
        return copies

    barrier = pltpu.get_barrier_semaphore()

    def greet(device):
        pl.semaphore_signal(barrier, inc=1, device_id=device, device_id_type=pl.DeviceIdType.MESH)

    @pl.when(z > 0)
    def _():
        greet(down_dev)

    @pl.when(z < shards - 1)
    def _():
        greet(up_dev)

    for device in (y_dev, x_dev, core_dev):
        greet(device)

    small_loads = [pltpu.make_async_copy(src, dst, small_sem.at[k]) for k, (src, dst) in enumerate(zip(small_in, small_held))]
    for copy in small_loads:
        copy.start()
    for t in range(2):
        for copy in block_loads(t):
            copy.start()
    for i in attn_mats + feed_mats:
        load_own(i).start()

    def begin():
        ends = jnp.where(z == 0, 1, 0) + jnp.where(z == shards - 1, 1, 0)
        pl.semaphore_wait(barrier, 5 - ends)

        @pl.when(z < shards - 1)
        def _():
            send_own_up(attn_mats)

        @pl.when(z > 0)
        def _():
            send_own_down(attn_mats)

        @pl.when(z == 0)
        def _():
            send_own_up(feed_mats)

        @pl.when(z == shards - 1)
        def _():
            send_own_down(feed_mats)

    begin()

    for copy in small_loads:
        copy.wait()
    as_rows = jnp.broadcast_to(routed[...].astype(F32), (8, rows))
    position = jnp.transpose(as_rows)[:, 0:1].astype(jnp.int32)
    flags = jnp.zeros((rows, 1), F32)
    for t in range(steps):
        for copy in block_loads(t):
            copy.wait()
        hit = position == 2 * t * rows + lax.broadcasted_iota(jnp.int32, (rows, 2 * rows), 1)
        chosen = jnp.where(hit, 1.0, 0.0)
        pick = chosen.astype(BF16)
        for k, buf in enumerate(stages[t % 2]):
            picked = mm(pick, buf[...].reshape(2 * rows, width))
            total[k] = picked if t == 0 else total[k] + picked
        if t + 2 < steps:
            for copy in block_loads(t + 2):
                copy.start()
        mask = valid[:, 2 * t * rows : 2 * (t + 1) * rows].astype(F32)
        flags = flags + jnp.sum(chosen * mask, axis=1, keepdims=True)
    columns[...] = jnp.broadcast_to(flags, columns.shape)

    def prepare(at, carry):
        row, cot = total[0, at], total[1, at]
        own_z[at] = row.astype(BF16)
        own_c[at] = cot.astype(BF16)
        gate_here = jnp.sum(row * w_router[...], axis=1, keepdims=True) * live(at)
        set_column(0, at, gate_here)
        factor = lax.rsqrt(jnp.mean(row * row, axis=1, keepdims=True) + EPS)
        h1[0, at] = (row * factor * first_gain[...]).astype(BF16)
        dfeed[0, at] = (gate_here * cot).astype(BF16)
        return carry

    row_tiles(rows, prepare)
    x_h1.start()
    x_dfeed.start()

    lane_head = lax.div(lax.broadcasted_iota(jnp.int32, (1, narrow), 1), HEAD_DIM)
    masks = [jnp.where(lane_head == h, 1.0, 0.0) for h in range(heads)]
    masks_low = [mask.astype(BF16) for mask in masks]

    def stacked(value):
        return jnp.concatenate([value * mask for mask in masks_low], axis=0) if heads > 1 else value

    def unstacked(value):
        if heads == 1:
            return value
        picked = value[0:rows] * masks[0]
        for h in range(1, heads):
            picked = picked + value[h * rows : (h + 1) * rows] * masks[h]
        return picked

    score_shape = (heads * rows, rows)
    causal = lax.rem(lax.broadcasted_iota(jnp.int32, score_shape, 0), rows) >= lax.broadcasted_iota(
        jnp.int32, score_shape, 1
    )

    for i in attn_mats:
        load_own(i).wait()

    @pl.when(edge)
    def _():
        for j in range(1, shards):
            arrive(attn_mats, j)
            follow(j)
            if j > 1:
                relay(attn_mats, j - 1)

    @pl.when(inner)
    def _():
        for i in attn_mats:
            for j in (1, 2):
                arrive_one(i, j)
        for j in (1, 2):
            follow(j)
        for j in range(3, shards):
            arrive(attn_mats, j)
            follow(j)
        for j in range(1, shards - 1):
            relay(attn_mats, j)

    x_h1.wait_recv()

    def attend(j, carry):
        s = order(j)

        @pl.when(j + 2 == shards)
        def _():
            arrive(up_mats[:1], 1)

        @pl.when(j + 1 == shards)
        def _():
            relay(attn_mats, j)
            arrive(up_mats[1:], 1)

        @pl.when(j > 0)
        def _():
            settle(0, j)

        low = mm(h1[...].reshape(2 * rows, width), w_qkv[s]).astype(BF16)
        query = low[:, 0:narrow] * jnp.asarray(HEAD_DIM**-0.5, BF16)
        qkv[s] = jnp.concatenate([query, low[:, narrow:]], axis=1).reshape(2, rows, 3 * narrow)
        for half in range(2):
            query = qkv[s, half, :, 0:narrow]
            key = qkv[s, half, :, narrow : 2 * narrow]
            value = qkv[s, half, :, 2 * narrow : 3 * narrow]
            scores = jnp.where(causal, mm_nt(stacked(query), key), -1e30)
            raised = jnp.exp(scores - jnp.max(scores, axis=1, keepdims=True))
            weights = (raised / jnp.sum(raised, axis=1, keepdims=True)).astype(BF16)
            prob[s, half] = weights
            ctx[s, half * rows : (half + 1) * rows] = unstacked(mm(weights, value)).astype(BF16)
        return carry

    lax.fori_loop(0, shards, attend, 0)

    def project_out(half):
        parts = [ctx[s, half * rows : (half + 1) * rows] for s in range(shards)]
        return mm(jnp.concatenate(parts, axis=1), w_out[...].reshape(shards * narrow, width))

    sent[0] = project_out(1).astype(BF16)
    for copy in x_att:
        copy.start()
    attended[...] = project_out(0)
    arrive(down_mats, 1)
    arrive(up_mats, 2)

    @pl.when(inner)
    def _():
        arrive(down_mats, 2)
        for j in range(3, shards):
            arrive(feed_mats, j)
        if quick:

            @pl.when(z == 1)
            def _():
                bypass(z, down_dev).start()

            @pl.when(z == shards - 2)
            def _():
                bypass(z, up_dev).start()

    def mix(at, carry):
        att = attended[at] + got[0, at].astype(F32)
        attended[at] = att
        mixed = own_z[at].astype(F32) + att
        factor = lax.rsqrt(jnp.mean(mixed * mixed, axis=1, keepdims=True) + EPS)
        h2[0, at] = (mixed * factor * second_gain[...]).astype(BF16)
        return carry

    for k in range(2):
        x_att[k].wait()
        row_tiles(rows // 2, mix, first=k * (rows // 2))
        x_h2[k].start()

        @pl.when(edge)
        def _():
            arrive(down_mats[k : k + 1], 2)


    x_dfeed.wait_recv()

    parts_of = (1 - y, y)

    def core_send(group, buf, into, s, a):
        src = buf.at[s, a, :, 1 - core]
        return remote(src, into.at[s, a], gc_s.at[group], gc_r.at[group, s, a], core_dev)

    halves = (1 - x, x)

    def columns_of(group, c):
        return slice(c * 2 * narrow, (c + 1) * 2 * narrow) if group == 1 else slice(0, 2 * hidden)

    def pieces(group):
        return range(2) if group == 1 else range(1)

    def sem_at(group, b, c):
        return 2 + 2 * b + c if group == 1 else b

    def y_send(group, buf, into, s, b, c):
        cols = columns_of(group, c)
        src = buf.at[s, 1 - y, b, core, :, cols]
        recv = gy_r.at[s, sem_at(group, b, c)]
        return remote(src, into.at[s, b, :, cols], gy_s.at[group], recv, y_dev)

    def z_send(group, buf, into, s, device, slot, b, c):
        cols = columns_of(group, c)
        src = buf.at[s, y, b, core, :, cols]
        recv = gz_r.at[slot, sem_at(group, b, c)]
        return remote(src, into.at[slot, b, :, cols], gz_s.at[group], recv, device)

    def add_into(ref, other):
        ref[...] = (ref[...].astype(F32) + other[...].astype(F32)).astype(BF16)

    def stage_core(group, buf, core_got, y_got, s):
        core_send(group, buf, core_got, s, 1 - y).wait_recv()
        for b in halves:
            add_into(buf.at[s, 1 - y, b, core], core_got.at[s, 1 - y, b])
            for c in pieces(group):
                y_send(group, buf, y_got, s, b, c).start()
        core_send(group, buf, core_got, s, y).wait_recv()
        for b in range(2):
            add_into(buf.at[s, y, b, core], core_got.at[s, y, b])

    def stage_y(group, buf, y_got, s, b, c):
        y_send(group, buf, y_got, s, b, c).wait_recv()
        cols = columns_of(group, c)
        add_into(buf.at[s, y, b, core, :, cols], y_got.at[s, b, :, cols])

    def line_in(group, buf, z_got, s, slot, b, c):
        z_send(group, buf, z_got, s, up_dev, slot, b, c).wait_recv()
        cols = columns_of(group, c)
        add_into(buf.at[s, y, b, core, :, cols], z_got.at[slot, b, :, cols])

    def stage_z(group, buf, z_got, s, b, c):
        @pl.when(s > z)
        def _():
            @pl.when(z > 0)
            def _():
                line_in(group, buf, z_got, s, s, b, c)

            z_send(group, buf, z_got, s, up_dev, s, b, c).start()

        @pl.when(s < z)
        def _():
            @pl.when(z < shards - 1)
            def _():
                line_in(group, buf, z_got, s, s, b, c)

            slot = jnp.where(s == z - 1, shards, s)
            z_send(group, buf, z_got, s, down_dev, slot, b, c).start()

    def swap(group, pair, c):
        cols = columns_of(group, c)
        index = 1 + c if group == 1 else 0
        return remote(pair.at[0, :, cols], pair.at[1, :, cols], gx_s.at[index], gx_r.at[index], x_dev)

    def stage_last(group, buf, y_got, z_got, pair, out):
        for b in halves:
            for c in pieces(group):
                cols = columns_of(group, c)
                stage_y(group, buf, y_got, z, b, c)
                out[b, :, cols] = buf[z, y, b, core, :, cols].astype(F32)

                @pl.when(z > 0)
                def _():
                    z_send(group, buf, z_got, z, up_dev, z, b, c).wait_recv()
                    out[b, :, cols] += z_got[z, b, :, cols].astype(F32)

                @pl.when(z < shards - 1)
                def _():
                    z_send(group, buf, z_got, z, up_dev, shards, b, c).wait_recv()
                    out[b, :, cols] += z_got[shards, b, :, cols].astype(F32)

                if b is halves[0]:
                    pair[0, :, cols] = out[b, :, cols].astype(BF16)
                    swap(group, pair, c).start()

    def stage_out(group, pair, out):
        for c in pieces(group):
            swap(group, pair, c).wait_recv()
        out[1 - x] = pair[1].astype(F32)

    def reversed_order(k):
        return order(shards - 1 - k)

    def store_grads(buf, s, a, left, right, lo, count):
        part = pl.ds(pl.multiple_of(2 * a * quarter, 2 * quarter), 2 * quarter)
        value = mm(left[part, :], right).astype(BF16)
        buf[s, a, :, :, :, lo : lo + count] = value.reshape(2, 2, cut, count)

    def line_half(group, buf, y_got, z_got, s, m):
        b = jnp.where(lax.rem(m, 2) == 0, 1 - x, x)
        for c in pieces(group):
            stage_y(group, buf, y_got, s, b, c)
            stage_z(group, buf, z_got, s, b, c)

    def feed_half(m):
        line_half(0, grads, y_f, z_f, order(leaving(lax.div(m, 2))), m)

    def attn_half(m):
        line_half(1, w_up, y_a, z_a, reversed_order(lax.div(m, 2)), m)

    def run_halves(step, first, last):
        def body(m, carry):
            step(m)
            return carry

        lax.fori_loop(first, last, body, 0)

    total_halves = 2 * (shards - 1)

    def leaving(k):
        if not quick:
            return shards - 1 - k
        ends, middle = jnp.where(edge, 2, 1), jnp.where(edge, 1, 2)
        return jnp.where(k == 0, ends, jnp.where(k == 1, 3, jnp.where(k == 2, middle, 0)))

    def feed_point(ends, middle):
        if quick and ends is not None:

            @pl.when(edge)
            def _():
                run_halves(feed_half, *ends)

        if quick and middle is not None:

            @pl.when(inner)
            def _():
                run_halves(feed_half, *middle)

    total[...] = jnp.zeros_like(total)
    turn_a[:, 0:rows] = jnp.transpose(h2[0])
    turn_b[...] = jnp.transpose(dfeed[...].reshape(2 * rows, width))
    for i in feed_mats:
        load_own(i).wait()

    def feed_grads(s):
        for a in parts_of:
            store_grads(grads, s, a, turn_a, dup[s], 0, hidden)
            store_grads(grads, s, a, turn_b, act[s], hidden, hidden)
            core_send(0, grads, core_f, s, a).start()

    def feed_core(s):
        stage_core(0, grads, core_f, y_f, s)

    def feed_chunk(s, half):
        part = pl.ds(pl.multiple_of(half * rows, rows), rows)
        up_here = w_up[s].reshape(width, hidden)
        wide[0] = mm(h2[half], up_here)
        wide[1] = mm_nt(dfeed[half], w_down[s])

        def turn(at, inside):
            active, slope = gelu_both(wide[0, at])
            out = pl.ds(pl.multiple_of(half * rows + at.start, TILE), TILE)
            act[s, out] = active.astype(BF16)
            dup[s, out] = (wide[1, at] * slope).astype(BF16)
            return inside

        row_tiles(rows, turn)
        total[half] += mm_nt(dup[s, part], up_here)

    def own_step(i, carry):
        j = jnp.where(edge, 2 * i, i) if quick else i
        active = inner | (i < 2) if quick else i >= 0

        @pl.when(active & (i > 0))
        def _():
            settle(1, j)

        @pl.when(active)
        def _():
            feed_chunk(order(j), 0)

        if quick:

            @pl.when(edge & (i == 0))
            def _():
                relay(feed_mats[:-1], 1)
                arrive(up_mats, 3)
                relay(feed_mats, 2)

            @pl.when(edge & (i == 1))
            def _():
                arrive(down_mats[:1], 3)

            @pl.when(inner & (i == 0))
            def _():
                relay(feed_mats, 1)

            @pl.when(inner & (i == 1))
            def _():
                relay(feed_mats, 2)

        else:

            @pl.when(edge & (j > 1) & (j + 1 < shards))
            def _():
                arrive(down_mats, j + 1)

            @pl.when(j + 2 < shards)
            def _():
                relay(feed_mats, j + 1)

            @pl.when(edge & (j + 3 < shards))
            def _():
                arrive(up_mats, j + 3)

        return carry

    lax.fori_loop(0, shards - 1, own_step, 0)
    for copy in x_h2:
        copy.wait_recv()
    turn_a[:, rows : 2 * rows] = jnp.transpose(h2[1])

    def other_step(k, carry):
        j, active = k, k >= 0
        if quick:
            j = jnp.where(edge, 2 - 2 * k, jnp.where(k < 2, 1 - k, 2))
            active = inner | (k < 2)

        @pl.when(active)
        def _():
            feed_chunk(order(j), 1)

        if quick:

            @pl.when(edge & (k == 0))
            def _():
                arrive(down_mats[1:], 3)

            @pl.when(k == 0)
            def _():
                feed_grads(order(leaving(0)))
                feed_core(order(leaving(0)))

            @pl.when(edge & (k == 0))
            def _():
                relay(up_mats, 3)

        return carry

    lax.fori_loop(0, shards - 1, other_step, 0)

    def last_step(k, carry):
        j, half, final = shards - 1, 1 - k, 0
        if quick:
            j = jnp.where(edge & (lax.rem(k, 2) == 1), 1, shards - 1)
            half = jnp.where(edge, jnp.where(k < 2, 1, 0), 1 - k)
            final = jnp.where(edge, 1, 0)

            @pl.when(inner & (k == 0))
            def _():
                relay(up_mats, shards - 1)

        @pl.when(k == 0)
        def _():
            relay(down_mats if quick else feed_mats, shards - 1)

        if quick:

            @pl.when(edge & (k == 0))
            def _():
                relay([by_z], 1)

        @pl.when(k <= final)
        def _():
            settle(1, j)

        feed_chunk(order(j), half)

        @pl.when(k == final)
        def _():
            sent[0] = total[1].astype(BF16)
            for copy in x_dh2:
                copy.start()

        if quick:

            @pl.when(edge & (k == 2))
            def _():
                feed_grads(order(leaving(1)))

            @pl.when(edge & (k == 3))
            def _():
                feed_core(order(leaving(1)))

        return carry

    lax.fori_loop(0, jnp.where(edge, 4, 2) if quick else 2, last_step, 0)
    first_left = jnp.where(edge, 2, 1) if quick else 0

    def feed_grads_step(k, carry):
        if quick:

            @pl.when((k == 2) & edge)
            def _():
                feed_half(0)

        feed_grads(order(leaving(k)))

        @pl.when(k > first_left)
        def _():
            feed_core(order(leaving(k - 1)))

        return carry

    lax.fori_loop(first_left, shards, feed_grads_step, 0)
    feed_point((1, 2), None)
    feed_core(z)

    def feed_rows(half):
        value = mm(act[0, half * rows : (half + 1) * rows], w_down[0])
        for s in range(1, shards):
            value += mm(act[s, half * rows : (half + 1) * rows], w_down[s])
        return value

    def second_back(at, carry):
        dh2 = total[0, at] + got[0, at].astype(F32)
        mixed = own_z[at].astype(F32) + attended[at]
        factor = lax.rsqrt(jnp.mean(mixed * mixed, axis=1, keepdims=True) + EPS)
        scaled = dh2 * second_gain[...]
        back = factor * scaled - mixed * (factor**3 * jnp.mean(mixed * scaled, axis=1, keepdims=True))
        dmixed[at] = back
        datt[0, at] = (gate(at) * own_c[at].astype(F32) + back).astype(BF16)
        return carry + fold_rows(dh2 * mixed * factor)

    second_sum = jnp.zeros((8, width), F32)
    for k in range(2):
        x_dh2[k].wait()
        second_sum = row_tiles(rows // 2, second_back, second_sum, first=k * (rows // 2))
        x_datt[k].start()
    sent[1] = feed_rows(1).astype(BF16)
    x_feed.start()
    feed_point((2, 3), (0, 1))
    feed_own[...] = feed_rows(0)

    def attend_back(half):
        part = slice(half * rows, (half + 1) * rows)

        def step(k, carry):
            s = reversed_order(k)
            dctx = mm_nt(datt[half], w_out[s]).astype(BF16)
            query = qkv[s, half, :, 0:narrow]
            key = qkv[s, half, :, narrow : 2 * narrow]
            value = qkv[s, half, :, 2 * narrow : 3 * narrow]
            weights = prob[s, half]
            dhead = stacked(dctx)
            dweights = mm_nt(dhead, value)
            full = weights.astype(F32)
            dscores = full * (dweights - jnp.sum(dweights * full, axis=1, keepdims=True))
            dscores = dscores.astype(BF16)
            dquery = unstacked(mm(dscores, key)) * HEAD_DIM**-0.5
            dkey = mm_tn(dscores, stacked(query))
            dvalue = mm_tn(weights, dhead)
            act[s, part, 0 : 3 * narrow] = jnp.concatenate([dquery, dkey, dvalue], axis=1).astype(BF16)
            return carry

        lax.fori_loop(0, shards, step, 0)

    def dh1_rows(half):
        part = slice(half * rows, (half + 1) * rows)
        value = mm_nt(act[0, part, 0 : 3 * narrow], w_qkv[0])
        for s in range(1, shards):
            value += mm_nt(act[s, part, 0 : 3 * narrow], w_qkv[s])
        return value

    attend_back(0)
    feed_point((3, 4), (1, 2))
    total[0] = dh1_rows(0)
    turn_a[...] = jnp.transpose(h1[...].reshape(2 * rows, width))
    drain(1)
    feed_point(None, (2, 3))
    for copy in x_datt:
        copy.wait_recv()
    turn_b[...] = jnp.transpose(datt[...].reshape(2 * rows, width))

    feed_point((4, 5), None)
    attend_back(1)
    sent[0] = dh1_rows(1).astype(BF16)
    x_dh1.start()
    feed_point((5, 6), (3, 5))

    def attn_grads(k, carry):
        s = reversed_order(k)
        for a in parts_of:
            store_grads(w_up, s, a, turn_a, act[s, :, 0 : 3 * narrow], 0, 3 * narrow)
            store_grads(w_up, s, a, turn_b, ctx[s], 3 * narrow, narrow)
            core_send(1, w_up, core_a, s, a).start()

        @pl.when(k > 0)
        def _():
            stage_core(1, w_up, core_a, y_a, reversed_order(k - 1))

        return carry

    lax.fori_loop(0, shards, attn_grads, 0)
    stage_core(1, w_up, core_a, y_a, z)

    x_feed.wait()

    def finish_forward(at, squares):
        branch = attended[at] + feed_own[at] + got[1, at].astype(F32)
        update = gate(at) * branch
        sent[1, at] = (own_z[at].astype(F32) + update).astype(BF16)
        dgate = jnp.sum(own_c[at].astype(F32) * branch, axis=1, keepdims=True)
        set_column(2, at, dgate * live(at))
        return squares + fold_rows(update * update)

    squares = row_tiles(rows, finish_forward, jnp.zeros((8, width), F32))
    put(0, sent.at[1]).start()
    count = jnp.sum(valid[...].astype(F32), axis=1, keepdims=True)
    energy = jnp.sum(jnp.sum(squares, axis=0, keepdims=True), axis=1, keepdims=True)
    rms = jnp.sqrt(energy / (width * jnp.maximum(count, 1.0)))

    if quick:
        feed_point(None, (5, 6))
    else:
        run_halves(feed_half, 0, total_halves)
    ahead = jnp.where(edge, 2, 1)
    run_halves(attn_half, 0, ahead)
    x_dh1.wait()

    def first_back(at, sums):
        dh1 = total[0, at] + got[0, at].astype(F32)
        row = own_z[at].astype(F32)
        factor = lax.rsqrt(jnp.mean(row * row, axis=1, keepdims=True) + EPS)
        scaled = dh1 * first_gain[...]
        back = factor * scaled - row * (factor**3 * jnp.mean(row * scaled, axis=1, keepdims=True))
        back = back + dmixed[at] + dscore(at) * w_router[...]
        got[1, at] = (own_c[at].astype(F32) + back).astype(BF16)
        return sums[0] + fold_rows(dscore(at) * row), sums[1] + fold_rows(dh1 * row * factor)

    zero = jnp.zeros((8, width), F32)
    router_sum, first_sum = row_tiles(rows, first_back, (zero, zero))
    put(1, got.at[1]).start()
    parts = [jnp.sum(part, axis=0, keepdims=True) for part in (router_sum, first_sum, second_sum)]
    small = jnp.concatenate(parts + [jnp.zeros((5, width), F32)], axis=0)

    def small_copy(k):
        return remote(small_send.at[k], small_got.at[k], sm_s.at[k], sm_r.at[k], small_devices[k])

    hops = len(small_devices)
    for k in range(hops):
        small_send[k] = small
        small_copy(k).start()
        if k > 0:
            attn_half(ahead + k)
        if k == hops - 1:

            @pl.when(inner)
            def _():
                attn_half(ahead + hops)

        small_copy(k).wait()
        small = small + small_got[k]
        if k == 0:
            attn_half(ahead)
    stage_last(0, grads, y_f, z_f, swap_f, feed_out)

    def small_spread(far, source):
        slot = hops + source
        return remote(
            small_send.at[hops], small_got.at[slot], sm_s.at[hops + far - 1], sm_r.at[slot], (dp, lax.rem(z + far, shards))
        )

    small_send[hops] = small
    small_got[hops + z] = small
    for far in range(1, shards):
        small_spread(far, z).start()

    run_halves(attn_half, ahead + hops + jnp.where(edge, 0, 1), total_halves)
    stage_last(1, w_up, y_a, z_a, swap_a, attn_out)
    for far in range(1, shards):
        small_spread(far, lax.rem(z + shards - far, shards)).wait_recv()
        small_spread(far, z).wait_send()
    small = small_got[hops]
    for k in range(1, shards):
        small = small + small_got[hops + k]
    row_at = lax.broadcasted_iota(jnp.int32, (8, 1), 0)
    small_send[0] = jnp.where(row_at == 3, rms, small)
    put(2, small_send.at[0]).start()
    stage_out(0, swap_f, feed_out)
    put(4, feed_out).start()
    put_half(x, 0).start()
    stage_out(1, swap_a, attn_out)
    put_half(1 - x, 1).start()

    drain(0)
    for copy in (x_h1, x_dfeed, *x_h2, *x_datt):
        copy.wait_send()

    for group, core_got, y_got, z_got in ((0, core_f, y_f, z_f), (1, core_a, y_a, z_a)):
        remote(core_got, core_got, gc_s.at[group], gc_r.at[group, 0, 0], core_dev).wait_send()
        remote(y_got, y_got, gy_s.at[group], gy_r.at[0, 0], y_dev).wait_send()
        moved = z_got.at[0 : shards - 1]
        remote(moved, moved, gz_s.at[group], gz_r.at[0, 0], up_dev).wait_send()

    swap(0, swap_f, 0).wait_send()
    for c in pieces(1):
        swap(1, swap_a, c).wait_send()
    for k, src in enumerate((sent.at[1], got.at[1], small_send.at[0], attn_out, feed_out)):
        if k != 3:
            put(k, src).wait()
    put_half(x, 0).wait()
    put_half(1 - x, 1).wait()


def run_block(size, operands):
    shards, rows, width = size["S"], size["R"], size["D"]
    heads, narrow, hidden, cut = size["hh"], size["n"], size["f"], size["DB"]
    mats = (2 if size["joined"] else 4) + 4
    stages = 3 + shards
    attn, feed = 4 * narrow, 2 * hidden
    dma = pltpu.SemaphoreType.DMA
    vmem = lambda *shape: pltpu.VMEM(shape, BF16)
    full = lambda *shape: pltpu.VMEM(shape, F32)
    scratch = [
        vmem(shards, width, 3 * narrow),
        vmem(shards, narrow, width),
        vmem(shards, 2, 2, 2, cut, hidden),
        vmem(shards, hidden, width),
        *[vmem(2, rows, width) for _ in range(4)],
        *[vmem(width, 2 * rows) for _ in range(2)],
        vmem(shards, 2, rows, 3 * narrow),
        vmem(shards, 2 * rows, narrow),
        vmem(shards, 2, heads * rows, rows),
        vmem(shards, 2 * rows, hidden),
        vmem(shards, 2 * rows, hidden),
        full(2, rows, width),
        full(2, rows, hidden),
        vmem(2, rows, width),
        vmem(2, rows, width),
        vmem(rows, width),
        vmem(rows, width),
        *[full(rows, width) for _ in range(3)],
        full(rows, 128),
        vmem(shards, 2, 2, 2, cut, feed),
        vmem(shards, 2, 2, cut, feed),
        vmem(shards, 2, cut, feed),
        vmem(shards + 1, 2, cut, feed),
        vmem(shards, 2, 2, cut, attn),
        vmem(shards, 2, cut, attn),
        vmem(shards + 1, 2, cut, attn),
        vmem(2, cut, feed),
        vmem(2, cut, attn),
        full(2, cut, attn),
        full(2, cut, feed),
        full(stages, 8, width),
        full(stages, 8, width),
        pltpu.VMEM((1, rows), jnp.int32),
        pltpu.VMEM((1, size["L"]), jnp.int32),
        *[full(1, width) for _ in range(3)],
        dma((mats,)),
        dma((2, 2)),
        dma((7,)),
        dma((5,)),
        dma((2, shards + 1)),
        dma((mats, shards)),
        dma((4,)),
        dma((mats, shards)),
        dma((2,)),
        dma((2, shards)),
        dma((12,)),
        dma((12,)),
        dma((2,)),
        dma((2, shards, 2)),
        dma((2,)),
        dma((shards, 6)),
        dma((2,)),
        dma((shards + 1, 6)),
        dma((3,)),
        dma((3,)),
        dma((stages,)),
        dma((stages,)),
        dma((2,)),
    ]
    far = pl.BlockSpec(memory_space=pl.ANY)
    outs = [
        jax.ShapeDtypeStruct((rows, width), BF16),
        jax.ShapeDtypeStruct((rows, width), BF16),
        jax.ShapeDtypeStruct((8, width), F32),
        jax.ShapeDtypeStruct((2, cut, attn), F32),
        jax.ShapeDtypeStruct((2, cut, feed), F32),
    ]
    return pl.pallas_call(
        functools.partial(block_kernel, size),
        out_shape=outs,
        in_specs=[far] * len(operands),
        out_specs=[pl.BlockSpec(memory_space=pltpu.HBM)] * len(outs),
        scratch_shapes=scratch,
        compiler_params=pltpu.CompilerParams(
            collective_id=0, has_side_effects=True, vmem_limit_bytes=64 * 2**20 - 65536
        ),
    )(*operands)


def place_kernel(size, assemble, routed, small, tokens, cotangent, *refs):
    length, width, rows = size["L"], size["D"], size["R"]
    gathered, refs = refs[: 4 if assemble else 2], refs[4 if assemble else 2 :]
    outs, refs = refs[: 12 if assemble else 2], refs[12 if assemble else 2 :]
    bases, staged, refs = refs[:2], refs[2 : 2 + len(gathered)], refs[2 + len(gathered) :]
    finals, (pick, keep, in_sem, out_sem, part_sem, final_sem) = refs[:-6], refs[-6:]
    block = 512
    steps = width // block

    def moving(src, dst, sem, k, b):
        at = (slice(None), pl.ds(b * block, block))
        return pltpu.make_async_copy(src[k].at[at], dst[k].at[at], sem.at[k, b])

    sources = (tokens, cotangent)
    parts = [pltpu.make_async_copy(src, dst, part_sem.at[k]) for k, (src, dst) in enumerate(zip(gathered, staged))]
    for copy in parts[:2]:
        copy.start()
    for b in range(steps):
        for k in range(2):
            moving(sources, bases, in_sem, k, b).start()
    for copy in parts[2:]:
        copy.start()
    line = lax.broadcasted_iota(jnp.int32, (length, rows), 0)
    chosen = jnp.where(line == routed[...], 1.0, 0.0)
    pick[...] = chosen.astype(BF16)
    keep[...] = jnp.broadcast_to((1.0 - jnp.sum(chosen, axis=1, keepdims=True)).astype(BF16), keep.shape)
    for copy in parts[:2]:
        copy.wait()
    for b in range(steps):
        for k in range(2):
            at = slice(b * block, (b + 1) * block)
            moving(sources, bases, in_sem, k, b).wait()
            kept = jnp.concatenate([keep[...]] * (block // 128), axis=1)
            bases[k][:, at] = mm(pick[...], staged[k][:, at]).astype(BF16) + bases[k][:, at] * kept
            moving(bases, outs, out_sem, k, b).start()
    last = []
    if assemble:
        for copy in parts[2:]:
            copy.wait()
        for k, value in enumerate(weight_outputs(size, *staged[2:])):
            finals[k][...] = value
            last.append(pltpu.make_async_copy(finals[k], outs[2 + k], final_sem.at[k]))
            last[-1].start()
        for k in range(3):
            outs[8 + k][...] = small[k : k + 1, :]
        outs[11][...] = small[3:4, 0:1]
    for b in range(steps):
        for k in range(2):
            moving(bases, outs, out_sem, k, b).wait()
    for copy in last:
        copy.wait()


def weight_outputs(size, attn, feed):
    narrow, hidden = size["n"], size["f"]

    def side_by_side(ref, lo, count):
        return jnp.concatenate([ref[0, :, lo : lo + count], ref[1, :, lo : lo + count]], axis=1)

    return (
        side_by_side(attn, 0, narrow),
        side_by_side(attn, narrow, narrow),
        side_by_side(attn, 2 * narrow, narrow),
        side_by_side(attn, 3 * narrow, narrow).T,
        side_by_side(feed, 0, hidden),
        side_by_side(feed, hidden, hidden).T,
    )


def place_rows(size, routed, tokens, cotangent, rows_res, rows_grad, small, attn, feed, assemble):
    length, width, rows = size["L"], size["D"], size["R"]
    cut, narrow, hidden = size["DB"], size["n"], size["f"]
    whole = lambda *shape: pl.BlockSpec(shape, lambda i: (0,) * len(shape))
    far = pl.BlockSpec(memory_space=pltpu.HBM)
    outs, out_specs = [jax.ShapeDtypeStruct((length, width), BF16)] * 2, [far] * 2
    gathered, finals = [rows_res, rows_grad], []
    if assemble:
        gathered += [attn, feed]
        finals = [(cut, 2 * narrow)] * 3 + [(2 * narrow, cut), (cut, 2 * hidden), (2 * hidden, cut)]
        tiny = [(1, width)] * 3 + [(1, 1)]
        outs = outs + [jax.ShapeDtypeStruct(shape, F32) for shape in finals + tiny]
        out_specs = out_specs + [far] * len(finals) + [whole(*shape) for shape in tiny]
    dma = pltpu.SemaphoreType.DMA
    return pl.pallas_call(
        functools.partial(place_kernel, size, assemble),
        grid=(1,),
        out_shape=outs,
        in_specs=[whole(1, rows), whole(*small.shape)] + [far] * (2 + len(gathered)),
        out_specs=out_specs,
        scratch_shapes=[
            *[pltpu.VMEM((length, width), BF16) for _ in range(2)],
            *[pltpu.VMEM(part.shape, part.dtype) for part in gathered],
            *[pltpu.VMEM(shape, F32) for shape in finals],
            pltpu.VMEM((length, rows), BF16),
            pltpu.VMEM((length, 128), BF16),
            dma((2, width // 512)),
            dma((2, width // 512)),
            dma((4,)),
            dma((6,)),
        ],
        compiler_params=pltpu.CompilerParams(vmem_limit_bytes=60 * 2**20),
    )(routed, small, tokens, cotangent, *gathered)


def shards_of(
    groups,
    tokens,
    cotangent,
    routed,
    valid_mask,
    w_router,
    first_gain,
    query_weight,
    key_weight,
    value_weight,
    output_weight,
    second_gain,
    up_weight,
    down_weight,
):
    shards, data = lax.axis_size("mp"), lax.axis_size("dp")
    _, length, width = tokens.shape
    rows = routed.shape[1]
    narrow = query_weight.shape[1] // 2
    hidden = up_weight.shape[1] // 2
    cut = width // 8
    chips_x = 1 << ((data // 2).bit_length() - 1) // 2
    size = dict(
        S=shards, ybit=2 * chips_x, R=rows, D=width, L=length, hh=narrow // HEAD_DIM,
        n=narrow, f=hidden, DB=cut, joined=narrow % 128 != 0,
    )
    dp = lax.axis_index("dp")
    x, y = (dp // 2) % 2, (dp // size["ybit"]) % 2
    qkv = (query_weight, key_weight, value_weight)
    if size["joined"]:
        halves = [lax.dynamic_slice_in_dim(weight, x * narrow, narrow, 1) for weight in qkv]
        qkv = (jnp.concatenate(halves, axis=1),)
    row = lambda vector: vector.reshape(1, width)
    operands = (
        tokens.reshape(-1, rows, width), cotangent.reshape(-1, rows, width), routed, valid_mask, row(w_router), row(first_gain), row(second_gain),
        *qkv, output_weight, up_weight.reshape(2, 2, 2, cut, 2 * hidden), down_weight,
    )
    rows_res, rows_grad, small, attn, feed = run_block(size, operands)
    whole_group = data == 8
    rms = small[3, 0:1]
    if not whole_group:
        block = 4 * y + 2 * x + dp % 2

        def over_groups(part):
            base = jnp.zeros((2, width, part.shape[2]), F32)
            placed = lax.dynamic_update_slice_in_dim(base, part, block * cut, 1)
            return lax.psum_scatter(placed, "dp", scatter_dimension=1, tiled=True)

        attn, feed = over_groups(attn), over_groups(feed)
        small = lax.psum(small, "dp") / 8.0
    placed = place_rows(size, routed, tokens[0], cotangent[0], rows_res, rows_grad, small, attn, feed, whole_group)
    residual, grad_tokens = placed[:2]
    if whole_group:
        vectors = [vector.reshape(width) for vector in placed[8:11]]
        weights, rms = placed[2:8], placed[11].reshape(1)
    else:
        vectors, weights = [small[k] for k in range(3)], weight_outputs(size, attn, feed)
    grad_query, grad_key, grad_value, grad_output, grad_up, grad_down = weights
    return (
        residual[None],
        grad_tokens[None],
        rms,
        vectors[0],
        vectors[1],
        grad_query,
        grad_key,
        grad_value,
        grad_output,
        vectors[2],
        grad_up,
        grad_down,
    )


def solution(mesh):
    in_specs = (
        P(("dp", "mp"), None, None),
        P(("dp", "mp"), None, None),
        P(("dp", "mp"), None),
        P(("dp", "mp"), None),
        P(),
        P(),
        P(None, "mp"),
        P(None, "mp"),
        P(None, "mp"),
        P("mp", None),
        P(),
        P(None, "mp"),
        P("mp", None),
    )
    out_specs = (
        P(("dp", "mp"), None, None),
        P(("dp", "mp"), None, None),
        P(("dp", "mp")),
        P(),
        P(),
        P("dp", "mp"),
        P("dp", "mp"),
        P("dp", "mp"),
        P("mp", "dp"),
        P(),
        P("dp", "mp"),
        P("mp", "dp"),
    )
    body = functools.partial(shards_of, mesh.shape["dp"] // 8)
    return jax.shard_map(body, mesh=mesh, in_specs=in_specs, out_specs=out_specs, check_vma=False)
```
